32 devices in a mesh: dp: 16 (over z, y, x), tensor: 2 (over core).
Axes of the slice: x: 2, y: 2, z: 4, core: 2. Of those that a mesh axis runs over, the one named last changes fastest.
Arguments:
- tokens: bfloat16 [32, 192, 2048], P('dp'), may hold values from -6 to 6
- cotangent: bfloat16 [32, 192, 2048], P('dp'), may hold values from -6 to 6
- lengths: int32 [32], replicated, may hold values from 1 to 192, 3840 in all
- permutation: int32 [32], replicated, may hold values from 0 to 31, each once
- w_qkv: float32 [2048, 6144], P('dp', 'tensor'), may hold values from -0.125 to 0.125
- w_dense: float32 [2048, 2048], P('dp', 'tensor'), may hold values from -0.375 to 0.375
- w_fc1: float32 [2048, 8192], P('dp', 'tensor'), may hold values from -0.125 to 0.125
- w_fc2: float32 [2048, 8192], P('dp', 'tensor'), may hold values from -0.0625 to 0.0625
- norm_vectors: float32 [6, 2048], replicated, may hold values from -1 to 4
- split_biases: float32 [2, 7168], P('tensor'), may hold values from -0.8 to 0.8
- row_state: float32 [4, 2048], P(None, 'dp'), may hold values from 384 to 12288
- col_state: float32 [2, 12288], P('tensor'), may hold values from 384 to 12288
- norm_moment: float32 [6, 2048], replicated, may hold values from 768 to 12288
- bias_moment: float32 [2, 7168], P('tensor'), may hold values from 384 to 6144
Outputs:
- mixed: bfloat16 [32, 192, 2048], P('dp')
- grad_tokens: bfloat16 [32, 192, 2048], P('dp')
- grad_qkv: float32 [2048, 6144], P('dp', 'tensor')
- grad_dense: float32 [2048, 2048], P('dp', 'tensor')
- grad_fc1: float32 [2048, 8192], P('dp', 'tensor')
- grad_fc2: float32 [2048, 8192], P('dp', 'tensor')
- new_qkv: float32 [2048, 6144], P('dp', 'tensor')
- new_dense: float32 [2048, 2048], P('dp', 'tensor')
- new_fc1: float32 [2048, 8192], P('dp', 'tensor')
- new_fc2: float32 [2048, 8192], P('dp', 'tensor')
- copy_qkv: bfloat16 [2048, 6144], P('dp', 'tensor')
- copy_dense: bfloat16 [2048, 2048], P('dp', 'tensor')
- copy_fc1: bfloat16 [2048, 8192], P('dp', 'tensor')
- copy_fc2: bfloat16 [2048, 8192], P('dp', 'tensor')
- row_state_new: float32 [4, 2048], P(None, 'dp')
- col_state_new: float32 [2, 12288], P('tensor')
- norm_grad: float32 [6, 2048], replicated
- norm_moment_new: float32 [6, 2048], replicated
- norm_new: float32 [6, 2048], replicated
- bias_grad: float32 [2, 7168], P('tensor')
- bias_moment_new: float32 [2, 7168], P('tensor')
- bias_new: float32 [2, 7168], P('tensor')
The draws below stay inside these ranges and needn't reach their ends.
Inputs may be any that keep to these rules, and one draw needn't show every extreme that they name: `permutation`: each sequence once.
All inputs are finite; a program needn't handle non-finite values.
Results may differ from the reference program's by a relative error of at most 0.03.
Values may be sent and summed in bfloat16 or wider, within the bound.
A program may use at most 512 MiB of HBM per device.

```python
import math
import jax
import jax.numpy as jnp
import numpy as np
from jax import lax

D = 2048
FF = 8192
HEADS = 8
HEAD_DIM = 256
ROT_DIMS = 64
L = 192
SEQS = 32
N_TENSOR = 2


def draw_norm_vectors(key, part):
    key = jax.random.fold_in(key, 11)
    first, second = jax.random.split(key, 2)
    place = jnp.arange(D, dtype=jnp.float32) / D
    rise = 0.6 * jnp.exp(jnp.log(3.0) * place)
    rough = jax.random.uniform(first, (2, D), jnp.float32, 0.75, 1.33)
    shifts = 0.2 * jnp.clip(jax.random.normal(second, (4, D), jnp.float32), -4.0, 4.0)
    gains = rise[None, :] * rough
    return jnp.stack([gains[0], shifts[0], gains[1], shifts[1], shifts[2], shifts[3]])


def steps_of(stream_key, extent, shards, low, top_value):
    level = 1.0
    for dim, shards_of in shards:
        steps = jax.random.uniform(jax.random.fold_in(jax.random.fold_in(stream_key, 6), dim), (shards_of,), jnp.float32, low / len(shards), top_value / len(shards))
        level = level * jnp.repeat(jnp.exp(steps), extent[dim] // shards_of).reshape((-1,) + (1,) * (len(extent) - 1 - dim))
    return level


def split_up(count, total, bound, skew):
    portions = [(1 << 20) // math.isqrt(grade ** skew) + 1 for grade in range(2, count + 1)]
    surplus, given = total - bound - (count - 1), [1] * (count - 1)
    while surplus > 0:
        candidates = [i for i in range(count - 1) if given[i] < bound]
        pool, budget = sum([portions[i] for i in candidates]), surplus
        for i in candidates:
            extra = min(bound - given[i], max(1, budget * portions[i] // pool), surplus)
            given[i] = given[i] + extra
            surplus = surplus - extra
    return np.array([bound] + given)


def uneven_parts(stream_key, amount, total, reach, lean):
    if amount == 2:
        one = jax.random.randint(stream_key, (), max(1, total - reach), min(reach, total - 1) + 1)
        return jnp.stack([one, total - one])
    sizes = jnp.asarray(split_up(amount, total, reach, lean), jnp.int32)
    couples = (amount - 1) // 2
    source_of, receiver = sizes[1:1 + 2 * couples:2], sizes[2:2 + 2 * couples:2]
    margin = jnp.minimum(source_of - 1, reach - receiver)
    moved = jax.random.randint(jax.random.fold_in(stream_key, 1), (couples,), 0, 1 << 20) % (margin + 1)
    sizes = sizes.at[1:1 + 2 * couples:2].set(source_of - moved).at[2:2 + 2 * couples:2].set(receiver + moved)
    return sizes[jax.random.permutation(jax.random.fold_in(stream_key, 2), amount)]


def noise(rng, shape, width, reach, cuts=(), kind=jnp.bfloat16):
    factor_of = steps_of(rng, shape, cuts, -0.22, 0.18) if cuts else 1.0
    drawn = jax.random.normal(rng, shape, jnp.float32) * width * factor_of
    return jnp.minimum(jnp.maximum(drawn, -reach), reach).astype(kind)


def setup_inputs(seed: int = 0) -> dict:
    key_of = jax.random.split(jax.random.key(seed), 15)
    tokens = noise(key_of[0], (SEQS, L, D), 1.0, 6.0, ((0, 16),))
    cotangent = noise(key_of[1], (SEQS, L, D), 1.0, 6.0, ((0, 16),))
    lengths = uneven_parts(key_of[2], SEQS, SEQS * L * 5 // 8, L, 1).astype(jnp.int32)
    permutation = jax.random.permutation(key_of[3], SEQS).astype(jnp.int32)
    w_qkv = noise(key_of[4], (D, 3 * D), D ** -0.5, 0.125, ((0, 16), (1, 2)), jnp.float32)
    w_dense = noise(key_of[5], (D, D), (D // 8) ** -0.5, 0.375, ((0, 16), (1, 2)), jnp.float32)
    w_fc1 = noise(key_of[6], (D, FF), D ** -0.5, 0.125, ((0, 16), (1, 2)), jnp.float32)
    w_fc2 = noise(key_of[7], (D, FF), FF ** -0.5, 0.0625, ((0, 16), (1, 2)), jnp.float32)
    norm_vectors = draw_norm_vectors(jax.random.fold_in(key_of[14], 71), 0)
    split_biases = noise(key_of[9], (N_TENSOR, (3 * D + FF) // N_TENSOR), 0.2, 0.8, ((0, 2),), jnp.float32)
    row_state = jnp.clip(jnp.exp(math.log(12288.0) - 3.465736 * jax.random.uniform(key_of[10], (4, D), jnp.float32) ** steps_of(key_of[10], (4, D), ((1, 16),), -0.2, 0.2)), 384.0, 12288.0)
    col_state = jnp.clip(jnp.exp(math.log(12288.0) - 3.465736 * jax.random.uniform(key_of[11], (N_TENSOR, (4 * D + 2 * FF) // N_TENSOR), jnp.float32) ** steps_of(key_of[11], (N_TENSOR, (4 * D + 2 * FF) // N_TENSOR), ((0, 2),), -0.2, 0.2)), 384.0, 12288.0)
    norm_moment = jnp.clip(jnp.exp(jax.random.uniform(key_of[12], (6, D), jnp.float32, math.log(768.0), math.log(12288.0))), 768.0, 12288.0)
    bias_moment = jnp.clip(jnp.exp(math.log(6144.0) - 2.7725887 * jax.random.uniform(key_of[13], (N_TENSOR, (3 * D + FF) // N_TENSOR), jnp.float32) ** steps_of(key_of[13], (N_TENSOR, (3 * D + FF) // N_TENSOR), ((0, 2),), -0.2, 0.2)), 384.0, 6144.0)
    return dict(tokens=tokens, cotangent=cotangent, lengths=lengths, permutation=permutation, w_qkv=w_qkv, w_dense=w_dense, w_fc1=w_fc1, w_fc2=w_fc2, norm_vectors=norm_vectors, split_biases=split_biases, row_state=row_state, col_state=col_state, norm_moment=norm_moment, bias_moment=bias_moment)


@jax.custom_vjp
def low(v):
    return lax.optimization_barrier(v.astype(jnp.bfloat16)).astype(jnp.float32)

@jax.custom_vjp
def low_back(v):
    return v

def low_keep(v):
    return (low(v), None)

def low_pass(kept, grad):
    return (grad,)

def back_keep(v):
    return (v, None)

def back_low(kept, grad):
    return (low(grad),)
low.defvjp(low_keep, low_pass)
low_back.defvjp(back_keep, back_low)
eps_norm = 1e-05
eps_second = 1e-30
decay = 0.5
rate_scale = 1.0
rate_norm = 0.5
rate_vector = 0.05
neg_large = -1e+30
highest = lax.Precision.HIGHEST

def matmul(left, right):
    return jnp.dot(left, right, precision=highest, preferred_element_type=jnp.float32)

def layer_norm(values, gain, shift):
    centre = values - lax.optimization_barrier(jnp.mean(values, -1, keepdims=True))
    spread = lax.optimization_barrier(jnp.mean(centre * centre, -1, keepdims=True))
    return centre * lax.rsqrt(spread + eps_norm) * gain + shift

def rotary_tables():
    half = ROT_DIMS // 2
    freq = 10000.0 ** (-2.0 * jnp.arange(half, dtype=jnp.float32) / ROT_DIMS)
    angle = jnp.arange(L, dtype=jnp.float32)[:, None] * freq[None, :]
    return (jnp.cos(angle), jnp.sin(angle))

def rotate(values, cosine, sine):
    half = ROT_DIMS // 2
    first = values[..., :half]
    second = values[..., half:ROT_DIMS]
    cos_b = cosine[:, None, :]
    sin_b = sine[:, None, :]
    return jnp.concatenate([first * cos_b - second * sin_b, second * cos_b + first * sin_b, values[..., ROT_DIMS:]], -1)

def block(inputs, w_qkv, w_dense, w_fc1, w_fc2, vectors, bias_qkv, bias_mlp, valid, causal, cosine, sine):
    norm_one = low(layer_norm(inputs, vectors[0], vectors[1]))
    norm_two = low(layer_norm(inputs, vectors[2], vectors[3]))
    qkv_all = low_back(matmul(norm_one, w_qkv) + bias_qkv).reshape(L, HEADS, 3, HEAD_DIM)
    query = low(rotate(qkv_all[:, :, 0], cosine, sine))
    keys = low(rotate(qkv_all[:, :, 1], cosine, sine))
    values = low(qkv_all[:, :, 2])
    scores = low_back(jnp.einsum('qhd,khd->hqk', query, keys, precision=highest) / math.sqrt(HEAD_DIM))
    scores = jnp.where(causal, scores, neg_large)
    peak = lax.optimization_barrier(jnp.max(scores, -1, keepdims=True))
    expo = jnp.exp(scores - peak)
    probs = low(expo / lax.optimization_barrier(jnp.sum(expo, -1, keepdims=True)))
    heads_out = low_back(low(jnp.einsum('hqk,khd->qhd', probs, values, precision=highest))).reshape(L, D)
    attn_out = matmul(heads_out, w_dense.T)
    pre_act = low_back(matmul(norm_two, w_fc1) + bias_mlp)
    hidden = low(jax.nn.gelu(pre_act, approximate=False))
    mlp_out = matmul(hidden, w_fc2.T)
    return valid[:, None] * (inputs + attn_out + mlp_out + vectors[4] + vectors[5])

def reference(tokens, cotangent, lengths, permutation, w_qkv, w_dense, w_fc1, w_fc2, norm_vectors, split_biases, row_state, col_state, norm_moment, bias_moment):
    qkv_part = 3 * D // N_TENSOR
    dense_part = D // N_TENSOR
    hidden_part = FF // N_TENSOR
    bias_qkv = split_biases[:, :qkv_part].reshape(-1)
    bias_mlp = split_biases[:, qkv_part:].reshape(-1)
    places = jnp.arange(L, dtype=jnp.int32)
    causal = places[:, None] >= places[None, :]
    cosine, sine = rotary_tables()
    params = (w_qkv, w_dense, w_fc1, w_fc2, norm_vectors, bias_qkv, bias_mlp)

    def one_sequence(carry, item):
        rows_in, rows_back, length = item
        valid = (places < length).astype(jnp.float32)

        def forward(inputs, p_qkv, p_dense, p_fc1, p_fc2, p_vec, p_bq, p_bm):
            return block(inputs, p_qkv, p_dense, p_fc1, p_fc2, p_vec, p_bq, p_bm, valid, causal, cosine, sine)
        result, pull = jax.vjp(forward, rows_in.astype(jnp.float32), *params)
        grads = pull(rows_back.astype(jnp.float32))
        carry = tuple((total + grad for total, grad in zip(carry, grads[1:])))
        return (carry, (result.astype(jnp.bfloat16), grads[0].astype(jnp.bfloat16)))
    start = tuple((jnp.zeros(item.shape, jnp.float32) for item in params))
    sums, (outputs, input_grads) = lax.scan(one_sequence, start, (tokens, cotangent, lengths))
    grad_qkv, grad_dense, grad_fc1, grad_fc2, norm_grad, grad_bq, grad_bm = sums
    mixed = jnp.take(outputs, permutation, axis=0)
    offsets = (0, qkv_part, qkv_part + dense_part, qkv_part + dense_part + hidden_part, qkv_part + dense_part + 2 * hidden_part)
    fans = (D, D // 8, D, FF)
    weights = (w_qkv, w_dense, w_fc1, w_fc2)
    gradients = (grad_qkv, grad_dense, grad_fc1, grad_fc2)
    new_list = []
    row_list = []
    col_list = []
    for index in range(4):
        grad = gradients[index]
        col_old = col_state[:, offsets[index]:offsets[index + 1]].reshape(-1)
        square = grad * grad + eps_second
        row_new = decay * row_state[index] + (1.0 - decay) * lax.optimization_barrier(jnp.mean(square, 1))
        col_new = decay * col_old + (1.0 - decay) * lax.optimization_barrier(jnp.mean(square, 0))
        second = row_new[:, None] * col_new[None, :] / jnp.mean(row_new)
        new_list.append(weights[index] - rate_scale / math.sqrt(fans[index]) * grad * lax.rsqrt(second))
        row_list.append(row_new)
        col_list.append(col_new.reshape(N_TENSOR, -1))
    row_state_new = jnp.stack(row_list)
    col_state_new = jnp.concatenate(col_list, 1)
    norm_moment_new = decay * norm_moment + (1.0 - decay) * (norm_grad * norm_grad + eps_second)
    norm_new = norm_vectors - rate_norm * norm_grad * lax.rsqrt(norm_moment_new)
    bias_grad = jnp.concatenate([grad_bq.reshape(N_TENSOR, qkv_part), grad_bm.reshape(N_TENSOR, hidden_part)], 1)
    bias_moment_new = decay * bias_moment + (1.0 - decay) * (bias_grad * bias_grad + eps_second)
    bias_new = split_biases - rate_vector * bias_grad * lax.rsqrt(bias_moment_new)
    return (mixed, input_grads, grad_qkv, grad_dense, grad_fc1, grad_fc2, new_list[0], new_list[1], new_list[2], new_list[3], new_list[0].astype(jnp.bfloat16), new_list[1].astype(jnp.bfloat16), new_list[2].astype(jnp.bfloat16), new_list[3].astype(jnp.bfloat16), row_state_new, col_state_new, norm_grad, norm_moment_new, norm_new, bias_grad, bias_moment_new, bias_new)
```

```python
from functools import partial
import math

import jax
import jax.numpy as jnp
from jax import lax
from jax.experimental import pallas as pl
from jax.experimental.pallas import tpu as pltpu
from jax.sharding import PartitionSpec as P

D = 2048
FF = 8192
HEADS = 8
LINE = 4

eps_norm = 1e-05
eps_second = 1e-30
decay = 0.5
rate_scale = 1.0
rate_norm = 0.5
rate_vector = 0.05
neg_large = -1e30

MESH = pl.DeviceIdType.MESH
ANY = pl.BlockSpec(memory_space=pl.ANY)
VMEM = pl.BlockSpec(memory_space=pltpu.VMEM)
SMEM = pl.BlockSpec(memory_space=pltpu.SMEM)


def rotary_tables(slot_len, rot_dims):
    half = rot_dims // 2
    freq = 10000.0 ** (-2.0 * jnp.arange(half, dtype=jnp.float32) / rot_dims)
    angle = jnp.arange(slot_len, dtype=jnp.float32)[:, None] * freq[None, :]
    return (jnp.cos(angle), jnp.sin(angle))


def rotate(values, cosine, sine, rot_dims):
    half = rot_dims // 2
    first = values[..., :half]
    second = values[..., half:rot_dims]
    return jnp.concatenate(
        [first * cosine - second * sine, second * cosine + first * sine, values[..., rot_dims:]], -1
    )


def contract_last(left, right):
    return lax.dot_general(
        left, right, (((1,), (1,)), ((), ())), preferred_element_type=jnp.float32
    )


def contract_first(left, right):
    return lax.dot_general(
        left, right, (((0,), (0,)), ((), ())), preferred_element_type=jnp.float32
    )


class Place:
    def __init__(self, groups):
        self.groups = groups
        data = lax.axis_index("dp")
        self.core = lax.axis_index("tensor")
        self.other = 1 - self.core
        self.line = data // groups
        self.group = data % groups

    def at(self, line, group, core):
        return (line * self.groups + group, core)

    def line_to(self, step):
        return (self.line + step) % LINE

    def line_from(self, step):
        return (self.line + LINE - step) % LINE

    def group_to(self, step):
        g = self.group
        if self.groups == 4:
            if step == 1:
                return g + 1 - 2 * (g % 2)
            if step == 2:
                return (g + 2) % 4
            return 3 - g
        return (g + step) % self.groups

    def group_from(self, step):
        if self.groups == 4:
            return self.group_to(step)
        return (self.group + self.groups - step) % self.groups

    def greet(self):
        barrier = pltpu.get_barrier_semaphore()
        count = 0
        for step in range(1, LINE):
            for core in (self.core, self.other):
                pl.semaphore_signal(
                    barrier, inc=1, device_id=self.at(self.line_to(step), self.group, core), device_id_type=MESH
                )
                count += 1
        for step in range(1, self.groups):
            pl.semaphore_signal(
                barrier, inc=1, device_id=self.at(self.line, self.group_to(step), self.core), device_id_type=MESH
            )
            count += 1
        pl.semaphore_signal(
            barrier, inc=1, device_id=self.at(self.line, self.group, self.other), device_id_type=MESH
        )
        pl.semaphore_wait(barrier, count + 1)


def remote(src, dst, send, recv, device):
    return pltpu.make_async_remote_copy(
        src_ref=src, dst_ref=dst, send_sem=send, recv_sem=recv, device_id=device, device_id_type=MESH
    )


def gather_kernel(groups, cols, *refs):
    count = len(cols)
    w_in = refs[:count]
    acts_in = refs[count : count + 2]
    w_out = refs[count + 2 : 2 * count + 2]
    acts_out = refs[2 * count + 2 : 2 * count + 4]
    (one_s, one_r, two_s, two_r, three_s, three_r, up_s, up_r, down_s, down_r, sib_s, sib_r, here) = refs[
        2 * count + 4 :
    ]
    me = Place(groups)
    c, g, k = me.line, me.group, me.core
    me.greet()
    sibling = me.at(c, g, me.other)
    sends = []
    started = []

    def block(ref, line, width):
        return ref.at[:, pl.ds(pl.multiple_of(line * width, 128), width)]

    def slot(line, group):
        return line * groups + group

    def hop_up(which, hop, start):
        origin = c - (hop - 1)
        copy = remote(
            acts_in[which].at[k] if hop == 1 else acts_out[which].at[origin, k],
            acts_out[which].at[origin, k],
            up_s.at[which, hop - 1],
            up_r.at[which, hop - 1],
            me.at(c + 1, g, k),
        )
        pl.when((c < LINE - 1) & (origin >= 0))(copy.start if start else copy.wait_send)

    def hop_down(which, hop, start):
        origin = c + (hop - 1)
        copy = remote(
            acts_in[which].at[k] if hop == 1 else acts_out[which].at[origin, k],
            acts_out[which].at[origin, k],
            down_s.at[which, hop - 1],
            down_r.at[which, hop - 1],
            me.at(c - 1, g, k),
        )
        pl.when((c > 0) & (origin < LINE))(copy.start if start else copy.wait_send)

    def to_sibling(which, way, hop, start):
        origin = c - hop if way == 0 else c + hop
        copy = remote(
            acts_out[which].at[origin, k],
            acts_out[which].at[origin, k],
            sib_s.at[which, way, hop - 1],
            sib_r.at[which, way, hop - 1],
            sibling,
        )
        ok = (origin >= 0) if way == 0 else (origin < LINE)
        pl.when(ok)(copy.start if start else copy.wait_send)

    def arrive(which, way, hop):
        origin = c - hop if way == 0 else c + hop
        sem = (up_r if way == 0 else down_r).at[which, hop - 1]
        dst = acts_out[which].at[origin, k]
        ok = (origin >= 0) if way == 0 else (origin < LINE)
        pl.when(ok)(remote(dst, dst, sem, sem, sibling).wait_recv)

    def arrive_sibling(which, way, hop):
        origin = c - hop if way == 0 else c + hop
        sem = sib_r.at[which, way, hop - 1]
        dst = acts_out[which].at[origin, me.other]
        ok = (origin >= 0) if way == 0 else (origin < LINE)
        pl.when(ok)(remote(dst, dst, sem, sem, sibling).wait_recv)

    local = []
    for which in range(2):
        local.append(pltpu.make_async_copy(acts_in[which], acts_out[which].at[c], here.at[count + which]))
    for m in range(count):
        local.append(pltpu.make_async_copy(block(w_in[m], c, cols[m]), w_out[m].at[slot(c, g)], here.at[m]))

    def stage_one(m):
        for step in range(1, LINE):
            to = me.line_to(step)
            copy = remote(
                block(w_in[m], to, cols[m]),
                w_out[m].at[slot(c, g)],
                one_s.at[m, step],
                one_r.at[m, step],
                me.at(to, g, k),
            )
            copy.start()
            sends.append(copy)

    def wait_one(m, step):
        dst = w_out[m].at[slot(me.line_from(step), g)]
        remote(dst, dst, one_s.at[m, step], one_r.at[m, step], sibling).wait_recv()

    def stage_two(m, step):
        where = w_out[m].at[slot(me.line_from(step), g)]
        src = block(w_in[m], c, cols[m]) if step == 0 else where
        for peer in range(1, 3 if groups == 4 else groups):
            copy = remote(
                src, where, two_s.at[m, step, peer], two_r.at[m, step, peer], me.at(c, me.group_to(peer), k)
            )
            copy.start()
            sends.append(copy)

    def wait_two(m, step, peer):
        dst = w_out[m].at[slot(me.line_from(step), me.group_from(peer))]
        remote(dst, dst, two_s.at[m, step, peer], two_r.at[m, step, peer], sibling).wait_recv()

    def stage_three(m, step):
        source, target = (1, 2) if step % 2 == 0 else (2, 1)
        where = w_out[m].at[slot(me.line_from(step), me.group_to(source))]
        copy = remote(where, where, three_s.at[m, step], three_r.at[m, step], me.at(c, me.group_to(target), k))
        copy.start()
        sends.append(copy)

    def wait_three(m, step):
        dst = w_out[m].at[slot(me.line_from(step), me.group_to(3))]
        remote(dst, dst, three_s.at[m, step], three_r.at[m, step], sibling).wait_recv()

    def relay(m):
        for step in range(LINE):
            for peer in (1, 2):
                wait_two(m, step, peer)
            stage_three(m, step)

    def pass_on(which, hop):
        for way in range(2):
            arrive(which, way, hop)
            if hop < LINE - 1:
                (hop_up if way == 0 else hop_down)(which, hop + 1, True)
            to_sibling(which, way, hop, True)

    def first_half(m):
        for step in range(1, LINE):
            wait_one(m, step)
            stage_two(m, step)

    order = list(range(count))
    near = groups == 4
    hop_up(0, 1, True)
    hop_down(0, 1, True)
    for m in order[:2]:
        stage_one(m)
        stage_two(m, 0)
    for copy in local:
        copy.start()
    hop_up(1, 1, True)
    hop_down(1, 1, True)
    for m in order[2:]:
        stage_one(m)
        stage_two(m, 0)
    first_half(0)
    pass_on(0, 1)
    first_half(1)
    if near:
        relay(0)
    pass_on(0, 2)
    first_half(2)
    pass_on(1, 1)
    if near:
        relay(1)
    first_half(3)
    pass_on(0, 3)
    pass_on(1, 2)
    if near:
        relay(2)
    pass_on(1, 3)
    if groups == 4:
        relay(order[-1])
        for m in order:
            for step in range(LINE):
                wait_three(m, step)
    else:
        for m in order:
            for step in range(LINE):
                for peer in range(1, groups):
                    wait_two(m, step, peer)
    for which in range(2):
        for hop in range(1, LINE):
            for way in range(2):
                arrive_sibling(which, way, hop)
    for copy in sends:
        copy.wait_send()
    for which in range(2):
        for hop in range(1, LINE):
            hop_up(which, hop, False)
            hop_down(which, hop, False)
            for way in range(2):
                to_sibling(which, way, hop, False)
    for copy in local:
        copy.wait()


def gather_all(groups, weights, tokens, cotangent):
    rows = weights[0].shape[0]
    cols = tuple(w.shape[1] // LINE for w in weights)
    count = len(weights)
    n_data = groups * LINE
    out_shape = [jax.ShapeDtypeStruct((n_data, rows, width), jnp.bfloat16) for width in cols]
    out_shape += [jax.ShapeDtypeStruct((LINE,) + tokens.shape, jnp.bfloat16)] * 2
    dma = pltpu.SemaphoreType.DMA
    peers = 3 if groups == 4 else groups
    return pl.pallas_call(
        partial(gather_kernel, groups, cols),
        out_shape=out_shape,
        in_specs=[ANY] * (count + 2),
        out_specs=[ANY] * (count + 2),
        scratch_shapes=[
            dma((count, LINE)),
            dma((count, LINE)),
            dma((count, LINE, peers)),
            dma((count, LINE, peers)),
            dma((count, LINE)),
            dma((count, LINE)),
            dma((2, LINE)),
            dma((2, LINE)),
            dma((2, LINE)),
            dma((2, LINE)),
            dma((2, 2, LINE)),
            dma((2, 2, LINE)),
            dma((count + 2,)),
        ],
        compiler_params=pltpu.CompilerParams(collective_id=0, has_side_effects=True),
        name="gather_all",
    )(*weights, tokens, cotangent)


def scatter_kernel(groups, cols, seq_dev, slot_len, *refs):
    count = len(cols)
    pick, m_ref, s_ref = refs[:3]
    g_in = refs[3 : 3 + count]
    mixed_ref, ssum_ref = refs[3 + count : 5 + count]
    g_out = refs[5 + count : 5 + 2 * count]
    rest = refs[5 + 2 * count :]
    m_own, m_got, m_line, m_all, m_send, s_own, s_got, s_line = rest[:8]
    g_own = rest[8 : 8 + count]
    g_got = rest[8 + count : 8 + 2 * count]
    (here, msib_s, msib_r, ssib_s, ssib_r, mline_s, mline_r, sline_s, sline_r, fin_s, fin_r, mall_s, mall_r,
     mout_s, mout_r, gp_s, gp_r, gl_s, gl_r) = rest[8 + 2 * count :]
    me = Place(groups)
    c, g, k = me.line, me.group, me.core
    me.greet()
    sibling = me.at(c, g, me.other)
    feat = D // (2 * LINE)
    seqs = LINE * seq_dev
    sends = []

    def go(copy):
        copy.start()
        sends.append(copy)

    def feature(ref, line, core):
        return ref.at[:, :, pl.ds(pl.multiple_of((line * 2 + core) * feat, 128), feat)]

    own_m, own_s = [], []
    for step in range(LINE):
        line = me.line_to(step)
        go(remote(s_ref.at[line, me.other], s_got.at[line], ssib_s.at[step], ssib_r.at[step], sibling))
        copy = pltpu.make_async_copy(s_ref.at[line, k], s_own.at[line], here.at[0, step])
        copy.start()
        own_s.append(copy)
    for step in range(LINE):
        line = me.line_to(step)
        go(remote(feature(m_ref, line, me.other), m_got.at[line], msib_s.at[step], msib_r.at[step], sibling))
        copy = pltpu.make_async_copy(feature(m_ref, line, k), m_own.at[line], here.at[1, step])
        copy.start()
        own_m.append(copy)
    own_g = []
    for m in range(count):
        for peer in range(1, groups):
            to = me.group_to(peer)
            go(remote(g_in[m].at[:, to], g_got[m].at[peer - 1], gp_s.at[m, peer], gp_r.at[m, peer], me.at(c, to, k)))
        copy = pltpu.make_async_copy(g_in[m].at[:, g], g_own[m], here.at[2, m])
        copy.start()
        own_g.append(copy)

    def add_rows(total, ref, others, rows, chunk):
        def body(i, carry):
            at = pl.ds(pl.multiple_of(i * chunk, chunk), chunk)
            acc = ref(at)[...].astype(jnp.float32)
            for other in others:
                acc = acc + other(at)[...].astype(jnp.float32)
            total(at)[...] = acc.astype(jnp.bfloat16)
            return carry

        lax.fori_loop(0, rows // chunk, body, 0)

    for step in (1, 2, 3, 0):
        line = me.line_to(step)
        remote(s_got.at[line], s_got.at[line], ssib_s.at[step], ssib_r.at[step], sibling).wait_recv()
        own_s[step].wait()
        add_rows(
            lambda at: s_own.at[line, at], lambda at: s_own.at[line, at], [lambda at: s_got.at[line, at]], slot_len, 16
        )
        if step:
            go(remote(s_own.at[line], s_line.at[step - 1], sline_s.at[step], sline_r.at[step], me.at(line, g, k)))
    for step in (1, 2, 3, 0):
        line = me.line_to(step)
        remote(m_got.at[line], m_got.at[line], msib_s.at[step], msib_r.at[step], sibling).wait_recv()
        own_m[step].wait()
        for s in range(seqs):
            add_rows(
                lambda at: m_own.at[line, s, at],
                lambda at: m_own.at[line, s, at],
                [lambda at: m_got.at[line, s, at]],
                slot_len,
                64,
            )
        if step:
            go(remote(m_own.at[line], m_line.at[step - 1], mline_s.at[step], mline_r.at[step], me.at(line, g, k)))

    keep = []

    def sum_groups(m):
        for peer in range(1, groups):
            dst = g_got[m].at[peer - 1]
            remote(dst, dst, gp_s.at[m, peer], gp_r.at[m, peer], sibling).wait_recv()
        own_g[m].wait()
        rows = g_own[m].shape[1]
        width = pl.ds(pl.multiple_of(c * cols[m], 128), cols[m])
        for step in (1, 2, 3, 0):
            line = me.line_to(step)
            add_rows(
                partial(lambda m, line, at: g_own[m].at[line, at], m, line),
                partial(lambda m, line, at: g_own[m].at[line, at], m, line),
                [partial(lambda m, line, p, at: g_got[m].at[p, line, at], m, line, p) for p in range(groups - 1)],
                rows,
                16,
            )
            if step:
                go(remote(g_own[m].at[line], g_out[m].at[:, width], gl_s.at[m, step], gl_r.at[m, step], me.at(line, g, k)))
            else:
                copy = pltpu.make_async_copy(g_own[m].at[line], g_out[m].at[:, width], here.at[2, m])
                copy.start()
                keep.append(copy)

    def finish_inputs():
        for step in range(1, LINE):
            dst = s_line.at[step - 1]
            remote(dst, dst, sline_s.at[step], sline_r.at[step], sibling).wait_recv()
        add_rows(
            lambda at: s_own.at[c, at],
            lambda at: s_own.at[c, at],
            [partial(lambda step, at: s_line.at[step, at], step) for step in range(LINE - 1)],
            slot_len,
            16,
        )
        go(remote(s_own.at[c], ssum_ref.at[k], fin_s, fin_r, sibling))
        mine_s = pltpu.make_async_copy(s_own.at[c], ssum_ref.at[k], here.at[0, 0])
        mine_s.start()
        keep.append(mine_s)

    sum_groups(0)
    finish_inputs()
    sum_groups(1)
    for step in range(1, LINE):
        dst = m_line.at[step - 1]
        remote(dst, dst, mline_s.at[step], mline_r.at[step], sibling).wait_recv()
    ours = pl.ds(g * seqs, seqs)
    for s in range(seqs):
        add_rows(
            lambda at: m_all.at[g * seqs + s, at],
            lambda at: m_own.at[c, s, at],
            [partial(lambda step, at: m_line.at[step, s, at], step) for step in range(LINE - 1)],
            slot_len,
            64,
        )
    for peer in range(1, groups):
        go(remote(m_all.at[ours], m_all.at[ours], mall_s.at[peer], mall_r.at[peer], me.at(c, me.group_to(peer), k)))

    sum_groups(2)
    sum_groups(3)

    for peer in range(1, groups):
        dst = m_all.at[pl.ds(me.group_from(peer) * seqs, seqs)]
        remote(dst, dst, mall_s.at[peer], mall_r.at[peer], sibling).wait_recv()
    mixed_cols = pl.ds(pl.multiple_of((c * 2 + k) * feat, 128), feat)
    for step in (1, 2, 3, 0):
        line = me.line_to(step)
        for s in range(seq_dev):
            m_send[line, s] = m_all[pick[line * seq_dev + s]]
        if step:
            go(remote(m_send.at[line], mixed_ref.at[:, :, mixed_cols], mout_s.at[0, step], mout_r.at[0, step], me.at(line, g, k)))
        else:
            copy = pltpu.make_async_copy(m_send.at[line], mixed_ref.at[:, :, mixed_cols], here.at[1, 0])
            copy.start()
            keep.append(copy)
        go(remote(m_send.at[line], mixed_ref.at[:, :, mixed_cols], mout_s.at[1, step], mout_r.at[1, step], me.at(line, g, me.other)))
    for m in range(count):
        for step in range(1, LINE):
            dst = g_out[m].at[:, pl.ds(pl.multiple_of(me.line_from(step) * cols[m], 128), cols[m])]
            remote(dst, dst, gl_s.at[m, step], gl_r.at[m, step], sibling).wait_recv()
    for step in range(LINE):
        for core, way in ((k, 0), (me.other, 1)):
            if step or way:
                dst = mixed_ref.at[
                    :, :, pl.ds(pl.multiple_of((me.line_from(step) * 2 + core) * feat, 128), feat)
                ]
                remote(dst, dst, mout_s.at[way, step], mout_r.at[way, step], sibling).wait_recv()
    dst = ssum_ref.at[me.other]
    remote(dst, dst, fin_s, fin_r, sibling).wait_recv()
    for copy in sends:
        copy.wait_send()
    for copy in keep:
        copy.wait()


def scatter_all(groups, cols, pick, mixed_part, s_part, grads):
    seq_dev, slot_len = s_part.shape[1:3]
    rows = grads[0].shape[2]
    count = len(cols)
    feat = D // (2 * LINE)
    seqs = LINE * seq_dev
    dma = pltpu.SemaphoreType.DMA
    low = jnp.bfloat16
    return pl.pallas_call(
        partial(scatter_kernel, groups, cols, seq_dev, slot_len),
        out_shape=[
            jax.ShapeDtypeStruct((seq_dev, slot_len, D), low),
            jax.ShapeDtypeStruct((seq_dev, slot_len, D), low),
        ]
        + [jax.ShapeDtypeStruct((rows, LINE * width), low) for width in cols],
        in_specs=[SMEM] + [ANY] * (2 + count),
        out_specs=[ANY] * (2 + count),
        scratch_shapes=[
            pltpu.VMEM((LINE, seqs, slot_len, feat), low),
            pltpu.VMEM((LINE, seqs, slot_len, feat), low),
            pltpu.VMEM((LINE - 1, seqs, slot_len, feat), low),
            pltpu.VMEM((groups * seqs, slot_len, feat), low),
            pltpu.VMEM((LINE, seq_dev, slot_len, feat), low),
            pltpu.VMEM((LINE, slot_len, D), low),
            pltpu.VMEM((LINE, slot_len, D), low),
            pltpu.VMEM((LINE - 1, slot_len, D), low),
        ]
        + [pltpu.VMEM((LINE, rows, width), low) for width in cols]
        + [pltpu.VMEM((groups - 1, LINE, rows, width), low) for width in cols]
        + [
            dma((3, LINE)),
            dma((LINE,)),
            dma((LINE,)),
            dma((LINE,)),
            dma((LINE,)),
            dma((LINE,)),
            dma((LINE,)),
            dma((LINE,)),
            dma((LINE,)),
            dma(()),
            dma(()),
            dma((groups,)),
            dma((groups,)),
            dma((2, LINE)),
            dma((2, LINE)),
            dma((count, groups)),
            dma((count, groups)),
            dma((count, LINE)),
            dma((count, LINE)),
        ],
        compiler_params=pltpu.CompilerParams(
            collective_id=1, has_side_effects=True, vmem_limit_bytes=58 * 1024 * 1024
        ),
        name="scatter_all",
    )(pick, mixed_part, s_part, *grads)


def sums_kernel(groups, v_ref, r_ref, tot_ref, both_ref, by_group, by_line, gs, gr, ls, lr, ss, sr):
    me = Place(groups)
    c, g, k = me.line, me.group, me.core
    me.greet()
    sibling = me.at(c, g, me.other)
    sends = []

    def go(copy):
        copy.start()
        sends.append(copy)

    both_ref[k] = r_ref[...]
    go(remote(r_ref, both_ref.at[k], ss.at[0], sr.at[0], sibling))
    for peer in range(1, groups):
        go(remote(v_ref, by_group.at[g], gs.at[peer], gr.at[peer], me.at(c, me.group_to(peer), k)))
    by_group[g] = v_ref[...]
    for peer in range(1, groups):
        dst = by_group.at[me.group_from(peer)]
        remote(dst, dst, gs.at[peer], gr.at[peer], sibling).wait_recv()
    acc = by_group[0]
    for i in range(1, groups):
        acc = acc + by_group[i]
    by_line[c] = acc
    for step in range(1, LINE):
        go(remote(by_line.at[c], by_line.at[c], ls.at[step], lr.at[step], me.at(me.line_to(step), g, k)))
    for step in range(1, LINE):
        dst = by_line.at[me.line_from(step)]
        remote(dst, dst, ls.at[step], lr.at[step], sibling).wait_recv()
    acc = by_line[0]
    for i in range(1, LINE):
        acc = acc + by_line[i]
    tot_ref[k] = acc
    go(remote(tot_ref.at[k], tot_ref.at[k], ss.at[1], sr.at[1], sibling))
    remote(both_ref.at[me.other], both_ref.at[me.other], ss.at[0], sr.at[0], sibling).wait_recv()
    remote(tot_ref.at[me.other], tot_ref.at[me.other], ss.at[1], sr.at[1], sibling).wait_recv()
    for copy in sends:
        copy.wait_send()


def small_sums(groups, vector, row_part):
    dma = pltpu.SemaphoreType.DMA
    return pl.pallas_call(
        partial(sums_kernel, groups),
        out_shape=[
            jax.ShapeDtypeStruct((2,) + vector.shape, jnp.float32),
            jax.ShapeDtypeStruct((2,) + row_part.shape, jnp.float32),
        ],
        in_specs=[VMEM, VMEM],
        out_specs=[VMEM, VMEM],
        scratch_shapes=[
            pltpu.VMEM((groups,) + vector.shape, jnp.float32),
            pltpu.VMEM((LINE,) + vector.shape, jnp.float32),
            dma((groups,)),
            dma((groups,)),
            dma((LINE,)),
            dma((LINE,)),
            dma((2,)),
            dma((2,)),
        ],
        compiler_params=pltpu.CompilerParams(
            collective_id=2, has_side_effects=True, vmem_limit_bytes=32 * 1024 * 1024
        ),
        name="small_sums",
    )(vector, row_part)


def per_device(
    tokens,
    cotangent,
    lengths,
    permutation,
    w_qkv,
    w_dense,
    w_fc1,
    w_fc2,
    norm_vectors,
    split_biases,
    row_state,
    col_state,
    norm_moment,
    bias_moment,
):
    f32, low = jnp.float32, jnp.bfloat16
    n_data = lax.axis_size("dp")
    groups = n_data // LINE
    data = lax.axis_index("dp")
    core = lax.axis_index("tensor")
    line = data // groups
    group = data % groups
    seq_dev, slot_len, width = tokens.shape
    rows_own = w_qkv.shape[0]
    seqs = LINE * seq_dev
    rows = seqs * slot_len
    head_dim = D // HEADS
    rot_dims = head_dim // 4
    root = math.sqrt(head_dim)
    weights = (w_qkv, w_dense, w_fc1, w_fc2)
    cols = tuple(w.shape[1] // LINE for w in weights)
    order = (0, 2, 1, 3)
    lows = [weights[i].astype(low) for i in order]
    got = gather_all(groups, lows, tokens, cotangent)
    full = [None] * 4
    for place, i in enumerate(order):
        full[i] = got[place].reshape(D, cols[i])
    x_all, back_all = got[4], got[5]
    inputs = x_all.reshape(rows, width).astype(f32)
    mine = (jnp.arange(LINE)[:, None] * groups + group) * seq_dev + jnp.arange(seq_dev)[None, :]
    my_lengths = jnp.take(lengths, mine.reshape(-1))
    places = jnp.arange(slot_len, dtype=jnp.int32)
    valid = (places[None, :] < my_lengths[:, None]).reshape(rows, 1)
    back = jnp.where(valid, back_all.reshape(rows, width), jnp.zeros((), low))
    gain_one, shift_one, gain_two, shift_two, bias_dense, bias_out = (norm_vectors[i] for i in range(6))
    centre = inputs - jnp.mean(inputs, -1, keepdims=True)
    scale = lax.rsqrt(jnp.mean(centre * centre, -1, keepdims=True) + eps_norm)
    unit = centre * scale
    norm_one = (unit * gain_one + shift_one).astype(low)
    norm_two = (unit * gain_two + shift_two).astype(low)
    bias_qkv = lax.dynamic_slice_in_dim(split_biases[0], line * cols[0], cols[0])
    bias_mlp = lax.dynamic_slice_in_dim(split_biases[0], LINE * cols[0] + line * cols[2], cols[2])
    qkv = (jnp.dot(norm_one, full[0], preferred_element_type=f32) + bias_qkv).reshape(seqs, slot_len, 3 * head_dim)
    pre = jnp.dot(norm_two, full[2], preferred_element_type=f32) + bias_mlp
    cosine, sine = rotary_tables(slot_len, rot_dims)
    query = rotate(qkv[:, :, :head_dim], cosine, sine, rot_dims).astype(low)
    keys = rotate(qkv[:, :, head_dim : 2 * head_dim], cosine, sine, rot_dims).astype(low)
    values = qkv[:, :, 2 * head_dim :].astype(low)
    causal = places[:, None] >= places[None, :]
    raw = jnp.einsum("sqd,skd->sqk", query, keys, preferred_element_type=f32) / root
    scores = jnp.where(causal, raw, neg_large)
    peak = jnp.max(scores, -1, keepdims=True)
    expo = jnp.exp(scores - peak)
    probs = expo / jnp.sum(expo, -1, keepdims=True)
    probs_low = probs.astype(low)
    attn = (
        jnp.einsum("sqk,skd->sqd", probs_low, values, preferred_element_type=f32).astype(low).reshape(rows, cols[1])
    )
    hidden, gelu_pull = jax.vjp(partial(jax.nn.gelu, approximate=False), pre)
    hidden = hidden.astype(low)
    feat = D // (2 * LINE)
    mine_feat = (jnp.arange(D) // feat) == (line * 2 + core)
    residual = jnp.where(mine_feat, inputs + (bias_dense + bias_out), 0.0)
    mixed_part = contract_last(attn, full[1]) + contract_last(hidden, full[3]) + residual
    mixed_part = jnp.where(valid, mixed_part, 0.0).astype(low)
    attn_grad = jnp.dot(back, full[1], preferred_element_type=f32).astype(low).reshape(seqs, slot_len, head_dim)
    hidden_grad = jnp.dot(back, full[3], preferred_element_type=f32)
    pre_grad = gelu_pull(hidden_grad)[0].astype(low)
    prob_grad = jnp.einsum("sqd,skd->sqk", attn_grad, values, preferred_element_type=f32)
    row_dot = jnp.sum(probs * prob_grad, -1, keepdims=True)
    score_grad = (probs * (prob_grad - row_dot)).astype(low)
    value_grad = jnp.einsum("sqk,sqd->skd", probs_low, attn_grad, preferred_element_type=f32)
    query_grad = jnp.einsum("sqk,skd->sqd", score_grad, keys, preferred_element_type=f32) / root
    key_grad = jnp.einsum("sqk,sqd->skd", score_grad, query, preferred_element_type=f32) / root
    qkv_grad = (
        jnp.concatenate(
            [rotate(query_grad, cosine, -sine, rot_dims), rotate(key_grad, cosine, -sine, rot_dims), value_grad], -1
        )
        .astype(low)
        .reshape(rows, cols[0])
    )
    norm_one_grad = contract_last(qkv_grad, full[0])
    norm_two_grad = contract_last(pre_grad, full[2])
    s_part = (norm_one_grad * gain_one + norm_two_grad * gain_two).astype(low)
    grads_part = [
        contract_first(norm_one, qkv_grad),
        contract_first(back, attn),
        contract_first(norm_two, pre_grad),
        contract_first(back, hidden),
    ]
    grads_part = [part.astype(low).reshape(LINE, groups, rows_own, -1) for part in grads_part]
    source = jnp.take(permutation, mine.reshape(-1))
    chip, inside = source // seq_dev, source % seq_dev
    pick = ((chip % groups) * seqs + (chip // groups) * seq_dev + inside).astype(jnp.int32)
    outs = scatter_all(
        groups,
        tuple(cols[i] for i in order),
        pick,
        mixed_part.reshape(seqs, slot_len, width),
        s_part.reshape(LINE, seq_dev, slot_len, width),
        [grads_part[i] for i in order],
    )
    mixed, s_sum = outs[:2]
    grads = [None] * 4
    for place, i in enumerate(order):
        grads[i] = outs[2 + place].astype(f32)
    own_x = tokens.reshape(-1, width).astype(f32)
    own_centre = own_x - jnp.mean(own_x, -1, keepdims=True)
    own_scale = lax.rsqrt(jnp.mean(own_centre * own_centre, -1, keepdims=True) + eps_norm)
    own_unit = own_centre * own_scale
    own_valid = (places[None, :] < lax.dynamic_slice_in_dim(lengths, data * seq_dev, seq_dev)[:, None]).reshape(-1, 1)
    own_back = jnp.where(own_valid, cotangent.reshape(-1, width), jnp.zeros((), low)).astype(f32)
    flow = s_sum.reshape(-1, width).astype(f32)
    through = own_scale * (
        flow - jnp.mean(flow, -1, keepdims=True) - own_unit * jnp.mean(flow * own_unit, -1, keepdims=True)
    )
    grad_tokens = (own_back + through).astype(low).reshape(seq_dev, slot_len, width)
    own_out = jnp.where(core == 0, jnp.sum(own_back, 0), 0.0)
    norm_part = jnp.stack(
        [
            jnp.sum(norm_one_grad * unit, 0),
            jnp.sum(norm_one_grad, 0),
            jnp.sum(norm_two_grad * unit, 0),
            jnp.sum(norm_two_grad, 0),
            own_out,
        ]
    )
    bias_vec = jnp.zeros((split_biases.shape[1],), f32)
    bias_vec = lax.dynamic_update_slice_in_dim(bias_vec, jnp.sum(qkv_grad.astype(f32), 0), line * cols[0], 0)
    bias_vec = lax.dynamic_update_slice_in_dim(
        bias_vec, jnp.sum(pre_grad.astype(f32), 0), LINE * cols[0] + line * cols[2], 0
    )
    squares = [grad * grad + eps_second for grad in grads]
    row_part = jnp.stack([jnp.sum(square, 1) for square in squares])
    col_part = jnp.concatenate([jnp.sum(square, 0) for square in squares])
    row_old = jnp.where(core == 0, jnp.sum(row_state, 1), 0.0)
    pieces = [norm_part.reshape(-1), bias_vec, col_part, row_old]
    total_len = sum(piece.shape[0] for piece in pieces)
    padded = -(-total_len // 1024) * 1024
    vector = jnp.concatenate(pieces + [jnp.zeros((padded - total_len,), f32)]).reshape(-1, 128)
    row_pad = -(-rows_own // 128) * 128
    row_block = jnp.zeros((8, row_pad), f32).at[:4, :rows_own].set(row_part)
    totals, row_both = small_sums(groups, vector, row_block)
    totals = totals.reshape(2, -1)
    row_total = (row_both[0] + row_both[1])[:4, :rows_own]
    at_bias = 5 * D
    at_col = at_bias + split_biases.shape[1]
    at_row = at_col + col_state.shape[1]
    both = totals[0] + totals[1]
    norm_total = both[:at_bias].reshape(5, D)
    norm_total = jnp.concatenate([norm_total, norm_total[4:]], 0)
    mine_total = lax.dynamic_index_in_dim(totals, core, 0, False)
    bias_total = mine_total[at_bias:at_col][None, :]
    col_total = mine_total[at_col:at_row]
    all_cols = both[at_col:at_row]
    row_old_sum = both[at_row : at_row + 4]
    col_new = decay * col_state + (1.0 - decay) * (col_total[None, :] / D)
    full_cols = (3.0 * D, 1.0 * D, 1.0 * FF, 1.0 * FF)
    rates = (
        rate_scale / math.sqrt(D),
        rate_scale / math.sqrt(D // 8),
        rate_scale / math.sqrt(D),
        rate_scale / math.sqrt(FF),
    )
    new_list, row_list = [], []
    edge = 0
    for i in range(4):
        wide = weights[i].shape[1]
        row_new = decay * row_state[i] + (1.0 - decay) * (row_total[i] / full_cols[i])
        mass = jnp.sum(all_cols[edge : edge + wide])
        mean = (decay * row_old_sum[i] + (1.0 - decay) * (mass / full_cols[i])) / D
        second = row_new[:, None] * col_new[0, edge : edge + wide][None, :] / mean
        new_list.append(weights[i] - rates[i] * grads[i] * lax.rsqrt(second))
        row_list.append(row_new)
        edge += wide
    row_new = jnp.stack(row_list)
    norm_moment_new = decay * norm_moment + (1.0 - decay) * (norm_total * norm_total + eps_second)
    norm_new = norm_vectors - rate_norm * norm_total * lax.rsqrt(norm_moment_new)
    bias_moment_new = decay * bias_moment + (1.0 - decay) * (bias_total * bias_total + eps_second)
    bias_new = split_biases - rate_vector * bias_total * lax.rsqrt(bias_moment_new)
    return (
        mixed,
        grad_tokens,
        *grads,
        *new_list,
        *[new.astype(low) for new in new_list],
        row_new,
        col_new,
        norm_total,
        norm_moment_new,
        norm_new,
        bias_total,
        bias_moment_new,
        bias_new,
    )


def solution(mesh):
    halves = P("dp", "tensor")
    split = P("tensor", None)
    in_specs = (
        P("dp", None, None),
        P("dp", None, None),
        P(),
        P(),
        halves,
        halves,
        halves,
        halves,
        P(),
        split,
        P(None, "dp"),
        split,
        P(),
        split,
    )
    out_specs = (
        (P("dp", None, None),) * 2
        + (halves,) * 12
        + (P(None, "dp"), split)
        + (P(),) * 3
        + (split,) * 3
    )
    return jax.shard_map(
        per_device, mesh=mesh, in_specs=in_specs, out_specs=out_specs, check_vma=False
    )
```

```python
from functools import partial
import math

import jax
import jax.numpy as jnp
from jax import lax
from jax.experimental import pallas as pl
from jax.experimental.pallas import tpu as pltpu
from jax.sharding import PartitionSpec as P

D = 2048
FF = 8192
HEADS = 8
LINE = 4

eps_norm = 1e-05
eps_second = 1e-30
decay = 0.5
rate_scale = 1.0
rate_norm = 0.5
rate_vector = 0.05
neg_large = -1e30

MESH = pl.DeviceIdType.MESH
ANY = pl.BlockSpec(memory_space=pl.ANY)
VMEM = pl.BlockSpec(memory_space=pltpu.VMEM)
SMEM = pl.BlockSpec(memory_space=pltpu.SMEM)


def turn_tables(slot_len, rot_dims, width):
    half = rot_dims // 2
    freq = 10000.0 ** (-2.0 * jnp.arange(half, dtype=jnp.float32) / rot_dims)
    angle = jnp.arange(slot_len, dtype=jnp.float32)[:, None] * freq[None, :]
    cosine, sine = jnp.cos(angle), jnp.sin(angle)
    none = jnp.zeros((slot_len, half), jnp.float32)
    rest = jnp.zeros((slot_len, width - rot_dims), jnp.float32)
    return jnp.stack(
        [
            jnp.concatenate([cosine, cosine, rest + 1.0], 1),
            jnp.concatenate([sine, none, rest], 1),
            jnp.concatenate([none, sine, rest], 1),
        ]
    )


class Place:
    def __init__(self, groups):
        self.groups = groups
        data = lax.axis_index("dp")
        self.core = lax.axis_index("tensor")
        self.other = 1 - self.core
        self.line = data // groups
        self.group = data % groups

    def at(self, line, group, core):
        return (line * self.groups + group, core)

    def line_to(self, step):
        return (self.line + step) % LINE

    def line_from(self, step):
        return (self.line + LINE - step) % LINE

    def group_to(self, step):
        g = self.group
        if self.groups == 4:
            if step == 1:
                return g + 1 - 2 * (g % 2)
            if step == 2:
                return (g + 2) % 4
            return 3 - g
        return (g + step) % self.groups

    def group_from(self, step):
        if self.groups == 4:
            return self.group_to(step)
        return (self.group + self.groups - step) % self.groups

    def greet(self):
        barrier = pltpu.get_barrier_semaphore()
        count = 0
        for step in range(1, LINE):
            for core in (self.core, self.other):
                pl.semaphore_signal(
                    barrier, inc=1, device_id=self.at(self.line_to(step), self.group, core), device_id_type=MESH
                )
                count += 1
        for step in range(1, self.groups):
            pl.semaphore_signal(
                barrier, inc=1, device_id=self.at(self.line, self.group_to(step), self.core), device_id_type=MESH
            )
            count += 1
        pl.semaphore_signal(
            barrier, inc=1, device_id=self.at(self.line, self.group, self.other), device_id_type=MESH
        )
        pl.semaphore_wait(barrier, count + 1)


def remote(src, dst, send, recv, device):
    return pltpu.make_async_remote_copy(
        src_ref=src, dst_ref=dst, send_sem=send, recv_sem=recv, device_id=device, device_id_type=MESH
    )


def dot(left, right):
    return jnp.dot(left, right, preferred_element_type=jnp.float32)


def gather_kernel(groups, cols, seq_dev, slot_len, *refs):
    count = len(cols)
    f32, low = jnp.float32, jnp.bfloat16
    w_in = refs[:count]
    acts_in = refs[count : count + 2]
    vec_ref, bias_ref, valid_ref, turn_ref = refs[count + 2 : count + 6]
    outs = refs[count + 6 : count + 16]
    n1_out, n2_out, back_out, qg_out, pg_out, attn_out, hid_out, m_out, s_out, early_ref = outs
    rest = refs[count + 16 :]
    w_out = rest[:count]
    acts_out = rest[count : count + 2]
    (qkv_keep, prob_keep, attn_keep, hid_keep, pg_keep, one_buf, two_buf, back_buf, m_buf, m_got, s_got, qkv_now,
     pre_now, stat_keep, norm_acc, bias_acc) = rest[count + 2 : count + 18]
    (one_s, one_r, two_s, two_r, three_s, three_r, up_s, up_r, down_s, down_r, sib_s, sib_r, here, out_a, out_b,
     out_c, out_d, msib_s, msib_r, ssib_s, ssib_r, mline_s, mline_r, s_here) = rest[count + 18 :]
    me = Place(groups)
    c, g, k = me.line, me.group, me.core
    me.greet()
    sibling = me.at(c, g, me.other)
    rows_own = w_in[0].shape[0]
    block_rows = seq_dev * slot_len
    near = groups == 4
    START, SENT = "start", "wait_send"

    def block(ref, line, width):
        return ref.at[:, pl.ds(pl.multiple_of(line * width, 128), width)]

    def place(m, line, group):
        return w_out[m].at[pl.ds(pl.multiple_of((line * groups + group) * rows_own, 32), rows_own)]

    def rows_of(which, line, core):
        return acts_out[which].at[pl.ds(pl.multiple_of((line * seq_dev + core) * slot_len, 32), slot_len)]

    def hop_up(which, hop, act):
        origin = c - (hop - 1)
        copy = remote(
            acts_in[which].at[k] if hop == 1 else rows_of(which, origin, k),
            rows_of(which, origin, k),
            up_s.at[which, hop - 1],
            up_r.at[which, hop - 1],
            me.at(c + 1, g, k),
        )
        pl.when((c < LINE - 1) & (origin >= 0))(getattr(copy, act))

    def hop_down(which, hop, act):
        origin = c + (hop - 1)
        copy = remote(
            acts_in[which].at[k] if hop == 1 else rows_of(which, origin, k),
            rows_of(which, origin, k),
            down_s.at[which, hop - 1],
            down_r.at[which, hop - 1],
            me.at(c - 1, g, k),
        )
        pl.when((c > 0) & (origin < LINE))(getattr(copy, act))

    def from_way(way, hop):
        origin = c - hop if way == 0 else c + hop
        return origin, (origin >= 0) if way == 0 else (origin < LINE)

    def to_sibling(which, way, hop, act):
        origin, ok = from_way(way, hop)
        rows = rows_of(which, origin, k)
        copy = remote(rows, rows, sib_s.at[which, way, hop - 1], sib_r.at[which, way, hop - 1], sibling)
        pl.when(ok)(getattr(copy, act))

    def arrive(which, way, hop):
        origin, ok = from_way(way, hop)
        sem = (up_r if way == 0 else down_r).at[which, hop - 1]
        rows = rows_of(which, origin, k)
        pl.when(ok)(remote(rows, rows, sem, sem, sibling).wait_recv)

    def arrive_sibling(which):
        for hop in range(1, LINE):
            for way in range(2):
                origin, ok = from_way(way, hop)
                sem = sib_r.at[which, way, hop - 1]
                rows = rows_of(which, origin, me.other)
                pl.when(ok)(remote(rows, rows, sem, sem, sibling).wait_recv)

    def pass_on(which, hop):
        for way in range(2):
            arrive(which, way, hop)
            if hop < LINE - 1:
                (hop_up if way == 0 else hop_down)(which, hop + 1, START)
            to_sibling(which, way, hop, START)

    def local_acts(which, act):
        for s in range(seq_dev):
            copy = pltpu.make_async_copy(acts_in[which].at[s], rows_of(which, c, s), here.at[count + which, s])
            getattr(copy, act)()

    def local_weight(m, act):
        copy = pltpu.make_async_copy(block(w_in[m], c, cols[m]), place(m, c, g), here.at[m, 0])
        getattr(copy, act)()

    def stage_one(m, act):
        for step in range(1, LINE):
            to = me.line_to(step)
            copy = remote(
                block(w_in[m], to, cols[m]),
                place(m, c, g),
                one_s.at[m, step],
                one_r.at[m, step],
                me.at(to, g, k),
            )
            getattr(copy, act)()

    def stage_two(m, step, act):
        where = place(m, me.line_from(step), g)
        src = block(w_in[m], c, cols[m]) if step == 0 else where
        for peer in range(1, 3 if near else groups):
            copy = remote(
                src, where, two_s.at[m, step, peer], two_r.at[m, step, peer], me.at(c, me.group_to(peer), k)
            )
            getattr(copy, act)()

    def first_half(m):
        for step in range(1, LINE):
            dst = place(m, me.line_from(step), g)
            remote(dst, dst, one_s.at[m, step], one_r.at[m, step], sibling).wait_recv()
            stage_two(m, step, START)

    def wait_two(m, step, peer):
        dst = place(m, me.line_from(step), me.group_from(peer))
        remote(dst, dst, two_s.at[m, step, peer], two_r.at[m, step, peer], sibling).wait_recv()

    def stage_three(m, step, act):
        source, target = (1, 2) if step % 2 == 0 else (2, 1)
        where = place(m, me.line_from(step), me.group_to(source))
        copy = remote(where, where, three_s.at[m, step], three_r.at[m, step], me.at(c, me.group_to(target), k))
        getattr(copy, act)()

    def relay(m):
        for step in range(LINE):
            for peer in range(1, 3 if near else groups):
                wait_two(m, step, peer)
            if near:
                stage_three(m, step, START)

    def last(m):
        if near:
            for step in range(LINE):
                dst = place(m, me.line_from(step), me.group_to(3))
                remote(dst, dst, three_s.at[m, step], three_r.at[m, step], sibling).wait_recv()

    hop_up(0, 1, START)
    hop_down(0, 1, START)
    for m in (0, 1):
        stage_one(m, START)
        stage_two(m, 0, START)
    local_acts(0, START)
    local_weight(0, START)
    local_weight(1, START)
    norm_acc[...] = jnp.zeros_like(norm_acc)
    bias_acc[...] = jnp.zeros_like(bias_acc)
    first_half(0)
    pass_on(0, 1)
    hop_up(1, 1, START)
    hop_down(1, 1, START)
    for m in (2, 3):
        stage_one(m, START)
        stage_two(m, 0, START)
    local_acts(1, START)
    local_weight(2, START)
    local_weight(3, START)
    first_half(1)
    relay(0)
    pass_on(0, 2)
    relay(1)
    pass_on(0, 3)
    local_acts(0, "wait")
    local_weight(0, "wait")
    local_weight(1, "wait")
    last(0)
    last(1)
    arrive_sibling(0)

    wq, w1, wd, w2 = w_out
    x_all, ct_all = acts_out
    head = cols[0] // 3
    half = head // 2
    chunk = 16
    wide = 512
    ways = D // wide
    root = math.sqrt(head)
    causal = lax.broadcasted_iota(jnp.int32, (slot_len, slot_len), 0) >= lax.broadcasted_iota(
        jnp.int32, (slot_len, slot_len), 1
    )

    def turn(v, sign):
        left = pltpu.roll(v, half - 32, 1)
        right = pltpu.roll(v, 32, 1)
        if sign > 0:
            return v * turn_ref[0] - left * turn_ref[1] + right * turn_ref[2]
        return v * turn_ref[0] + left * turn_ref[1] - right * turn_ref[2]

    def contract(left, right, dims):
        return lax.dot_general(left, right, ((dims[0], dims[1]), ((), ())), preferred_element_type=f32)

    def put_one(i, line, act):
        rows = pl.ds(pl.multiple_of(line * block_rows, 128), block_rows)
        getattr(pltpu.make_async_copy(one_buf, n1_out.at[rows], out_a), act)()
        getattr(pltpu.make_async_copy(two_buf.at[0], n2_out.at[rows], out_b.at[0]), act)()

    @pl.loop(0, LINE)
    def forward(i):
        line = (c + i) % LINE
        base = pl.multiple_of(line * block_rows, 128)

        @pl.when(i == 0)
        def _():
            first_half(2)
            first_half(3)

        @pl.when(i == 1)
        def _():
            pass_on(1, 1)
            relay(2)

        @pl.when(i == 2)
        def _():
            pass_on(1, 2)
            relay(3)

        @pl.when(i == 3)
        def _():
            pass_on(1, 3)

        @pl.when(i >= 1)
        def _():
            put_one(i, line, "wait")

        @pl.loop(0, block_rows // chunk)
        def norm(j):
            at = pl.ds(pl.multiple_of(base + j * chunk, chunk), chunk)
            to = pl.ds(pl.multiple_of(j * chunk, chunk), chunk)
            x = x_all[at, :].astype(f32)
            mean = jnp.mean(x, -1, keepdims=True)
            centre = x - mean
            scale = lax.rsqrt(jnp.mean(centre * centre, -1, keepdims=True) + eps_norm)
            stat_keep[at, 0:1] = mean
            stat_keep[at, 1:2] = scale
            unit = centre * scale
            one_buf[to, :] = (unit * vec_ref[0:1, :] + vec_ref[1:2, :]).astype(low)
            two_buf[0, to, :] = (unit * vec_ref[2:3, :] + vec_ref[3:4, :]).astype(low)

        put_one(i, line, "start")
        qkv_now[...] = dot(one_buf[...], wq[...]) + bias_ref[0:1, : cols[0]]
        pre_now[...] = dot(two_buf[0], w1[...]) + bias_ref[0:1, cols[0] :]

        for s in range(seq_dev):
            part = slice(s * slot_len, (s + 1) * slot_len)
            rows = pl.ds(pl.multiple_of(base + s * slot_len, 32), slot_len)
            qkv_keep[rows, 0:half] = turn(qkv_now[part, 0:half], 1).astype(low)
            qkv_keep[rows, half:head] = qkv_now[part, half:head].astype(low)
            qkv_keep[rows, head : head + half] = turn(qkv_now[part, head : head + half], 1).astype(low)
            qkv_keep[rows, head + half :] = qkv_now[part, head + half :].astype(low)
            query = qkv_keep[rows, :head]
            keys = qkv_keep[rows, head : 2 * head]
            values = qkv_keep[rows, 2 * head :]
            scores = jnp.where(causal, contract(query, keys, ((1,), (1,))) / root, neg_large)
            expo = jnp.exp(scores - jnp.max(scores, -1, keepdims=True))
            probs = expo / jnp.sum(expo, -1, keepdims=True)
            prob_keep[line * seq_dev + s] = probs
            attn_keep[rows, :] = dot(probs.astype(low), values).astype(low)

        @pl.loop(0, block_rows // chunk)
        def act(j):
            at = pl.ds(pl.multiple_of(base + j * chunk, chunk), chunk)
            pre = pre_now[pl.ds(pl.multiple_of(j * chunk, chunk), chunk), :]
            area = 0.5 * (1.0 + lax.erf(pre * math.sqrt(0.5)))
            hid_keep[at, :] = (pre * area).astype(low)
            pg_keep[at, :] = (area + pre * (jnp.exp(-0.5 * pre * pre) * (1.0 / math.sqrt(2.0 * math.pi)))).astype(low)

    put_one(LINE - 1, (c + LINE - 1) % LINE, "wait")
    local_acts(1, "wait")
    local_weight(2, "wait")
    local_weight(3, "wait")
    last(2)
    last(3)
    arrive_sibling(1)

    def put_back(line, act):
        rows = pl.ds(pl.multiple_of(line * block_rows, 128), block_rows)
        getattr(pltpu.make_async_copy(back_buf, back_out.at[rows], out_c), act)()

    def pair_m(i, act):
        line = (c + i) % LINE
        copy = remote(m_buf.at[i % 2, me.other], m_got.at[line], msib_s.at[i], msib_r.at[i], sibling)
        getattr(copy, act)()

    def line_m(i, act):
        line = (c + i) % LINE
        for step in range(1, LINE):
            to = me.line_to(step)
            copy = remote(
                m_buf.at[i % 2, k, to], m_out.at[c, line], mline_s.at[i, step], mline_r.at[i, step], me.at(to, g, k)
            )
            getattr(copy, act)()
        copy = pltpu.make_async_copy(m_buf.at[i % 2, k, c], m_out.at[c, line], mline_s.at[i, 0])
        getattr(copy, "wait" if act == SENT else act)()

    def pair_s(i, act):
        line = (c + i) % LINE
        rows = pl.ds(pl.multiple_of(me.other * slot_len, 32), slot_len)
        copy = remote(two_buf.at[i % 2, rows], s_got.at[line], ssib_s.at[i], ssib_r.at[i], sibling)
        getattr(copy, act)()

    def put_s(i, act):
        line = (c + i) % LINE
        rows = pl.ds(pl.multiple_of(k * slot_len, 32), slot_len)
        getattr(pltpu.make_async_copy(two_buf.at[i % 2, rows], s_out.at[line], s_here.at[i]), act)()

    def finish_s(i):
        line = (c + i) % LINE
        pair_s(i, "wait_recv")

        @pl.loop(0, slot_len // chunk)
        def add(j):
            at = pl.ds(pl.multiple_of(k * slot_len + j * chunk, chunk), chunk)
            to = pl.ds(pl.multiple_of(j * chunk, chunk), chunk)
            total = two_buf[i % 2, at, :].astype(f32) + s_got[line, to, :].astype(f32)
            two_buf[i % 2, at, :] = total.astype(low)

        put_s(i, START)

    def put_rest(line, act):
        rows = pl.ds(pl.multiple_of(line * block_rows, 128), block_rows)
        for place_at, (buf, out) in enumerate(
            ((qkv_keep, qg_out), (pg_keep, pg_out), (attn_keep, attn_out), (hid_keep, hid_out))
        ):
            getattr(pltpu.make_async_copy(buf.at[rows], out.at[rows], out_d.at[place_at, line]), act)()

    mine = c * 2 + k

    @pl.loop(0, LINE)
    def backward(i):
        line = (c + i) % LINE
        base = pl.multiple_of(line * block_rows, 128)
        whole = pl.ds(base, block_rows)
        slot = i % 2

        @pl.when(i >= 2)
        def _():
            line_m(i - 2, SENT)

        live = valid_ref[whole, :]

        @pl.loop(0, ways)
        def output(j):
            at = pl.ds(pl.multiple_of(j * wide, 128), wide)
            total = contract(attn_keep[whole, :], wd[at, :], ((1,), (1,)))
            total = total + contract(hid_keep[whole, :], w2[at, :], ((1,), (1,)))
            feature = (lax.broadcasted_iota(jnp.int32, (1, wide), 1) + j * wide) // (D // (2 * LINE))
            mask = jnp.where(feature == mine, 1.0, 0.0)
            extra = x_all[whole, at].astype(f32) + (vec_ref[4:5, at] + vec_ref[5:6, at])
            total = ((total + mask * extra) * live).astype(low)
            m_buf[slot, 0, j] = total[:, : wide // 2]
            m_buf[slot, 1, j] = total[:, wide // 2 :]

        pair_m(i, START)

        @pl.when(i >= 1)
        def _():
            put_back(line, "wait")

        back_buf[...] = (ct_all[whole, :].astype(f32) * live).astype(low)
        put_back(line, "start")
        attn_grad = dot(back_buf[...], wd[...]).astype(low)
        pre_now[...] = dot(back_buf[...], w2[...])

        @pl.when(i == 0)
        def _():
            rows = pl.ds(pl.multiple_of(k * slot_len, 32), slot_len)
            total = jnp.sum(back_buf[rows, :].astype(f32).reshape(slot_len // 8, 8, D), 0)
            norm_acc[4] = total

        @pl.loop(0, block_rows // chunk)
        def act(j):
            at = pl.ds(pl.multiple_of(base + j * chunk, chunk), chunk)
            grad = pre_now[pl.ds(pl.multiple_of(j * chunk, chunk), chunk), :] * pg_keep[at, :].astype(f32)
            grad = grad.astype(low)
            pg_keep[at, :] = grad
            grad = grad.astype(f32)
            bias_acc[:, cols[0] :] += grad[:8] + grad[8:]

        for s in range(seq_dev):
            rows = pl.ds(pl.multiple_of(base + s * slot_len, 32), slot_len)
            grad = attn_grad[s * slot_len : (s + 1) * slot_len]
            query = qkv_keep[rows, :head]
            keys = qkv_keep[rows, head : 2 * head]
            values = qkv_keep[rows, 2 * head :]
            probs = prob_keep[line * seq_dev + s]
            prob_grad = contract(grad, values, ((1,), (1,)))
            row_dot = jnp.sum(probs * prob_grad, -1, keepdims=True)
            score_grad = (probs * (prob_grad - row_dot)).astype(low)
            value_grad = contract(probs.astype(low), grad, ((0,), (0,)))
            query_grad = dot(score_grad, keys) / root
            key_grad = contract(score_grad, query, ((0,), (0,))) / root
            qkv_keep[rows, 0:half] = turn(query_grad[:, :half], -1).astype(low)
            qkv_keep[rows, half:head] = query_grad[:, half:].astype(low)
            qkv_keep[rows, head : head + half] = turn(key_grad[:, :half], -1).astype(low)
            qkv_keep[rows, head + half : 2 * head] = key_grad[:, half:].astype(low)
            qkv_keep[rows, 2 * head :] = value_grad.astype(low)
            summed = qkv_keep[rows, :].astype(f32).reshape(slot_len // 8, 8, cols[0])
            bias_acc[:, : cols[0]] += jnp.sum(summed, 0)

        put_rest(line, "start")
        mean = stat_keep[whole, 0:1]
        scale = stat_keep[whole, 1:2]

        @pl.when(i >= 2)
        def _():
            pair_s(i - 2, SENT)
            put_s(i - 2, "wait")

        @pl.loop(0, ways)
        def inputs(j):
            at = pl.ds(pl.multiple_of(j * wide, 128), wide)
            first = contract(qkv_keep[whole, :], wq[at, :], ((1,), (1,)))
            second = contract(pg_keep[whole, :], w1[at, :], ((1,), (1,)))
            two_buf[slot, :, at] = (first * vec_ref[0:1, at] + second * vec_ref[2:3, at]).astype(low)
            unit = (x_all[whole, at].astype(f32) - mean) * scale
            for place_at, value in enumerate((first * unit, first, second * unit, second)):
                norm_acc[place_at, :, at] += jnp.sum(value.reshape(block_rows // 8, 8, wide), 0)

        pair_s(i, START)
        pair_m(i, "wait_recv")

        @pl.loop(0, LINE)
        def add_outer(p):
            @pl.loop(0, block_rows // 64)
            def add(j):
                at = pl.ds(pl.multiple_of(j * 64, 64), 64)
                total = m_buf[slot, k, p, at, :].astype(f32) + m_got[line, p, at, :].astype(f32)
                m_buf[slot, k, p, at, :] = total.astype(low)

        line_m(i, START)
        pair_m(i, SENT)

        @pl.when(i >= 1)
        def _():
            finish_s(i - 1)

    finish_s(LINE - 1)
    for r in range(5):
        total = jnp.sum(norm_acc[r], 0, keepdims=True)
        for t in range(D // 128):
            early_ref[r * (D // 128) + t : r * (D // 128) + t + 1, :] = total[:, t * 128 : (t + 1) * 128]
    at_bias = 5 * (D // 128)
    total = jnp.sum(bias_acc[...], 0, keepdims=True)
    for t in range((cols[0] + cols[1]) // 128):
        early_ref[at_bias + t : at_bias + t + 1, :] = total[:, t * 128 : (t + 1) * 128]
    at_row = at_bias + (cols[0] + cols[1]) // 128
    early_ref[at_row : at_row + 1, :] = vec_ref[6:7, :128]
    early_ref[at_row + 1 :, :] = jnp.zeros((early_ref.shape[0] - at_row - 1, 128), f32)
    put_back(0, "wait")
    for i in range(LINE):
        put_rest(i, "wait")
    for i in (LINE - 2, LINE - 1):
        line_m(i, SENT)
        pair_s(i, SENT)
        put_s(i, "wait")
    for step in range(1, LINE):
        source = me.line_from(step)
        for i in range(LINE):
            dst = m_out.at[source, (source + i) % LINE]
            remote(dst, dst, mline_s.at[i, step], mline_r.at[i, step], sibling).wait_recv()
    for m in range(count):
        stage_one(m, SENT)
        for step in range(LINE):
            stage_two(m, step, SENT)
            if near:
                stage_three(m, step, SENT)
    for which in range(2):
        for hop in range(1, LINE):
            hop_up(which, hop, SENT)
            hop_down(which, hop, SENT)
            for way in range(2):
                to_sibling(which, way, hop, SENT)


def gather_all(groups, weights, tokens, cotangent, vectors, biases, valid, turns):
    rows_own = weights[0].shape[0]
    seq_dev, slot_len, width = tokens.shape
    cols = tuple(w.shape[1] // LINE for w in weights)
    count = len(weights)
    block_rows = seq_dev * slot_len
    rows = LINE * block_rows
    f32, low = jnp.float32, jnp.bfloat16
    dma = pltpu.SemaphoreType.DMA
    peers = 3 if groups == 4 else groups
    out_widths = (D, D, D, cols[0], cols[1], cols[2], cols[3])
    feat = D // (2 * LINE)
    early_rows = -(-(5 * D + cols[0] + cols[1] + 128) // 1024) * 8
    return pl.pallas_call(
        partial(gather_kernel, groups, cols, seq_dev, slot_len),
        out_shape=[jax.ShapeDtypeStruct((rows, w), low) for w in out_widths]
        + [
            jax.ShapeDtypeStruct((LINE, LINE, block_rows, feat), low),
            jax.ShapeDtypeStruct((LINE, slot_len, D), low),
            jax.ShapeDtypeStruct((early_rows, 128), f32),
        ],
        in_specs=[ANY] * (count + 2) + [VMEM] * 4,
        out_specs=[ANY] * 9 + [VMEM],
        scratch_shapes=[pltpu.VMEM((D, w), low) for w in cols]
        + [pltpu.VMEM((rows, D), low)] * 2
        + [
            pltpu.VMEM((rows, cols[0]), low),
            pltpu.VMEM((LINE * seq_dev, slot_len, slot_len), f32),
            pltpu.VMEM((rows, cols[2]), low),
            pltpu.VMEM((rows, cols[3]), low),
            pltpu.VMEM((rows, cols[1]), low),
            pltpu.VMEM((block_rows, D), low),
            pltpu.VMEM((2, block_rows, D), low),
            pltpu.VMEM((block_rows, D), low),
            pltpu.VMEM((2, 2, LINE, block_rows, feat), low),
            pltpu.VMEM((LINE, LINE, block_rows, feat), low),
            pltpu.VMEM((LINE, slot_len, D), low),
            pltpu.VMEM((block_rows, cols[0]), f32),
            pltpu.VMEM((block_rows, cols[1]), f32),
            pltpu.VMEM((rows, 2), f32),
            pltpu.VMEM((5, 8, D), f32),
            pltpu.VMEM((8, cols[0] + cols[1]), f32),
            dma((count, LINE)),
            dma((count, LINE)),
            dma((count, LINE, peers)),
            dma((count, LINE, peers)),
            dma((count, LINE)),
            dma((count, LINE)),
            dma((2, LINE)),
            dma((2, LINE)),
            dma((2, LINE)),
            dma((2, LINE)),
            dma((2, 2, LINE)),
            dma((2, 2, LINE)),
            dma((count + 2, seq_dev)),
            dma(()),
            dma((2,)),
            dma(()),
            dma((4, LINE)),
            dma((LINE,)),
            dma((LINE,)),
            dma((LINE,)),
            dma((LINE,)),
            dma((LINE, LINE)),
            dma((LINE, LINE)),
            dma((LINE,)),
        ],
        compiler_params=pltpu.CompilerParams(
            collective_id=0, has_side_effects=True, vmem_limit_bytes=62 * 1024 * 1024
        ),
        name="gather_all",
    )(*weights, tokens, cotangent, vectors, biases, valid, turns)


def scatter_kernel(groups, cols, seq_dev, slot_len, rows_own, *refs):
    count = len(cols)
    f32, low = jnp.float32, jnp.bfloat16
    pick, m_ref, s_ref = refs[:3]
    lefts_in = refs[3:6]
    rights_in = refs[6 : 6 + count]
    early_ref = refs[6 + count]
    mixed_ref, ssum_ref = refs[7 + count : 9 + count]
    g_out = refs[9 + count : 9 + 2 * count]
    early_out, col_out, row_out = refs[9 + 2 * count : 12 + 2 * count]
    rest = refs[12 + 2 * count :]
    left_buf, right_a, right_b, right_c = rest[:4]
    g_own = rest[4 : 4 + count]
    g_got = rest[4 + count : 4 + 2 * count]
    (m_in, m_all, m_send, s_own, s_line, early_group, col_now, col_group, row_keep, row_turn) = rest[
        4 + 2 * count : 14 + 2 * count
    ]
    (here, sline_s, sline_r, fin_s, fin_r, mall_s, mall_r, mout_s, mout_r, gp_s, gp_r, gl_s, gl_r, eg_s, eg_r, el_s,
     el_r, es_s, es_r, cg_s, cg_r, cl_s, cl_r, cs_s, cs_r, rl_s, rl_r, keep_sem) = rest[14 + 2 * count :]
    me = Place(groups)
    c, g, k = me.line, me.group, me.core
    me.greet()
    sibling = me.at(c, g, me.other)
    feat = D // (2 * LINE)
    seqs = LINE * seq_dev
    rows = seqs * slot_len
    double = groups == 4
    sends = []

    def go(copy):
        copy.start()
        sends.append(copy)

    def to_group(step):
        return (g + step) % groups

    def from_group(step):
        return (g + groups - step) % groups

    def arrived(dst, send, recv):
        remote(dst, dst, send, recv, sibling).wait_recv()

    def add_rows(total, parts, count_rows, chunk):
        @pl.loop(0, count_rows // chunk)
        def body(i):
            at = pl.ds(pl.multiple_of(i * chunk, chunk), chunk)
            acc = parts[0](at)[...].astype(f32)
            for part in parts[1:]:
                acc = acc + part(at)[...].astype(f32)
            total(at)[...] = acc.astype(low)

    def load(src, dst, sem):
        copy = pltpu.make_async_copy(src, dst, sem)
        copy.start()
        return copy

    got_m = load(m_ref, m_in, here.at[0])
    got_back = load(lefts_in[2], left_buf.at[0], here.at[1])
    got_d = load(rights_in[2], right_c, here.at[2])
    got_2 = load(rights_in[3], right_a, here.at[3])
    for step in range(1, LINE):
        line = me.line_to(step)
        go(remote(s_ref.at[line], s_line.at[step - 1], sline_s.at[step], sline_r.at[step], me.at(line, g, k)))
    got_s = load(s_ref.at[c], s_own, here.at[4])
    for step in range(1, groups):
        go(remote(early_ref, early_group.at[g], eg_s.at[step], eg_r.at[step], me.at(c, to_group(step), k)))
    early_group[g] = early_ref[...]
    if double:
        got_one = load(lefts_in[0], left_buf.at[1], here.at[5])
        got_q = load(rights_in[0], right_b, here.at[6])

    got_m.wait()
    ours = pl.ds(g * seqs, seqs)
    for s in range(seqs):
        line, part = s // seq_dev, s % seq_dev
        add_rows(
            lambda at: m_all.at[g * seqs + s, at],
            [partial(lambda p, at: m_in.at[p, s, at], p) for p in range(LINE)],
            slot_len,
            64,
        )
    for step in range(1, groups):
        go(remote(m_all.at[ours], m_all.at[ours], mall_s.at[step], mall_r.at[step], me.at(c, to_group(step), k)))

    per = 128 // rows_own

    def tile_products(m, left, right, tiles):
        lhs = jnp.concatenate(
            [left[:, pl.ds(pl.multiple_of((l * groups + p) * rows_own, 128), 128)] for l, p in tiles], 1
        )
        wide = 256 if cols[m] % 512 else 512
        for n in range(cols[m] // wide):
            at = slice(n * wide, (n + 1) * wide)
            out = lax.dot_general(lhs, right[:, at], (((0,), (0,)), ((), ())), preferred_element_type=f32).astype(low)
            for t, (l, p) in enumerate(tiles):
                for q in range(per):
                    row = t * 128 + q * rows_own
                    g_own[m][l, p + q, :, at] = out[row : row + rows_own]

    def send_group(m, step, act):
        to = to_group(step)
        copy = remote(
            g_own[m].at[:, to], g_got[m].at[step - 1], gp_s.at[m, step], gp_r.at[m, step], me.at(c, to, k)
        )
        getattr(copy, act)()

    def products(left, pairs):
        if groups == 4:

            @pl.loop(0, groups)
            def body(t):
                step = (t + 1) % groups
                to = to_group(step)
                for m, right in pairs:
                    tile_products(m, left, right, [(l, to) for l in range(LINE)])

                    @pl.when(step > 0)
                    def _():
                        send_group(m, step, "start")
        else:

            @pl.loop(0, LINE)
            def body(l):
                for m, right in pairs:
                    tile_products(m, left, right, [(l, t * per) for t in range(4)])

            for m, _ in pairs:
                for step in range(1, groups):
                    send_group(m, step, "start")

    got_back.wait()
    got_d.wait()
    got_2.wait()
    products(left_buf.at[0], ((3, right_a), (2, right_c)))
    if double:
        got_two = load(lefts_in[1], left_buf.at[0], here.at[1])
        got_1 = load(rights_in[1], right_a, here.at[3])
        got_one.wait()
        got_q.wait()
        products(left_buf.at[1], ((0, right_b),))
    else:
        got_one = load(lefts_in[0], left_buf.at[0], here.at[1])
        got_q = load(rights_in[0], right_b, here.at[2])
        got_1 = load(rights_in[1], right_a, here.at[3])
        got_one.wait()
        got_q.wait()
        products(left_buf.at[0], ((0, right_b),))
        got_two = load(lefts_in[1], left_buf.at[0], here.at[1])

    for step in range(1, groups):
        arrived(early_group.at[from_group(step)], eg_s.at[step], eg_r.at[step])
    acc = early_group[0]
    for i in range(1, groups):
        acc = acc + early_group[i]
    early_out[k, c] = acc
    for step in range(1, LINE):
        go(remote(early_out.at[k, c], early_out.at[k, c], el_s.at[step], el_r.at[step], me.at(me.line_to(step), g, k)))

    got_two.wait()
    got_1.wait()
    products(left_buf.at[0], ((1, right_a),))

    got_s.wait()
    for step in range(1, LINE):
        arrived(s_line.at[step - 1], sline_s.at[step], sline_r.at[step])
    add_rows(
        lambda at: s_own.at[at],
        [lambda at: s_own.at[at]] + [partial(lambda p, at: s_line.at[p, at], p) for p in range(LINE - 1)],
        slot_len,
        16,
    )
    go(remote(s_own, ssum_ref.at[k], fin_s, fin_r, sibling))
    keep = [load(s_own, ssum_ref.at[k], keep_sem.at[0])]

    row_keep[...] = jnp.zeros_like(row_keep)

    def sum_groups(m, first):
        for step in range(1, groups):
            arrived(g_got[m].at[step - 1], gp_s.at[m, step], gp_r.at[m, step])
        width = pl.ds(pl.multiple_of(c * cols[m], 128), cols[m])
        total = jnp.zeros((8, cols[m]), f32)
        for step in (1, 2, 3, 0):
            line = me.line_to(step)

            def body(i, carry, line=line):
                at = pl.ds(pl.multiple_of(i * 16, 16), 16)
                acc = g_own[m][line, g, at, :].astype(f32)
                for p in range(groups - 1):
                    acc = acc + g_got[m][p, line, at, :].astype(f32)
                g_own[m][line, g, at, :] = acc.astype(low)
                square = acc * acc + eps_second
                row_keep[line, at, m : m + 1] = jnp.sum(square, 1, keepdims=True)
                return carry + square[:8] + square[8:]

            total = lax.fori_loop(0, rows_own // 16, body, total)
            if step:
                go(
                    remote(
                        g_own[m].at[line, g], g_out[m].at[:, width], gl_s.at[m, step], gl_r.at[m, step],
                        me.at(line, g, k),
                    )
                )
            else:
                keep.append(load(g_own[m].at[line, g], g_out[m].at[:, width], keep_sem.at[2 + m]))
        total = jnp.sum(total, 0, keepdims=True)
        for t in range(cols[m] // 128):
            col_now[first + t : first + t + 1, :] = total[:, t * 128 : (t + 1) * 128]

    firsts = []
    edge = 0
    for m in range(count):
        firsts.append(edge)
        edge += cols[m] // 128
    sum_groups(3, firsts[3])
    sum_groups(2, firsts[2])

    for step in range(1, groups):
        arrived(m_all.at[pl.ds(from_group(step) * seqs, seqs)], mall_s.at[step], mall_r.at[step])
    mixed_cols = pl.ds(pl.multiple_of((c * 2 + k) * feat, 128), feat)
    for step in (1, 2, 3, 0):
        line = me.line_to(step)
        for s in range(seq_dev):
            m_send[line, s] = m_all[pick[line * seq_dev + s]]
        where = mixed_ref.at[:, :, mixed_cols]
        if step:
            go(remote(m_send.at[line], where, mout_s.at[0, step], mout_r.at[0, step], me.at(line, g, k)))
        else:
            keep.append(load(m_send.at[line], where, keep_sem.at[1]))
        go(remote(m_send.at[line], where, mout_s.at[1, step], mout_r.at[1, step], me.at(line, g, me.other)))

    sum_groups(0, firsts[0])
    sum_groups(1, firsts[1])

    for step in range(1, groups):
        go(remote(col_now, col_group.at[g], cg_s.at[step], cg_r.at[step], me.at(c, to_group(step), k)))
    col_group[g] = col_now[...]
    for step in (1, 2, 3, 0):
        line = me.line_to(step)
        row_turn[line] = jnp.transpose(row_keep[line])[:8]
        if step:
            go(remote(row_turn.at[line], row_out.at[k, c], rl_s.at[0, step], rl_r.at[0, step], me.at(line, g, k)))
        else:
            row_out[k, c] = row_turn[line]
        go(remote(row_turn.at[line], row_out.at[k, c], rl_s.at[1, step], rl_r.at[1, step], me.at(line, g, me.other)))
    for step in range(1, groups):
        arrived(col_group.at[from_group(step)], cg_s.at[step], cg_r.at[step])
    acc = col_group[0]
    for i in range(1, groups):
        acc = acc + col_group[i]
    col_out[k, c] = acc
    for step in range(1, LINE):
        go(remote(col_out.at[k, c], col_out.at[k, c], cl_s.at[step], cl_r.at[step], me.at(me.line_to(step), g, k)))
    for step in range(1, LINE):
        arrived(early_out.at[k, me.line_from(step)], el_s.at[step], el_r.at[step])
    go(remote(early_out.at[k], early_out.at[k], es_s, es_r, sibling))
    for step in range(1, LINE):
        arrived(col_out.at[k, me.line_from(step)], cl_s.at[step], cl_r.at[step])
    go(remote(col_out.at[k], col_out.at[k], cs_s, cs_r, sibling))

    for m in range(count):
        for step in range(1, LINE):
            dst = g_out[m].at[:, pl.ds(pl.multiple_of(me.line_from(step) * cols[m], 128), cols[m])]
            arrived(dst, gl_s.at[m, step], gl_r.at[m, step])
    for step in range(LINE):
        source = me.line_from(step)
        for core, way in ((k, 0), (me.other, 1)):
            if step or way:
                dst = mixed_ref.at[:, :, pl.ds(pl.multiple_of((source * 2 + core) * feat, 128), feat)]
                arrived(dst, mout_s.at[way, step], mout_r.at[way, step])
                arrived(row_out.at[core, source], rl_s.at[way, step], rl_r.at[way, step])
    arrived(ssum_ref.at[me.other], fin_s, fin_r)
    arrived(early_out.at[me.other], es_s, es_r)
    arrived(col_out.at[me.other], cs_s, cs_r)
    for copy in sends:
        copy.wait_send()
    for m in range(count):
        for step in range(1, groups):
            send_group(m, step, "wait_send")
    for copy in keep:
        copy.wait()


def scatter_all(groups, cols, seq_dev, rows_own, pick, m_line, s_pair, lefts, rights, early):
    slot_len = s_pair.shape[1]
    rows = lefts[0].shape[0]
    count = len(cols)
    feat = D // (2 * LINE)
    seqs = LINE * seq_dev
    dma = pltpu.SemaphoreType.DMA
    f32, low = jnp.float32, jnp.bfloat16
    col_rows = sum(cols) // 128
    return pl.pallas_call(
        partial(scatter_kernel, groups, cols, seq_dev, slot_len, rows_own),
        out_shape=[
            jax.ShapeDtypeStruct((seq_dev, slot_len, D), low),
            jax.ShapeDtypeStruct((seq_dev, slot_len, D), low),
        ]
        + [jax.ShapeDtypeStruct((rows_own, LINE * width), low) for width in cols]
        + [
            jax.ShapeDtypeStruct((2, LINE) + early.shape, f32),
            jax.ShapeDtypeStruct((2, LINE, col_rows, 128), f32),
            jax.ShapeDtypeStruct((2, LINE, 8, 128), f32),
        ],
        in_specs=[SMEM] + [ANY] * (5 + count) + [VMEM],
        out_specs=[ANY] * (2 + count) + [VMEM] * 3,
        scratch_shapes=[
            pltpu.VMEM((2 if groups == 4 else 1, rows, D), low),
            pltpu.VMEM((rows, cols[1]), low),
            pltpu.VMEM((rows, cols[0]), low),
            pltpu.VMEM((rows, cols[2]), low),
        ]
        + [pltpu.VMEM((LINE, groups, rows_own, width), low) for width in cols]
        + [pltpu.VMEM((groups - 1, LINE, rows_own, width), low) for width in cols]
        + [
            pltpu.VMEM((LINE, seqs, slot_len, feat), low),
            pltpu.VMEM((groups * seqs, slot_len, feat), low),
            pltpu.VMEM((LINE, seq_dev, slot_len, feat), low),
            pltpu.VMEM((slot_len, D), low),
            pltpu.VMEM((LINE - 1, slot_len, D), low),
            pltpu.VMEM((groups,) + early.shape, f32),
            pltpu.VMEM((col_rows, 128), f32),
            pltpu.VMEM((groups, col_rows, 128), f32),
            pltpu.VMEM((LINE, 128, 128), f32),
            pltpu.VMEM((LINE, 8, 128), f32),
            dma((7,)),
            dma((LINE,)),
            dma((LINE,)),
            dma(()),
            dma(()),
            dma((groups,)),
            dma((groups,)),
            dma((2, LINE)),
            dma((2, LINE)),
            dma((count, groups)),
            dma((count, groups)),
            dma((count, LINE)),
            dma((count, LINE)),
            dma((groups,)),
            dma((groups,)),
            dma((LINE,)),
            dma((LINE,)),
            dma(()),
            dma(()),
            dma((groups,)),
            dma((groups,)),
            dma((LINE,)),
            dma((LINE,)),
            dma(()),
            dma(()),
            dma((2, LINE)),
            dma((2, LINE)),
            dma((2 + count,)),
        ],
        compiler_params=pltpu.CompilerParams(
            collective_id=1, has_side_effects=True, vmem_limit_bytes=62 * 1024 * 1024
        ),
        name="scatter_all",
    )(pick, m_line.reshape(LINE, seqs, slot_len, feat), s_pair, *lefts, *rights, early)


def per_device(
    tokens,
    cotangent,
    lengths,
    permutation,
    w_qkv,
    w_dense,
    w_fc1,
    w_fc2,
    norm_vectors,
    split_biases,
    row_state,
    col_state,
    norm_moment,
    bias_moment,
):
    f32, low = jnp.float32, jnp.bfloat16
    n_data = lax.axis_size("dp")
    groups = n_data // LINE
    data = lax.axis_index("dp")
    core = lax.axis_index("tensor")
    line = data // groups
    group = data % groups
    seq_dev, slot_len, width = tokens.shape
    rows_own = w_qkv.shape[0]
    seqs = LINE * seq_dev
    rows = seqs * slot_len
    head_dim = D // HEADS
    rot_dims = head_dim // 4
    weights = (w_qkv, w_dense, w_fc1, w_fc2)
    cols = tuple(w.shape[1] // LINE for w in weights)
    order = (0, 2, 1, 3)
    lows = [weights[i].astype(low) for i in order]
    mine = (jnp.arange(LINE)[:, None] * groups + group) * seq_dev + jnp.arange(seq_dev)[None, :]
    my_lengths = jnp.take(lengths, mine.reshape(-1))
    places = jnp.arange(slot_len, dtype=jnp.int32)
    valid = (places[None, :] < my_lengths[:, None]).astype(f32).reshape(rows, 1)
    bias_qkv = lax.dynamic_slice_in_dim(split_biases, line * cols[0], cols[0], 1)
    bias_mlp = lax.dynamic_slice_in_dim(split_biases, LINE * cols[0] + line * cols[2], cols[2], 1)
    row_old = jnp.where(core == 0, jnp.sum(row_state, 1), 0.0)
    extra = jnp.zeros((2, D), f32).at[0, :4].set(row_old)
    vectors = jnp.concatenate([norm_vectors, extra], 0)
    (norm_one, norm_two, back, qkv_grad, pre_grad, attn, hidden, m_line, s_pair, early) = gather_all(
        groups, lows, tokens, cotangent, vectors, jnp.concatenate([bias_qkv, bias_mlp], 1), valid,
        turn_tables(slot_len, rot_dims, head_dim // 2),
    )
    source = jnp.take(permutation, mine.reshape(-1))
    chip, inside = source // seq_dev, source % seq_dev
    pick = ((chip % groups) * seqs + (chip // groups) * seq_dev + inside).astype(jnp.int32)
    outs = scatter_all(
        groups,
        tuple(cols[i] for i in order),
        seq_dev,
        rows_own,
        pick,
        m_line,
        s_pair,
        (norm_one, norm_two, back),
        (qkv_grad, pre_grad, attn, hidden),
        early,
    )
    mixed, s_sum = outs[:2]
    early_all, col_all, row_all = outs[6:]
    grads = [None] * 4
    for place, i in enumerate(order):
        grads[i] = outs[2 + place].astype(f32)
    own_x = tokens.reshape(-1, width).astype(f32)
    own_centre = own_x - jnp.mean(own_x, -1, keepdims=True)
    own_scale = lax.rsqrt(jnp.mean(own_centre * own_centre, -1, keepdims=True) + eps_norm)
    own_unit = own_centre * own_scale
    own_valid = (places[None, :] < lax.dynamic_slice_in_dim(lengths, data * seq_dev, seq_dev)[:, None]).reshape(-1, 1)
    own_back = jnp.where(own_valid, cotangent.reshape(-1, width), jnp.zeros((), low)).astype(f32)
    flow = s_sum.reshape(-1, width).astype(f32)
    through = own_scale * (
        flow - jnp.mean(flow, -1, keepdims=True) - own_unit * jnp.mean(flow * own_unit, -1, keepdims=True)
    )
    grad_tokens = (own_back + through).astype(low).reshape(seq_dev, slot_len, width)
    early_all = early_all.reshape(2, LINE, -1)
    at_bias = 5 * D
    at_row = at_bias + cols[0] + cols[2]
    both = jnp.sum(early_all, (0, 1))
    norm_total = both[:at_bias].reshape(5, D)
    norm_total = jnp.concatenate([norm_total, norm_total[4:]], 0)
    bias_mine = lax.dynamic_index_in_dim(early_all, core, 0, False)[:, at_bias:at_row]
    bias_total = jnp.concatenate([bias_mine[:, : cols[0]].reshape(-1), bias_mine[:, cols[0] :].reshape(-1)])[None, :]
    row_old_sum = both[at_row : at_row + 4]
    row_total = jnp.sum(row_all, (0, 1))[:, :rows_own]
    col_mine = lax.dynamic_index_in_dim(col_all, core, 0, False).reshape(LINE, -1)
    mass_all = jnp.sum(col_all, (0, 1)).reshape(-1)
    row_at, col_at, mass_at, edge = [None] * 4, [None] * 4, [None] * 4, 0
    for place, i in enumerate(order):
        row_at[i] = row_total[place]
        col_at[i] = col_mine[:, edge : edge + cols[i]].reshape(-1)
        mass_at[i] = jnp.sum(mass_all[edge : edge + cols[i]])
        edge += cols[i]
    col_total = jnp.concatenate(col_at)
    col_new = decay * col_state + (1.0 - decay) * (col_total[None, :] / D)
    full_cols = (3.0 * D, 1.0 * D, 1.0 * FF, 1.0 * FF)
    rates = (
        rate_scale / math.sqrt(D),
        rate_scale / math.sqrt(D // 8),
        rate_scale / math.sqrt(D),
        rate_scale / math.sqrt(FF),
    )
    new_list, row_list = [], []
    edge = 0
    for i in range(4):
        wide = weights[i].shape[1]
        row_new = decay * row_state[i] + (1.0 - decay) * (row_at[i] / full_cols[i])
        mean = (decay * row_old_sum[i] + (1.0 - decay) * (mass_at[i] / full_cols[i])) / D
        second = row_new[:, None] * col_new[0, edge : edge + wide][None, :] / mean
        new_list.append(weights[i] - rates[i] * grads[i] * lax.rsqrt(second))
        row_list.append(row_new)
        edge += wide
    row_new = jnp.stack(row_list)
    norm_moment_new = decay * norm_moment + (1.0 - decay) * (norm_total * norm_total + eps_second)
    norm_new = norm_vectors - rate_norm * norm_total * lax.rsqrt(norm_moment_new)
    bias_moment_new = decay * bias_moment + (1.0 - decay) * (bias_total * bias_total + eps_second)
    bias_new = split_biases - rate_vector * bias_total * lax.rsqrt(bias_moment_new)
    return (
        mixed,
        grad_tokens,
        *grads,
        *new_list,
        *[new.astype(low) for new in new_list],
        row_new,
        col_new,
        norm_total,
        norm_moment_new,
        norm_new,
        bias_total,
        bias_moment_new,
        bias_new,
    )


def solution(mesh):
    halves = P("dp", "tensor")
    split = P("tensor", None)
    in_specs = (
        P("dp", None, None),
        P("dp", None, None),
        P(),
        P(),
        halves,
        halves,
        halves,
        halves,
        P(),
        split,
        P(None, "dp"),
        split,
        P(),
        split,
    )
    out_specs = (
        (P("dp", None, None),) * 2
        + (halves,) * 12
        + (P(None, "dp"), split)
        + (P(),) * 3
        + (split,) * 3
    )
    return jax.shard_map(
        per_device, mesh=mesh, in_specs=in_specs, out_specs=out_specs, check_vma=False
    )
```

```python
from functools import partial
import math

import jax
import jax.numpy as jnp
import numpy as np
from jax import lax
from jax.experimental import pallas as pl
from jax.experimental.pallas import tpu as pltpu
from jax.sharding import PartitionSpec as P

D = 2048
FF = 8192
HEADS = 8
LINE = 4

eps_norm = 1e-05
eps_second = 1e-30
decay = 0.5
rate_scale = 1.0
rate_norm = 0.5
rate_vector = 0.05
neg_large = -1e30

MESH = pl.DeviceIdType.MESH
ANY = pl.BlockSpec(memory_space=pl.ANY)
VMEM = pl.BlockSpec(memory_space=pltpu.VMEM)
SMEM = pl.BlockSpec(memory_space=pltpu.SMEM)


def turn_tables(slot_len, rot_dims, width):
    half = rot_dims // 2
    freq = np.float32(10000.0) ** (np.float32(-2.0) * np.arange(half, dtype=np.float32) / np.float32(rot_dims))
    angle = np.arange(slot_len, dtype=np.float32)[:, None] * freq[None, :].astype(np.float32)
    tables = np.zeros((3, slot_len, width), np.float32)
    tables[0] = 1.0
    tables[0, :, :half] = tables[0, :, half:rot_dims] = np.cos(angle)
    tables[1, :, :half] = tables[2, :, half:rot_dims] = np.sin(angle)
    return tables


class Place:
    def __init__(self, groups):
        self.groups = groups
        data = lax.axis_index("dp")
        self.core = lax.axis_index("tensor")
        self.other = 1 - self.core
        self.line = data // groups
        self.group = data % groups

    def at(self, line, group, core):
        return (line * self.groups + group, core)

    def line_to(self, step):
        return (self.line + step) % LINE

    def line_from(self, step):
        return (self.line + LINE - step) % LINE

    def group_to(self, step):
        g = self.group
        if self.groups == 4:
            if step == 1:
                return g + 1 - 2 * (g % 2)
            if step == 2:
                return (g + 2) % 4
            return 3 - g
        return (g + step) % self.groups

    def group_from(self, step):
        if self.groups == 4:
            return self.group_to(step)
        return (self.group + self.groups - step) % self.groups

    def greet(self):
        barrier = pltpu.get_barrier_semaphore()
        count = 0
        for step in range(1, LINE):
            for core in (self.core, self.other):
                pl.semaphore_signal(
                    barrier, inc=1, device_id=self.at(self.line_to(step), self.group, core), device_id_type=MESH
                )
                count += 1
        for step in range(1, self.groups):
            pl.semaphore_signal(
                barrier, inc=1, device_id=self.at(self.line, self.group_to(step), self.core), device_id_type=MESH
            )
            count += 1
        pl.semaphore_signal(
            barrier, inc=1, device_id=self.at(self.line, self.group, self.other), device_id_type=MESH
        )
        pl.semaphore_wait(barrier, count + 1)


def remote(src, dst, send, recv, device):
    return pltpu.make_async_remote_copy(
        src_ref=src, dst_ref=dst, send_sem=send, recv_sem=recv, device_id=device, device_id_type=MESH
    )


def dot(left, right):
    return jnp.dot(left, right, preferred_element_type=jnp.float32)


def gather_kernel(groups, cols, seq_dev, slot_len, *refs):
    count = len(cols)
    f32, low = jnp.float32, jnp.bfloat16
    w_in = refs[:count]
    acts_in = refs[count : count + 2]
    vec_ref, bias_ref, valid_ref, turn_ref = refs[count + 2 : count + 6]
    outs = refs[count + 6 : count + 18]
    (n1_out, n2_out, qg_out, pg_out, near_out, far_out, s_out, gd_own, g2_own, gd_got, g2_got, early_ref) = outs
    rest = refs[count + 18 :]
    w_out = rest[:count]
    acts_out = rest[count : count + 2]
    (qkv_keep, prob_keep, attn_keep, hid_keep, pg_keep, one_buf, two_buf, back_buf, m_buf, m_got, m_half, s_got,
     qkv_now, pre_now, stat_keep, norm_acc, bias_acc) = rest[count + 2 : count + 19]
    (one_s, one_r, two_s, two_r, three_s, three_r, row_s, row_r, sib_s, sib_r, here, out_a, out_b,
     out_d, msib_s, msib_r, ssib_s, ssib_r, half_s, half_r, far_s, far_r, near_sem, s_here, gp_s, gp_r,
     g_here) = rest[count + 19 :]
    me = Place(groups)
    c, g, k = me.line, me.group, me.core
    me.greet()
    sibling = me.at(c, g, me.other)
    rows_own = w_in[0].shape[0]
    block_rows = seq_dev * slot_len
    near = groups == 4
    START, SENT = "start", "wait_send"

    def block(ref, line, width):
        return ref.at[:, pl.ds(pl.multiple_of(line * width, 128), width)]

    def place(m, line, group):
        return w_out[m].at[pl.ds(pl.multiple_of((line * groups + group) * rows_own, 32), rows_own)]

    def rows_of(which, line, core):
        return acts_out[which].at[pl.ds(pl.multiple_of((line * seq_dev + core) * slot_len, 32), slot_len)]

    partner = c + 1 - 2 * (c % 2)
    beyond = (c + 2) % LINE

    def row_send(which, q, act):
        origin = beyond if q == 2 else c
        copy = remote(
            rows_of(which, beyond, k) if q == 2 else acts_in[which].at[k],
            rows_of(which, origin, k),
            row_s.at[which, q],
            row_r.at[which, q],
            me.at(beyond if q == 1 else partner, g, k),
        )
        getattr(copy, act)()

    def row_origin(q):
        return (partner, beyond, (partner + 2) % LINE)[q]

    def to_sibling(which, q, act):
        rows = rows_of(which, row_origin(q), k)
        copy = remote(rows, rows, sib_s.at[which, q], sib_r.at[which, q], sibling)
        getattr(copy, act)()

    def pass_on(which, q):
        rows = rows_of(which, row_origin(q), k)
        remote(rows, rows, row_s.at[which, q], row_r.at[which, q], sibling).wait_recv()
        if q == 1:
            row_send(which, 2, START)
        to_sibling(which, q, START)

    def arrive_sibling(which):
        for q in range(3):
            rows = rows_of(which, row_origin(q), me.other)
            remote(rows, rows, sib_s.at[which, q], sib_r.at[which, q], sibling).wait_recv()

    def local_acts(which, act):
        for s in range(seq_dev):
            copy = pltpu.make_async_copy(acts_in[which].at[s], rows_of(which, c, s), here.at[count + which, s])
            getattr(copy, act)()

    def local_weight(m, act):
        copy = pltpu.make_async_copy(block(w_in[m], c, cols[m]), place(m, c, g), here.at[m, 0])
        getattr(copy, act)()

    def stage_one(m, act):
        for step in range(1, LINE):
            to = me.line_to(step)
            copy = remote(
                block(w_in[m], to, cols[m]),
                place(m, c, g),
                one_s.at[m, step],
                one_r.at[m, step],
                me.at(to, g, k),
            )
            getattr(copy, act)()

    def stage_two(m, step, act):
        where = place(m, me.line_from(step), g)
        src = block(w_in[m], c, cols[m]) if step == 0 else where
        for peer in range(1, 3 if near else groups):
            copy = remote(
                src, where, two_s.at[m, step, peer], two_r.at[m, step, peer], me.at(c, me.group_to(peer), k)
            )
            getattr(copy, act)()

    def first_half(m):
        for step in range(1, LINE):
            dst = place(m, me.line_from(step), g)
            remote(dst, dst, one_s.at[m, step], one_r.at[m, step], sibling).wait_recv()
            stage_two(m, step, START)

    def wait_two(m, step, peer):
        dst = place(m, me.line_from(step), me.group_from(peer))
        remote(dst, dst, two_s.at[m, step, peer], two_r.at[m, step, peer], sibling).wait_recv()

    def stage_three(m, step, act):
        source, target = (1, 2) if step % 2 == 0 else (2, 1)
        where = place(m, me.line_from(step), me.group_to(source))
        copy = remote(where, where, three_s.at[m, step], three_r.at[m, step], me.at(c, me.group_to(target), k))
        getattr(copy, act)()

    def relay(m):
        for step in range(LINE):
            for peer in range(1, 3 if near else groups):
                wait_two(m, step, peer)
            if near:
                stage_three(m, step, START)

    def last(m):
        if near:
            for step in range(LINE):
                dst = place(m, me.line_from(step), me.group_to(3))
                remote(dst, dst, three_s.at[m, step], three_r.at[m, step], sibling).wait_recv()

    row_send(0, 1, START)
    row_send(0, 0, START)
    for m in (0, 1):
        stage_one(m, START)
        stage_two(m, 0, START)
    local_acts(0, START)
    local_weight(0, START)
    local_weight(1, START)
    norm_acc[...] = jnp.zeros_like(norm_acc)
    bias_acc[...] = jnp.zeros_like(bias_acc)
    first_half(0)
    pass_on(0, 1)
    for m in (2, 3):
        stage_one(m, START)
        stage_two(m, 0, START)
    local_acts(1, START)
    local_weight(2, START)
    local_weight(3, START)
    pass_on(0, 0)
    first_half(1)
    row_send(1, 1, START)
    row_send(1, 0, START)
    relay(0)
    pass_on(0, 2)
    relay(1)
    local_acts(0, "wait")
    local_weight(0, "wait")
    local_weight(1, "wait")
    last(0)
    last(1)
    arrive_sibling(0)

    wq, w1, wd, w2 = w_out
    x_all, ct_all = acts_out
    head = cols[0] // 3
    half = head // 2
    chunk = 16
    wide = 512
    ways = D // wide
    root = math.sqrt(head)
    causal = lax.broadcasted_iota(jnp.int32, (slot_len, slot_len), 0) >= lax.broadcasted_iota(
        jnp.int32, (slot_len, slot_len), 1
    )

    def turn(v, sign):
        left = pltpu.roll(v, half - 32, 1)
        right = pltpu.roll(v, 32, 1)
        if sign > 0:
            return v * turn_ref[0] - left * turn_ref[1] + right * turn_ref[2]
        return v * turn_ref[0] + left * turn_ref[1] - right * turn_ref[2]

    def contract(left, right, dims):
        return lax.dot_general(left, right, ((dims[0], dims[1]), ((), ())), preferred_element_type=f32)

    def put_one(i, line, act):
        rows = pl.ds(pl.multiple_of(line * block_rows, 128), block_rows)
        getattr(pltpu.make_async_copy(one_buf, n1_out.at[rows], out_a), act)()
        getattr(pltpu.make_async_copy(two_buf.at[0], n2_out.at[rows], out_b.at[0]), act)()

    @pl.loop(0, LINE)
    def forward(i):
        line = (c + i) % LINE
        base = pl.multiple_of(line * block_rows, 128)

        @pl.when(i == 0)
        def _():
            first_half(2)
            first_half(3)

        @pl.when(i == 1)
        def _():
            relay(2)
            pass_on(1, 1)

        @pl.when(i == 2)
        def _():
            relay(3)
            pass_on(1, 0)

        @pl.when(i >= 1)
        def _():
            put_one(i, line, "wait")

        @pl.loop(0, block_rows // chunk)
        def norm(j):
            at = pl.ds(pl.multiple_of(base + j * chunk, chunk), chunk)
            to = pl.ds(pl.multiple_of(j * chunk, chunk), chunk)
            x = x_all[at, :].astype(f32)
            mean = jnp.mean(x, -1, keepdims=True)
            centre = x - mean
            scale = lax.rsqrt(jnp.mean(centre * centre, -1, keepdims=True) + eps_norm)
            stat_keep[at, 0:1] = mean
            stat_keep[at, 1:2] = scale
            unit = centre * scale
            one_buf[to, :] = (unit * vec_ref[0:1, :] + vec_ref[1:2, :]).astype(low)
            two_buf[0, to, :] = (unit * vec_ref[2:3, :] + vec_ref[3:4, :]).astype(low)

        put_one(i, line, "start")
        qkv_now[...] = dot(one_buf[...], wq[...]) + bias_ref[0:1, : cols[0]]
        pre_now[...] = dot(two_buf[0], w1[...]) + bias_ref[0:1, cols[0] :]

        for s in range(seq_dev):
            part = slice(s * slot_len, (s + 1) * slot_len)
            rows = pl.ds(pl.multiple_of(base + s * slot_len, 32), slot_len)
            qkv_keep[rows, 0:half] = turn(qkv_now[part, 0:half], 1).astype(low)
            qkv_keep[rows, half:head] = qkv_now[part, half:head].astype(low)
            qkv_keep[rows, head : head + half] = turn(qkv_now[part, head : head + half], 1).astype(low)
            qkv_keep[rows, head + half :] = qkv_now[part, head + half :].astype(low)
            query = qkv_keep[rows, :head]
            keys = qkv_keep[rows, head : 2 * head]
            values = qkv_keep[rows, 2 * head :]
            scores = jnp.where(causal, contract(query, keys, ((1,), (1,))) / root, neg_large)
            expo = jnp.exp(scores - jnp.max(scores, -1, keepdims=True))
            probs = expo / jnp.sum(expo, -1, keepdims=True)
            prob_keep[line * seq_dev + s] = probs
            attn_keep[rows, :] = (dot(probs.astype(low), values) * valid_ref[rows, :]).astype(low)

        @pl.loop(0, block_rows // chunk)
        def act(j):
            at = pl.ds(pl.multiple_of(base + j * chunk, chunk), chunk)
            pre = pre_now[pl.ds(pl.multiple_of(j * chunk, chunk), chunk), :]
            area = 0.5 * (1.0 + lax.erf(pre * math.sqrt(0.5)))
            hid_keep[at, :] = (pre * area * valid_ref[at, :]).astype(low)
            pg_keep[at, :] = (area + pre * (jnp.exp(-0.5 * pre * pre) * (1.0 / math.sqrt(2.0 * math.pi)))).astype(low)

    put_one(LINE - 1, (c + LINE - 1) % LINE, "wait")
    local_weight(2, "wait")
    local_weight(3, "wait")
    last(2)
    last(3)
    mine = c * 2 + k

    def pair_m(i, act):
        copy = remote(m_buf.at[i % 2, me.other], m_got.at[i], msib_s.at[i], msib_r.at[i], sibling)
        getattr(copy, act)()

    def half_m(i, act):
        for q, to in enumerate((partner, (partner + 2) % LINE)):
            copy = remote(
                m_got.at[i, to], m_half.at[i, q], half_s.at[i, q], half_r.at[i, q], me.at(partner, g, k)
            )
            getattr(copy, act)()

    def far_m(i, act):
        copy = remote(m_got.at[i, beyond], far_out.at[i], far_s.at[i], far_r.at[i], me.at(beyond, g, k))
        getattr(copy, act)()

    def near_m(i, act):
        getattr(pltpu.make_async_copy(m_got.at[i, c], near_out.at[i], near_sem.at[i]), act)()

    def sent_m(i):
        half_m(i, SENT)
        far_m(i, SENT)
        near_m(i, "wait")

    def second_m(i):
        half_m(i, "wait_recv")

        @pl.loop(0, block_rows // 64)
        def add(j):
            at = pl.ds(pl.multiple_of(j * 64, 64), 64)
            for q, to in enumerate((c, beyond)):
                total = m_got[i, to, at, :].astype(f32) + m_half[i, q, at, :].astype(f32)
                m_got[i, to, at, :] = total.astype(low)

        far_m(i, START)
        near_m(i, START)

    def pair_add(i):
        pair_m(i, "wait_recv")

        @pl.loop(0, LINE)
        def add_outer(p):
            @pl.loop(0, block_rows // 64)
            def add(j):
                at = pl.ds(pl.multiple_of(j * 64, 64), 64)
                total = m_buf[i % 2, k, p, at, :].astype(f32) + m_got[i, p, at, :].astype(f32)
                m_got[i, p, at, :] = total.astype(low)

        half_m(i, START)

    @pl.loop(0, LINE)
    def outputs(i):
        base = pl.multiple_of(i * block_rows, 128)
        whole = pl.ds(base, block_rows)
        slot = i % 2

        @pl.when(i == 1)
        def _():
            pass_on(1, 2)

        @pl.when(i >= 2)
        def _():
            pair_m(i - 2, SENT)

        live = valid_ref[whole, :]

        @pl.loop(0, ways)
        def output(j):
            at = pl.ds(pl.multiple_of(j * wide, 128), wide)
            total = contract(attn_keep[whole, :], wd[at, :], ((1,), (1,)))
            total = total + contract(hid_keep[whole, :], w2[at, :], ((1,), (1,)))
            feature = (lax.broadcasted_iota(jnp.int32, (1, wide), 1) + j * wide) // (D // (2 * LINE))
            mask = jnp.where(feature == mine, 1.0, 0.0)
            extra = x_all[whole, at].astype(f32) + (vec_ref[4:5, at] + vec_ref[5:6, at])
            total = ((total + mask * extra) * live).astype(low)
            m_buf[slot, 0, j] = total[:, : wide // 2]
            m_buf[slot, 1, j] = total[:, wide // 2 :]

        pair_m(i, START)

        @pl.when(i >= 1)
        def _():
            pair_add(i - 1)

    local_acts(1, "wait")
    arrive_sibling(1)

    per = 128 // rows_own
    part_cols = 256
    fits = block_rows // 128
    pieces = (cols[2] + cols[3]) // part_cols
    dense_pieces = cols[2] // part_cols

    def out_group(i):
        flip_x, flip_y = 1 - i % 2, 1 - i // 2
        return (g // 2 + flip_y) % 2 * 2 + (g % 2 + flip_x) % 2

    def out_products(i):
        slot = i % 2
        if near:
            to = out_group(i)
            tiles = [(l, to) for l in range(LINE)]
        else:
            tiles = [(i, t * per) for t in range(LINE)]
        lhs = jnp.concatenate(
            [ct_all[:, pl.ds(pl.multiple_of((l * groups + p) * rows_own, 128), 128)] for l, p in tiles], 1
        )
        first = 0
        for right in (attn_keep, hid_keep):
            out = contract(lhs, right[...], ((0,), (0,))).astype(low)
            for n in range(right.shape[1] // part_cols):
                nb = first + n
                for t in range(LINE):
                    m_buf[slot, nb // fits, t, (nb % fits) * 128 : (nb % fits + 1) * 128, :] = out[
                        t * 128 : (t + 1) * 128, n * part_cols : (n + 1) * part_cols
                    ]
            first += right.shape[1] // part_cols

    def out_piece(i, nb, to):
        row = (nb % fits) * 128
        if near:
            return m_buf.at[i % 2, nb // fits, :, pl.ds(row, 128), :]
        return m_buf.at[i % 2, nb // fits, to // per, pl.ds(pl.multiple_of(row + (to % per) * rows_own, 32), rows_own), :]

    def out_place(refs, i, nb, step):
        ref, n = (refs[0], nb) if nb < dense_pieces else (refs[1], nb - dense_pieces)
        at = pl.ds(n * part_cols, part_cols)
        if step is not None:
            ref = ref.at[step - 1]
        return ref.at[:, :, at] if near else ref.at[i, :, at]

    def out_send(i, step, act):
        to = out_group(i) if near else (g + step) % groups
        for nb in range(pieces):
            sem = (0 if near else i, step, nb)
            copy = remote(
                out_piece(i, nb, to), out_place((gd_got, g2_got), i, nb, step), gp_s.at[sem], gp_r.at[sem],
                me.at(c, to, k),
            )
            getattr(copy, act)()

    def out_keep(i, act):
        for nb in range(pieces):
            copy = pltpu.make_async_copy(
                out_piece(i, nb, g), out_place((gd_own, g2_own), i, nb, None), g_here.at[0 if near else i, nb]
            )
            getattr(copy, act)()

    def out_sends(i, act):
        local = "wait" if act == SENT else act
        if near:

            @pl.when(i < groups - 1)
            def _():
                out_send(i, groups - 1 - i, act)

            @pl.when(i == groups - 1)
            def _():
                out_keep(i, local)
        else:
            for step in range(1, groups):
                out_send(i, step, act)
            out_keep(i, local)

    def pair_s(i, act):
        line = (c + i) % LINE
        rows = pl.ds(pl.multiple_of(me.other * slot_len, 32), slot_len)
        copy = remote(two_buf.at[i % 2, rows], s_got.at[line], ssib_s.at[i], ssib_r.at[i], sibling)
        getattr(copy, act)()

    def put_s(i, act):
        line = (c + i) % LINE
        rows = pl.ds(pl.multiple_of(k * slot_len, 32), slot_len)
        getattr(pltpu.make_async_copy(two_buf.at[i % 2, rows], s_out.at[line], s_here.at[i]), act)()

    def finish_s(i):
        line = (c + i) % LINE
        pair_s(i, "wait_recv")

        @pl.loop(0, slot_len // chunk)
        def add(j):
            at = pl.ds(pl.multiple_of(k * slot_len + j * chunk, chunk), chunk)
            to = pl.ds(pl.multiple_of(j * chunk, chunk), chunk)
            total = two_buf[i % 2, at, :].astype(f32) + s_got[line, to, :].astype(f32)
            two_buf[i % 2, at, :] = total.astype(low)

        put_s(i, START)

    def put_rest(line, act):
        rows = pl.ds(pl.multiple_of(line * block_rows, 128), block_rows)
        for place_at, (buf, out) in enumerate(((qkv_keep, qg_out), (pg_keep, pg_out))):
            getattr(pltpu.make_async_copy(buf.at[rows], out.at[rows], out_d.at[place_at, line]), act)()

    @pl.loop(0, LINE)
    def backward(i):
        line = (c + i) % LINE
        base = pl.multiple_of(line * block_rows, 128)
        whole = pl.ds(base, block_rows)
        slot = i % 2

        @pl.when(i == 0)
        def _():
            pair_m(LINE - 2, SENT)

        @pl.when(i == 1)
        def _():
            pair_m(LINE - 1, SENT)

        @pl.when(i >= 2)
        def _():
            out_sends(i - 2, SENT)

        out_products(i)
        out_sends(i, START)

        @pl.when(i == 0)
        def _():
            pair_add(LINE - 1)

        @pl.when((i == 1) | (i == 2))
        def _():
            second_m(i * 2 - 2)
            second_m(i * 2 - 1)

        live = valid_ref[whole, :]
        back_buf[...] = (ct_all[whole, :].astype(f32) * live).astype(low)
        attn_grad = dot(back_buf[...], wd[...]).astype(low)
        pre_now[...] = dot(back_buf[...], w2[...])

        @pl.when(i == 0)
        def _():
            rows = pl.ds(pl.multiple_of(k * slot_len, 32), slot_len)
            total = jnp.sum(back_buf[rows, :].astype(f32).reshape(slot_len // 8, 8, D), 0)
            norm_acc[4] = total

        @pl.loop(0, block_rows // chunk)
        def act(j):
            at = pl.ds(pl.multiple_of(base + j * chunk, chunk), chunk)
            grad = pre_now[pl.ds(pl.multiple_of(j * chunk, chunk), chunk), :] * pg_keep[at, :].astype(f32)
            grad = grad.astype(low)
            pg_keep[at, :] = grad
            grad = grad.astype(f32)
            bias_acc[:, cols[0] :] += grad[:8] + grad[8:]

        for s in range(seq_dev):
            rows = pl.ds(pl.multiple_of(base + s * slot_len, 32), slot_len)
            grad = attn_grad[s * slot_len : (s + 1) * slot_len]
            query = qkv_keep[rows, :head]
            keys = qkv_keep[rows, head : 2 * head]
            values = qkv_keep[rows, 2 * head :]
            probs = prob_keep[line * seq_dev + s]
            prob_grad = contract(grad, values, ((1,), (1,)))
            row_dot = jnp.sum(probs * prob_grad, -1, keepdims=True)
            score_grad = (probs * (prob_grad - row_dot)).astype(low)
            value_grad = contract(probs.astype(low), grad, ((0,), (0,)))
            query_grad = dot(score_grad, keys) / root
            key_grad = contract(score_grad, query, ((0,), (0,))) / root
            qkv_keep[rows, 0:half] = turn(query_grad[:, :half], -1).astype(low)
            qkv_keep[rows, half:head] = query_grad[:, half:].astype(low)
            qkv_keep[rows, head : head + half] = turn(key_grad[:, :half], -1).astype(low)
            qkv_keep[rows, head + half : 2 * head] = key_grad[:, half:].astype(low)
            qkv_keep[rows, 2 * head :] = value_grad.astype(low)
            summed = qkv_keep[rows, :].astype(f32).reshape(slot_len // 8, 8, cols[0])
            bias_acc[:, : cols[0]] += jnp.sum(summed, 0)

        put_rest(line, "start")
        mean = stat_keep[whole, 0:1]
        scale = stat_keep[whole, 1:2]

        @pl.when(i >= 2)
        def _():
            pair_s(i - 2, SENT)
            put_s(i - 2, "wait")

        @pl.loop(0, ways)
        def inputs(j):
            at = pl.ds(pl.multiple_of(j * wide, 128), wide)
            first = contract(qkv_keep[whole, :], wq[at, :], ((1,), (1,)))
            second = contract(pg_keep[whole, :], w1[at, :], ((1,), (1,)))
            two_buf[slot, :, at] = (first * vec_ref[0:1, at] + second * vec_ref[2:3, at]).astype(low)
            unit = (x_all[whole, at].astype(f32) - mean) * scale
            for place_at, value in enumerate((first * unit, first, second * unit, second)):
                norm_acc[place_at, :, at] += jnp.sum(value.reshape(block_rows // 8, 8, wide), 0)

        pair_s(i, START)

        @pl.when(i >= 1)
        def _():
            finish_s(i - 1)

    finish_s(LINE - 1)
    for r in range(5):
        total = jnp.sum(norm_acc[r], 0, keepdims=True)
        for t in range(D // 128):
            early_ref[r * (D // 128) + t : r * (D // 128) + t + 1, :] = total[:, t * 128 : (t + 1) * 128]
    at_bias = 5 * (D // 128)
    total = jnp.sum(bias_acc[...], 0, keepdims=True)
    for t in range((cols[0] + cols[1]) // 128):
        early_ref[at_bias + t : at_bias + t + 1, :] = total[:, t * 128 : (t + 1) * 128]
    at_row = at_bias + (cols[0] + cols[1]) // 128
    early_ref[at_row : at_row + 1, :] = vec_ref[6:7, :128]
    early_ref[at_row + 1 :, :] = jnp.zeros((early_ref.shape[0] - at_row - 1, 128), f32)
    for i in range(LINE):
        put_rest(i, "wait")
        sent_m(i)
        far_m(i, "wait_recv")
    for i in (LINE - 2, LINE - 1):
        pair_s(i, SENT)
        put_s(i, "wait")
        out_sends(i, SENT)
    for step in range(1, groups):
        for nb in range(pieces):
            for i in range(1 if near else LINE):
                dst = out_place((gd_got, g2_got), i, nb, step)
                sem = (i, step, nb)
                remote(dst, dst, gp_s.at[sem], gp_r.at[sem], sibling).wait_recv()
    for m in range(count):
        stage_one(m, SENT)
        for step in range(LINE):
            stage_two(m, step, SENT)
            if near:
                stage_three(m, step, SENT)
    for which in range(2):
        for q in range(3):
            row_send(which, q, SENT)
            to_sibling(which, q, SENT)


def gather_all(groups, weights, tokens, cotangent, vectors, biases, valid, turns):
    rows_own = weights[0].shape[0]
    seq_dev, slot_len, width = tokens.shape
    cols = tuple(w.shape[1] // LINE for w in weights)
    count = len(weights)
    block_rows = seq_dev * slot_len
    rows = LINE * block_rows
    f32, low = jnp.float32, jnp.bfloat16
    dma = pltpu.SemaphoreType.DMA
    peers = 3 if groups == 4 else groups
    out_widths = (D, D, cols[0], cols[1])
    pieces = (cols[2] + cols[3]) // 256
    feat = D // (2 * LINE)
    early_rows = -(-(5 * D + cols[0] + cols[1] + 128) // 1024) * 8
    return pl.pallas_call(
        partial(gather_kernel, groups, cols, seq_dev, slot_len),
        out_shape=[jax.ShapeDtypeStruct((rows, w), low) for w in out_widths]
        + [
            jax.ShapeDtypeStruct((LINE, block_rows, feat), low),
            jax.ShapeDtypeStruct((LINE, block_rows, feat), low),
            jax.ShapeDtypeStruct((LINE, slot_len, D), low),
            jax.ShapeDtypeStruct((LINE, rows_own, cols[2]), low),
            jax.ShapeDtypeStruct((LINE, rows_own, cols[3]), low),
            jax.ShapeDtypeStruct((groups - 1, LINE, rows_own, cols[2]), low),
            jax.ShapeDtypeStruct((groups - 1, LINE, rows_own, cols[3]), low),
            jax.ShapeDtypeStruct((early_rows, 128), f32),
        ],
        in_specs=[ANY] * (count + 2) + [VMEM] * 4,
        out_specs=[ANY] * 11 + [VMEM],
        scratch_shapes=[pltpu.VMEM((D, w), low) for w in cols]
        + [pltpu.VMEM((rows, D), low)] * 2
        + [
            pltpu.VMEM((rows, cols[0]), low),
            pltpu.VMEM((LINE * seq_dev, slot_len, slot_len), f32),
            pltpu.VMEM((rows, cols[2]), low),
            pltpu.VMEM((rows, cols[3]), low),
            pltpu.VMEM((rows, cols[1]), low),
            pltpu.VMEM((block_rows, D), low),
            pltpu.VMEM((2, block_rows, D), low),
            pltpu.VMEM((block_rows, D), low),
            pltpu.VMEM((2, 2, LINE, block_rows, feat), low),
            pltpu.VMEM((LINE, LINE, block_rows, feat), low),
            pltpu.VMEM((LINE, 2, block_rows, feat), low),
            pltpu.VMEM((LINE, slot_len, D), low),
            pltpu.VMEM((block_rows, cols[0]), f32),
            pltpu.VMEM((block_rows, cols[1]), f32),
            pltpu.VMEM((rows, 2), f32),
            pltpu.VMEM((5, 8, D), f32),
            pltpu.VMEM((8, cols[0] + cols[1]), f32),
            dma((count, LINE)),
            dma((count, LINE)),
            dma((count, LINE, peers)),
            dma((count, LINE, peers)),
            dma((count, LINE)),
            dma((count, LINE)),
            dma((2, 3)),
            dma((2, 3)),
            dma((2, 3)),
            dma((2, 3)),
            dma((count + 2, seq_dev)),
            dma(()),
            dma((2,)),
            dma((2, LINE)),
            dma((LINE,)),
            dma((LINE,)),
            dma((LINE,)),
            dma((LINE,)),
            dma((LINE, 2)),
            dma((LINE, 2)),
            dma((LINE,)),
            dma((LINE,)),
            dma((LINE,)),
            dma((LINE,)),
            dma((LINE, groups, pieces)),
            dma((LINE, groups, pieces)),
            dma((LINE, pieces)),
        ],
        compiler_params=pltpu.CompilerParams(
            collective_id=0, has_side_effects=True, vmem_limit_bytes=62 * 1024 * 1024
        ),
        name="gather_all",
    )(*weights, tokens, cotangent, vectors, biases, valid, turns)


def scatter_kernel(groups, cols, seq_dev, slot_len, rows_own, *refs):
    count = len(cols)
    f32, low = jnp.float32, jnp.bfloat16
    pick = refs[0]
    lefts_in = refs[1:3]
    rights_in = refs[3:5]
    near_ref, far_ref, s_ref = refs[5:8]
    done_own, done_got = refs[8:10], refs[10:12]
    early_ref = refs[12]
    mixed_ref, ssum_ref = refs[13:15]
    g_out = refs[15 : 15 + count]
    early_out, col_out, row_out = refs[15 + count : 18 + count]
    rest = refs[18 + count :]
    left_buf, right_a, right_b = rest[:3]
    g_own = rest[3 : 3 + count]
    g_got = rest[3 + count : 3 + 2 * count]
    (m_in, m_all, m_send, s_own, s_half, s_far, early_group, col_now, col_group, row_keep, row_turn) = rest[
        3 + 2 * count : 14 + 2 * count
    ]
    (here, half_s, half_r, far_s, far_r, fin_s, fin_r, mall_s, mall_r, mout_s, mout_r, gp_s, gp_r, gl_s, gl_r, eg_s,
     eg_r, el_s, el_r, es_s, es_r, cg_s, cg_r, cl_s, cl_r, cs_s, cs_r, rl_s, rl_r, keep_sem) = rest[14 + 2 * count :]
    me = Place(groups)
    c, g, k = me.line, me.group, me.core
    me.greet()
    sibling = me.at(c, g, me.other)
    feat = D // (2 * LINE)
    seqs = LINE * seq_dev
    rows = seqs * slot_len
    double = groups == 4
    sends = []

    def go(copy):
        copy.start()
        sends.append(copy)

    def to_group(step):
        return (g + step) % groups

    def from_group(step):
        return (g + groups - step) % groups

    def arrived(dst, send, recv):
        remote(dst, dst, send, recv, sibling).wait_recv()

    def add_rows(total, parts, count_rows, chunk):
        @pl.loop(0, count_rows // chunk)
        def body(i):
            at = pl.ds(pl.multiple_of(i * chunk, chunk), chunk)
            acc = parts[0](at)[...].astype(f32)
            for part in parts[1:]:
                acc = acc + part(at)[...].astype(f32)
            total(at)[...] = acc.astype(low)

    def load(src, dst, sem):
        copy = pltpu.make_async_copy(src, dst, sem)
        copy.start()
        return copy

    partner = c + 1 - 2 * (c % 2)
    beyond = (c + 2) % LINE
    for q, to in enumerate((partner, (partner + 2) % LINE)):
        go(remote(s_ref.at[to], s_half.at[q], half_s.at[q], half_r.at[q], me.at(partner, g, k)))
    got_one = load(lefts_in[0], left_buf.at[0], here.at[0])
    got_q = load(rights_in[0], right_b, here.at[1])
    got_done = []
    for q in range(2):
        got_done.append(load(done_own[q], g_own[2 + q].at[:, 0], here.at[2 + 2 * q]))
        got_done.append(load(done_got[q], g_got[2 + q], here.at[3 + 2 * q]))
    if double:
        got_two = load(lefts_in[1], left_buf.at[1], here.at[6])
        got_1 = load(rights_in[1], right_a, here.at[7])
    got_s = [load(s_ref.at[c], s_own.at[0], here.at[8]), load(s_ref.at[beyond], s_own.at[1], here.at[9])]
    got_m = [load(near_ref, m_in.at[0], here.at[10]), load(far_ref, m_in.at[1], here.at[11])]
    for step in range(1, groups):
        go(remote(early_ref, early_group.at[g], eg_s.at[step], eg_r.at[step], me.at(c, to_group(step), k)))
    early_group[g] = early_ref[...]

    per = 128 // rows_own

    def tile_products(m, left, right, tiles):
        lhs = jnp.concatenate(
            [left[:, pl.ds(pl.multiple_of((l * groups + p) * rows_own, 128), 128)] for l, p in tiles], 1
        )
        for n in range(1):
            at = slice(0, cols[m])
            out = lax.dot_general(lhs, right[:, at], (((0,), (0,)), ((), ())), preferred_element_type=f32).astype(low)
            for t, (l, p) in enumerate(tiles):
                for q in range(per):
                    row = t * 128 + q * rows_own
                    g_own[m][l, p + q, :, at] = out[row : row + rows_own]

    def send_group(m, step, act):
        to = to_group(step)
        copy = remote(
            g_own[m].at[:, to], g_got[m].at[step - 1], gp_s.at[m, step], gp_r.at[m, step], me.at(c, to, k)
        )
        getattr(copy, act)()

    across, beside, above = me.group_to(3), me.group_to(1), me.group_to(2)
    two_phase = groups == 4

    def phase_one(m, way, act):
        lines = pl.ds(0, 2) if way == 0 else pl.ds(2, 2)
        to = beside if way == 0 else above
        for q, block in enumerate((to, across)):
            copy = remote(
                g_own[m].at[lines, block], g_got[m].at[q, lines], gp_s.at[m, way * 2 + q], gp_r.at[m, way * 2 + q],
                me.at(c, to, k),
            )
            getattr(copy, act)()

    def phase_two(m, way, act):
        lines = pl.ds(0, 2) if way == 0 else pl.ds(2, 2)
        to = above if way == 0 else beside
        copy = remote(
            g_own[m].at[lines, to], g_got[m].at[2, lines], gp_s.at[m, 4 + way], gp_r.at[m, 4 + way], me.at(c, to, k)
        )
        getattr(copy, act)()

    def between_phases(m):
        for way in range(2):
            phase_one(m, way, "wait_recv")
            to = above if way == 0 else beside
            for line in (way * 2, way * 2 + 1):
                add_rows(
                    lambda at: g_own[m].at[line, to, at],
                    [lambda at: g_own[m].at[line, to, at], lambda at: g_got[m].at[1, line, at]],
                    rows_own,
                    16,
                )
            phase_two(m, way, "start")

    def products(left, pairs):
        if two_phase:

            @pl.loop(0, groups)
            def body(t):
                flip_x, flip_y = (t + 1) % 2, (3 - t) // 2 * (1 - t // 3)
                to = (g // 2 + flip_y) % 2 * 2 + (g % 2 + flip_x) % 2
                for m, right in pairs:
                    tile_products(m, left, right, [(l, to) for l in range(LINE)])
                    for way in range(2):

                        @pl.when(t == 2 - way)
                        def _():
                            phase_one(m, way, "start")
        else:

            @pl.loop(0, LINE)
            def body(l):
                for m, right in pairs:
                    tile_products(m, left, right, [(l, t * per) for t in range(4)])

            for m, _ in pairs:
                for step in range(1, groups):
                    send_group(m, step, "start")

    def sum_groups(m, first):
        got = range(groups - 1)
        if m < 2 and two_phase:
            for way in range(2):
                phase_two(m, way, "wait_recv")
            got = (0, 2)
        elif m < 2:
            for step in range(1, groups):
                arrived(g_got[m].at[step - 1], gp_s.at[m, step], gp_r.at[m, step])
        mine = g if m < 2 else 0
        width = pl.ds(pl.multiple_of(c * cols[m], 128), cols[m])
        total = jnp.zeros((8, cols[m]), f32)
        for step in (2, 1, 3, 0):
            line = me.line_to(step)

            def body(i, carry, line=line):
                at = pl.ds(pl.multiple_of(i * 16, 16), 16)
                acc = g_own[m][line, mine, at, :].astype(f32)
                for p in got:
                    acc = acc + g_got[m][p, line, at, :].astype(f32)
                g_own[m][line, mine, at, :] = acc.astype(low)
                square = acc * acc + eps_second
                row_keep[line, at, m : m + 1] = jnp.sum(square, 1, keepdims=True)
                return carry + square[:8] + square[8:]

            total = lax.fori_loop(0, rows_own // 16, body, total)
            src = g_own[m].at[line, mine]
            if step:
                go(remote(src, g_out[m].at[:, width], gl_s.at[m, step], gl_r.at[m, step], me.at(line, g, k)))
            else:
                keep.append(load(src, g_out[m].at[:, width], keep_sem.at[2 + m]))
        total = jnp.sum(total, 0, keepdims=True)
        for t in range(cols[m] // 128):
            col_now[first + t : first + t + 1, :] = total[:, t * 128 : (t + 1) * 128]

    keep = []
    row_keep[...] = jnp.zeros_like(row_keep)
    got_one.wait()
    got_q.wait()
    products(left_buf.at[0], ((0, right_b),))
    if not double:
        got_two = load(lefts_in[1], left_buf.at[0], here.at[6])
        got_1 = load(rights_in[1], right_a, here.at[7])
    got_two.wait()
    got_1.wait()
    products(left_buf.at[1 if double else 0], ((1, right_a),))

    firsts = []
    edge = 0
    for m in range(count):
        firsts.append(edge)
        edge += cols[m] // 128
    for copy in got_done:
        copy.wait()
    if two_phase:
        between_phases(0)
    sum_groups(3, firsts[3])
    sum_groups(2, firsts[2])
    if two_phase:
        between_phases(1)

    for q in range(2):
        got_s[q].wait()
        arrived(s_half.at[q], half_s.at[q], half_r.at[q])
        add_rows(
            lambda at: s_own.at[q, at], [lambda at: s_own.at[q, at], lambda at: s_half.at[q, at]], slot_len, 16
        )
    go(remote(s_own.at[1], s_far, far_s, far_r, me.at(beyond, g, k)))

    for copy in got_m:
        copy.wait()
    ours = pl.ds(g * seqs, seqs)
    for s in range(seqs):
        add_rows(
            lambda at: m_all.at[g * seqs + s, at],
            [lambda at: m_in.at[0, s, at], lambda at: m_in.at[1, s, at]],
            slot_len,
            64,
        )
    for step in range(1, groups):
        go(remote(m_all.at[ours], m_all.at[ours], mall_s.at[step], mall_r.at[step], me.at(c, to_group(step), k)))

    for step in range(1, groups):
        arrived(early_group.at[from_group(step)], eg_s.at[step], eg_r.at[step])
    acc = early_group[0]
    for i in range(1, groups):
        acc = acc + early_group[i]
    early_out[k, c] = acc
    for step in range(1, LINE):
        go(remote(early_out.at[k, c], early_out.at[k, c], el_s.at[step], el_r.at[step], me.at(me.line_to(step), g, k)))

    sum_groups(0, firsts[0])
    arrived(s_far, far_s, far_r)
    add_rows(lambda at: s_own.at[0, at], [lambda at: s_own.at[0, at], lambda at: s_far.at[at]], slot_len, 16)
    go(remote(s_own.at[0], ssum_ref.at[k], fin_s, fin_r, sibling))
    keep.append(load(s_own.at[0], ssum_ref.at[k], keep_sem.at[0]))
    sum_groups(1, firsts[1])

    for step in range(1, groups):
        go(remote(col_now, col_group.at[g], cg_s.at[step], cg_r.at[step], me.at(c, to_group(step), k)))
    col_group[g] = col_now[...]
    for step in (1, 2, 3, 0):
        line = me.line_to(step)
        row_turn[line] = jnp.transpose(row_keep[line])[:8]
        if step:
            go(remote(row_turn.at[line], row_out.at[k, c], rl_s.at[0, step], rl_r.at[0, step], me.at(line, g, k)))
        else:
            row_out[k, c] = row_turn[line]
        go(remote(row_turn.at[line], row_out.at[k, c], rl_s.at[1, step], rl_r.at[1, step], me.at(line, g, me.other)))
    for step in range(1, groups):
        arrived(col_group.at[from_group(step)], cg_s.at[step], cg_r.at[step])
    acc = col_group[0]
    for i in range(1, groups):
        acc = acc + col_group[i]
    col_out[k, c] = acc
    for step in range(1, LINE):
        go(remote(col_out.at[k, c], col_out.at[k, c], cl_s.at[step], cl_r.at[step], me.at(me.line_to(step), g, k)))
    for step in range(1, groups):
        arrived(m_all.at[pl.ds(from_group(step) * seqs, seqs)], mall_s.at[step], mall_r.at[step])
    mixed_cols = pl.ds(pl.multiple_of((c * 2 + k) * feat, 128), feat)
    for step in (1, 2, 3, 0):
        line = me.line_to(step)
        for s in range(seq_dev):
            m_send[line, s] = m_all[pick[line * seq_dev + s]]
        where = mixed_ref.at[:, :, mixed_cols]
        if step:
            go(remote(m_send.at[line], where, mout_s.at[0, step], mout_r.at[0, step], me.at(line, g, k)))
        else:
            keep.append(load(m_send.at[line], where, keep_sem.at[1]))
            go(remote(m_send.at[line], where, mout_s.at[1, 0], mout_r.at[1, 0], sibling))
    for step in range(1, LINE):
        arrived(early_out.at[k, me.line_from(step)], el_s.at[step], el_r.at[step])
    go(remote(early_out.at[k], early_out.at[k], es_s, es_r, sibling))
    for step in range(1, LINE):
        arrived(col_out.at[k, me.line_from(step)], cl_s.at[step], cl_r.at[step])
    go(remote(col_out.at[k], col_out.at[k], cs_s, cs_r, sibling))

    for step in range(1, LINE):
        where = mixed_ref.at[:, :, pl.ds(pl.multiple_of((me.line_from(step) * 2 + k) * feat, 128), feat)]
        arrived(where, mout_s.at[0, step], mout_r.at[0, step])
        go(remote(where, where, mout_s.at[1, step], mout_r.at[1, step], sibling))
    for m in range(count):
        for step in range(1, LINE):
            dst = g_out[m].at[:, pl.ds(pl.multiple_of(me.line_from(step) * cols[m], 128), cols[m])]
            arrived(dst, gl_s.at[m, step], gl_r.at[m, step])
    for step in range(LINE):
        source = me.line_from(step)
        dst = mixed_ref.at[:, :, pl.ds(pl.multiple_of((source * 2 + me.other) * feat, 128), feat)]
        arrived(dst, mout_s.at[1, step], mout_r.at[1, step])
        for core, way in ((k, 0), (me.other, 1)):
            if step or way:
                arrived(row_out.at[core, source], rl_s.at[way, step], rl_r.at[way, step])
    arrived(ssum_ref.at[me.other], fin_s, fin_r)
    arrived(early_out.at[me.other], es_s, es_r)
    arrived(col_out.at[me.other], cs_s, cs_r)
    for copy in sends:
        copy.wait_send()
    for m in range(2):
        if two_phase:
            for way in range(2):
                phase_one(m, way, "wait_send")
                phase_two(m, way, "wait_send")
        else:
            for step in range(1, groups):
                send_group(m, step, "wait_send")
    for copy in keep:
        copy.wait()


def scatter_all(groups, cols, seq_dev, rows_own, pick, lefts, rights, between):
    near, far, s_pair, *done, early = between
    slot_len = s_pair.shape[1]
    rows = lefts[0].shape[0]
    count = len(cols)
    feat = D // (2 * LINE)
    seqs = LINE * seq_dev
    blocks = (seqs, slot_len, feat)
    dma = pltpu.SemaphoreType.DMA
    f32, low = jnp.float32, jnp.bfloat16
    col_rows = sum(cols) // 128
    return pl.pallas_call(
        partial(scatter_kernel, groups, cols, seq_dev, slot_len, rows_own),
        out_shape=[
            jax.ShapeDtypeStruct((seq_dev, slot_len, D), low),
            jax.ShapeDtypeStruct((seq_dev, slot_len, D), low),
        ]
        + [jax.ShapeDtypeStruct((rows_own, LINE * width), low) for width in cols]
        + [
            jax.ShapeDtypeStruct((2, LINE) + early.shape, f32),
            jax.ShapeDtypeStruct((2, LINE, col_rows, 128), f32),
            jax.ShapeDtypeStruct((2, LINE, 8, 128), f32),
        ],
        in_specs=[SMEM] + [ANY] * 11 + [VMEM],
        out_specs=[ANY] * (2 + count) + [VMEM] * 3,
        scratch_shapes=[
            pltpu.VMEM((2 if groups == 4 else 1, rows, D), low),
            pltpu.VMEM((rows, cols[1]), low),
            pltpu.VMEM((rows, cols[0]), low),
        ]
        + [pltpu.VMEM((LINE, groups if m < 2 else 1, rows_own, width), low) for m, width in enumerate(cols)]
        + [pltpu.VMEM((groups - 1, LINE, rows_own, width), low) for width in cols]
        + [
            pltpu.VMEM((2, seqs, slot_len, feat), low),
            pltpu.VMEM((groups * seqs, slot_len, feat), low),
            pltpu.VMEM((LINE, seq_dev, slot_len, feat), low),
            pltpu.VMEM((2, slot_len, D), low),
            pltpu.VMEM((2, slot_len, D), low),
            pltpu.VMEM((slot_len, D), low),
            pltpu.VMEM((groups,) + early.shape, f32),
            pltpu.VMEM((col_rows, 128), f32),
            pltpu.VMEM((groups, col_rows, 128), f32),
            pltpu.VMEM((LINE, 128, 128), f32),
            pltpu.VMEM((LINE, 8, 128), f32),
            dma((12,)),
            dma((2,)),
            dma((2,)),
            dma(()),
            dma(()),
            dma(()),
            dma(()),
            dma((groups,)),
            dma((groups,)),
            dma((2, LINE)),
            dma((2, LINE)),
            dma((count, max(groups, 6))),
            dma((count, max(groups, 6))),
            dma((count, LINE)),
            dma((count, LINE)),
            dma((groups,)),
            dma((groups,)),
            dma((LINE,)),
            dma((LINE,)),
            dma(()),
            dma(()),
            dma((groups,)),
            dma((groups,)),
            dma((LINE,)),
            dma((LINE,)),
            dma(()),
            dma(()),
            dma((2, LINE)),
            dma((2, LINE)),
            dma((2 + count,)),
        ],
        compiler_params=pltpu.CompilerParams(
            collective_id=1, has_side_effects=True, vmem_limit_bytes=62 * 1024 * 1024
        ),
        name="scatter_all",
    )(pick, *lefts, *rights, near.reshape(blocks), far.reshape(blocks), s_pair, *done, early)


def prepare_kernel(groups, cols, seq_dev, slot_len, *refs):
    (spot, lengths, permutation, wq, w1, wd, w2, vectors, biases, rows_state) = refs[:10]
    lows = refs[10:14]
    valid, own_valid, all_vectors, all_biases, pick = refs[14:]
    f32 = jnp.float32
    for src, dst in zip((wq, w1, wd, w2), lows):
        dst[...] = src[...].astype(jnp.bfloat16)

    @pl.when(pl.program_id(0) == 0)
    def _():
        data, core = spot[0], spot[1]
        line, group = data // groups, data % groups
        times = lax.broadcasted_iota(jnp.int32, (slot_len, 1), 0)
        for place in range(LINE):
            for s in range(seq_dev):
                slot = (place * groups + group) * seq_dev + s
                at = place * seq_dev + s
                valid[at * slot_len : (at + 1) * slot_len, :] = jnp.where(times < lengths[slot], 1.0, 0.0)
                source = permutation[slot]
                chip = source // seq_dev
                pick[at] = (chip % groups) * (LINE * seq_dev) + (chip // groups) * seq_dev + source % seq_dev
        for s in range(seq_dev):
            own_valid[s * slot_len : (s + 1) * slot_len, :] = jnp.where(
                times < lengths[data * seq_dev + s], 1.0, 0.0
            )
        all_vectors[0:6, :] = vectors[...]
        all_vectors[6:8, :] = jnp.zeros((2, D), f32)
        lane = lax.broadcasted_iota(jnp.int32, (1, 128), 1)
        total = jnp.zeros((1, 128), f32)
        for m in range(4):
            total = total + jnp.where(lane == m, jnp.sum(rows_state[m : m + 1, :], 1, keepdims=True), 0.0)
        all_vectors[6:7, 0:128] = jnp.where(core == 0, total, jnp.zeros_like(total))
        all_biases[:, : cols[0]] = biases[:, pl.ds(pl.multiple_of(line * cols[0], 128), cols[0])]
        all_biases[:, cols[0] :] = biases[:, pl.ds(pl.multiple_of(LINE * cols[0] + line * cols[1], 128), cols[1])]


def prepare(groups, seq_dev, slot_len, spot, lengths, permutation, weights, vectors, biases, rows_state):
    f32, low = jnp.float32, jnp.bfloat16
    rows_own = weights[0].shape[0]
    cols = tuple(w.shape[1] // LINE for w in weights)
    tall = 32
    steps = rows_own // tall
    seqs = LINE * seq_dev

    def whole(shape):
        return pl.BlockSpec(shape, lambda i: (0,) * len(shape))

    blocks = [pl.BlockSpec((tall, w.shape[1]), lambda i: (i, 0)) for w in weights]
    return pl.pallas_call(
        partial(prepare_kernel, groups, cols, seq_dev, slot_len),
        grid=(steps,),
        out_shape=[jax.ShapeDtypeStruct(w.shape, low) for w in weights]
        + [
            jax.ShapeDtypeStruct((seqs * slot_len, 1), f32),
            jax.ShapeDtypeStruct((seq_dev * slot_len, 1), f32),
            jax.ShapeDtypeStruct((8, D), f32),
            jax.ShapeDtypeStruct((1, cols[0] + cols[1]), f32),
            jax.ShapeDtypeStruct((seqs,), jnp.int32),
        ],
        in_specs=[SMEM] * 3 + blocks + [whole(vectors.shape), whole(biases.shape), whole(rows_state.shape)],
        out_specs=blocks
        + [
            whole((seqs * slot_len, 1)),
            whole((seq_dev * slot_len, 1)),
            whole((8, D)),
            whole((1, cols[0] + cols[1])),
            SMEM,
        ],
        compiler_params=pltpu.CompilerParams(vmem_limit_bytes=60 * 1024 * 1024),
        name="prepare",
    )(spot, lengths, permutation, *weights, vectors, biases, rows_state)


def finish_kernel(order, cols, rows_own, *refs):
    f32, low = jnp.float32, jnp.bfloat16
    spot = refs[0]
    g_in, w_in = refs[1:5], refs[5:9]
    (s_sum, tokens, cotangent, own_valid, early, col_all, row_all, row_state, col_state, vectors, moments, biases,
     bias_moments) = refs[9:22]
    grads, news, copies = refs[22:26], refs[26:30], refs[30:34]
    (grad_tokens, row_new, col_new, norm_total, norm_moment_new, norm_new, bias_total, bias_moment_new,
     bias_new) = refs[34:43]
    row_factor, col_factor, turn = refs[43:]
    step = pl.program_id(0)
    widths = [w.shape[1] for w in w_in]
    edges = [sum(widths[:i]) for i in range(5)]
    tiles = D // 128

    @pl.when(step == 0)
    def _():
        core = spot[1]
        both = early[0, 0]
        rows_all = row_all[0, 0]
        mass_all = col_all[0, 0]
        for n in range(1, 2 * LINE):
            both = both + early[n // LINE, n % LINE]
            rows_all = rows_all + row_all[n // LINE, n % LINE]
            mass_all = mass_all + col_all[n // LINE, n % LINE]
        for r in range(6):
            for t in range(tiles):
                at = min(r, 4) * tiles + t
                norm_total[r : r + 1, t * 128 : (t + 1) * 128] = both[at : at + 1]
        grad = norm_total[...]
        moment = decay * moments[...] + (1.0 - decay) * (grad * grad + eps_second)
        norm_moment_new[...] = moment
        norm_new[...] = vectors[...] - rate_norm * grad * lax.rsqrt(moment)
        first = 5 * tiles
        parts = ((cols[0] // 128, 0), (cols[1] // 128, LINE * cols[0]))
        for line in range(LINE):
            at = first
            for count, base in parts:
                for t in range(count):
                    to = base + (line * count + t) * 128
                    bias_total[:, to : to + 128] = early[core, line, at : at + 1, :]
                    at += 1
        grad = bias_total[...]
        moment = decay * bias_moments[...] + (1.0 - decay) * (grad * grad + eps_second)
        bias_moment_new[...] = moment
        bias_new[...] = biases[...] - rate_vector * grad * lax.rsqrt(moment)
        at_row = first + (cols[0] + cols[1]) // 128
        full_cols = (3.0 * D, 1.0 * D, 1.0 * FF, 1.0 * FF)
        rates = (
            rate_scale / math.sqrt(D),
            rate_scale / math.sqrt(D // 8),
            rate_scale / math.sqrt(D),
            rate_scale / math.sqrt(FF),
        )
        turn[...] = jnp.zeros_like(turn)
        at = 0
        for m, i in enumerate(order):
            count = cols[m] // 128
            new = decay * row_state[i : i + 1, :] + (1.0 - decay) * (rows_all[m : m + 1, :rows_own] / full_cols[i])
            row_new[i : i + 1, :] = new
            mass = jnp.sum(jnp.sum(mass_all[at : at + count], 1, keepdims=True), 0, keepdims=True)
            mean = (decay * both[at_row : at_row + 1, i : i + 1] + (1.0 - decay) * (mass / full_cols[i])) / D
            turn[i : i + 1, :rows_own] = rates[i] * lax.rsqrt(new / mean)
            for line in range(LINE):
                for t in range(count):
                    to = edges[i] + (line * count + t) * 128
                    col_new[:, to : to + 128] = col_all[core, line, at + t : at + t + 1, :]
            at += count
        row_factor[...] = jnp.transpose(turn[...])
        new = decay * col_state[...] + (1.0 - decay) * (col_new[...] / D)
        col_new[...] = new
        col_factor[...] = lax.rsqrt(new)

    tall = w_in[0].shape[0]
    for half in range(tall // 16):
        rows = pl.ds(pl.multiple_of(step * tall + half * 16, 16), 16)
        part = slice(half * 16, half * 16 + 16)
        for i in range(4):
            factor = row_factor[rows, i : i + 1]
            for n in range(widths[i] // 1024):
                at = slice(n * 1024, (n + 1) * 1024)
                grad = g_in[i][part, at].astype(f32)
                new = w_in[i][part, at] - grad * factor * col_factor[:, edges[i] + n * 1024 : edges[i] + (n + 1) * 1024]
                grads[i][part, at] = grad
                news[i][part, at] = new
                copies[i][part, at] = new.astype(low)

    @pl.loop(0, tokens.shape[0] // 16)
    def body(j):
        at = pl.ds(pl.multiple_of(j * 16, 16), 16)
        x = tokens[at, :].astype(f32)
        centre = x - jnp.mean(x, -1, keepdims=True)
        scale = lax.rsqrt(jnp.mean(centre * centre, -1, keepdims=True) + eps_norm)
        unit = centre * scale
        flow = s_sum[at, :].astype(f32)
        through = flow - jnp.mean(flow, -1, keepdims=True) - unit * jnp.mean(flow * unit, -1, keepdims=True)
        grad_tokens[at, :] = (cotangent[at, :].astype(f32) * own_valid[at, :] + scale * through).astype(low)


def finish(order, spot, grads, weights, s_sum, tokens, cotangent, own_valid, *small):
    f32, low = jnp.float32, jnp.bfloat16
    rows_own = weights[0].shape[0]
    tall = 32
    steps = rows_own // tall
    cols = tuple(weights[i].shape[1] // LINE for i in order)
    rows = tokens.shape[0]
    row_state, col_state, vectors, _, biases = small[3:8]

    def whole(shape):
        return pl.BlockSpec(shape, lambda i: (0,) * len(shape))

    blocks = [pl.BlockSpec((tall, w.shape[1]), lambda i: (i, 0)) for w in weights]
    acts = pl.BlockSpec((rows // steps, D), lambda i: (i, 0))
    small_out = [row_state.shape, col_state.shape] + [vectors.shape] * 3 + [biases.shape] * 3
    return pl.pallas_call(
        partial(finish_kernel, order, cols, rows_own),
        grid=(steps,),
        out_shape=[jax.ShapeDtypeStruct(w.shape, f32) for w in weights] * 2
        + [jax.ShapeDtypeStruct(w.shape, low) for w in weights]
        + [jax.ShapeDtypeStruct((rows, D), low)]
        + [jax.ShapeDtypeStruct(shape, f32) for shape in small_out],
        in_specs=[SMEM]
        + blocks * 2
        + [acts] * 3
        + [pl.BlockSpec((rows // steps, 1), lambda i: (i, 0))]
        + [whole(a.shape) for a in small],
        out_specs=blocks * 3 + [acts] + [whole(shape) for shape in small_out],
        scratch_shapes=[
            pltpu.VMEM((128, 128), f32),
            pltpu.VMEM(col_state.shape, f32),
            pltpu.VMEM((128, 128), f32),
        ],
        compiler_params=pltpu.CompilerParams(vmem_limit_bytes=60 * 1024 * 1024),
        name="finish",
    )(spot, *grads, *weights, s_sum, tokens, cotangent, own_valid, *small)


def per_device(
    tokens,
    cotangent,
    lengths,
    permutation,
    w_qkv,
    w_dense,
    w_fc1,
    w_fc2,
    norm_vectors,
    split_biases,
    row_state,
    col_state,
    norm_moment,
    bias_moment,
):
    groups = lax.axis_size("dp") // LINE
    seq_dev, slot_len, width = tokens.shape
    rows_own = w_qkv.shape[0]
    head_dim = D // HEADS
    weights = (w_qkv, w_dense, w_fc1, w_fc2)
    order = (0, 2, 1, 3)
    cols = tuple(weights[i].shape[1] // LINE for i in order)
    spot = jnp.stack([lax.axis_index("dp"), lax.axis_index("tensor")]).astype(jnp.int32)
    *lows, valid, own_valid, vectors, biases, pick = prepare(
        groups, seq_dev, slot_len, spot, lengths, permutation, [weights[i] for i in order], norm_vectors,
        split_biases, row_state,
    )
    turns = jnp.asarray(turn_tables(slot_len, head_dim // 4, head_dim // 2))
    norm_one, norm_two, qkv_grad, pre_grad, *between = gather_all(
        groups, lows, tokens, cotangent, vectors, biases, valid, turns
    )
    mixed, s_sum, *outs = scatter_all(
        groups, cols, seq_dev, rows_own, pick, (norm_one, norm_two), (qkv_grad, pre_grad), between
    )
    grads = [outs[order.index(i)] for i in range(4)]
    early_all, col_all, row_all = outs[4:]
    results = finish(
        order, spot, grads, weights, s_sum.reshape(-1, width), tokens.reshape(-1, width),
        cotangent.reshape(-1, width), own_valid, early_all, col_all, row_all, row_state, col_state, norm_vectors,
        norm_moment, split_biases, bias_moment,
    )
    return (mixed, results[12].reshape(tokens.shape), *results[:12], *results[13:])


def solution(mesh):
    halves = P("dp", "tensor")
    split = P("tensor", None)
    in_specs = (
        P("dp", None, None),
        P("dp", None, None),
        P(),
        P(),
        halves,
        halves,
        halves,
        halves,
        P(),
        split,
        P(None, "dp"),
        split,
        P(),
        split,
    )
    out_specs = (
        (P("dp", None, None),) * 2
        + (halves,) * 12
        + (P(None, "dp"), split)
        + (P(),) * 3
        + (split,) * 3
    )
    return jax.shard_map(
        per_device, mesh=mesh, in_specs=in_specs, out_specs=out_specs, check_vma=False
    )
```

```python
from functools import partial
import math

import jax
import jax.numpy as jnp
import numpy as np
from jax import lax
from jax.experimental import pallas as pl
from jax.experimental.pallas import tpu as pltpu
from jax.sharding import PartitionSpec as P

D = 2048
FF = 8192
HEADS = 8
LINE = 4

eps_norm = 1e-05
eps_second = 1e-30
decay = 0.5
rate_scale = 1.0
rate_norm = 0.5
rate_vector = 0.05
neg_large = -1e30

MESH = pl.DeviceIdType.MESH
ANY = pl.BlockSpec(memory_space=pl.ANY)
VMEM = pl.BlockSpec(memory_space=pltpu.VMEM)
SMEM = pl.BlockSpec(memory_space=pltpu.SMEM)


def turn_tables(slot_len, rot_dims, width):
    half = rot_dims // 2
    freq = np.float32(10000.0) ** (np.float32(-2.0) * np.arange(half, dtype=np.float32) / np.float32(rot_dims))
    angle = np.arange(slot_len, dtype=np.float32)[:, None] * freq[None, :].astype(np.float32)
    tables = np.zeros((3, slot_len, width), np.float32)
    tables[0] = 1.0
    tables[0, :, :half] = tables[0, :, half:rot_dims] = np.cos(angle)
    tables[1, :, :half] = tables[2, :, half:rot_dims] = np.sin(angle)
    return tables


class Place:
    def __init__(self, groups):
        self.groups = groups
        data = lax.axis_index("dp")
        self.core = lax.axis_index("tensor")
        self.other = 1 - self.core
        self.line = data // groups
        self.group = data % groups

    def at(self, line, group, core):
        return (line * self.groups + group, core)

    def line_to(self, step):
        return (self.line + step) % LINE

    def line_from(self, step):
        return (self.line + LINE - step) % LINE

    def group_to(self, step):
        g = self.group
        if self.groups == 4:
            if step == 1:
                return g + 1 - 2 * (g % 2)
            if step == 2:
                return (g + 2) % 4
            return 3 - g
        return (g + step) % self.groups

    def group_from(self, step):
        if self.groups == 4:
            return self.group_to(step)
        return (self.group + self.groups - step) % self.groups

    def greet(self):
        barrier = pltpu.get_barrier_semaphore()
        count = 0
        for step in range(1, LINE):
            for core in (self.core, self.other):
                pl.semaphore_signal(
                    barrier, inc=1, device_id=self.at(self.line_to(step), self.group, core), device_id_type=MESH
                )
                count += 1
        for step in range(1, self.groups):
            pl.semaphore_signal(
                barrier, inc=1, device_id=self.at(self.line, self.group_to(step), self.core), device_id_type=MESH
            )
            count += 1
        pl.semaphore_signal(
            barrier, inc=1, device_id=self.at(self.line, self.group, self.other), device_id_type=MESH
        )
        pl.semaphore_wait(barrier, count + 1)


def remote(src, dst, send, recv, device):
    return pltpu.make_async_remote_copy(
        src_ref=src, dst_ref=dst, send_sem=send, recv_sem=recv, device_id=device, device_id_type=MESH
    )


def dot(left, right):
    return jnp.dot(left, right, preferred_element_type=jnp.float32)


def turned(blocks):
    eye = lax.broadcasted_iota(jnp.int32, (256, 256), 0) == lax.broadcasted_iota(jnp.int32, (256, 256), 1)
    eye = jnp.where(eye, 1.0, 0.0).astype(jnp.bfloat16)
    parts = []
    for n in range(0, len(blocks), 2):
        pair = jnp.concatenate(blocks[n : n + 2], 1)
        part = lax.dot_general(eye, pair, (((1,), (1,)), ((), ())), preferred_element_type=jnp.float32)
        parts.append(part.astype(jnp.bfloat16))
    return jnp.concatenate(parts, 0)


def gather_kernel(groups, cols, seq_dev, slot_len, *refs):
    count = len(cols)
    f32, low = jnp.float32, jnp.bfloat16
    w_in = refs[:count]
    acts_in = refs[count : count + 2]
    vec_ref, bias_ref, valid_ref, turn_ref = refs[count + 2 : count + 6]
    outs = refs[count + 6 : count + 18]
    (n1_out, n2_out, qg_out, pg_out, near_out, far_out, s_out, gd_own, g2_own, gd_got, g2_got, early_ref) = outs
    rest = refs[count + 18 :]
    w_out = rest[:count]
    acts_out = rest[count : count + 2]
    (qkv_keep, prob_keep, attn_keep, hid_keep, pg_keep, one_buf, two_buf, back_buf, m_buf, m_got, m_half, s_got,
     qkv_now, pre_now, stat_keep, norm_acc, bias_acc) = rest[count + 2 : count + 19]
    (one_s, one_r, two_s, two_r, three_s, three_r, row_s, row_r, sib_s, sib_r, here, out_a, out_b,
     out_d, msib_s, msib_r, ssib_s, ssib_r, half_s, half_r, far_s, far_r, near_sem, s_here, gp_s, gp_r,
     g_here) = rest[count + 19 :]
    me = Place(groups)
    c, g, k = me.line, me.group, me.core
    me.greet()
    sibling = me.at(c, g, me.other)
    rows_own = w_in[0].shape[0]
    block_rows = seq_dev * slot_len
    near = groups == 4
    START, SENT = "start", "wait_send"

    def block(ref, line, width):
        return ref.at[:, pl.ds(pl.multiple_of(line * width, 128), width)]

    def place(m, line, group):
        return w_out[m].at[pl.ds(pl.multiple_of((line * groups + group) * rows_own, 32), rows_own)]

    def rows_of(which, line, core):
        return acts_out[which].at[pl.ds(pl.multiple_of((line * seq_dev + core) * slot_len, 32), slot_len)]

    partner = c + 1 - 2 * (c % 2)
    beyond = (c + 2) % LINE

    def row_send(which, q, act):
        origin = beyond if q == 2 else c
        copy = remote(
            rows_of(which, beyond, k) if q == 2 else acts_in[which].at[k],
            rows_of(which, origin, k),
            row_s.at[which, q],
            row_r.at[which, q],
            me.at(beyond if q == 1 else partner, g, k),
        )
        getattr(copy, act)()

    def row_origin(q):
        return (partner, beyond, (partner + 2) % LINE)[q]

    def to_sibling(which, q, act):
        rows = rows_of(which, row_origin(q), k)
        copy = remote(rows, rows, sib_s.at[which, q], sib_r.at[which, q], sibling)
        getattr(copy, act)()

    def pass_on(which, q):
        rows = rows_of(which, row_origin(q), k)
        remote(rows, rows, row_s.at[which, q], row_r.at[which, q], sibling).wait_recv()
        if q == 1:
            row_send(which, 2, START)
        to_sibling(which, q, START)

    def arrive_sibling(which):
        for q in range(3):
            rows = rows_of(which, row_origin(q), me.other)
            remote(rows, rows, sib_s.at[which, q], sib_r.at[which, q], sibling).wait_recv()

    def local_acts(which, act):
        for s in range(seq_dev):
            copy = pltpu.make_async_copy(acts_in[which].at[s], rows_of(which, c, s), here.at[count + which, s])
            getattr(copy, act)()

    def local_weight(m, act):
        copy = pltpu.make_async_copy(block(w_in[m], c, cols[m]), place(m, c, g), here.at[m, 0])
        getattr(copy, act)()

    def stage_one(m, act):
        for step in range(1, LINE):
            to = me.line_to(step)
            copy = remote(
                block(w_in[m], to, cols[m]),
                place(m, c, g),
                one_s.at[m, step],
                one_r.at[m, step],
                me.at(to, g, k),
            )
            getattr(copy, act)()

    def stage_two(m, step, act):
        where = place(m, me.line_from(step), g)
        src = block(w_in[m], c, cols[m]) if step == 0 else where
        for peer in range(1, 3 if near else groups):
            copy = remote(
                src, where, two_s.at[m, step, peer], two_r.at[m, step, peer], me.at(c, me.group_to(peer), k)
            )
            getattr(copy, act)()

    def first_half(m):
        for step in range(1, LINE):
            dst = place(m, me.line_from(step), g)
            remote(dst, dst, one_s.at[m, step], one_r.at[m, step], sibling).wait_recv()
            stage_two(m, step, START)

    def wait_two(m, step, peer):
        dst = place(m, me.line_from(step), me.group_from(peer))
        remote(dst, dst, two_s.at[m, step, peer], two_r.at[m, step, peer], sibling).wait_recv()

    def stage_three(m, step, act):
        source, target = (1, 2) if step % 2 == 0 else (2, 1)
        where = place(m, me.line_from(step), me.group_to(source))
        copy = remote(where, where, three_s.at[m, step], three_r.at[m, step], me.at(c, me.group_to(target), k))
        getattr(copy, act)()

    def relay(m):
        for step in range(LINE):
            for peer in range(1, 3 if near else groups):
                wait_two(m, step, peer)
            if near:
                stage_three(m, step, START)

    def last(m):
        if near:
            for step in range(LINE):
                dst = place(m, me.line_from(step), me.group_to(3))
                remote(dst, dst, three_s.at[m, step], three_r.at[m, step], sibling).wait_recv()

    row_send(0, 1, START)
    row_send(0, 0, START)
    for m in (0, 1):
        stage_one(m, START)
        stage_two(m, 0, START)
    local_acts(0, START)
    local_weight(0, START)
    local_weight(1, START)
    norm_acc[...] = jnp.zeros_like(norm_acc)
    bias_acc[...] = jnp.zeros_like(bias_acc)
    first_half(0)
    pass_on(0, 1)
    for m in (2, 3):
        stage_one(m, START)
        stage_two(m, 0, START)
    local_acts(1, START)
    local_weight(2, START)
    local_weight(3, START)
    pass_on(0, 0)
    first_half(1)
    row_send(1, 1, START)
    row_send(1, 0, START)
    relay(0)
    pass_on(0, 2)
    relay(1)
    local_acts(0, "wait")
    local_weight(0, "wait")
    local_weight(1, "wait")
    last(0)
    last(1)
    arrive_sibling(0)

    wq, w1, wd, w2 = w_out
    x_all, ct_all = acts_out
    head = cols[0] // 3
    half = head // 2
    chunk = 16
    wide = 512
    ways = D // wide
    root = math.sqrt(head)
    causal = lax.broadcasted_iota(jnp.int32, (slot_len, slot_len), 0) >= lax.broadcasted_iota(
        jnp.int32, (slot_len, slot_len), 1
    )

    def turn(v, sign):
        left = pltpu.roll(v, half - 32, 1)
        right = pltpu.roll(v, 32, 1)
        if sign > 0:
            return v * turn_ref[0] - left * turn_ref[1] + right * turn_ref[2]
        return v * turn_ref[0] + left * turn_ref[1] - right * turn_ref[2]

    def contract(left, right, dims):
        return lax.dot_general(left, right, ((dims[0], dims[1]), ((), ())), preferred_element_type=f32)

    def put_one(i, line, act):
        rows = pl.ds(pl.multiple_of(line * block_rows, 128), block_rows)
        getattr(pltpu.make_async_copy(one_buf, n1_out.at[rows], out_a), act)()
        getattr(pltpu.make_async_copy(two_buf.at[0], n2_out.at[rows], out_b.at[0]), act)()

    @pl.loop(0, LINE)
    def forward(i):
        line = (c + i) % LINE
        base = pl.multiple_of(line * block_rows, 128)

        @pl.when(i == 0)
        def _():
            first_half(2)
            first_half(3)

        @pl.when(i == 1)
        def _():
            relay(2)
            pass_on(1, 1)

        @pl.when(i == 2)
        def _():
            relay(3)
            pass_on(1, 0)

        @pl.when(i >= 1)
        def _():
            put_one(i, line, "wait")

        @pl.loop(0, block_rows // chunk)
        def norm(j):
            at = pl.ds(pl.multiple_of(base + j * chunk, chunk), chunk)
            to = pl.ds(pl.multiple_of(j * chunk, chunk), chunk)
            x = x_all[at, :].astype(f32)
            mean = jnp.mean(x, -1, keepdims=True)
            centre = x - mean
            scale = lax.rsqrt(jnp.mean(centre * centre, -1, keepdims=True) + eps_norm)
            stat_keep[at, 0:1] = mean
            stat_keep[at, 1:2] = scale
            unit = centre * scale
            one_buf[to, :] = (unit * vec_ref[0:1, :] + vec_ref[1:2, :]).astype(low)
            two_buf[0, to, :] = (unit * vec_ref[2:3, :] + vec_ref[3:4, :]).astype(low)

        put_one(i, line, "start")
        qkv_now[...] = dot(one_buf[...], wq[...]) + bias_ref[0:1, : cols[0]]
        pre_now[...] = dot(two_buf[0], w1[...]) + bias_ref[0:1, cols[0] :]

        for s in range(seq_dev):
            part = slice(s * slot_len, (s + 1) * slot_len)
            rows = pl.ds(pl.multiple_of(base + s * slot_len, 32), slot_len)
            qkv_keep[rows, 0:half] = turn(qkv_now[part, 0:half], 1).astype(low)
            qkv_keep[rows, half:head] = qkv_now[part, half:head].astype(low)
            qkv_keep[rows, head : head + half] = turn(qkv_now[part, head : head + half], 1).astype(low)
            qkv_keep[rows, head + half :] = qkv_now[part, head + half :].astype(low)
            query = qkv_keep[rows, :head]
            keys = qkv_keep[rows, head : 2 * head]
            values = qkv_keep[rows, 2 * head :]
            scores = jnp.where(causal, contract(query, keys, ((1,), (1,))) / root, neg_large)
            expo = jnp.exp(scores - jnp.max(scores, -1, keepdims=True))
            probs = expo / jnp.sum(expo, -1, keepdims=True)
            prob_keep[line * seq_dev + s] = probs
            attn_keep[rows, :] = (dot(probs.astype(low), values) * valid_ref[rows, :]).astype(low)

        @pl.loop(0, block_rows // chunk)
        def act(j):
            at = pl.ds(pl.multiple_of(base + j * chunk, chunk), chunk)
            pre = pre_now[pl.ds(pl.multiple_of(j * chunk, chunk), chunk), :]
            area = 0.5 * (1.0 + lax.erf(pre * math.sqrt(0.5)))
            hid_keep[at, :] = (pre * area * valid_ref[at, :]).astype(low)
            pg_keep[at, :] = (area + pre * (jnp.exp(-0.5 * pre * pre) * (1.0 / math.sqrt(2.0 * math.pi)))).astype(low)

    put_one(LINE - 1, (c + LINE - 1) % LINE, "wait")
    local_weight(2, "wait")
    local_weight(3, "wait")
    last(2)
    last(3)
    mine = c * 2 + k

    def pair_m(i, act):
        copy = remote(m_buf.at[i % 2, me.other], m_got.at[i], msib_s.at[i], msib_r.at[i], sibling)
        getattr(copy, act)()

    def half_m(i, act):
        for q, to in enumerate((partner, (partner + 2) % LINE)):
            copy = remote(
                m_got.at[i, to], m_half.at[i, q], half_s.at[i, q], half_r.at[i, q], me.at(partner, g, k)
            )
            getattr(copy, act)()

    def far_m(i, act):
        copy = remote(m_got.at[i, beyond], far_out.at[i], far_s.at[i], far_r.at[i], me.at(beyond, g, k))
        getattr(copy, act)()

    def near_m(i, act):
        getattr(pltpu.make_async_copy(m_got.at[i, c], near_out.at[i], near_sem.at[i]), act)()

    def sent_m(i):
        half_m(i, SENT)
        far_m(i, SENT)
        near_m(i, "wait")

    def second_m(i):
        half_m(i, "wait_recv")

        @pl.loop(0, block_rows // 64)
        def add(j):
            at = pl.ds(pl.multiple_of(j * 64, 64), 64)
            for q, to in enumerate((c, beyond)):
                total = m_got[i, to, at, :].astype(f32) + m_half[i, q, at, :].astype(f32)
                m_got[i, to, at, :] = total.astype(low)

        far_m(i, START)
        near_m(i, START)

    def pair_add(i):
        pair_m(i, "wait_recv")

        @pl.loop(0, LINE)
        def add_outer(p):
            @pl.loop(0, block_rows // 64)
            def add(j):
                at = pl.ds(pl.multiple_of(j * 64, 64), 64)
                total = m_buf[i % 2, k, p, at, :].astype(f32) + m_got[i, p, at, :].astype(f32)
                m_got[i, p, at, :] = total.astype(low)

        half_m(i, START)

    @pl.loop(0, LINE)
    def outputs(i):
        base = pl.multiple_of(i * block_rows, 128)
        whole = pl.ds(base, block_rows)
        slot = i % 2

        @pl.when(i == 1)
        def _():
            pass_on(1, 2)

        @pl.when(i >= 2)
        def _():
            pair_m(i - 2, SENT)

        live = valid_ref[whole, :]

        @pl.loop(0, ways)
        def output(j):
            at = pl.ds(pl.multiple_of(j * wide, 128), wide)
            total = contract(attn_keep[whole, :], wd[at, :], ((1,), (1,)))
            total = total + contract(hid_keep[whole, :], w2[at, :], ((1,), (1,)))
            feature = (lax.broadcasted_iota(jnp.int32, (1, wide), 1) + j * wide) // (D // (2 * LINE))
            mask = jnp.where(feature == mine, 1.0, 0.0)
            extra = x_all[whole, at].astype(f32) + (vec_ref[4:5, at] + vec_ref[5:6, at])
            total = ((total + mask * extra) * live).astype(low)
            m_buf[slot, 0, j] = total[:, : wide // 2]
            m_buf[slot, 1, j] = total[:, wide // 2 :]

        pair_m(i, START)

        @pl.when(i >= 1)
        def _():
            pair_add(i - 1)

    local_acts(1, "wait")
    arrive_sibling(1)

    per = 128 // rows_own
    part_cols = 256
    fits = block_rows // 128
    pieces = (cols[2] + cols[3]) // part_cols
    dense_pieces = cols[2] // part_cols

    def out_group(i):
        flip_x, flip_y = 1 - i % 2, 1 - i // 2
        return (g // 2 + flip_y) % 2 * 2 + (g % 2 + flip_x) % 2

    def out_products(i):
        slot = i % 2
        if near:
            to = out_group(i)
            tiles = [(l, to) for l in range(LINE)]
        else:
            tiles = [(i, t * per) for t in range(LINE)]
        lhs = turned([ct_all[:, pl.ds(pl.multiple_of((l * groups + p) * rows_own, 128), 128)] for l, p in tiles])
        first = 0
        for right in (attn_keep, hid_keep):
            out = dot(lhs, right[...]).astype(low)
            for n in range(right.shape[1] // part_cols):
                nb = first + n
                for t in range(LINE):
                    m_buf[slot, nb // fits, t, (nb % fits) * 128 : (nb % fits + 1) * 128, :] = out[
                        t * 128 : (t + 1) * 128, n * part_cols : (n + 1) * part_cols
                    ]
            first += right.shape[1] // part_cols

    def out_piece(i, nb, to):
        row = (nb % fits) * 128
        if near:
            return m_buf.at[i % 2, nb // fits, :, pl.ds(row, 128), :]
        return m_buf.at[i % 2, nb // fits, to // per, pl.ds(pl.multiple_of(row + (to % per) * rows_own, 32), rows_own), :]

    def out_place(refs, i, nb, step):
        ref, n = (refs[0], nb) if nb < dense_pieces else (refs[1], nb - dense_pieces)
        at = pl.ds(n * part_cols, part_cols)
        if step is not None:
            ref = ref.at[step - 1]
        return ref.at[:, :, at] if near else ref.at[i, :, at]

    def out_send(i, step, act):
        to = out_group(i) if near else (g + step) % groups
        for nb in range(pieces):
            sem = (0 if near else i, step, nb)
            copy = remote(
                out_piece(i, nb, to), out_place((gd_got, g2_got), i, nb, step), gp_s.at[sem], gp_r.at[sem],
                me.at(c, to, k),
            )
            getattr(copy, act)()

    def out_keep(i, act):
        for nb in range(pieces):
            copy = pltpu.make_async_copy(
                out_piece(i, nb, g), out_place((gd_own, g2_own), i, nb, None), g_here.at[0 if near else i, nb]
            )
            getattr(copy, act)()

    def out_sends(i, act):
        local = "wait" if act == SENT else act
        if near:

            @pl.when(i < groups - 1)
            def _():
                out_send(i, groups - 1 - i, act)

            @pl.when(i == groups - 1)
            def _():
                out_keep(i, local)
        else:
            for step in range(1, groups):
                out_send(i, step, act)
            out_keep(i, local)

    def pair_s(i, act):
        line = (c + i) % LINE
        rows = pl.ds(pl.multiple_of(me.other * slot_len, 32), slot_len)
        copy = remote(two_buf.at[i % 2, rows], s_got.at[line], ssib_s.at[i], ssib_r.at[i], sibling)
        getattr(copy, act)()

    def put_s(i, act):
        line = (c + i) % LINE
        rows = pl.ds(pl.multiple_of(k * slot_len, 32), slot_len)
        getattr(pltpu.make_async_copy(two_buf.at[i % 2, rows], s_out.at[line], s_here.at[i]), act)()

    def finish_s(i):
        line = (c + i) % LINE
        pair_s(i, "wait_recv")

        @pl.loop(0, slot_len // chunk)
        def add(j):
            at = pl.ds(pl.multiple_of(k * slot_len + j * chunk, chunk), chunk)
            to = pl.ds(pl.multiple_of(j * chunk, chunk), chunk)
            total = two_buf[i % 2, at, :].astype(f32) + s_got[line, to, :].astype(f32)
            two_buf[i % 2, at, :] = total.astype(low)

        put_s(i, START)

    def put_rest(line, act):
        rows = pl.ds(pl.multiple_of(line * block_rows, 128), block_rows)
        for place_at, (buf, out) in enumerate(((qkv_keep, qg_out), (pg_keep, pg_out))):
            getattr(pltpu.make_async_copy(buf.at[rows], out.at[rows], out_d.at[place_at, line]), act)()

    @pl.loop(0, LINE)
    def backward(i):
        line = (c + i) % LINE
        base = pl.multiple_of(line * block_rows, 128)
        whole = pl.ds(base, block_rows)
        slot = i % 2

        @pl.when(i == 0)
        def _():
            pair_m(LINE - 2, SENT)

        @pl.when(i == 1)
        def _():
            pair_m(LINE - 1, SENT)

        @pl.when(i >= 2)
        def _():
            out_sends(i - 2, SENT)

        out_products(i)
        out_sends(i, START)

        @pl.when(i == 0)
        def _():
            pair_add(LINE - 1)

        @pl.when((i == 1) | (i == 2))
        def _():
            second_m(i * 2 - 2)
            second_m(i * 2 - 1)

        live = valid_ref[whole, :]
        back_buf[...] = (ct_all[whole, :].astype(f32) * live).astype(low)
        attn_grad = dot(back_buf[...], wd[...]).astype(low)
        pre_now[...] = dot(back_buf[...], w2[...])

        @pl.when(i == 0)
        def _():
            rows = pl.ds(pl.multiple_of(k * slot_len, 32), slot_len)
            total = jnp.sum(back_buf[rows, :].astype(f32).reshape(slot_len // 8, 8, D), 0)
            norm_acc[4] = total

        @pl.loop(0, block_rows // chunk)
        def act(j):
            at = pl.ds(pl.multiple_of(base + j * chunk, chunk), chunk)
            grad = pre_now[pl.ds(pl.multiple_of(j * chunk, chunk), chunk), :] * pg_keep[at, :].astype(f32)
            grad = grad.astype(low)
            pg_keep[at, :] = grad
            grad = grad.astype(f32)
            bias_acc[:, cols[0] :] += grad[:8] + grad[8:]

        for s in range(seq_dev):
            rows = pl.ds(pl.multiple_of(base + s * slot_len, 32), slot_len)
            grad = attn_grad[s * slot_len : (s + 1) * slot_len]
            query = qkv_keep[rows, :head]
            keys = qkv_keep[rows, head : 2 * head]
            values = qkv_keep[rows, 2 * head :]
            probs = prob_keep[line * seq_dev + s]
            prob_grad = contract(grad, values, ((1,), (1,)))
            row_dot = jnp.sum(probs * prob_grad, -1, keepdims=True)
            score_grad = (probs * (prob_grad - row_dot)).astype(low)
            value_grad = contract(probs.astype(low), grad, ((0,), (0,)))
            query_grad = dot(score_grad, keys) / root
            key_grad = contract(score_grad, query, ((0,), (0,))) / root
            qkv_keep[rows, 0:half] = turn(query_grad[:, :half], -1).astype(low)
            qkv_keep[rows, half:head] = query_grad[:, half:].astype(low)
            qkv_keep[rows, head : head + half] = turn(key_grad[:, :half], -1).astype(low)
            qkv_keep[rows, head + half : 2 * head] = key_grad[:, half:].astype(low)
            qkv_keep[rows, 2 * head :] = value_grad.astype(low)
            summed = qkv_keep[rows, :].astype(f32).reshape(slot_len // 8, 8, cols[0])
            bias_acc[:, : cols[0]] += jnp.sum(summed, 0)

        put_rest(line, "start")
        mean = stat_keep[whole, 0:1]
        scale = stat_keep[whole, 1:2]

        @pl.when(i >= 2)
        def _():
            pair_s(i - 2, SENT)
            put_s(i - 2, "wait")

        @pl.loop(0, ways)
        def inputs(j):
            at = pl.ds(pl.multiple_of(j * wide, 128), wide)
            first = contract(qkv_keep[whole, :], wq[at, :], ((1,), (1,)))
            second = contract(pg_keep[whole, :], w1[at, :], ((1,), (1,)))
            two_buf[slot, :, at] = (first * vec_ref[0:1, at] + second * vec_ref[2:3, at]).astype(low)
            unit = (x_all[whole, at].astype(f32) - mean) * scale
            for place_at, value in enumerate((first * unit, first, second * unit, second)):
                norm_acc[place_at, :, at] += jnp.sum(value.reshape(block_rows // 8, 8, wide), 0)

        pair_s(i, START)

        @pl.when(i >= 1)
        def _():
            finish_s(i - 1)

    finish_s(LINE - 1)
    for r in range(5):
        total = jnp.sum(norm_acc[r], 0, keepdims=True)
        for t in range(D // 128):
            early_ref[r * (D // 128) + t : r * (D // 128) + t + 1, :] = total[:, t * 128 : (t + 1) * 128]
    at_bias = 5 * (D // 128)
    total = jnp.sum(bias_acc[...], 0, keepdims=True)
    for t in range((cols[0] + cols[1]) // 128):
        early_ref[at_bias + t : at_bias + t + 1, :] = total[:, t * 128 : (t + 1) * 128]
    at_row = at_bias + (cols[0] + cols[1]) // 128
    early_ref[at_row : at_row + 1, :] = vec_ref[6:7, :128]
    early_ref[at_row + 1 :, :] = jnp.zeros((early_ref.shape[0] - at_row - 1, 128), f32)
    for i in range(LINE):
        put_rest(i, "wait")
        sent_m(i)
        far_m(i, "wait_recv")
    for i in (LINE - 2, LINE - 1):
        pair_s(i, SENT)
        put_s(i, "wait")
        out_sends(i, SENT)
    for step in range(1, groups):
        for nb in range(pieces):
            for i in range(1 if near else LINE):
                dst = out_place((gd_got, g2_got), i, nb, step)
                sem = (i, step, nb)
                remote(dst, dst, gp_s.at[sem], gp_r.at[sem], sibling).wait_recv()
    for m in range(count):
        stage_one(m, SENT)
        for step in range(LINE):
            stage_two(m, step, SENT)
            if near:
                stage_three(m, step, SENT)
    for which in range(2):
        for q in range(3):
            row_send(which, q, SENT)
            to_sibling(which, q, SENT)


def gather_all(groups, weights, tokens, cotangent, vectors, biases, valid, turns):
    rows_own = weights[0].shape[0]
    seq_dev, slot_len, width = tokens.shape
    cols = tuple(w.shape[1] // LINE for w in weights)
    count = len(weights)
    block_rows = seq_dev * slot_len
    rows = LINE * block_rows
    f32, low = jnp.float32, jnp.bfloat16
    dma = pltpu.SemaphoreType.DMA
    peers = 3 if groups == 4 else groups
    out_widths = (D, D, cols[0], cols[1])
    pieces = (cols[2] + cols[3]) // 256
    feat = D // (2 * LINE)
    early_rows = -(-(5 * D + cols[0] + cols[1] + 128) // 1024) * 8
    return pl.pallas_call(
        partial(gather_kernel, groups, cols, seq_dev, slot_len),
        out_shape=[jax.ShapeDtypeStruct((rows, w), low) for w in out_widths]
        + [
            jax.ShapeDtypeStruct((LINE, block_rows, feat), low),
            jax.ShapeDtypeStruct((LINE, block_rows, feat), low),
            jax.ShapeDtypeStruct((LINE, slot_len, D), low),
            jax.ShapeDtypeStruct((LINE, rows_own, cols[2]), low),
            jax.ShapeDtypeStruct((LINE, rows_own, cols[3]), low),
            jax.ShapeDtypeStruct((groups - 1, LINE, rows_own, cols[2]), low),
            jax.ShapeDtypeStruct((groups - 1, LINE, rows_own, cols[3]), low),
            jax.ShapeDtypeStruct((early_rows, 128), f32),
        ],
        in_specs=[ANY] * (count + 2) + [VMEM] * 4,
        out_specs=[ANY] * 11 + [VMEM],
        scratch_shapes=[pltpu.VMEM((D, w), low) for w in cols]
        + [pltpu.VMEM((rows, D), low)] * 2
        + [
            pltpu.VMEM((rows, cols[0]), low),
            pltpu.VMEM((LINE * seq_dev, slot_len, slot_len), f32),
            pltpu.VMEM((rows, cols[2]), low),
            pltpu.VMEM((rows, cols[3]), low),
            pltpu.VMEM((rows, cols[1]), low),
            pltpu.VMEM((block_rows, D), low),
            pltpu.VMEM((2, block_rows, D), low),
            pltpu.VMEM((block_rows, D), low),
            pltpu.VMEM((2, 2, LINE, block_rows, feat), low),
            pltpu.VMEM((LINE, LINE, block_rows, feat), low),
            pltpu.VMEM((LINE, 2, block_rows, feat), low),
            pltpu.VMEM((LINE, slot_len, D), low),
            pltpu.VMEM((block_rows, cols[0]), f32),
            pltpu.VMEM((block_rows, cols[1]), f32),
            pltpu.VMEM((rows, 2), f32),
            pltpu.VMEM((5, 8, D), f32),
            pltpu.VMEM((8, cols[0] + cols[1]), f32),
            dma((count, LINE)),
            dma((count, LINE)),
            dma((count, LINE, peers)),
            dma((count, LINE, peers)),
            dma((count, LINE)),
            dma((count, LINE)),
            dma((2, 3)),
            dma((2, 3)),
            dma((2, 3)),
            dma((2, 3)),
            dma((count + 2, seq_dev)),
            dma(()),
            dma((2,)),
            dma((2, LINE)),
            dma((LINE,)),
            dma((LINE,)),
            dma((LINE,)),
            dma((LINE,)),
            dma((LINE, 2)),
            dma((LINE, 2)),
            dma((LINE,)),
            dma((LINE,)),
            dma((LINE,)),
            dma((LINE,)),
            dma((LINE, groups, pieces)),
            dma((LINE, groups, pieces)),
            dma((LINE, pieces)),
        ],
        compiler_params=pltpu.CompilerParams(
            collective_id=0, has_side_effects=True, vmem_limit_bytes=62 * 1024 * 1024
        ),
        name="gather_all",
    )(*weights, tokens, cotangent, vectors, biases, valid, turns)


def scatter_kernel(groups, cols, seq_dev, slot_len, rows_own, *refs):
    count = len(cols)
    f32, low = jnp.float32, jnp.bfloat16
    pick = refs[0]
    lefts_in = refs[1:3]
    rights_in = refs[3:5]
    near_ref, far_ref, s_ref = refs[5:8]
    done_own, done_got = refs[8:10], refs[10:12]
    early_ref = refs[12]
    mixed_ref, ssum_ref = refs[13:15]
    g_out = refs[15 : 15 + count]
    early_out, col_out, row_out = refs[15 + count : 18 + count]
    rest = refs[18 + count :]
    left_buf, right_a, right_b = rest[:3]
    g_own = rest[3 : 3 + count]
    g_got = rest[3 + count : 3 + 2 * count]
    (m_in, m_all, m_send, s_own, s_half, s_far, early_group, col_now, col_group, row_keep, row_turn) = rest[
        3 + 2 * count : 14 + 2 * count
    ]
    (here, half_s, half_r, far_s, far_r, fin_s, fin_r, mall_s, mall_r, mout_s, mout_r, gp_s, gp_r, gl_s, gl_r, eg_s,
     eg_r, el_s, el_r, es_s, es_r, cg_s, cg_r, cl_s, cl_r, cs_s, cs_r, rl_s, rl_r, keep_sem) = rest[14 + 2 * count :]
    me = Place(groups)
    c, g, k = me.line, me.group, me.core
    me.greet()
    sibling = me.at(c, g, me.other)
    feat = D // (2 * LINE)
    seqs = LINE * seq_dev
    rows = seqs * slot_len
    double = groups == 4
    sends = []

    def go(copy):
        copy.start()
        sends.append(copy)

    def to_group(step):
        return (g + step) % groups

    def from_group(step):
        return (g + groups - step) % groups

    def arrived(dst, send, recv):
        remote(dst, dst, send, recv, sibling).wait_recv()

    def add_rows(total, parts, count_rows, chunk):
        @pl.loop(0, count_rows // chunk)
        def body(i):
            at = pl.ds(pl.multiple_of(i * chunk, chunk), chunk)
            acc = parts[0](at)[...].astype(f32)
            for part in parts[1:]:
                acc = acc + part(at)[...].astype(f32)
            total(at)[...] = acc.astype(low)

    def load(src, dst, sem):
        copy = pltpu.make_async_copy(src, dst, sem)
        copy.start()
        return copy

    partner = c + 1 - 2 * (c % 2)
    beyond = (c + 2) % LINE
    for q, to in enumerate((partner, (partner + 2) % LINE)):
        go(remote(s_ref.at[to], s_half.at[q], half_s.at[q], half_r.at[q], me.at(partner, g, k)))
    got_m = [load(near_ref, m_in.at[0], here.at[10]), load(far_ref, m_in.at[1], here.at[11])]
    got_done = []
    for q in range(2):
        got_done.append(load(done_own[q], g_own[2 + q].at[:, 0], here.at[2 + 2 * q]))
        got_done.append(load(done_got[q], g_got[2 + q], here.at[3 + 2 * q]))
    got_two = load(lefts_in[1], left_buf.at[0], here.at[6])
    got_1 = load(rights_in[1], right_a, here.at[7])
    if double:
        got_one = load(lefts_in[0], left_buf.at[1], here.at[0])
        got_q = load(rights_in[0], right_b, here.at[1])
    got_s = [load(s_ref.at[c], s_own.at[0], here.at[8]), load(s_ref.at[beyond], s_own.at[1], here.at[9])]
    for step in range(1, groups):
        go(remote(early_ref, early_group.at[g], eg_s.at[step], eg_r.at[step], me.at(c, to_group(step), k)))
    early_group[g] = early_ref[...]

    per = 128 // rows_own

    def tile_products(m, left, right, tiles):
        lhs = turned([left[:, pl.ds(pl.multiple_of((l * groups + p) * rows_own, 128), 128)] for l, p in tiles])
        out = dot(lhs, right[...]).astype(low)
        for t, (l, p) in enumerate(tiles):
            for q in range(per):
                row = t * 128 + q * rows_own
                g_own[m][l, p + q] = out[row : row + rows_own]

    def send_group(m, step, act):
        to = to_group(step)
        copy = remote(
            g_own[m].at[:, to], g_got[m].at[step - 1], gp_s.at[m, step], gp_r.at[m, step], me.at(c, to, k)
        )
        getattr(copy, act)()

    across, beside, above = me.group_to(3), me.group_to(1), me.group_to(2)
    two_phase = groups == 4

    def phase_one(m, way, act):
        lines = pl.ds(0, 2) if way == 0 else pl.ds(2, 2)
        to = beside if way == 0 else above
        for q, block in enumerate((to, across)):
            copy = remote(
                g_own[m].at[lines, block], g_got[m].at[q, lines], gp_s.at[m, way * 2 + q], gp_r.at[m, way * 2 + q],
                me.at(c, to, k),
            )
            getattr(copy, act)()

    def phase_two(m, way, act):
        lines = pl.ds(0, 2) if way == 0 else pl.ds(2, 2)
        to = above if way == 0 else beside
        copy = remote(
            g_own[m].at[lines, to], g_got[m].at[2, lines], gp_s.at[m, 4 + way], gp_r.at[m, 4 + way], me.at(c, to, k)
        )
        getattr(copy, act)()

    def between_phases(m):
        for way in range(2):
            phase_one(m, way, "wait_recv")
            to = above if way == 0 else beside
            for line in (way * 2, way * 2 + 1):
                add_rows(
                    lambda at: g_own[m].at[line, to, at],
                    [lambda at: g_own[m].at[line, to, at], lambda at: g_got[m].at[1, line, at]],
                    rows_own,
                    16,
                )
            phase_two(m, way, "start")

    def products(left, pairs):
        if two_phase:

            @pl.loop(0, groups)
            def body(t):
                flip_x, flip_y = (t + 1) % 2, (3 - t) // 2 * (1 - t // 3)
                to = (g // 2 + flip_y) % 2 * 2 + (g % 2 + flip_x) % 2
                for m, right in pairs:
                    tile_products(m, left, right, [(l, to) for l in range(LINE)])
                    for way in range(2):

                        @pl.when(t == 2 - way)
                        def _():
                            phase_one(m, way, "start")
        else:

            @pl.loop(0, LINE)
            def body(l):
                for m, right in pairs:
                    tile_products(m, left, right, [(l, t * per) for t in range(4)])

            for m, _ in pairs:
                for step in range(1, groups):
                    send_group(m, step, "start")

    def sum_groups(m, first):
        got = range(groups - 1)
        if m < 2 and two_phase:
            for way in range(2):
                phase_two(m, way, "wait_recv")
            got = (0, 2)
        elif m < 2:
            for step in range(1, groups):
                arrived(g_got[m].at[step - 1], gp_s.at[m, step], gp_r.at[m, step])
        mine = g if m < 2 else 0
        width = pl.ds(pl.multiple_of(c * cols[m], 128), cols[m])
        total = jnp.zeros((8, cols[m]), f32)
        for step in (2, 1, 3, 0):
            line = me.line_to(step)

            def body(i, carry, line=line):
                at = pl.ds(pl.multiple_of(i * 16, 16), 16)
                acc = g_own[m][line, mine, at, :].astype(f32)
                for p in got:
                    acc = acc + g_got[m][p, line, at, :].astype(f32)
                g_own[m][line, mine, at, :] = acc.astype(low)
                square = acc * acc + eps_second
                row_keep[line, at, m : m + 1] = jnp.sum(square, 1, keepdims=True)
                return carry + square[:8] + square[8:]

            total = lax.fori_loop(0, rows_own // 16, body, total)
            src = g_own[m].at[line, mine]
            if step:
                go(remote(src, g_out[m].at[:, width], gl_s.at[m, step], gl_r.at[m, step], me.at(line, g, k)))
            else:
                keep.append(load(src, g_out[m].at[:, width], keep_sem.at[2 + m]))
        total = jnp.sum(total, 0, keepdims=True)
        for t in range(cols[m] // 128):
            col_now[first + t : first + t + 1, :] = total[:, t * 128 : (t + 1) * 128]

    keep = []
    row_keep[...] = jnp.zeros_like(row_keep)
    firsts = []
    edge = 0
    for m in range(count):
        firsts.append(edge)
        edge += cols[m] // 128
    for copy in got_m:
        copy.wait()
    ours = pl.ds(g * seqs, seqs)
    for s in range(seqs):
        add_rows(
            lambda at: m_all.at[g * seqs + s, at],
            [lambda at: m_in.at[0, s, at], lambda at: m_in.at[1, s, at]],
            slot_len,
            64,
        )
    for step in range(1, groups):
        go(remote(m_all.at[ours], m_all.at[ours], mall_s.at[step], mall_r.at[step], me.at(c, to_group(step), k)))

    for copy in got_done:
        copy.wait()
    sum_groups(3, firsts[3])
    sum_groups(2, firsts[2])
    got_two.wait()
    got_1.wait()
    products(left_buf.at[0], ((1, right_a),))
    if not double:
        got_one = load(lefts_in[0], left_buf.at[0], here.at[0])
        got_q = load(rights_in[0], right_b, here.at[1])

    for q in range(2):
        got_s[q].wait()
        arrived(s_half.at[q], half_s.at[q], half_r.at[q])
        add_rows(
            lambda at: s_own.at[q, at], [lambda at: s_own.at[q, at], lambda at: s_half.at[q, at]], slot_len, 16
        )
    go(remote(s_own.at[1], s_far, far_s, far_r, me.at(beyond, g, k)))

    got_one.wait()
    got_q.wait()
    products(left_buf.at[1 if double else 0], ((0, right_b),))
    if two_phase:
        between_phases(1)
    for step in range(1, groups):
        arrived(early_group.at[from_group(step)], eg_s.at[step], eg_r.at[step])
    acc = early_group[0]
    for i in range(1, groups):
        acc = acc + early_group[i]
    early_out[k, c] = acc
    for step in range(1, LINE):
        go(remote(early_out.at[k, c], early_out.at[k, c], el_s.at[step], el_r.at[step], me.at(me.line_to(step), g, k)))

    for step in range(1, groups):
        arrived(m_all.at[pl.ds(from_group(step) * seqs, seqs)], mall_s.at[step], mall_r.at[step])
    mixed_cols = pl.ds(pl.multiple_of((c * 2 + k) * feat, 128), feat)
    for step in (1, 2, 3, 0):
        line = me.line_to(step)
        for s in range(seq_dev):
            m_send[line, s] = m_all[pick[line * seq_dev + s]]
        where = mixed_ref.at[:, :, mixed_cols]
        if step:
            go(remote(m_send.at[line], where, mout_s.at[0, step], mout_r.at[0, step], me.at(line, g, k)))
        else:
            keep.append(load(m_send.at[line], where, keep_sem.at[1]))
            go(remote(m_send.at[line], where, mout_s.at[1, 0], mout_r.at[1, 0], sibling))
    if two_phase:
        between_phases(0)
    sum_groups(1, firsts[1])
    sum_groups(0, firsts[0])

    for step in range(1, groups):
        go(remote(col_now, col_group.at[g], cg_s.at[step], cg_r.at[step], me.at(c, to_group(step), k)))
    col_group[g] = col_now[...]
    for step in (1, 2, 3, 0):
        line = me.line_to(step)
        row_turn[line] = jnp.transpose(row_keep[line])[:8]
        if step:
            go(remote(row_turn.at[line], row_out.at[k, c], rl_s.at[0, step], rl_r.at[0, step], me.at(line, g, k)))
        else:
            row_out[k, c] = row_turn[line]
        go(remote(row_turn.at[line], row_out.at[k, c], rl_s.at[1, step], rl_r.at[1, step], me.at(line, g, me.other)))
    for step in range(1, groups):
        arrived(col_group.at[from_group(step)], cg_s.at[step], cg_r.at[step])
    acc = col_group[0]
    for i in range(1, groups):
        acc = acc + col_group[i]
    col_out[k, c] = acc
    for step in range(1, LINE):
        go(remote(col_out.at[k, c], col_out.at[k, c], cl_s.at[step], cl_r.at[step], me.at(me.line_to(step), g, k)))
    arrived(s_far, far_s, far_r)
    add_rows(lambda at: s_own.at[0, at], [lambda at: s_own.at[0, at], lambda at: s_far.at[at]], slot_len, 16)
    go(remote(s_own.at[0], ssum_ref.at[k], fin_s, fin_r, sibling))
    keep.append(load(s_own.at[0], ssum_ref.at[k], keep_sem.at[0]))
    for step in range(1, LINE):
        arrived(early_out.at[k, me.line_from(step)], el_s.at[step], el_r.at[step])
    go(remote(early_out.at[k], early_out.at[k], es_s, es_r, sibling))
    for step in range(1, LINE):
        arrived(col_out.at[k, me.line_from(step)], cl_s.at[step], cl_r.at[step])
    go(remote(col_out.at[k], col_out.at[k], cs_s, cs_r, sibling))

    for step in range(1, LINE):
        where = mixed_ref.at[:, :, pl.ds(pl.multiple_of((me.line_from(step) * 2 + k) * feat, 128), feat)]
        arrived(where, mout_s.at[0, step], mout_r.at[0, step])
        go(remote(where, where, mout_s.at[1, step], mout_r.at[1, step], sibling))
    for m in range(count):
        for step in range(1, LINE):
            dst = g_out[m].at[:, pl.ds(pl.multiple_of(me.line_from(step) * cols[m], 128), cols[m])]
            arrived(dst, gl_s.at[m, step], gl_r.at[m, step])
    for step in range(LINE):
        source = me.line_from(step)
        dst = mixed_ref.at[:, :, pl.ds(pl.multiple_of((source * 2 + me.other) * feat, 128), feat)]
        arrived(dst, mout_s.at[1, step], mout_r.at[1, step])
        for core, way in ((k, 0), (me.other, 1)):
            if step or way:
                arrived(row_out.at[core, source], rl_s.at[way, step], rl_r.at[way, step])
    arrived(ssum_ref.at[me.other], fin_s, fin_r)
    arrived(early_out.at[me.other], es_s, es_r)
    arrived(col_out.at[me.other], cs_s, cs_r)
    for copy in sends:
        copy.wait_send()
    for m in range(2):
        if two_phase:
            for way in range(2):
                phase_one(m, way, "wait_send")
                phase_two(m, way, "wait_send")
        else:
            for step in range(1, groups):
                send_group(m, step, "wait_send")
    for copy in keep:
        copy.wait()


def scatter_all(groups, cols, seq_dev, rows_own, pick, lefts, rights, between):
    near, far, s_pair, *done, early = between
    slot_len = s_pair.shape[1]
    rows = lefts[0].shape[0]
    count = len(cols)
    feat = D // (2 * LINE)
    seqs = LINE * seq_dev
    blocks = (seqs, slot_len, feat)
    dma = pltpu.SemaphoreType.DMA
    f32, low = jnp.float32, jnp.bfloat16
    col_rows = sum(cols) // 128
    return pl.pallas_call(
        partial(scatter_kernel, groups, cols, seq_dev, slot_len, rows_own),
        out_shape=[
            jax.ShapeDtypeStruct((seq_dev, slot_len, D), low),
            jax.ShapeDtypeStruct((seq_dev, slot_len, D), low),
        ]
        + [jax.ShapeDtypeStruct((rows_own, LINE * width), low) for width in cols]
        + [
            jax.ShapeDtypeStruct((2, LINE) + early.shape, f32),
            jax.ShapeDtypeStruct((2, LINE, col_rows, 128), f32),
            jax.ShapeDtypeStruct((2, LINE, 8, 128), f32),
        ],
        in_specs=[SMEM] + [ANY] * 11 + [VMEM],
        out_specs=[ANY] * (2 + count) + [VMEM] * 3,
        scratch_shapes=[
            pltpu.VMEM((2 if groups == 4 else 1, rows, D), low),
            pltpu.VMEM((rows, cols[1]), low),
            pltpu.VMEM((rows, cols[0]), low),
        ]
        + [pltpu.VMEM((LINE, groups if m < 2 else 1, rows_own, width), low) for m, width in enumerate(cols)]
        + [pltpu.VMEM((groups - 1, LINE, rows_own, width), low) for width in cols]
        + [
            pltpu.VMEM((2, seqs, slot_len, feat), low),
            pltpu.VMEM((groups * seqs, slot_len, feat), low),
            pltpu.VMEM((LINE, seq_dev, slot_len, feat), low),
            pltpu.VMEM((2, slot_len, D), low),
            pltpu.VMEM((2, slot_len, D), low),
            pltpu.VMEM((slot_len, D), low),
            pltpu.VMEM((groups,) + early.shape, f32),
            pltpu.VMEM((col_rows, 128), f32),
            pltpu.VMEM((groups, col_rows, 128), f32),
            pltpu.VMEM((LINE, 128, 128), f32),
            pltpu.VMEM((LINE, 8, 128), f32),
            dma((12,)),
            dma((2,)),
            dma((2,)),
            dma(()),
            dma(()),
            dma(()),
            dma(()),
            dma((groups,)),
            dma((groups,)),
            dma((2, LINE)),
            dma((2, LINE)),
            dma((count, max(groups, 6))),
            dma((count, max(groups, 6))),
            dma((count, LINE)),
            dma((count, LINE)),
            dma((groups,)),
            dma((groups,)),
            dma((LINE,)),
            dma((LINE,)),
            dma(()),
            dma(()),
            dma((groups,)),
            dma((groups,)),
            dma((LINE,)),
            dma((LINE,)),
            dma(()),
            dma(()),
            dma((2, LINE)),
            dma((2, LINE)),
            dma((2 + count,)),
        ],
        compiler_params=pltpu.CompilerParams(
            collective_id=1, has_side_effects=True, vmem_limit_bytes=62 * 1024 * 1024
        ),
        name="scatter_all",
    )(pick, *lefts, *rights, near.reshape(blocks), far.reshape(blocks), s_pair, *done, early)


def prepare_kernel(groups, cols, seq_dev, slot_len, *refs):
    (spot, lengths, permutation, wq, w1, wd, w2, vectors, biases, rows_state) = refs[:10]
    lows = refs[10:14]
    valid, own_valid, all_vectors, all_biases, pick = refs[14:]
    f32 = jnp.float32
    for src, dst in zip((wq, w1, wd, w2), lows):
        dst[...] = src[...].astype(jnp.bfloat16)

    @pl.when(pl.program_id(0) == 0)
    def _():
        data, core = spot[0], spot[1]
        line, group = data // groups, data % groups
        times = lax.broadcasted_iota(jnp.int32, (slot_len, 1), 0)
        for place in range(LINE):
            for s in range(seq_dev):
                slot = (place * groups + group) * seq_dev + s
                at = place * seq_dev + s
                valid[at * slot_len : (at + 1) * slot_len, :] = jnp.where(times < lengths[slot], 1.0, 0.0)
                source = permutation[slot]
                chip = source // seq_dev
                pick[at] = (chip % groups) * (LINE * seq_dev) + (chip // groups) * seq_dev + source % seq_dev
        for s in range(seq_dev):
            own_valid[s * slot_len : (s + 1) * slot_len, :] = jnp.where(
                times < lengths[data * seq_dev + s], 1.0, 0.0
            )
        all_vectors[0:6, :] = vectors[...]
        all_vectors[6:8, :] = jnp.zeros((2, D), f32)
        lane = lax.broadcasted_iota(jnp.int32, (1, 128), 1)
        total = jnp.zeros((1, 128), f32)
        for m in range(4):
            total = total + jnp.where(lane == m, jnp.sum(rows_state[m : m + 1, :], 1, keepdims=True), 0.0)
        all_vectors[6:7, 0:128] = jnp.where(core == 0, total, jnp.zeros_like(total))
        all_biases[:, : cols[0]] = biases[:, pl.ds(pl.multiple_of(line * cols[0], 128), cols[0])]
        all_biases[:, cols[0] :] = biases[:, pl.ds(pl.multiple_of(LINE * cols[0] + line * cols[1], 128), cols[1])]


def prepare(groups, seq_dev, slot_len, spot, lengths, permutation, weights, vectors, biases, rows_state):
    f32, low = jnp.float32, jnp.bfloat16
    rows_own = weights[0].shape[0]
    cols = tuple(w.shape[1] // LINE for w in weights)
    tall = 32
    steps = rows_own // tall
    seqs = LINE * seq_dev

    def whole(shape):
        return pl.BlockSpec(shape, lambda i: (0,) * len(shape))

    blocks = [pl.BlockSpec((tall, w.shape[1]), lambda i: (i, 0)) for w in weights]
    return pl.pallas_call(
        partial(prepare_kernel, groups, cols, seq_dev, slot_len),
        grid=(steps,),
        out_shape=[jax.ShapeDtypeStruct(w.shape, low) for w in weights]
        + [
            jax.ShapeDtypeStruct((seqs * slot_len, 1), f32),
            jax.ShapeDtypeStruct((seq_dev * slot_len, 1), f32),
            jax.ShapeDtypeStruct((8, D), f32),
            jax.ShapeDtypeStruct((1, cols[0] + cols[1]), f32),
            jax.ShapeDtypeStruct((seqs,), jnp.int32),
        ],
        in_specs=[SMEM] * 3 + blocks + [whole(vectors.shape), whole(biases.shape), whole(rows_state.shape)],
        out_specs=blocks
        + [
            whole((seqs * slot_len, 1)),
            whole((seq_dev * slot_len, 1)),
            whole((8, D)),
            whole((1, cols[0] + cols[1])),
            SMEM,
        ],
        compiler_params=pltpu.CompilerParams(vmem_limit_bytes=60 * 1024 * 1024),
        name="prepare",
    )(spot, lengths, permutation, *weights, vectors, biases, rows_state)


def finish_kernel(order, cols, rows_own, *refs):
    f32, low = jnp.float32, jnp.bfloat16
    spot = refs[0]
    g_in, w_in = refs[1:5], refs[5:9]
    (s_sum, tokens, cotangent, own_valid, early, col_all, row_all, row_state, col_state, vectors, moments, biases,
     bias_moments) = refs[9:22]
    grads, news, copies = refs[22:26], refs[26:30], refs[30:34]
    (grad_tokens, row_new, col_new, norm_total, norm_moment_new, norm_new, bias_total, bias_moment_new,
     bias_new) = refs[34:43]
    row_factor, col_factor, turn = refs[43:]
    step = pl.program_id(0)
    widths = [w.shape[1] for w in w_in]
    edges = [sum(widths[:i]) for i in range(5)]
    tiles = D // 128

    @pl.when(step == 0)
    def _():
        core = spot[1]
        both = early[0, 0]
        rows_all = row_all[0, 0]
        mass_all = col_all[0, 0]
        for n in range(1, 2 * LINE):
            both = both + early[n // LINE, n % LINE]
            rows_all = rows_all + row_all[n // LINE, n % LINE]
            mass_all = mass_all + col_all[n // LINE, n % LINE]
        for r in range(6):
            for t in range(tiles):
                at = min(r, 4) * tiles + t
                norm_total[r : r + 1, t * 128 : (t + 1) * 128] = both[at : at + 1]
        grad = norm_total[...]
        moment = decay * moments[...] + (1.0 - decay) * (grad * grad + eps_second)
        norm_moment_new[...] = moment
        norm_new[...] = vectors[...] - rate_norm * grad * lax.rsqrt(moment)
        first = 5 * tiles
        parts = ((cols[0] // 128, 0), (cols[1] // 128, LINE * cols[0]))
        for line in range(LINE):
            at = first
            for count, base in parts:
                for t in range(count):
                    to = base + (line * count + t) * 128
                    bias_total[:, to : to + 128] = early[core, line, at : at + 1, :]
                    at += 1
        grad = bias_total[...]
        moment = decay * bias_moments[...] + (1.0 - decay) * (grad * grad + eps_second)
        bias_moment_new[...] = moment
        bias_new[...] = biases[...] - rate_vector * grad * lax.rsqrt(moment)
        at_row = first + (cols[0] + cols[1]) // 128
        full_cols = (3.0 * D, 1.0 * D, 1.0 * FF, 1.0 * FF)
        rates = (
            rate_scale / math.sqrt(D),
            rate_scale / math.sqrt(D // 8),
            rate_scale / math.sqrt(D),
            rate_scale / math.sqrt(FF),
        )
        turn[...] = jnp.zeros_like(turn)
        at = 0
        for m, i in enumerate(order):
            count = cols[m] // 128
            new = decay * row_state[i : i + 1, :] + (1.0 - decay) * (rows_all[m : m + 1, :rows_own] / full_cols[i])
            row_new[i : i + 1, :] = new
            mass = jnp.sum(jnp.sum(mass_all[at : at + count], 1, keepdims=True), 0, keepdims=True)
            mean = (decay * both[at_row : at_row + 1, i : i + 1] + (1.0 - decay) * (mass / full_cols[i])) / D
            turn[i : i + 1, :rows_own] = rates[i] * lax.rsqrt(new / mean)
            for line in range(LINE):
                for t in range(count):
                    to = edges[i] + (line * count + t) * 128
                    col_new[:, to : to + 128] = col_all[core, line, at + t : at + t + 1, :]
            at += count
        row_factor[...] = jnp.transpose(turn[...])
        new = decay * col_state[...] + (1.0 - decay) * (col_new[...] / D)
        col_new[...] = new
        col_factor[...] = lax.rsqrt(new)

    tall = w_in[0].shape[0]
    for half in range(tall // 16):
        rows = pl.ds(pl.multiple_of(step * tall + half * 16, 16), 16)
        part = slice(half * 16, half * 16 + 16)
        for i in range(4):
            factor = row_factor[rows, i : i + 1]
            for n in range(widths[i] // 1024):
                at = slice(n * 1024, (n + 1) * 1024)
                grad = g_in[i][part, at].astype(f32)
                new = w_in[i][part, at] - grad * factor * col_factor[:, edges[i] + n * 1024 : edges[i] + (n + 1) * 1024]
                grads[i][part, at] = grad
                news[i][part, at] = new
                copies[i][part, at] = new.astype(low)

    @pl.loop(0, tokens.shape[0] // 16)
    def body(j):
        at = pl.ds(pl.multiple_of(j * 16, 16), 16)
        x = tokens[at, :].astype(f32)
        centre = x - jnp.mean(x, -1, keepdims=True)
        scale = lax.rsqrt(jnp.mean(centre * centre, -1, keepdims=True) + eps_norm)
        unit = centre * scale
        flow = s_sum[at, :].astype(f32)
        through = flow - jnp.mean(flow, -1, keepdims=True) - unit * jnp.mean(flow * unit, -1, keepdims=True)
        grad_tokens[at, :] = (cotangent[at, :].astype(f32) * own_valid[at, :] + scale * through).astype(low)


def finish(order, spot, grads, weights, s_sum, tokens, cotangent, own_valid, *small):
    f32, low = jnp.float32, jnp.bfloat16
    rows_own = weights[0].shape[0]
    tall = 32
    steps = rows_own // tall
    cols = tuple(weights[i].shape[1] // LINE for i in order)
    rows = tokens.shape[0]
    row_state, col_state, vectors, _, biases = small[3:8]

    def whole(shape):
        return pl.BlockSpec(shape, lambda i: (0,) * len(shape))

    blocks = [pl.BlockSpec((tall, w.shape[1]), lambda i: (i, 0)) for w in weights]
    acts = pl.BlockSpec((rows // steps, D), lambda i: (i, 0))
    small_out = [row_state.shape, col_state.shape] + [vectors.shape] * 3 + [biases.shape] * 3
    return pl.pallas_call(
        partial(finish_kernel, order, cols, rows_own),
        grid=(steps,),
        out_shape=[jax.ShapeDtypeStruct(w.shape, f32) for w in weights] * 2
        + [jax.ShapeDtypeStruct(w.shape, low) for w in weights]
        + [jax.ShapeDtypeStruct((rows, D), low)]
        + [jax.ShapeDtypeStruct(shape, f32) for shape in small_out],
        in_specs=[SMEM]
        + blocks * 2
        + [acts] * 3
        + [pl.BlockSpec((rows // steps, 1), lambda i: (i, 0))]
        + [whole(a.shape) for a in small],
        out_specs=blocks * 3 + [acts] + [whole(shape) for shape in small_out],
        scratch_shapes=[
            pltpu.VMEM((128, 128), f32),
            pltpu.VMEM(col_state.shape, f32),
            pltpu.VMEM((128, 128), f32),
        ],
        compiler_params=pltpu.CompilerParams(vmem_limit_bytes=60 * 1024 * 1024),
        name="finish",
    )(spot, *grads, *weights, s_sum, tokens, cotangent, own_valid, *small)


def per_device(
    tokens,
    cotangent,
    lengths,
    permutation,
    w_qkv,
    w_dense,
    w_fc1,
    w_fc2,
    norm_vectors,
    split_biases,
    row_state,
    col_state,
    norm_moment,
    bias_moment,
):
    groups = lax.axis_size("dp") // LINE
    seq_dev, slot_len, width = tokens.shape
    rows_own = w_qkv.shape[0]
    head_dim = D // HEADS
    weights = (w_qkv, w_dense, w_fc1, w_fc2)
    order = (0, 2, 1, 3)
    cols = tuple(weights[i].shape[1] // LINE for i in order)
    spot = jnp.stack([lax.axis_index("dp"), lax.axis_index("tensor")]).astype(jnp.int32)
    *lows, valid, own_valid, vectors, biases, pick = prepare(
        groups, seq_dev, slot_len, spot, lengths, permutation, [weights[i] for i in order], norm_vectors,
        split_biases, row_state,
    )
    turns = jnp.asarray(turn_tables(slot_len, head_dim // 4, head_dim // 2))
    norm_one, norm_two, qkv_grad, pre_grad, *between = gather_all(
        groups, lows, tokens, cotangent, vectors, biases, valid, turns
    )
    mixed, s_sum, *outs = scatter_all(
        groups, cols, seq_dev, rows_own, pick, (norm_one, norm_two), (qkv_grad, pre_grad), between
    )
    grads = [outs[order.index(i)] for i in range(4)]
    early_all, col_all, row_all = outs[4:]
    results = finish(
        order, spot, grads, weights, s_sum.reshape(-1, width), tokens.reshape(-1, width),
        cotangent.reshape(-1, width), own_valid, early_all, col_all, row_all, row_state, col_state, norm_vectors,
        norm_moment, split_biases, bias_moment,
    )
    return (mixed, results[12].reshape(tokens.shape), *results[:12], *results[13:])


def solution(mesh):
    halves = P("dp", "tensor")
    split = P("tensor", None)
    in_specs = (
        P("dp", None, None),
        P("dp", None, None),
        P(),
        P(),
        halves,
        halves,
        halves,
        halves,
        P(),
        split,
        P(None, "dp"),
        split,
        P(),
        split,
    )
    out_specs = (
        (P("dp", None, None),) * 2
        + (halves,) * 12
        + (P(None, "dp"), split)
        + (P(),) * 3
        + (split,) * 3
    )
    return jax.shard_map(
        per_device, mesh=mesh, in_specs=in_specs, out_specs=out_specs, check_vma=False
    )
```

```python
from functools import partial
import math

import jax
import jax.numpy as jnp
import numpy as np
from jax import lax
from jax.experimental import pallas as pl
from jax.experimental.pallas import tpu as pltpu
from jax.sharding import PartitionSpec as P

D = 2048
FF = 8192
HEADS = 8
LINE = 4

eps_norm = 1e-05
eps_second = 1e-30
decay = 0.5
rate_scale = 1.0
rate_norm = 0.5
rate_vector = 0.05
neg_large = -1e30

MESH = pl.DeviceIdType.MESH
ANY = pl.BlockSpec(memory_space=pl.ANY)
VMEM = pl.BlockSpec(memory_space=pltpu.VMEM)
SMEM = pl.BlockSpec(memory_space=pltpu.SMEM)


def turn_tables(slot_len, rot_dims, width):
    half = rot_dims // 2
    freq = np.float32(10000.0) ** (np.float32(-2.0) * np.arange(half, dtype=np.float32) / np.float32(rot_dims))
    angle = np.arange(slot_len, dtype=np.float32)[:, None] * freq[None, :].astype(np.float32)
    tables = np.zeros((3, slot_len, width), np.float32)
    tables[0] = 1.0
    tables[0, :, :half] = tables[0, :, half:rot_dims] = np.cos(angle)
    tables[1, :, :half] = tables[2, :, half:rot_dims] = np.sin(angle)
    return tables


class Place:
    def __init__(self, groups):
        self.groups = groups
        data = lax.axis_index("dp")
        self.core = lax.axis_index("tensor")
        self.other = 1 - self.core
        self.line = data // groups
        self.group = data % groups

    def at(self, line, group, core):
        return (line * self.groups + group, core)

    def line_to(self, step):
        return (self.line + step) % LINE

    def line_from(self, step):
        return (self.line + LINE - step) % LINE

    def group_to(self, step):
        g = self.group
        if self.groups == 4:
            if step == 1:
                return g + 1 - 2 * (g % 2)
            if step == 2:
                return (g + 2) % 4
            return 3 - g
        return (g + step) % self.groups

    def group_from(self, step):
        if self.groups == 4:
            return self.group_to(step)
        return (self.group + self.groups - step) % self.groups

    def greet(self):
        barrier = pltpu.get_barrier_semaphore()
        count = 0
        for step in range(1, LINE):
            for core in (self.core, self.other):
                pl.semaphore_signal(
                    barrier, inc=1, device_id=self.at(self.line_to(step), self.group, core), device_id_type=MESH
                )
                count += 1
        for step in range(1, self.groups):
            pl.semaphore_signal(
                barrier, inc=1, device_id=self.at(self.line, self.group_to(step), self.core), device_id_type=MESH
            )
            count += 1
        pl.semaphore_signal(
            barrier, inc=1, device_id=self.at(self.line, self.group, self.other), device_id_type=MESH
        )
        pl.semaphore_wait(barrier, count + 1)


def remote(src, dst, send, recv, device):
    return pltpu.make_async_remote_copy(
        src_ref=src, dst_ref=dst, send_sem=send, recv_sem=recv, device_id=device, device_id_type=MESH
    )


def dot(left, right):
    return jnp.dot(left, right, preferred_element_type=jnp.float32)


def turned(blocks):
    eye = lax.broadcasted_iota(jnp.int32, (256, 256), 0) == lax.broadcasted_iota(jnp.int32, (256, 256), 1)
    eye = jnp.where(eye, 1.0, 0.0).astype(jnp.bfloat16)
    parts = []
    for n in range(0, len(blocks), 2):
        pair = jnp.concatenate(blocks[n : n + 2], 1)
        part = lax.dot_general(eye, pair, (((1,), (1,)), ((), ())), preferred_element_type=jnp.float32)
        parts.append(part.astype(jnp.bfloat16))
    return jnp.concatenate(parts, 0)


def gather_kernel(groups, cols, seq_dev, slot_len, *refs):
    count = len(cols)
    f32, low = jnp.float32, jnp.bfloat16
    w_in = refs[:count]
    acts_in = refs[count : count + 2]
    vec_ref, bias_ref, valid_ref, turn_ref = refs[count + 2 : count + 6]
    outs = refs[count + 6 : count + 19]
    (n1_out, n2_out, qg_out, pg_out, near_out, far_out, s_out, s_far, gd_own, g2_own, gd_got, g2_got, early_ref) = outs
    rest = refs[count + 19 :]
    w_out = rest[:count]
    acts_out = rest[count : count + 2]
    (qkv_keep, prob_keep, attn_keep, hid_keep, pg_keep, one_buf, two_buf, back_buf, m_buf, m_got, m_half, s_got,
     s_half, qkv_now, pre_now, stat_keep, norm_acc, bias_acc) = rest[count + 2 : count + 20]
    (one_s, one_r, two_s, two_r, three_s, three_r, row_s, row_r, sib_s, sib_r, here, out_a, out_b,
     out_d, msib_s, msib_r, ssib_s, ssib_r, half_s, half_r, far_s, far_r, near_sem, s_here, s1_s, s1_r,
     s2_s, s2_r, gp_s, gp_r, g_here) = rest[count + 20 :]
    me = Place(groups)
    c, g, k = me.line, me.group, me.core
    me.greet()
    sibling = me.at(c, g, me.other)
    rows_own = w_in[0].shape[0]
    block_rows = seq_dev * slot_len
    near = groups == 4
    START, SENT = "start", "wait_send"

    def block(ref, line, width):
        return ref.at[:, pl.ds(pl.multiple_of(line * width, 128), width)]

    def place(m, line, group):
        return w_out[m].at[pl.ds(pl.multiple_of((line * groups + group) * rows_own, 32), rows_own)]

    def rows_of(which, line, core):
        return acts_out[which].at[pl.ds(pl.multiple_of((line * seq_dev + core) * slot_len, 32), slot_len)]

    partner = c + 1 - 2 * (c % 2)
    beyond = (c + 2) % LINE

    def row_send(which, q, act):
        origin = beyond if q == 2 else c
        copy = remote(
            rows_of(which, beyond, k) if q == 2 else acts_in[which].at[k],
            rows_of(which, origin, k),
            row_s.at[which, q],
            row_r.at[which, q],
            me.at(beyond if q == 1 else partner, g, k),
        )
        getattr(copy, act)()

    def row_origin(q):
        return (partner, beyond, (partner + 2) % LINE)[q]

    def to_sibling(which, q, act):
        rows = rows_of(which, row_origin(q), k)
        copy = remote(rows, rows, sib_s.at[which, q], sib_r.at[which, q], sibling)
        getattr(copy, act)()

    def pass_on(which, q):
        rows = rows_of(which, row_origin(q), k)
        remote(rows, rows, row_s.at[which, q], row_r.at[which, q], sibling).wait_recv()
        if q == 1:
            row_send(which, 2, START)
        to_sibling(which, q, START)

    def arrive_sibling(which):
        for q in range(3):
            rows = rows_of(which, row_origin(q), me.other)
            remote(rows, rows, sib_s.at[which, q], sib_r.at[which, q], sibling).wait_recv()

    def local_acts(which, act):
        for s in range(seq_dev):
            copy = pltpu.make_async_copy(acts_in[which].at[s], rows_of(which, c, s), here.at[count + which, s])
            getattr(copy, act)()

    def local_weight(m, act):
        copy = pltpu.make_async_copy(block(w_in[m], c, cols[m]), place(m, c, g), here.at[m, 0])
        getattr(copy, act)()

    def stage_one(m, act):
        for step in range(1, LINE):
            to = me.line_to(step)
            copy = remote(
                block(w_in[m], to, cols[m]),
                place(m, c, g),
                one_s.at[m, step],
                one_r.at[m, step],
                me.at(to, g, k),
            )
            getattr(copy, act)()

    def stage_two(m, step, act):
        where = place(m, me.line_from(step), g)
        src = block(w_in[m], c, cols[m]) if step == 0 else where
        for peer in range(1, 3 if near else groups):
            copy = remote(
                src, where, two_s.at[m, step, peer], two_r.at[m, step, peer], me.at(c, me.group_to(peer), k)
            )
            getattr(copy, act)()

    def first_half(m):
        for step in range(1, LINE):
            dst = place(m, me.line_from(step), g)
            remote(dst, dst, one_s.at[m, step], one_r.at[m, step], sibling).wait_recv()
            stage_two(m, step, START)

    def wait_two(m, step, peer):
        dst = place(m, me.line_from(step), me.group_from(peer))
        remote(dst, dst, two_s.at[m, step, peer], two_r.at[m, step, peer], sibling).wait_recv()

    def stage_three(m, step, act):
        source, target = (1, 2) if step % 2 == 0 else (2, 1)
        where = place(m, me.line_from(step), me.group_to(source))
        copy = remote(where, where, three_s.at[m, step], three_r.at[m, step], me.at(c, me.group_to(target), k))
        getattr(copy, act)()

    def relay(m):
        for step in range(LINE):
            for peer in range(1, 3 if near else groups):
                wait_two(m, step, peer)
            if near:
                stage_three(m, step, START)

    def last(m):
        if near:
            for step in range(LINE):
                dst = place(m, me.line_from(step), me.group_to(3))
                remote(dst, dst, three_s.at[m, step], three_r.at[m, step], sibling).wait_recv()

    row_send(0, 1, START)
    row_send(0, 0, START)
    for m in (0, 1):
        stage_one(m, START)
        stage_two(m, 0, START)
    local_acts(0, START)
    local_weight(0, START)
    local_weight(1, START)
    norm_acc[...] = jnp.zeros_like(norm_acc)
    bias_acc[...] = jnp.zeros_like(bias_acc)
    first_half(0)
    pass_on(0, 1)
    for m in (2, 3):
        stage_one(m, START)
        stage_two(m, 0, START)
    local_acts(1, START)
    local_weight(2, START)
    local_weight(3, START)
    pass_on(0, 0)
    first_half(1)
    row_send(1, 1, START)
    row_send(1, 0, START)
    relay(0)
    pass_on(0, 2)
    relay(1)
    local_acts(0, "wait")
    local_weight(0, "wait")
    local_weight(1, "wait")
    last(0)
    last(1)
    arrive_sibling(0)

    wq, w1, wd, w2 = w_out
    x_all, ct_all = acts_out
    head = cols[0] // 3
    half = head // 2
    chunk = 16
    wide = 512
    ways = D // wide
    root = math.sqrt(head)
    causal = lax.broadcasted_iota(jnp.int32, (slot_len, slot_len), 0) >= lax.broadcasted_iota(
        jnp.int32, (slot_len, slot_len), 1
    )

    def turn(v, sign):
        left = pltpu.roll(v, half - 32, 1)
        right = pltpu.roll(v, 32, 1)
        if sign > 0:
            return v * turn_ref[0] - left * turn_ref[1] + right * turn_ref[2]
        return v * turn_ref[0] + left * turn_ref[1] - right * turn_ref[2]

    def contract(left, right, dims):
        return lax.dot_general(left, right, ((dims[0], dims[1]), ((), ())), preferred_element_type=f32)

    def put_one(i, line, act):
        rows = pl.ds(pl.multiple_of(line * block_rows, 128), block_rows)
        getattr(pltpu.make_async_copy(one_buf, n1_out.at[rows], out_a), act)()
        getattr(pltpu.make_async_copy(two_buf.at[0], n2_out.at[rows], out_b.at[0]), act)()

    @pl.loop(0, LINE)
    def forward(i):
        line = (c + i) % LINE
        base = pl.multiple_of(line * block_rows, 128)

        @pl.when(i == 0)
        def _():
            first_half(2)
            first_half(3)

        @pl.when(i == 1)
        def _():
            relay(2)
            pass_on(1, 1)

        @pl.when(i == 2)
        def _():
            relay(3)
            pass_on(1, 0)

        @pl.when(i >= 1)
        def _():
            put_one(i, line, "wait")

        @pl.loop(0, block_rows // chunk)
        def norm(j):
            at = pl.ds(pl.multiple_of(base + j * chunk, chunk), chunk)
            to = pl.ds(pl.multiple_of(j * chunk, chunk), chunk)
            x = x_all[at, :].astype(f32)
            mean = jnp.mean(x, -1, keepdims=True)
            centre = x - mean
            scale = lax.rsqrt(jnp.mean(centre * centre, -1, keepdims=True) + eps_norm)
            stat_keep[at, 0:1] = mean
            stat_keep[at, 1:2] = scale
            unit = centre * scale
            one_buf[to, :] = (unit * vec_ref[0:1, :] + vec_ref[1:2, :]).astype(low)
            two_buf[0, to, :] = (unit * vec_ref[2:3, :] + vec_ref[3:4, :]).astype(low)

        put_one(i, line, "start")
        qkv_now[...] = dot(one_buf[...], wq[...]) + bias_ref[0:1, : cols[0]]
        pre_now[...] = dot(two_buf[0], w1[...]) + bias_ref[0:1, cols[0] :]

        for s in range(seq_dev):
            part = slice(s * slot_len, (s + 1) * slot_len)
            rows = pl.ds(pl.multiple_of(base + s * slot_len, 32), slot_len)
            qkv_keep[rows, 0:half] = turn(qkv_now[part, 0:half], 1).astype(low)
            qkv_keep[rows, half:head] = qkv_now[part, half:head].astype(low)
            qkv_keep[rows, head : head + half] = turn(qkv_now[part, head : head + half], 1).astype(low)
            qkv_keep[rows, head + half :] = qkv_now[part, head + half :].astype(low)
            query = qkv_keep[rows, :head]
            keys = qkv_keep[rows, head : 2 * head]
            values = qkv_keep[rows, 2 * head :]
            scores = jnp.where(causal, contract(query, keys, ((1,), (1,))) / root, neg_large)
            expo = jnp.exp(scores - jnp.max(scores, -1, keepdims=True))
            probs = expo / jnp.sum(expo, -1, keepdims=True)
            prob_keep[line * seq_dev + s] = probs
            attn_keep[rows, :] = (dot(probs.astype(low), values) * valid_ref[rows, :]).astype(low)

        @pl.loop(0, block_rows // chunk)
        def act(j):
            at = pl.ds(pl.multiple_of(base + j * chunk, chunk), chunk)
            pre = pre_now[pl.ds(pl.multiple_of(j * chunk, chunk), chunk), :]
            area = 0.5 * (1.0 + lax.erf(pre * math.sqrt(0.5)))
            hid_keep[at, :] = (pre * area * valid_ref[at, :]).astype(low)
            pg_keep[at, :] = (area + pre * (jnp.exp(-0.5 * pre * pre) * (1.0 / math.sqrt(2.0 * math.pi)))).astype(low)

    put_one(LINE - 1, (c + LINE - 1) % LINE, "wait")
    local_weight(2, "wait")
    local_weight(3, "wait")
    last(2)
    last(3)
    mine = c * 2 + k

    def pair_m(i, act):
        copy = remote(m_buf.at[i % 2, me.other], m_got.at[i], msib_s.at[i], msib_r.at[i], sibling)
        getattr(copy, act)()

    def half_m(i, act):
        for q, to in enumerate((partner, (partner + 2) % LINE)):
            copy = remote(
                m_got.at[i, to], m_half.at[i, q], half_s.at[i, q], half_r.at[i, q], me.at(partner, g, k)
            )
            getattr(copy, act)()

    def far_m(i, act):
        copy = remote(m_got.at[i, beyond], far_out.at[i], far_s.at[i], far_r.at[i], me.at(beyond, g, k))
        getattr(copy, act)()

    def near_m(i, act):
        getattr(pltpu.make_async_copy(m_got.at[i, c], near_out.at[i], near_sem.at[i]), act)()

    def sent_m(i):
        half_m(i, SENT)
        far_m(i, SENT)
        near_m(i, "wait")

    def second_m(i):
        half_m(i, "wait_recv")

        @pl.loop(0, block_rows // 64)
        def add(j):
            at = pl.ds(pl.multiple_of(j * 64, 64), 64)
            for q, to in enumerate((c, beyond)):
                total = m_got[i, to, at, :].astype(f32) + m_half[i, q, at, :].astype(f32)
                m_got[i, to, at, :] = total.astype(low)

        far_m(i, START)
        near_m(i, START)

    def pair_add(i):
        pair_m(i, "wait_recv")

        @pl.loop(0, LINE)
        def add_outer(p):
            @pl.loop(0, block_rows // 64)
            def add(j):
                at = pl.ds(pl.multiple_of(j * 64, 64), 64)
                total = m_buf[i % 2, k, p, at, :].astype(f32) + m_got[i, p, at, :].astype(f32)
                m_got[i, p, at, :] = total.astype(low)

        half_m(i, START)

    @pl.loop(0, LINE)
    def outputs(i):
        base = pl.multiple_of(i * block_rows, 128)
        whole = pl.ds(base, block_rows)
        slot = i % 2

        @pl.when(i == 1)
        def _():
            pass_on(1, 2)

        @pl.when(i >= 2)
        def _():
            pair_m(i - 2, SENT)

        live = valid_ref[whole, :]

        @pl.loop(0, ways)
        def output(j):
            at = pl.ds(pl.multiple_of(j * wide, 128), wide)
            total = contract(attn_keep[whole, :], wd[at, :], ((1,), (1,)))
            total = total + contract(hid_keep[whole, :], w2[at, :], ((1,), (1,)))
            feature = (lax.broadcasted_iota(jnp.int32, (1, wide), 1) + j * wide) // (D // (2 * LINE))
            mask = jnp.where(feature == mine, 1.0, 0.0)
            extra = x_all[whole, at].astype(f32) + (vec_ref[4:5, at] + vec_ref[5:6, at])
            total = ((total + mask * extra) * live).astype(low)
            m_buf[slot, 0, j] = total[:, : wide // 2]
            m_buf[slot, 1, j] = total[:, wide // 2 :]

        pair_m(i, START)

        @pl.when(i >= 1)
        def _():
            pair_add(i - 1)

    local_acts(1, "wait")
    arrive_sibling(1)

    per = 128 // rows_own
    part_cols = 256
    fits = block_rows // 128
    pieces = (cols[2] + cols[3]) // part_cols
    dense_pieces = cols[2] // part_cols

    def own_spot(t, nb):
        row, column = divmod(t * pieces + nb, D // part_cols)
        return slice(row * 128, (row + 1) * 128), slice(column * part_cols, (column + 1) * part_cols)

    def out_group(i):
        flip_x, flip_y = 1 - i % 2, 1 - i // 2
        return (g // 2 + flip_y) % 2 * 2 + (g % 2 + flip_x) % 2

    def out_products(i):
        slot = i % 2
        if near:
            to = out_group(i)
            tiles = [(l, to) for l in range(LINE)]
        else:
            tiles = [(i, t * per) for t in range(LINE)]
        lhs = turned([ct_all[:, pl.ds(pl.multiple_of((l * groups + p) * rows_own, 128), 128)] for l, p in tiles])
        first = 0
        for right in (attn_keep, hid_keep):
            out = dot(lhs, right[...]).astype(low)
            for n in range(right.shape[1] // part_cols):
                nb = first + n
                part = out[:, n * part_cols : (n + 1) * part_cols]

                @pl.when((i < groups - 1) | (not near))
                def _(part=part, nb=nb):
                    for t in range(LINE):
                        m_buf[slot, nb // fits, t, (nb % fits) * 128 : (nb % fits + 1) * 128, :] = part[
                            t * 128 : (t + 1) * 128
                        ]

                if near:

                    @pl.when(i == groups - 1)
                    def _(part=part, nb=nb):
                        for t in range(LINE):
                            rows, at = own_spot(t, nb)
                            one_buf[rows, at] = part[t * 128 : (t + 1) * 128]

            first += right.shape[1] // part_cols

    def out_piece(i, nb, to):
        row = (nb % fits) * 128
        if near:
            return m_buf.at[i % 2, nb // fits, :, pl.ds(row, 128), :]
        return m_buf.at[i % 2, nb // fits, to // per, pl.ds(pl.multiple_of(row + (to % per) * rows_own, 32), rows_own), :]

    def out_place(refs, i, nb, step):
        ref, n = (refs[0], nb) if nb < dense_pieces else (refs[1], nb - dense_pieces)
        at = pl.ds(n * part_cols, part_cols)
        if step is not None:
            ref = ref.at[step - 1]
        return ref.at[:, :, at] if near else ref.at[i, :, at]

    def out_send(i, step, act):
        to = out_group(i) if near else (g + step) % groups
        for nb in range(pieces):
            sem = (0 if near else i, step, nb)
            copy = remote(
                out_piece(i, nb, to), out_place((gd_got, g2_got), i, nb, step), gp_s.at[sem], gp_r.at[sem],
                me.at(c, to, k),
            )
            getattr(copy, act)()

    def out_keep(i, act):
        for nb in range(pieces):
            if near:
                for t in range(LINE):
                    rows, at = own_spot(t, nb)
                    dst = out_place((gd_own, g2_own), i, nb, None)
                    copy = pltpu.make_async_copy(
                        one_buf.at[pl.ds(rows.start, 128), pl.ds(at.start, part_cols)], dst.at[t], g_here.at[t, nb]
                    )
                    getattr(copy, act)()
            else:
                copy = pltpu.make_async_copy(
                    out_piece(i, nb, g), out_place((gd_own, g2_own), i, nb, None), g_here.at[i, nb]
                )
                getattr(copy, act)()

    def out_sends(i, act):
        local = "wait" if act == SENT else act
        if near:

            @pl.when(i < groups - 1)
            def _():
                out_send(i, groups - 1 - i, act)

            @pl.when(i == groups - 1)
            def _():
                out_keep(i, local)
        else:
            for step in range(1, groups):
                out_send(i, step, act)
            out_keep(i, local)

    def line_at(i):
        first = partner + (c - partner) * (i % 2)
        return (first + 2 * (1 - i // 2)) % LINE

    def pair_s(i, act):
        rows = pl.ds(pl.multiple_of(me.other * slot_len, 32), slot_len)
        copy = remote(two_buf.at[i % 2, rows], s_got.at[i], ssib_s.at[i], ssib_r.at[i], sibling)
        getattr(copy, act)()

    def put_s(i, act):
        getattr(pltpu.make_async_copy(s_got.at[i], s_out.at[i - 2], s_here.at[i]), act)()

    def s_one(act):
        getattr(remote(s_got.at[0], s_half, s1_s, s1_r, me.at(partner, g, k)), act)()

    def s_two(act):
        getattr(remote(s_got.at[1], s_far, s2_s, s2_r, me.at(beyond, g, k)), act)()

    def finish_s(i):
        pair_s(i, "wait_recv")
        if i == 1:
            s_one("wait_recv")

        @pl.loop(0, slot_len // chunk)
        def add(j):
            at = pl.ds(pl.multiple_of(k * slot_len + j * chunk, chunk), chunk)
            to = pl.ds(pl.multiple_of(j * chunk, chunk), chunk)
            total = two_buf[i % 2, at, :].astype(f32) + s_got[i, to, :].astype(f32)
            if i == 1:
                total = total + s_half[to, :].astype(f32)
            s_got[i, to, :] = total.astype(low)

        if i == 0:
            s_one(START)
        elif i == 1:
            s_two(START)
        else:
            put_s(i, START)

    def put_rest(line, act):
        rows = pl.ds(pl.multiple_of(line * block_rows, 128), block_rows)
        for place_at, (buf, out) in enumerate(((qkv_keep, qg_out), (pg_keep, pg_out))):
            getattr(pltpu.make_async_copy(buf.at[rows], out.at[rows], out_d.at[place_at, line]), act)()

    @pl.loop(0, LINE)
    def backward(i):
        line = line_at(i)
        base = pl.multiple_of(line * block_rows, 128)
        whole = pl.ds(base, block_rows)
        slot = i % 2

        @pl.when(i == 0)
        def _():
            pair_m(LINE - 2, SENT)

        @pl.when(i == 1)
        def _():
            pair_m(LINE - 1, SENT)

        @pl.when((i == 2) if near else (i >= 2))
        def _():
            out_sends(i - 2, SENT)

        out_products(i)
        out_sends(i, START)

        @pl.when(i == 0)
        def _():
            pair_add(LINE - 1)

        for late in (0, 2):

            @pl.when(i == late + 1)
            def _(late=late):
                finish_s(late)

        @pl.when((i == 1) | (i == 2))
        def _():
            second_m(i * 2 - 2)
            second_m(i * 2 - 1)

        live = valid_ref[whole, :]
        back_buf[...] = (ct_all[whole, :].astype(f32) * live).astype(low)
        attn_grad = dot(back_buf[...], wd[...]).astype(low)
        pre_now[...] = dot(back_buf[...], w2[...])

        @pl.when(i == LINE - 1)
        def _():
            rows = pl.ds(pl.multiple_of(k * slot_len, 32), slot_len)
            total = jnp.sum(back_buf[rows, :].astype(f32).reshape(slot_len // 8, 8, D), 0)
            norm_acc[4] = total

        @pl.loop(0, block_rows // chunk)
        def act(j):
            at = pl.ds(pl.multiple_of(base + j * chunk, chunk), chunk)
            grad = pre_now[pl.ds(pl.multiple_of(j * chunk, chunk), chunk), :] * pg_keep[at, :].astype(f32)
            grad = grad.astype(low)
            pg_keep[at, :] = grad
            grad = grad.astype(f32)
            bias_acc[:, cols[0] :] += grad[:8] + grad[8:]

        for s in range(seq_dev):
            rows = pl.ds(pl.multiple_of(base + s * slot_len, 32), slot_len)
            grad = attn_grad[s * slot_len : (s + 1) * slot_len]
            query = qkv_keep[rows, :head]
            keys = qkv_keep[rows, head : 2 * head]
            values = qkv_keep[rows, 2 * head :]
            probs = prob_keep[line * seq_dev + s]
            prob_grad = contract(grad, values, ((1,), (1,)))
            row_dot = jnp.sum(probs * prob_grad, -1, keepdims=True)
            score_grad = (probs * (prob_grad - row_dot)).astype(low)
            value_grad = contract(probs.astype(low), grad, ((0,), (0,)))
            query_grad = dot(score_grad, keys) / root
            key_grad = contract(score_grad, query, ((0,), (0,))) / root
            qkv_keep[rows, 0:half] = turn(query_grad[:, :half], -1).astype(low)
            qkv_keep[rows, half:head] = query_grad[:, half:].astype(low)
            qkv_keep[rows, head : head + half] = turn(key_grad[:, :half], -1).astype(low)
            qkv_keep[rows, head + half : 2 * head] = key_grad[:, half:].astype(low)
            qkv_keep[rows, 2 * head :] = value_grad.astype(low)
            summed = qkv_keep[rows, :].astype(f32).reshape(slot_len // 8, 8, cols[0])
            bias_acc[:, : cols[0]] += jnp.sum(summed, 0)

        put_rest(line, "start")
        mean = stat_keep[whole, 0:1]
        scale = stat_keep[whole, 1:2]

        @pl.when(i >= 2)
        def _():
            pair_s(i - 2, SENT)

        @pl.loop(0, ways)
        def inputs(j):
            at = pl.ds(pl.multiple_of(j * wide, 128), wide)
            first = contract(qkv_keep[whole, :], wq[at, :], ((1,), (1,)))
            second = contract(pg_keep[whole, :], w1[at, :], ((1,), (1,)))
            two_buf[slot, :, at] = (first * vec_ref[0:1, at] + second * vec_ref[2:3, at]).astype(low)
            unit = (x_all[whole, at].astype(f32) - mean) * scale
            for place_at, value in enumerate((first * unit, first, second * unit, second)):
                norm_acc[place_at, :, at] += jnp.sum(value.reshape(block_rows // 8, 8, wide), 0)

        pair_s(i, START)

        @pl.when(i == 2)
        def _():
            finish_s(1)

    finish_s(LINE - 1)
    for r in range(5):
        total = jnp.sum(norm_acc[r], 0, keepdims=True)
        for t in range(D // 128):
            early_ref[r * (D // 128) + t : r * (D // 128) + t + 1, :] = total[:, t * 128 : (t + 1) * 128]
    at_bias = 5 * (D // 128)
    total = jnp.sum(bias_acc[...], 0, keepdims=True)
    for t in range((cols[0] + cols[1]) // 128):
        early_ref[at_bias + t : at_bias + t + 1, :] = total[:, t * 128 : (t + 1) * 128]
    at_row = at_bias + (cols[0] + cols[1]) // 128
    early_ref[at_row : at_row + 1, :] = vec_ref[6:7, :128]
    early_ref[at_row + 1 :, :] = jnp.zeros((early_ref.shape[0] - at_row - 1, 128), f32)
    for i in range(LINE):
        put_rest(i, "wait")
        sent_m(i)
        far_m(i, "wait_recv")
    for i in (LINE - 2, LINE - 1):
        pair_s(i, SENT)
        put_s(i, "wait")
    for i in range(1 if near else 2, LINE):
        out_sends(i, SENT)
    s_one(SENT)
    s_two(SENT)
    s_two("wait_recv")
    for step in range(1, groups):
        for nb in range(pieces):
            for i in range(1 if near else LINE):
                dst = out_place((gd_got, g2_got), i, nb, step)
                sem = (i, step, nb)
                remote(dst, dst, gp_s.at[sem], gp_r.at[sem], sibling).wait_recv()
    for m in range(count):
        stage_one(m, SENT)
        for step in range(LINE):
            stage_two(m, step, SENT)
            if near:
                stage_three(m, step, SENT)
    for which in range(2):
        for q in range(3):
            row_send(which, q, SENT)
            to_sibling(which, q, SENT)


def gather_all(groups, weights, tokens, cotangent, vectors, biases, valid, turns):
    rows_own = weights[0].shape[0]
    seq_dev, slot_len, width = tokens.shape
    cols = tuple(w.shape[1] // LINE for w in weights)
    count = len(weights)
    block_rows = seq_dev * slot_len
    rows = LINE * block_rows
    f32, low = jnp.float32, jnp.bfloat16
    dma = pltpu.SemaphoreType.DMA
    peers = 3 if groups == 4 else groups
    out_widths = (D, D, cols[0], cols[1])
    pieces = (cols[2] + cols[3]) // 256
    feat = D // (2 * LINE)
    early_rows = -(-(5 * D + cols[0] + cols[1] + 128) // 1024) * 8
    return pl.pallas_call(
        partial(gather_kernel, groups, cols, seq_dev, slot_len),
        out_shape=[jax.ShapeDtypeStruct((rows, w), low) for w in out_widths]
        + [
            jax.ShapeDtypeStruct((LINE, block_rows, feat), low),
            jax.ShapeDtypeStruct((LINE, block_rows, feat), low),
            jax.ShapeDtypeStruct((2, slot_len, D), low),
            jax.ShapeDtypeStruct((slot_len, D), low),
            jax.ShapeDtypeStruct((LINE, rows_own, cols[2]), low),
            jax.ShapeDtypeStruct((LINE, rows_own, cols[3]), low),
            jax.ShapeDtypeStruct((groups - 1, LINE, rows_own, cols[2]), low),
            jax.ShapeDtypeStruct((groups - 1, LINE, rows_own, cols[3]), low),
            jax.ShapeDtypeStruct((early_rows, 128), f32),
        ],
        in_specs=[ANY] * (count + 2) + [VMEM] * 4,
        out_specs=[ANY] * 12 + [VMEM],
        scratch_shapes=[pltpu.VMEM((D, w), low) for w in cols]
        + [pltpu.VMEM((rows, D), low)] * 2
        + [
            pltpu.VMEM((rows, cols[0]), low),
            pltpu.VMEM((LINE * seq_dev, slot_len, slot_len), f32),
            pltpu.VMEM((rows, cols[2]), low),
            pltpu.VMEM((rows, cols[3]), low),
            pltpu.VMEM((rows, cols[1]), low),
            pltpu.VMEM((block_rows, D), low),
            pltpu.VMEM((2, block_rows, D), low),
            pltpu.VMEM((block_rows, D), low),
            pltpu.VMEM((2, 2, LINE, block_rows, feat), low),
            pltpu.VMEM((LINE, LINE, block_rows, feat), low),
            pltpu.VMEM((LINE, 2, block_rows, feat), low),
            pltpu.VMEM((LINE, slot_len, D), low),
            pltpu.VMEM((slot_len, D), low),
            pltpu.VMEM((block_rows, cols[0]), f32),
            pltpu.VMEM((block_rows, cols[1]), f32),
            pltpu.VMEM((rows, 2), f32),
            pltpu.VMEM((5, 8, D), f32),
            pltpu.VMEM((8, cols[0] + cols[1]), f32),
            dma((count, LINE)),
            dma((count, LINE)),
            dma((count, LINE, peers)),
            dma((count, LINE, peers)),
            dma((count, LINE)),
            dma((count, LINE)),
            dma((2, 3)),
            dma((2, 3)),
            dma((2, 3)),
            dma((2, 3)),
            dma((count + 2, seq_dev)),
            dma(()),
            dma((2,)),
            dma((2, LINE)),
            dma((LINE,)),
            dma((LINE,)),
            dma((LINE,)),
            dma((LINE,)),
            dma((LINE, 2)),
            dma((LINE, 2)),
            dma((LINE,)),
            dma((LINE,)),
            dma((LINE,)),
            dma((LINE,)),
            dma(()),
            dma(()),
            dma(()),
            dma(()),
            dma((LINE, groups, pieces)),
            dma((LINE, groups, pieces)),
            dma((LINE, pieces)),
        ],
        compiler_params=pltpu.CompilerParams(
            collective_id=0, has_side_effects=True, vmem_limit_bytes=62 * 1024 * 1024
        ),
        name="gather_all",
    )(*weights, tokens, cotangent, vectors, biases, valid, turns)


def scatter_kernel(groups, cols, seq_dev, slot_len, rows_own, *refs):
    count = len(cols)
    f32, low = jnp.float32, jnp.bfloat16
    pick = refs[0]
    lefts_in = refs[1:3]
    rights_in = refs[3:5]
    near_ref, far_ref, s_ref, s_far_ref = refs[5:9]
    done_own, done_got = refs[9:11], refs[11:13]
    early_ref = refs[13]
    mixed_ref, ssum_ref = refs[14:16]
    g_out = refs[16 : 16 + count]
    early_out, col_out, row_out = refs[16 + count : 19 + count]
    rest = refs[19 + count :]
    left_buf, right_a, right_b = rest[:3]
    g_own = rest[3 : 3 + count]
    g_got = rest[3 + count : 3 + 2 * count]
    (m_in, m_all, m_send, s_own, s_half, s_far, early_group, col_now, col_group, row_keep, row_turn) = rest[
        3 + 2 * count : 14 + 2 * count
    ]
    (here, half_s, half_r, fin_s, fin_r, mall_s, mall_r, mout_s, mout_r, gp_s, gp_r, gl_s, gl_r, eg_s,
     eg_r, el_s, el_r, es_s, es_r, cg_s, cg_r, cl_s, cl_r, cs_s, cs_r, rl_s, rl_r, keep_sem) = rest[14 + 2 * count :]
    me = Place(groups)
    c, g, k = me.line, me.group, me.core
    me.greet()
    sibling = me.at(c, g, me.other)
    feat = D // (2 * LINE)
    seqs = LINE * seq_dev
    rows = seqs * slot_len
    double = groups == 4
    sends = []

    def go(copy):
        copy.start()
        sends.append(copy)

    def to_group(step):
        return (g + step) % groups

    def from_group(step):
        return (g + groups - step) % groups

    def arrived(dst, send, recv):
        remote(dst, dst, send, recv, sibling).wait_recv()

    def add_rows(total, parts, count_rows, chunk):
        @pl.loop(0, count_rows // chunk)
        def body(i):
            at = pl.ds(pl.multiple_of(i * chunk, chunk), chunk)
            acc = parts[0](at)[...].astype(f32)
            for part in parts[1:]:
                acc = acc + part(at)[...].astype(f32)
            total(at)[...] = acc.astype(low)

    def load(src, dst, sem):
        copy = pltpu.make_async_copy(src, dst, sem)
        copy.start()
        return copy

    partner = c + 1 - 2 * (c % 2)
    go(remote(s_ref.at[0], s_half, half_s, half_r, me.at(partner, g, k)))
    got_m = [load(near_ref, m_in.at[0], here.at[10]), load(far_ref, m_in.at[1], here.at[11])]
    got_done = []
    for q in range(2):
        got_done.append(load(done_own[q], g_own[2 + q].at[:, 0], here.at[2 + 2 * q]))
        got_done.append(load(done_got[q], g_got[2 + q], here.at[3 + 2 * q]))
    got_two = load(lefts_in[1], left_buf.at[0], here.at[6])
    got_1 = load(rights_in[1], right_a, here.at[7])
    if double:
        got_one = load(lefts_in[0], left_buf.at[1], here.at[0])
        got_q = load(rights_in[0], right_b, here.at[1])
    got_s = [load(s_ref.at[1], s_own, here.at[8]), load(s_far_ref, s_far, here.at[9])]
    for step in range(1, groups):
        go(remote(early_ref, early_group.at[g], eg_s.at[step], eg_r.at[step], me.at(c, to_group(step), k)))
    early_group[g] = early_ref[...]

    per = 128 // rows_own

    def tile_products(m, left, right, tiles):
        lhs = turned([left[:, pl.ds(pl.multiple_of((l * groups + p) * rows_own, 128), 128)] for l, p in tiles])
        out = dot(lhs, right[...]).astype(low)
        for t, (l, p) in enumerate(tiles):
            for q in range(per):
                row = t * 128 + q * rows_own
                g_own[m][l, p + q] = out[row : row + rows_own]

    def send_group(m, step, act):
        to = to_group(step)
        copy = remote(
            g_own[m].at[:, to], g_got[m].at[step - 1], gp_s.at[m, step], gp_r.at[m, step], me.at(c, to, k)
        )
        getattr(copy, act)()

    across, beside, above = me.group_to(3), me.group_to(1), me.group_to(2)
    two_phase = groups == 4

    def phase_one(m, way, act):
        lines = pl.ds(0, 2) if way == 0 else pl.ds(2, 2)
        to = beside if way == 0 else above
        for q, block in enumerate((to, across)):
            copy = remote(
                g_own[m].at[lines, block], g_got[m].at[q, lines], gp_s.at[m, way * 2 + q], gp_r.at[m, way * 2 + q],
                me.at(c, to, k),
            )
            getattr(copy, act)()

    def phase_two(m, way, act):
        lines = pl.ds(0, 2) if way == 0 else pl.ds(2, 2)
        to = above if way == 0 else beside
        copy = remote(
            g_own[m].at[lines, to], g_got[m].at[2, lines], gp_s.at[m, 4 + way], gp_r.at[m, 4 + way], me.at(c, to, k)
        )
        getattr(copy, act)()

    def between_phases(m):
        for way in range(2):
            phase_one(m, way, "wait_recv")
            to = above if way == 0 else beside
            for line in (way * 2, way * 2 + 1):
                add_rows(
                    lambda at: g_own[m].at[line, to, at],
                    [lambda at: g_own[m].at[line, to, at], lambda at: g_got[m].at[1, line, at]],
                    rows_own,
                    16,
                )
            phase_two(m, way, "start")

    def products(left, pairs):
        if two_phase:

            @pl.loop(0, groups)
            def body(t):
                flip_x, flip_y = (t + 1) % 2, (3 - t) // 2 * (1 - t // 3)
                to = (g // 2 + flip_y) % 2 * 2 + (g % 2 + flip_x) % 2
                for m, right in pairs:
                    tile_products(m, left, right, [(l, to) for l in range(LINE)])
                    for way in range(2):

                        @pl.when(t == 2 - way)
                        def _():
                            phase_one(m, way, "start")
        else:

            @pl.loop(0, LINE)
            def body(l):
                for m, right in pairs:
                    tile_products(m, left, right, [(l, t * per) for t in range(4)])

            for m, _ in pairs:
                for step in range(1, groups):
                    send_group(m, step, "start")

    def sum_groups(m, first):
        got = range(groups - 1)
        if m < 2 and two_phase:
            for way in range(2):
                phase_two(m, way, "wait_recv")
            got = (0, 2)
        elif m < 2:
            for step in range(1, groups):
                arrived(g_got[m].at[step - 1], gp_s.at[m, step], gp_r.at[m, step])
        mine = g if m < 2 else 0
        width = pl.ds(pl.multiple_of(c * cols[m], 128), cols[m])
        total = jnp.zeros((8, cols[m]), f32)
        for step in (2, 1, 3, 0):
            line = me.line_to(step)

            def body(i, carry, line=line):
                at = pl.ds(pl.multiple_of(i * 16, 16), 16)
                acc = g_own[m][line, mine, at, :].astype(f32)
                for p in got:
                    acc = acc + g_got[m][p, line, at, :].astype(f32)
                g_own[m][line, mine, at, :] = acc.astype(low)
                square = acc * acc + eps_second
                row_keep[line, at, m : m + 1] = jnp.sum(square, 1, keepdims=True)
                return carry + square[:8] + square[8:]

            total = lax.fori_loop(0, rows_own // 16, body, total)
            src = g_own[m].at[line, mine]
            if step:
                go(remote(src, g_out[m].at[:, width], gl_s.at[m, step], gl_r.at[m, step], me.at(line, g, k)))
            else:
                keep.append(load(src, g_out[m].at[:, width], keep_sem.at[2 + m]))
        total = jnp.sum(total, 0, keepdims=True)
        for t in range(cols[m] // 128):
            col_now[first + t : first + t + 1, :] = total[:, t * 128 : (t + 1) * 128]

    keep = []
    row_keep[...] = jnp.zeros_like(row_keep)
    firsts = []
    edge = 0
    for m in range(count):
        firsts.append(edge)
        edge += cols[m] // 128
    for copy in got_m:
        copy.wait()
    ours = pl.ds(g * seqs, seqs)
    for s in range(seqs):
        add_rows(
            lambda at: m_all.at[g * seqs + s, at],
            [lambda at: m_in.at[0, s, at], lambda at: m_in.at[1, s, at]],
            slot_len,
            64,
        )
    for step in range(1, groups):
        go(remote(m_all.at[ours], m_all.at[ours], mall_s.at[step], mall_r.at[step], me.at(c, to_group(step), k)))

    for copy in got_done:
        copy.wait()
    sum_groups(3, firsts[3])
    sum_groups(2, firsts[2])
    got_two.wait()
    got_1.wait()
    products(left_buf.at[0], ((1, right_a),))
    if not double:
        got_one = load(lefts_in[0], left_buf.at[0], here.at[0])
        got_q = load(rights_in[0], right_b, here.at[1])

    for copy in got_s:
        copy.wait()
    arrived(s_half, half_s, half_r)
    add_rows(
        lambda at: s_own.at[at],
        [lambda at: s_own.at[at], lambda at: s_half.at[at], lambda at: s_far.at[at]],
        slot_len,
        16,
    )
    go(remote(s_own, ssum_ref.at[k], fin_s, fin_r, sibling))
    keep.append(load(s_own, ssum_ref.at[k], keep_sem.at[0]))
    got_one.wait()
    got_q.wait()
    products(left_buf.at[1 if double else 0], ((0, right_b),))
    if two_phase:
        between_phases(1)
    for step in range(1, groups):
        arrived(early_group.at[from_group(step)], eg_s.at[step], eg_r.at[step])
    acc = early_group[0]
    for i in range(1, groups):
        acc = acc + early_group[i]
    early_out[k, c] = acc
    for step in range(1, LINE):
        go(remote(early_out.at[k, c], early_out.at[k, c], el_s.at[step], el_r.at[step], me.at(me.line_to(step), g, k)))

    for step in range(1, groups):
        arrived(m_all.at[pl.ds(from_group(step) * seqs, seqs)], mall_s.at[step], mall_r.at[step])
    mixed_cols = pl.ds(pl.multiple_of((c * 2 + k) * feat, 128), feat)
    for step in (1, 2, 3, 0):
        line = me.line_to(step)
        for s in range(seq_dev):
            m_send[line, s] = m_all[pick[line * seq_dev + s]]
        where = mixed_ref.at[:, :, mixed_cols]
        if step:
            go(remote(m_send.at[line], where, mout_s.at[0, step], mout_r.at[0, step], me.at(line, g, k)))
        else:
            keep.append(load(m_send.at[line], where, keep_sem.at[1]))
            go(remote(m_send.at[line], where, mout_s.at[1, 0], mout_r.at[1, 0], sibling))
    if two_phase:
        between_phases(0)
    sum_groups(1, firsts[1])
    sum_groups(0, firsts[0])

    for step in range(1, groups):
        go(remote(col_now, col_group.at[g], cg_s.at[step], cg_r.at[step], me.at(c, to_group(step), k)))
    col_group[g] = col_now[...]
    for step in (1, 2, 3, 0):
        line = me.line_to(step)
        row_turn[line] = jnp.transpose(row_keep[line])[:8]
        if step:
            go(remote(row_turn.at[line], row_out.at[k, c], rl_s.at[0, step], rl_r.at[0, step], me.at(line, g, k)))
        else:
            row_out[k, c] = row_turn[line]
        go(remote(row_turn.at[line], row_out.at[k, c], rl_s.at[1, step], rl_r.at[1, step], me.at(line, g, me.other)))
    for step in range(1, groups):
        arrived(col_group.at[from_group(step)], cg_s.at[step], cg_r.at[step])
    acc = col_group[0]
    for i in range(1, groups):
        acc = acc + col_group[i]
    col_out[k, c] = acc
    for step in range(1, LINE):
        go(remote(col_out.at[k, c], col_out.at[k, c], cl_s.at[step], cl_r.at[step], me.at(me.line_to(step), g, k)))
    for step in range(1, LINE):
        arrived(early_out.at[k, me.line_from(step)], el_s.at[step], el_r.at[step])
    go(remote(early_out.at[k], early_out.at[k], es_s, es_r, sibling))
    for step in range(1, LINE):
        arrived(col_out.at[k, me.line_from(step)], cl_s.at[step], cl_r.at[step])
    go(remote(col_out.at[k], col_out.at[k], cs_s, cs_r, sibling))

    for step in range(1, LINE):
        where = mixed_ref.at[:, :, pl.ds(pl.multiple_of((me.line_from(step) * 2 + k) * feat, 128), feat)]
        arrived(where, mout_s.at[0, step], mout_r.at[0, step])
        go(remote(where, where, mout_s.at[1, step], mout_r.at[1, step], sibling))
    for m in range(count):
        for step in range(1, LINE):
            dst = g_out[m].at[:, pl.ds(pl.multiple_of(me.line_from(step) * cols[m], 128), cols[m])]
            arrived(dst, gl_s.at[m, step], gl_r.at[m, step])
    for step in range(LINE):
        source = me.line_from(step)
        dst = mixed_ref.at[:, :, pl.ds(pl.multiple_of((source * 2 + me.other) * feat, 128), feat)]
        arrived(dst, mout_s.at[1, step], mout_r.at[1, step])
        for core, way in ((k, 0), (me.other, 1)):
            if step or way:
                arrived(row_out.at[core, source], rl_s.at[way, step], rl_r.at[way, step])
    arrived(ssum_ref.at[me.other], fin_s, fin_r)
    arrived(early_out.at[me.other], es_s, es_r)
    arrived(col_out.at[me.other], cs_s, cs_r)
    for copy in sends:
        copy.wait_send()
    for m in range(2):
        if two_phase:
            for way in range(2):
                phase_one(m, way, "wait_send")
                phase_two(m, way, "wait_send")
        else:
            for step in range(1, groups):
                send_group(m, step, "wait_send")
    for copy in keep:
        copy.wait()


def scatter_all(groups, cols, seq_dev, rows_own, pick, lefts, rights, between):
    near, far, s_pair, s_far, *done, early = between
    slot_len = s_pair.shape[1]
    rows = lefts[0].shape[0]
    count = len(cols)
    feat = D // (2 * LINE)
    seqs = LINE * seq_dev
    blocks = (seqs, slot_len, feat)
    dma = pltpu.SemaphoreType.DMA
    f32, low = jnp.float32, jnp.bfloat16
    col_rows = sum(cols) // 128
    return pl.pallas_call(
        partial(scatter_kernel, groups, cols, seq_dev, slot_len, rows_own),
        out_shape=[
            jax.ShapeDtypeStruct((seq_dev, slot_len, D), low),
            jax.ShapeDtypeStruct((seq_dev, slot_len, D), low),
        ]
        + [jax.ShapeDtypeStruct((rows_own, LINE * width), low) for width in cols]
        + [
            jax.ShapeDtypeStruct((2, LINE) + early.shape, f32),
            jax.ShapeDtypeStruct((2, LINE, col_rows, 128), f32),
            jax.ShapeDtypeStruct((2, LINE, 8, 128), f32),
        ],
        in_specs=[SMEM] + [ANY] * 12 + [VMEM],
        out_specs=[ANY] * (2 + count) + [VMEM] * 3,
        scratch_shapes=[
            pltpu.VMEM((2 if groups == 4 else 1, rows, D), low),
            pltpu.VMEM((rows, cols[1]), low),
            pltpu.VMEM((rows, cols[0]), low),
        ]
        + [pltpu.VMEM((LINE, groups if m < 2 else 1, rows_own, width), low) for m, width in enumerate(cols)]
        + [pltpu.VMEM((groups - 1, LINE, rows_own, width), low) for width in cols]
        + [
            pltpu.VMEM((2, seqs, slot_len, feat), low),
            pltpu.VMEM((groups * seqs, slot_len, feat), low),
            pltpu.VMEM((LINE, seq_dev, slot_len, feat), low),
            pltpu.VMEM((slot_len, D), low),
            pltpu.VMEM((slot_len, D), low),
            pltpu.VMEM((slot_len, D), low),
            pltpu.VMEM((groups,) + early.shape, f32),
            pltpu.VMEM((col_rows, 128), f32),
            pltpu.VMEM((groups, col_rows, 128), f32),
            pltpu.VMEM((LINE, 128, 128), f32),
            pltpu.VMEM((LINE, 8, 128), f32),
            dma((12,)),
            dma(()),
            dma(()),
            dma(()),
            dma(()),
            dma((groups,)),
            dma((groups,)),
            dma((2, LINE)),
            dma((2, LINE)),
            dma((count, max(groups, 6))),
            dma((count, max(groups, 6))),
            dma((count, LINE)),
            dma((count, LINE)),
            dma((groups,)),
            dma((groups,)),
            dma((LINE,)),
            dma((LINE,)),
            dma(()),
            dma(()),
            dma((groups,)),
            dma((groups,)),
            dma((LINE,)),
            dma((LINE,)),
            dma(()),
            dma(()),
            dma((2, LINE)),
            dma((2, LINE)),
            dma((2 + count,)),
        ],
        compiler_params=pltpu.CompilerParams(
            collective_id=1, has_side_effects=True, vmem_limit_bytes=62 * 1024 * 1024
        ),
        name="scatter_all",
    )(pick, *lefts, *rights, near.reshape(blocks), far.reshape(blocks), s_pair, s_far, *done, early)


def prepare_kernel(groups, cols, seq_dev, slot_len, *refs):
    (spot, lengths, permutation, wq, w1, wd, w2, vectors, biases, rows_state) = refs[:10]
    lows = refs[10:14]
    valid, own_valid, all_vectors, all_biases, pick = refs[14:]
    f32 = jnp.float32
    for src, dst in zip((wq, w1, wd, w2), lows):
        dst[...] = src[...].astype(jnp.bfloat16)

    @pl.when(pl.program_id(0) == 0)
    def _():
        data, core = spot[0], spot[1]
        line, group = data // groups, data % groups
        times = lax.broadcasted_iota(jnp.int32, (slot_len, 1), 0)
        for place in range(LINE):
            for s in range(seq_dev):
                slot = (place * groups + group) * seq_dev + s
                at = place * seq_dev + s
                valid[at * slot_len : (at + 1) * slot_len, :] = jnp.where(times < lengths[slot], 1.0, 0.0)
                source = permutation[slot]
                chip = source // seq_dev
                pick[at] = (chip % groups) * (LINE * seq_dev) + (chip // groups) * seq_dev + source % seq_dev
        for s in range(seq_dev):
            own_valid[s * slot_len : (s + 1) * slot_len, :] = jnp.where(
                times < lengths[data * seq_dev + s], 1.0, 0.0
            )
        all_vectors[0:6, :] = vectors[...]
        all_vectors[6:8, :] = jnp.zeros((2, D), f32)
        lane = lax.broadcasted_iota(jnp.int32, (1, 128), 1)
        total = jnp.zeros((1, 128), f32)
        for m in range(4):
            total = total + jnp.where(lane == m, jnp.sum(rows_state[m : m + 1, :], 1, keepdims=True), 0.0)
        all_vectors[6:7, 0:128] = jnp.where(core == 0, total, jnp.zeros_like(total))
        all_biases[:, : cols[0]] = biases[:, pl.ds(pl.multiple_of(line * cols[0], 128), cols[0])]
        all_biases[:, cols[0] :] = biases[:, pl.ds(pl.multiple_of(LINE * cols[0] + line * cols[1], 128), cols[1])]


def prepare(groups, seq_dev, slot_len, spot, lengths, permutation, weights, vectors, biases, rows_state):
    f32, low = jnp.float32, jnp.bfloat16
    rows_own = weights[0].shape[0]
    cols = tuple(w.shape[1] // LINE for w in weights)
    tall = 32
    steps = rows_own // tall
    seqs = LINE * seq_dev

    def whole(shape):
        return pl.BlockSpec(shape, lambda i: (0,) * len(shape))

    blocks = [pl.BlockSpec((tall, w.shape[1]), lambda i: (i, 0)) for w in weights]
    return pl.pallas_call(
        partial(prepare_kernel, groups, cols, seq_dev, slot_len),
        grid=(steps,),
        out_shape=[jax.ShapeDtypeStruct(w.shape, low) for w in weights]
        + [
            jax.ShapeDtypeStruct((seqs * slot_len, 1), f32),
            jax.ShapeDtypeStruct((seq_dev * slot_len, 1), f32),
            jax.ShapeDtypeStruct((8, D), f32),
            jax.ShapeDtypeStruct((1, cols[0] + cols[1]), f32),
            jax.ShapeDtypeStruct((seqs,), jnp.int32),
        ],
        in_specs=[SMEM] * 3 + blocks + [whole(vectors.shape), whole(biases.shape), whole(rows_state.shape)],
        out_specs=blocks
        + [
            whole((seqs * slot_len, 1)),
            whole((seq_dev * slot_len, 1)),
            whole((8, D)),
            whole((1, cols[0] + cols[1])),
            SMEM,
        ],
        compiler_params=pltpu.CompilerParams(vmem_limit_bytes=60 * 1024 * 1024),
        name="prepare",
    )(spot, lengths, permutation, *weights, vectors, biases, rows_state)


def finish_kernel(order, cols, rows_own, *refs):
    f32, low = jnp.float32, jnp.bfloat16
    spot = refs[0]
    g_in, w_in = refs[1:5], refs[5:9]
    (s_sum, tokens, cotangent, own_valid, early, col_all, row_all, row_state, col_state, vectors, moments, biases,
     bias_moments) = refs[9:22]
    grads, news, copies = refs[22:26], refs[26:30], refs[30:34]
    (grad_tokens, row_new, col_new, norm_total, norm_moment_new, norm_new, bias_total, bias_moment_new,
     bias_new) = refs[34:43]
    row_factor, col_factor, turn = refs[43:]
    step = pl.program_id(0)
    widths = [w.shape[1] for w in w_in]
    edges = [sum(widths[:i]) for i in range(5)]
    tiles = D // 128

    @pl.when(step == 0)
    def _():
        core = spot[1]
        both = early[0, 0]
        rows_all = row_all[0, 0]
        mass_all = col_all[0, 0]
        for n in range(1, 2 * LINE):
            both = both + early[n // LINE, n % LINE]
            rows_all = rows_all + row_all[n // LINE, n % LINE]
            mass_all = mass_all + col_all[n // LINE, n % LINE]
        for r in range(6):
            for t in range(tiles):
                at = min(r, 4) * tiles + t
                norm_total[r : r + 1, t * 128 : (t + 1) * 128] = both[at : at + 1]
        grad = norm_total[...]
        moment = decay * moments[...] + (1.0 - decay) * (grad * grad + eps_second)
        norm_moment_new[...] = moment
        norm_new[...] = vectors[...] - rate_norm * grad * lax.rsqrt(moment)
        first = 5 * tiles
        parts = ((cols[0] // 128, 0), (cols[1] // 128, LINE * cols[0]))
        for line in range(LINE):
            at = first
            for count, base in parts:
                for t in range(count):
                    to = base + (line * count + t) * 128
                    bias_total[:, to : to + 128] = early[core, line, at : at + 1, :]
                    at += 1
        grad = bias_total[...]
        moment = decay * bias_moments[...] + (1.0 - decay) * (grad * grad + eps_second)
        bias_moment_new[...] = moment
        bias_new[...] = biases[...] - rate_vector * grad * lax.rsqrt(moment)
        at_row = first + (cols[0] + cols[1]) // 128
        full_cols = (3.0 * D, 1.0 * D, 1.0 * FF, 1.0 * FF)
        rates = (
            rate_scale / math.sqrt(D),
            rate_scale / math.sqrt(D // 8),
            rate_scale / math.sqrt(D),
            rate_scale / math.sqrt(FF),
        )
        turn[...] = jnp.zeros_like(turn)
        at = 0
        for m, i in enumerate(order):
            count = cols[m] // 128
            new = decay * row_state[i : i + 1, :] + (1.0 - decay) * (rows_all[m : m + 1, :rows_own] / full_cols[i])
            row_new[i : i + 1, :] = new
            mass = jnp.sum(jnp.sum(mass_all[at : at + count], 1, keepdims=True), 0, keepdims=True)
            mean = (decay * both[at_row : at_row + 1, i : i + 1] + (1.0 - decay) * (mass / full_cols[i])) / D
            turn[i : i + 1, :rows_own] = rates[i] * lax.rsqrt(new / mean)
            for line in range(LINE):
                for t in range(count):
                    to = edges[i] + (line * count + t) * 128
                    col_new[:, to : to + 128] = col_all[core, line, at + t : at + t + 1, :]
            at += count
        row_factor[...] = jnp.transpose(turn[...])
        new = decay * col_state[...] + (1.0 - decay) * (col_new[...] / D)
        col_new[...] = new
        col_factor[...] = lax.rsqrt(new)

    tall = w_in[0].shape[0]
    for half in range(tall // 16):
        rows = pl.ds(pl.multiple_of(step * tall + half * 16, 16), 16)
        part = slice(half * 16, half * 16 + 16)
        for i in range(4):
            factor = row_factor[rows, i : i + 1]
            for n in range(widths[i] // 1024):
                at = slice(n * 1024, (n + 1) * 1024)
                grad = g_in[i][part, at].astype(f32)
                new = w_in[i][part, at] - grad * factor * col_factor[:, edges[i] + n * 1024 : edges[i] + (n + 1) * 1024]
                grads[i][part, at] = grad
                news[i][part, at] = new
                copies[i][part, at] = new.astype(low)

    @pl.loop(0, tokens.shape[0] // 16)
    def body(j):
        at = pl.ds(pl.multiple_of(j * 16, 16), 16)
        x = tokens[at, :].astype(f32)
        centre = x - jnp.mean(x, -1, keepdims=True)
        scale = lax.rsqrt(jnp.mean(centre * centre, -1, keepdims=True) + eps_norm)
        unit = centre * scale
        flow = s_sum[at, :].astype(f32)
        through = flow - jnp.mean(flow, -1, keepdims=True) - unit * jnp.mean(flow * unit, -1, keepdims=True)
        grad_tokens[at, :] = (cotangent[at, :].astype(f32) * own_valid[at, :] + scale * through).astype(low)


def finish(order, spot, grads, weights, s_sum, tokens, cotangent, own_valid, *small):
    f32, low = jnp.float32, jnp.bfloat16
    rows_own = weights[0].shape[0]
    tall = 32
    steps = rows_own // tall
    cols = tuple(weights[i].shape[1] // LINE for i in order)
    rows = tokens.shape[0]
    row_state, col_state, vectors, _, biases = small[3:8]

    def whole(shape):
        return pl.BlockSpec(shape, lambda i: (0,) * len(shape))

    blocks = [pl.BlockSpec((tall, w.shape[1]), lambda i: (i, 0)) for w in weights]
    acts = pl.BlockSpec((rows // steps, D), lambda i: (i, 0))
    small_out = [row_state.shape, col_state.shape] + [vectors.shape] * 3 + [biases.shape] * 3
    return pl.pallas_call(
        partial(finish_kernel, order, cols, rows_own),
        grid=(steps,),
        out_shape=[jax.ShapeDtypeStruct(w.shape, f32) for w in weights] * 2
        + [jax.ShapeDtypeStruct(w.shape, low) for w in weights]
        + [jax.ShapeDtypeStruct((rows, D), low)]
        + [jax.ShapeDtypeStruct(shape, f32) for shape in small_out],
        in_specs=[SMEM]
        + blocks * 2
        + [acts] * 3
        + [pl.BlockSpec((rows // steps, 1), lambda i: (i, 0))]
        + [whole(a.shape) for a in small],
        out_specs=blocks * 3 + [acts] + [whole(shape) for shape in small_out],
        scratch_shapes=[
            pltpu.VMEM((128, 128), f32),
            pltpu.VMEM(col_state.shape, f32),
            pltpu.VMEM((128, 128), f32),
        ],
        compiler_params=pltpu.CompilerParams(vmem_limit_bytes=60 * 1024 * 1024),
        name="finish",
    )(spot, *grads, *weights, s_sum, tokens, cotangent, own_valid, *small)


def per_device(
    tokens,
    cotangent,
    lengths,
    permutation,
    w_qkv,
    w_dense,
    w_fc1,
    w_fc2,
    norm_vectors,
    split_biases,
    row_state,
    col_state,
    norm_moment,
    bias_moment,
):
    groups = lax.axis_size("dp") // LINE
    seq_dev, slot_len, width = tokens.shape
    rows_own = w_qkv.shape[0]
    head_dim = D // HEADS
    weights = (w_qkv, w_dense, w_fc1, w_fc2)
    order = (0, 2, 1, 3)
    cols = tuple(weights[i].shape[1] // LINE for i in order)
    spot = jnp.stack([lax.axis_index("dp"), lax.axis_index("tensor")]).astype(jnp.int32)
    *lows, valid, own_valid, vectors, biases, pick = prepare(
        groups, seq_dev, slot_len, spot, lengths, permutation, [weights[i] for i in order], norm_vectors,
        split_biases, row_state,
    )
    turns = jnp.asarray(turn_tables(slot_len, head_dim // 4, head_dim // 2))
    norm_one, norm_two, qkv_grad, pre_grad, *between = gather_all(
        groups, lows, tokens, cotangent, vectors, biases, valid, turns
    )
    mixed, s_sum, *outs = scatter_all(
        groups, cols, seq_dev, rows_own, pick, (norm_one, norm_two), (qkv_grad, pre_grad), between
    )
    grads = [outs[order.index(i)] for i in range(4)]
    early_all, col_all, row_all = outs[4:]
    results = finish(
        order, spot, grads, weights, s_sum.reshape(-1, width), tokens.reshape(-1, width),
        cotangent.reshape(-1, width), own_valid, early_all, col_all, row_all, row_state, col_state, norm_vectors,
        norm_moment, split_biases, bias_moment,
    )
    return (mixed, results[12].reshape(tokens.shape), *results[:12], *results[13:])


def solution(mesh):
    halves = P("dp", "tensor")
    split = P("tensor", None)
    in_specs = (
        P("dp", None, None),
        P("dp", None, None),
        P(),
        P(),
        halves,
        halves,
        halves,
        halves,
        P(),
        split,
        P(None, "dp"),
        split,
        P(),
        split,
    )
    out_specs = (
        (P("dp", None, None),) * 2
        + (halves,) * 12
        + (P(None, "dp"), split)
        + (P(),) * 3
        + (split,) * 3
    )
    return jax.shard_map(
        per_device, mesh=mesh, in_specs=in_specs, out_specs=out_specs, check_vma=False
    )
```

```python
from functools import partial
import math

import jax
import jax.numpy as jnp
import numpy as np
from jax import lax
from jax.experimental import pallas as pl
from jax.experimental.pallas import tpu as pltpu
from jax.sharding import PartitionSpec as P

D = 2048
FF = 8192
HEADS = 8
LINE = 4

eps_norm = 1e-05
eps_second = 1e-30
decay = 0.5
rate_scale = 1.0
rate_norm = 0.5
rate_vector = 0.05
neg_large = -1e30

MESH = pl.DeviceIdType.MESH
ANY = pl.BlockSpec(memory_space=pl.ANY)
VMEM = pl.BlockSpec(memory_space=pltpu.VMEM)
SMEM = pl.BlockSpec(memory_space=pltpu.SMEM)


def turn_tables(slot_len, rot_dims, width):
    half = rot_dims // 2
    freq = np.float32(10000.0) ** (np.float32(-2.0) * np.arange(half, dtype=np.float32) / np.float32(rot_dims))
    angle = np.arange(slot_len, dtype=np.float32)[:, None] * freq[None, :].astype(np.float32)
    tables = np.zeros((3, slot_len, width), np.float32)
    tables[0] = 1.0
    tables[0, :, :half] = tables[0, :, half:rot_dims] = np.cos(angle)
    tables[1, :, :half] = tables[2, :, half:rot_dims] = np.sin(angle)
    return tables


class Place:
    def __init__(self, groups):
        self.groups = groups
        data = lax.axis_index("dp")
        self.core = lax.axis_index("tensor")
        self.other = 1 - self.core
        self.line = data // groups
        self.group = data % groups

    def at(self, line, group, core):
        return (line * self.groups + group, core)

    def line_to(self, step):
        return (self.line + step) % LINE

    def line_from(self, step):
        return (self.line + LINE - step) % LINE

    def group_to(self, step):
        g = self.group
        if self.groups == 4:
            if step == 1:
                return g + 1 - 2 * (g % 2)
            if step == 2:
                return (g + 2) % 4
            return 3 - g
        return (g + step) % self.groups

    def group_from(self, step):
        if self.groups == 4:
            return self.group_to(step)
        return (self.group + self.groups - step) % self.groups

    def greet(self):
        barrier = pltpu.get_barrier_semaphore()
        count = 0
        for step in range(1, LINE):
            for core in (self.core, self.other):
                pl.semaphore_signal(
                    barrier, inc=1, device_id=self.at(self.line_to(step), self.group, core), device_id_type=MESH
                )
                count += 1
        for step in range(1, self.groups):
            pl.semaphore_signal(
                barrier, inc=1, device_id=self.at(self.line, self.group_to(step), self.core), device_id_type=MESH
            )
            count += 1
        pl.semaphore_signal(
            barrier, inc=1, device_id=self.at(self.line, self.group, self.other), device_id_type=MESH
        )
        pl.semaphore_wait(barrier, count + 1)


def remote(src, dst, send, recv, device):
    return pltpu.make_async_remote_copy(
        src_ref=src, dst_ref=dst, send_sem=send, recv_sem=recv, device_id=device, device_id_type=MESH
    )


def dot(left, right):
    return jnp.dot(left, right, preferred_element_type=jnp.float32)


def turned(blocks):
    eye = lax.broadcasted_iota(jnp.int32, (256, 256), 0) == lax.broadcasted_iota(jnp.int32, (256, 256), 1)
    eye = jnp.where(eye, 1.0, 0.0).astype(jnp.bfloat16)
    parts = []
    for n in range(0, len(blocks), 2):
        pair = jnp.concatenate(blocks[n : n + 2], 1)
        part = lax.dot_general(eye, pair, (((1,), (1,)), ((), ())), preferred_element_type=jnp.float32)
        parts.append(part.astype(jnp.bfloat16))
    return jnp.concatenate(parts, 0)


def gather_kernel(groups, cols, seq_dev, slot_len, *refs):
    count = len(cols)
    f32, low = jnp.float32, jnp.bfloat16
    w_in = refs[:count]
    acts_in = refs[count : count + 2]
    vec_ref, bias_ref, valid_ref, turn_ref = refs[count + 2 : count + 6]
    outs = refs[count + 6 : count + 18]
    (n1_out, n2_out, qg_out, pg_out, near_out, far_out, s_out, gd_own, g2_own, gd_got, g2_got, early_ref) = outs
    rest = refs[count + 18 :]
    w_out = rest[:count]
    acts_out = rest[count : count + 2]
    (qkv_keep, prob_keep, attn_keep, hid_keep, pg_keep, one_buf, two_buf, back_buf, m_buf, m_got, m_half, s_got,
     qkv_now, pre_now, stat_keep, norm_acc, bias_acc) = rest[count + 2 : count + 19]
    (one_s, one_r, two_s, two_r, three_s, three_r, row_s, row_r, sib_s, sib_r, here, out_a, out_b,
     out_d, msib_s, msib_r, ssib_s, ssib_r, half_s, half_r, far_s, far_r, near_sem, s_here, gp_s, gp_r,
     g_here) = rest[count + 19 :]
    me = Place(groups)
    c, g, k = me.line, me.group, me.core
    me.greet()
    sibling = me.at(c, g, me.other)
    rows_own = w_in[0].shape[0]
    block_rows = seq_dev * slot_len
    near = groups == 4
    START, SENT = "start", "wait_send"

    def block(ref, line, width):
        return ref.at[:, pl.ds(pl.multiple_of(line * width, 128), width)]

    def place(m, line, group):
        return w_out[m].at[pl.ds(pl.multiple_of((line * groups + group) * rows_own, 32), rows_own)]

    def rows_of(which, line, core):
        return acts_out[which].at[pl.ds(pl.multiple_of((line * seq_dev + core) * slot_len, 32), slot_len)]

    partner = c + 1 - 2 * (c % 2)
    beyond = (c + 2) % LINE

    def row_send(which, q, act):
        origin = beyond if q == 2 else c
        copy = remote(
            rows_of(which, beyond, k) if q == 2 else acts_in[which].at[k],
            rows_of(which, origin, k),
            row_s.at[which, q],
            row_r.at[which, q],
            me.at(beyond if q == 1 else partner, g, k),
        )
        getattr(copy, act)()

    def row_origin(q):
        return (partner, beyond, (partner + 2) % LINE)[q]

    def to_sibling(which, q, act):
        rows = rows_of(which, row_origin(q), k)
        copy = remote(rows, rows, sib_s.at[which, q], sib_r.at[which, q], sibling)
        getattr(copy, act)()

    def pass_on(which, q):
        rows = rows_of(which, row_origin(q), k)
        remote(rows, rows, row_s.at[which, q], row_r.at[which, q], sibling).wait_recv()
        if q == 1:
            row_send(which, 2, START)
        to_sibling(which, q, START)

    def arrive_sibling(which):
        for q in range(3):
            rows = rows_of(which, row_origin(q), me.other)
            remote(rows, rows, sib_s.at[which, q], sib_r.at[which, q], sibling).wait_recv()

    def local_acts(which, act):
        for s in range(seq_dev):
            copy = pltpu.make_async_copy(acts_in[which].at[s], rows_of(which, c, s), here.at[count + which, s])
            getattr(copy, act)()

    def local_weight(m, act):
        copy = pltpu.make_async_copy(block(w_in[m], c, cols[m]), place(m, c, g), here.at[m, 0])
        getattr(copy, act)()

    def stage_one(m, act):
        for step in range(1, LINE):
            to = me.line_to(step)
            copy = remote(
                block(w_in[m], to, cols[m]),
                place(m, c, g),
                one_s.at[m, step],
                one_r.at[m, step],
                me.at(to, g, k),
            )
            getattr(copy, act)()

    def stage_two(m, step, act):
        where = place(m, me.line_from(step), g)
        src = block(w_in[m], c, cols[m]) if step == 0 else where
        for peer in range(1, 3 if near else groups):
            copy = remote(
                src, where, two_s.at[m, step, peer], two_r.at[m, step, peer], me.at(c, me.group_to(peer), k)
            )
            getattr(copy, act)()

    def first_half(m):
        for step in range(1, LINE):
            dst = place(m, me.line_from(step), g)
            remote(dst, dst, one_s.at[m, step], one_r.at[m, step], sibling).wait_recv()
            stage_two(m, step, START)

    def wait_two(m, step, peer):
        dst = place(m, me.line_from(step), me.group_from(peer))
        remote(dst, dst, two_s.at[m, step, peer], two_r.at[m, step, peer], sibling).wait_recv()

    def stage_three(m, step, act):
        source, target = (1, 2) if step % 2 == 0 else (2, 1)
        where = place(m, me.line_from(step), me.group_to(source))
        copy = remote(where, where, three_s.at[m, step], three_r.at[m, step], me.at(c, me.group_to(target), k))
        getattr(copy, act)()

    def relay(m):
        for step in range(LINE):
            for peer in range(1, 3 if near else groups):
                wait_two(m, step, peer)
            if near:
                stage_three(m, step, START)

    def last(m):
        if near:
            for step in range(LINE):
                dst = place(m, me.line_from(step), me.group_to(3))
                remote(dst, dst, three_s.at[m, step], three_r.at[m, step], sibling).wait_recv()

    row_send(0, 1, START)
    row_send(0, 0, START)
    for m in (0, 1):
        stage_one(m, START)
        stage_two(m, 0, START)
    local_acts(0, START)
    local_weight(0, START)
    local_weight(1, START)
    norm_acc[...] = jnp.zeros_like(norm_acc)
    bias_acc[...] = jnp.zeros_like(bias_acc)
    first_half(0)
    pass_on(0, 1)
    for m in (2, 3):
        stage_one(m, START)
        stage_two(m, 0, START)
    local_acts(1, START)
    local_weight(2, START)
    local_weight(3, START)
    pass_on(0, 0)
    first_half(1)
    row_send(1, 1, START)
    row_send(1, 0, START)
    relay(0)
    pass_on(0, 2)
    relay(1)
    local_acts(0, "wait")
    local_weight(0, "wait")
    local_weight(1, "wait")
    last(0)
    last(1)
    arrive_sibling(0)

    wq, w1, wd, w2 = w_out
    x_all, ct_all = acts_out
    head = cols[0] // 3
    half = head // 2
    chunk = 16
    wide = 512
    ways = D // wide
    root = math.sqrt(head)
    causal = lax.broadcasted_iota(jnp.int32, (slot_len, slot_len), 0) >= lax.broadcasted_iota(
        jnp.int32, (slot_len, slot_len), 1
    )

    def turn(v, sign):
        left = pltpu.roll(v, half - 32, 1)
        right = pltpu.roll(v, 32, 1)
        if sign > 0:
            return v * turn_ref[0] - left * turn_ref[1] + right * turn_ref[2]
        return v * turn_ref[0] + left * turn_ref[1] - right * turn_ref[2]

    def contract(left, right, dims):
        return lax.dot_general(left, right, ((dims[0], dims[1]), ((), ())), preferred_element_type=f32)

    def put_one(i, line, act):
        rows = pl.ds(pl.multiple_of(line * block_rows, 128), block_rows)
        getattr(pltpu.make_async_copy(one_buf, n1_out.at[rows], out_a), act)()
        getattr(pltpu.make_async_copy(two_buf.at[0], n2_out.at[rows], out_b.at[0]), act)()

    @pl.loop(0, LINE)
    def forward(i):
        line = (c + i) % LINE
        base = pl.multiple_of(line * block_rows, 128)

        @pl.when(i == 0)
        def _():
            first_half(2)
            first_half(3)

        @pl.when(i == 1)
        def _():
            relay(2)
            pass_on(1, 1)

        @pl.when(i == 2)
        def _():
            relay(3)
            pass_on(1, 0)

        @pl.when(i >= 1)
        def _():
            put_one(i, line, "wait")

        @pl.loop(0, block_rows // chunk)
        def norm(j):
            at = pl.ds(pl.multiple_of(base + j * chunk, chunk), chunk)
            to = pl.ds(pl.multiple_of(j * chunk, chunk), chunk)
            x = x_all[at, :].astype(f32)
            mean = jnp.mean(x, -1, keepdims=True)
            centre = x - mean
            scale = lax.rsqrt(jnp.mean(centre * centre, -1, keepdims=True) + eps_norm)
            stat_keep[at, 0:1] = mean
            stat_keep[at, 1:2] = scale
            unit = centre * scale
            one_buf[to, :] = (unit * vec_ref[0:1, :] + vec_ref[1:2, :]).astype(low)
            two_buf[0, to, :] = (unit * vec_ref[2:3, :] + vec_ref[3:4, :]).astype(low)

        put_one(i, line, "start")
        qkv_now[...] = dot(one_buf[...], wq[...]) + bias_ref[0:1, : cols[0]]
        pre_now[...] = dot(two_buf[0], w1[...]) + bias_ref[0:1, cols[0] :]

        for s in range(seq_dev):
            part = slice(s * slot_len, (s + 1) * slot_len)
            rows = pl.ds(pl.multiple_of(base + s * slot_len, 32), slot_len)
            qkv_keep[rows, 0:half] = turn(qkv_now[part, 0:half], 1).astype(low)
            qkv_keep[rows, half:head] = qkv_now[part, half:head].astype(low)
            qkv_keep[rows, head : head + half] = turn(qkv_now[part, head : head + half], 1).astype(low)
            qkv_keep[rows, head + half :] = qkv_now[part, head + half :].astype(low)
            query = qkv_keep[rows, :head]
            keys = qkv_keep[rows, head : 2 * head]
            values = qkv_keep[rows, 2 * head :]
            scores = jnp.where(causal, contract(query, keys, ((1,), (1,))) / root, neg_large)
            expo = jnp.exp(scores - jnp.max(scores, -1, keepdims=True))
            probs = expo / jnp.sum(expo, -1, keepdims=True)
            prob_keep[line * seq_dev + s] = probs
            attn_keep[rows, :] = (dot(probs.astype(low), values) * valid_ref[rows, :]).astype(low)

        @pl.loop(0, block_rows // chunk)
        def act(j):
            at = pl.ds(pl.multiple_of(base + j * chunk, chunk), chunk)
            pre = pre_now[pl.ds(pl.multiple_of(j * chunk, chunk), chunk), :]
            area = 0.5 * (1.0 + lax.erf(pre * math.sqrt(0.5)))
            hid_keep[at, :] = (pre * area * valid_ref[at, :]).astype(low)
            pg_keep[at, :] = (area + pre * (jnp.exp(-0.5 * pre * pre) * (1.0 / math.sqrt(2.0 * math.pi)))).astype(low)

    put_one(LINE - 1, (c + LINE - 1) % LINE, "wait")
    local_weight(2, "wait")
    local_weight(3, "wait")
    last(2)
    last(3)
    mine = c * 2 + k

    def pair_m(i, act):
        copy = remote(m_buf.at[i % 2, me.other], m_got.at[i], msib_s.at[i], msib_r.at[i], sibling)
        getattr(copy, act)()

    def half_m(i, act):
        for q, to in enumerate((partner, (partner + 2) % LINE)):
            copy = remote(
                m_got.at[i, to], m_half.at[i, q], half_s.at[i, q], half_r.at[i, q], me.at(partner, g, k)
            )
            getattr(copy, act)()

    def far_m(i, act):
        copy = remote(m_got.at[i, beyond], far_out.at[i], far_s.at[i], far_r.at[i], me.at(beyond, g, k))
        getattr(copy, act)()

    def near_m(i, act):
        getattr(pltpu.make_async_copy(m_got.at[i, c], near_out.at[i], near_sem.at[i]), act)()

    def sent_m(i):
        half_m(i, SENT)
        far_m(i, SENT)
        near_m(i, "wait")

    def second_m(i):
        half_m(i, "wait_recv")

        @pl.loop(0, block_rows // 64)
        def add(j):
            at = pl.ds(pl.multiple_of(j * 64, 64), 64)
            for q, to in enumerate((c, beyond)):
                total = m_got[i, to, at, :].astype(f32) + m_half[i, q, at, :].astype(f32)
                m_got[i, to, at, :] = total.astype(low)

        far_m(i, START)
        near_m(i, START)

    def pair_add(i):
        pair_m(i, "wait_recv")

        @pl.loop(0, LINE)
        def add_outer(p):
            @pl.loop(0, block_rows // 64)
            def add(j):
                at = pl.ds(pl.multiple_of(j * 64, 64), 64)
                total = m_buf[i % 2, k, p, at, :].astype(f32) + m_got[i, p, at, :].astype(f32)
                m_got[i, p, at, :] = total.astype(low)

        half_m(i, START)

    @pl.loop(0, LINE)
    def outputs(i):
        base = pl.multiple_of(i * block_rows, 128)
        whole = pl.ds(base, block_rows)
        slot = i % 2

        @pl.when(i == 1)
        def _():
            pass_on(1, 2)

        @pl.when(i >= 2)
        def _():
            pair_m(i - 2, SENT)

        live = valid_ref[whole, :]

        @pl.loop(0, ways)
        def output(j):
            at = pl.ds(pl.multiple_of(j * wide, 128), wide)
            total = contract(attn_keep[whole, :], wd[at, :], ((1,), (1,)))
            total = total + contract(hid_keep[whole, :], w2[at, :], ((1,), (1,)))
            feature = (lax.broadcasted_iota(jnp.int32, (1, wide), 1) + j * wide) // (D // (2 * LINE))
            mask = jnp.where(feature == mine, 1.0, 0.0)
            extra = x_all[whole, at].astype(f32) + (vec_ref[4:5, at] + vec_ref[5:6, at])
            total = ((total + mask * extra) * live).astype(low)
            m_buf[slot, 0, j] = total[:, : wide // 2]
            m_buf[slot, 1, j] = total[:, wide // 2 :]

        pair_m(i, START)

        @pl.when(i >= 1)
        def _():
            pair_add(i - 1)

    pair_add(LINE - 1)
    pair_m(LINE - 2, SENT)
    pair_m(LINE - 1, SENT)
    local_acts(1, "wait")
    arrive_sibling(1)

    per = 128 // rows_own
    part_cols = 256
    fits = block_rows // 128
    pieces = (cols[2] + cols[3]) // part_cols
    dense_pieces = cols[2] // part_cols

    def out_group(i):
        flip_x, flip_y = 1 - i % 2, 1 - i // 2
        return (g // 2 + flip_y) % 2 * 2 + (g % 2 + flip_x) % 2

    def flat_piece(i, t, nb):
        row, column = divmod(t * pieces + nb, D // part_cols)
        at = (pl.ds(row * 128, 128), pl.ds(column * part_cols, part_cols))
        return one_buf.at[at] if i == 2 else two_buf.at[(1,) + at]

    def out_products(i):
        if near:
            to = out_group(i)
            tiles = [(l, to) for l in range(LINE)]
        else:
            tiles = [(i, t * per) for t in range(LINE)]
        lhs = turned([ct_all[:, pl.ds(pl.multiple_of((l * groups + p) * rows_own, 128), 128)] for l, p in tiles])
        first = 0
        for right in (attn_keep, hid_keep):
            out = dot(lhs, right[...]).astype(low)
            for n in range(right.shape[1] // part_cols):
                nb = first + n
                for t in range(LINE):
                    part = out[t * 128 : (t + 1) * 128, n * part_cols : (n + 1) * part_cols]
                    if near and i >= 2:
                        flat_piece(i, t, nb)[...] = part
                    else:
                        m_buf[i % 2, nb // fits, t, (nb % fits) * 128 : (nb % fits + 1) * 128, :] = part
            first += right.shape[1] // part_cols

    def out_place(refs, nb, step):
        ref, n = (refs[0], nb) if nb < dense_pieces else (refs[1], nb - dense_pieces)
        at = pl.ds(n * part_cols, part_cols)
        if step is not None:
            ref = ref.at[step - 1]
        return ref.at[:, :, at]

    def out_copies(i, step):
        to = g if step is None else (out_group(i) if near else (g + step) % groups)
        for nb in range(pieces):
            dst = out_place((gd_own, g2_own) if step is None else (gd_got, g2_got), nb, step)
            row = (nb % fits) * 128
            if near and i < 2:
                yield m_buf.at[i % 2, nb // fits, :, pl.ds(row, 128), :], dst, (0, nb)
            elif near:
                for t in range(LINE):
                    yield flat_piece(i, t, nb), dst.at[t], (t, nb)
            else:
                rows = pl.ds(pl.multiple_of(row + (to % per) * rows_own, 32), rows_own)
                yield m_buf.at[i % 2, nb // fits, to // per, rows, :], dst.at[i], (i, nb)

    def out_sends(i, act):
        for step in (groups - 1 - i,) if near else range(groups):
            if step == 0:
                for src, dst, (t, nb) in out_copies(i, None):
                    copy = pltpu.make_async_copy(src, dst, g_here.at[t, nb])
                    getattr(copy, "wait" if act == SENT else act)()
            else:
                to = out_group(i) if near else (g + step) % groups
                for src, dst, (t, nb) in out_copies(i, step):
                    copy = remote(src, dst, gp_s.at[t, step, nb], gp_r.at[t, step, nb], me.at(c, to, k))
                    getattr(copy, act)()

    for i in range(LINE):
        if i >= 2 and not near:
            out_sends(i - 2, SENT)
        out_products(i)
        out_sends(i, START)

    def pair_s(i, act):
        line = (c + i) % LINE
        rows = pl.ds(pl.multiple_of(me.other * slot_len, 32), slot_len)
        copy = remote(two_buf.at[i % 2, rows], s_got.at[line], ssib_s.at[i], ssib_r.at[i], sibling)
        getattr(copy, act)()

    def put_s(i, act):
        line = (c + i) % LINE
        rows = pl.ds(pl.multiple_of(k * slot_len, 32), slot_len)
        getattr(pltpu.make_async_copy(two_buf.at[i % 2, rows], s_out.at[line], s_here.at[i]), act)()

    def finish_s(i):
        line = (c + i) % LINE
        pair_s(i, "wait_recv")

        @pl.loop(0, slot_len // chunk)
        def add(j):
            at = pl.ds(pl.multiple_of(k * slot_len + j * chunk, chunk), chunk)
            to = pl.ds(pl.multiple_of(j * chunk, chunk), chunk)
            total = two_buf[i % 2, at, :].astype(f32) + s_got[line, to, :].astype(f32)
            two_buf[i % 2, at, :] = total.astype(low)

        put_s(i, START)

    def put_rest(line, act):
        rows = pl.ds(pl.multiple_of(line * block_rows, 128), block_rows)
        for place_at, (buf, out) in enumerate(((qkv_keep, qg_out), (pg_keep, pg_out))):
            getattr(pltpu.make_async_copy(buf.at[rows], out.at[rows], out_d.at[place_at, line]), act)()

    @pl.loop(0, LINE)
    def backward(i):
        line = (c + i) % LINE
        base = pl.multiple_of(line * block_rows, 128)
        whole = pl.ds(base, block_rows)
        slot = i % 2

        if near:

            @pl.when(i == 1)
            def _():
                out_sends(LINE - 1, SENT)

        @pl.when((i == 1) | (i == 2))
        def _():
            second_m(i * 2 - 2)
            second_m(i * 2 - 1)

        live = valid_ref[whole, :]
        back_buf[...] = (ct_all[whole, :].astype(f32) * live).astype(low)
        attn_grad = dot(back_buf[...], wd[...]).astype(low)
        pre_now[...] = dot(back_buf[...], w2[...])

        @pl.when(i == 0)
        def _():
            rows = pl.ds(pl.multiple_of(k * slot_len, 32), slot_len)
            total = jnp.sum(back_buf[rows, :].astype(f32).reshape(slot_len // 8, 8, D), 0)
            norm_acc[4] = total

        @pl.loop(0, block_rows // chunk)
        def act(j):
            at = pl.ds(pl.multiple_of(base + j * chunk, chunk), chunk)
            grad = pre_now[pl.ds(pl.multiple_of(j * chunk, chunk), chunk), :] * pg_keep[at, :].astype(f32)
            grad = grad.astype(low)
            pg_keep[at, :] = grad
            grad = grad.astype(f32)
            bias_acc[:, cols[0] :] += grad[:8] + grad[8:]

        for s in range(seq_dev):
            rows = pl.ds(pl.multiple_of(base + s * slot_len, 32), slot_len)
            grad = attn_grad[s * slot_len : (s + 1) * slot_len]
            query = qkv_keep[rows, :head]
            keys = qkv_keep[rows, head : 2 * head]
            values = qkv_keep[rows, 2 * head :]
            probs = prob_keep[line * seq_dev + s]
            prob_grad = contract(grad, values, ((1,), (1,)))
            row_dot = jnp.sum(probs * prob_grad, -1, keepdims=True)
            score_grad = (probs * (prob_grad - row_dot)).astype(low)
            value_grad = contract(probs.astype(low), grad, ((0,), (0,)))
            query_grad = dot(score_grad, keys) / root
            key_grad = contract(score_grad, query, ((0,), (0,))) / root
            qkv_keep[rows, 0:half] = turn(query_grad[:, :half], -1).astype(low)
            qkv_keep[rows, half:head] = query_grad[:, half:].astype(low)
            qkv_keep[rows, head : head + half] = turn(key_grad[:, :half], -1).astype(low)
            qkv_keep[rows, head + half : 2 * head] = key_grad[:, half:].astype(low)
            qkv_keep[rows, 2 * head :] = value_grad.astype(low)
            summed = qkv_keep[rows, :].astype(f32).reshape(slot_len // 8, 8, cols[0])
            bias_acc[:, : cols[0]] += jnp.sum(summed, 0)

        put_rest(line, "start")
        mean = stat_keep[whole, 0:1]
        scale = stat_keep[whole, 1:2]

        @pl.when(i >= 2)
        def _():
            pair_s(i - 2, SENT)
            put_s(i - 2, "wait")

        @pl.loop(0, ways)
        def inputs(j):
            at = pl.ds(pl.multiple_of(j * wide, 128), wide)
            first = contract(qkv_keep[whole, :], wq[at, :], ((1,), (1,)))
            second = contract(pg_keep[whole, :], w1[at, :], ((1,), (1,)))
            two_buf[slot, :, at] = (first * vec_ref[0:1, at] + second * vec_ref[2:3, at]).astype(low)
            unit = (x_all[whole, at].astype(f32) - mean) * scale
            for place_at, value in enumerate((first * unit, first, second * unit, second)):
                norm_acc[place_at, :, at] += jnp.sum(value.reshape(block_rows // 8, 8, wide), 0)

        pair_s(i, START)

        @pl.when(i >= 1)
        def _():
            finish_s(i - 1)

    finish_s(LINE - 1)
    for r in range(5):
        total = jnp.sum(norm_acc[r], 0, keepdims=True)
        for t in range(D // 128):
            early_ref[r * (D // 128) + t : r * (D // 128) + t + 1, :] = total[:, t * 128 : (t + 1) * 128]
    at_bias = 5 * (D // 128)
    total = jnp.sum(bias_acc[...], 0, keepdims=True)
    for t in range((cols[0] + cols[1]) // 128):
        early_ref[at_bias + t : at_bias + t + 1, :] = total[:, t * 128 : (t + 1) * 128]
    at_row = at_bias + (cols[0] + cols[1]) // 128
    early_ref[at_row : at_row + 1, :] = vec_ref[6:7, :128]
    early_ref[at_row + 1 :, :] = jnp.zeros((early_ref.shape[0] - at_row - 1, 128), f32)
    for i in range(LINE):
        put_rest(i, "wait")
        sent_m(i)
        far_m(i, "wait_recv")
    for i in (LINE - 2, LINE - 1):
        pair_s(i, SENT)
        put_s(i, "wait")
    for i in range(LINE - 1) if near else (LINE - 2, LINE - 1):
        out_sends(i, SENT)
    for i in range(LINE):
        for step in (groups - 1 - i,) if near else range(1, groups):
            if step:
                for _, dst, (t, nb) in out_copies(i, step):
                    remote(dst, dst, gp_s.at[t, step, nb], gp_r.at[t, step, nb], sibling).wait_recv()
    for m in range(count):
        stage_one(m, SENT)
        for step in range(LINE):
            stage_two(m, step, SENT)
            if near:
                stage_three(m, step, SENT)
    for which in range(2):
        for q in range(3):
            row_send(which, q, SENT)
            to_sibling(which, q, SENT)


def gather_all(groups, weights, tokens, cotangent, vectors, biases, valid, turns):
    rows_own = weights[0].shape[0]
    seq_dev, slot_len, width = tokens.shape
    cols = tuple(w.shape[1] // LINE for w in weights)
    count = len(weights)
    block_rows = seq_dev * slot_len
    rows = LINE * block_rows
    f32, low = jnp.float32, jnp.bfloat16
    dma = pltpu.SemaphoreType.DMA
    peers = 3 if groups == 4 else groups
    out_widths = (D, D, cols[0], cols[1])
    pieces = (cols[2] + cols[3]) // 256
    feat = D // (2 * LINE)
    early_rows = -(-(5 * D + cols[0] + cols[1] + 128) // 1024) * 8
    return pl.pallas_call(
        partial(gather_kernel, groups, cols, seq_dev, slot_len),
        out_shape=[jax.ShapeDtypeStruct((rows, w), low) for w in out_widths]
        + [
            jax.ShapeDtypeStruct((LINE, block_rows, feat), low),
            jax.ShapeDtypeStruct((LINE, block_rows, feat), low),
            jax.ShapeDtypeStruct((LINE, slot_len, D), low),
            jax.ShapeDtypeStruct((LINE, rows_own, cols[2]), low),
            jax.ShapeDtypeStruct((LINE, rows_own, cols[3]), low),
            jax.ShapeDtypeStruct((groups - 1, LINE, rows_own, cols[2]), low),
            jax.ShapeDtypeStruct((groups - 1, LINE, rows_own, cols[3]), low),
            jax.ShapeDtypeStruct((early_rows, 128), f32),
        ],
        in_specs=[ANY] * (count + 2) + [VMEM] * 4,
        out_specs=[ANY] * 11 + [VMEM],
        scratch_shapes=[pltpu.VMEM((D, w), low) for w in cols]
        + [pltpu.VMEM((rows, D), low)] * 2
        + [
            pltpu.VMEM((rows, cols[0]), low),
            pltpu.VMEM((LINE * seq_dev, slot_len, slot_len), f32),
            pltpu.VMEM((rows, cols[2]), low),
            pltpu.VMEM((rows, cols[3]), low),
            pltpu.VMEM((rows, cols[1]), low),
            pltpu.VMEM((block_rows, D), low),
            pltpu.VMEM((2, block_rows, D), low),
            pltpu.VMEM((block_rows, D), low),
            pltpu.VMEM((2, 2, LINE, block_rows, feat), low),
            pltpu.VMEM((LINE, LINE, block_rows, feat), low),
            pltpu.VMEM((LINE, 2, block_rows, feat), low),
            pltpu.VMEM((LINE, slot_len, D), low),
            pltpu.VMEM((block_rows, cols[0]), f32),
            pltpu.VMEM((block_rows, cols[1]), f32),
            pltpu.VMEM((rows, 2), f32),
            pltpu.VMEM((5, 8, D), f32),
            pltpu.VMEM((8, cols[0] + cols[1]), f32),
            dma((count, LINE)),
            dma((count, LINE)),
            dma((count, LINE, peers)),
            dma((count, LINE, peers)),
            dma((count, LINE)),
            dma((count, LINE)),
            dma((2, 3)),
            dma((2, 3)),
            dma((2, 3)),
            dma((2, 3)),
            dma((count + 2, seq_dev)),
            dma(()),
            dma((2,)),
            dma((2, LINE)),
            dma((LINE,)),
            dma((LINE,)),
            dma((LINE,)),
            dma((LINE,)),
            dma((LINE, 2)),
            dma((LINE, 2)),
            dma((LINE,)),
            dma((LINE,)),
            dma((LINE,)),
            dma((LINE,)),
            dma((LINE, groups, pieces)),
            dma((LINE, groups, pieces)),
            dma((LINE, pieces)),
        ],
        compiler_params=pltpu.CompilerParams(
            collective_id=0, has_side_effects=True, vmem_limit_bytes=62 * 1024 * 1024
        ),
        name="gather_all",
    )(*weights, tokens, cotangent, vectors, biases, valid, turns)


def scatter_kernel(groups, cols, seq_dev, slot_len, rows_own, *refs):
    count = len(cols)
    f32, low = jnp.float32, jnp.bfloat16
    pick = refs[0]
    lefts_in = refs[1:3]
    rights_in = refs[3:5]
    near_ref, far_ref, s_ref = refs[5:8]
    done_own, done_got = refs[8:10], refs[10:12]
    early_ref = refs[12]
    mixed_ref, ssum_ref = refs[13:15]
    g_out = refs[15 : 15 + count]
    early_out, col_out, row_out = refs[15 + count : 18 + count]
    rest = refs[18 + count :]
    left_buf, right_a, right_b = rest[:3]
    g_own = rest[3 : 3 + count]
    g_got = rest[3 + count : 3 + 2 * count]
    (m_in, m_all, m_send, s_own, s_half, s_far, early_group, col_now, col_group, row_keep, row_turn) = rest[
        3 + 2 * count : 14 + 2 * count
    ]
    (here, half_s, half_r, far_s, far_r, fin_s, fin_r, mall_s, mall_r, mout_s, mout_r, gp_s, gp_r, gl_s, gl_r, eg_s,
     eg_r, el_s, el_r, es_s, es_r, cg_s, cg_r, cl_s, cl_r, cs_s, cs_r, rl_s, rl_r, keep_sem) = rest[14 + 2 * count :]
    me = Place(groups)
    c, g, k = me.line, me.group, me.core
    me.greet()
    sibling = me.at(c, g, me.other)
    feat = D // (2 * LINE)
    seqs = LINE * seq_dev
    rows = seqs * slot_len
    double = groups == 4
    sends = []

    def go(copy):
        copy.start()
        sends.append(copy)

    def to_group(step):
        return (g + step) % groups

    def from_group(step):
        return (g + groups - step) % groups

    def arrived(dst, send, recv):
        remote(dst, dst, send, recv, sibling).wait_recv()

    def add_rows(total, parts, count_rows, chunk):
        @pl.loop(0, count_rows // chunk)
        def body(i):
            at = pl.ds(pl.multiple_of(i * chunk, chunk), chunk)
            acc = parts[0](at)[...].astype(f32)
            for part in parts[1:]:
                acc = acc + part(at)[...].astype(f32)
            total(at)[...] = acc.astype(low)

    def load(src, dst, sem):
        copy = pltpu.make_async_copy(src, dst, sem)
        copy.start()
        return copy

    partner = c + 1 - 2 * (c % 2)
    beyond = (c + 2) % LINE
    for q, to in enumerate((partner, (partner + 2) % LINE)):
        go(remote(s_ref.at[to], s_half.at[q], half_s.at[q], half_r.at[q], me.at(partner, g, k)))
    got_m = [load(near_ref, m_in.at[0], here.at[10]), load(far_ref, m_in.at[1], here.at[11])]
    got_done = []
    for q in range(2):
        got_done.append(load(done_own[q], g_own[2 + q].at[:, 0], here.at[2 + 2 * q]))
        got_done.append(load(done_got[q], g_got[2 + q], here.at[3 + 2 * q]))
    got_two = load(lefts_in[1], left_buf.at[0], here.at[6])
    got_1 = load(rights_in[1], right_a, here.at[7])
    if double:
        got_one = load(lefts_in[0], left_buf.at[1], here.at[0])
        got_q = load(rights_in[0], right_b, here.at[1])
    got_s = [load(s_ref.at[c], s_own.at[0], here.at[8]), load(s_ref.at[beyond], s_own.at[1], here.at[9])]
    for step in range(1, groups):
        go(remote(early_ref, early_group.at[g], eg_s.at[step], eg_r.at[step], me.at(c, to_group(step), k)))
    early_group[g] = early_ref[...]

    per = 128 // rows_own

    def tile_products(m, left, right, tiles):
        lhs = turned([left[:, pl.ds(pl.multiple_of((l * groups + p) * rows_own, 128), 128)] for l, p in tiles])
        out = dot(lhs, right[...]).astype(low)
        for t, (l, p) in enumerate(tiles):
            for q in range(per):
                row = t * 128 + q * rows_own
                g_own[m][l, p + q] = out[row : row + rows_own]

    def send_group(m, step, act):
        to = to_group(step)
        copy = remote(
            g_own[m].at[:, to], g_got[m].at[step - 1], gp_s.at[m, step], gp_r.at[m, step], me.at(c, to, k)
        )
        getattr(copy, act)()

    across, beside, above = me.group_to(3), me.group_to(1), me.group_to(2)
    two_phase = groups == 4

    def phase_one(m, way, act):
        lines = pl.ds(0, 2) if way == 0 else pl.ds(2, 2)
        to = beside if way == 0 else above
        for q, block in enumerate((to, across)):
            copy = remote(
                g_own[m].at[lines, block], g_got[m].at[q, lines], gp_s.at[m, way * 2 + q], gp_r.at[m, way * 2 + q],
                me.at(c, to, k),
            )
            getattr(copy, act)()

    def phase_two(m, way, act):
        lines = pl.ds(0, 2) if way == 0 else pl.ds(2, 2)
        to = above if way == 0 else beside
        copy = remote(
            g_own[m].at[lines, to], g_got[m].at[2, lines], gp_s.at[m, 4 + way], gp_r.at[m, 4 + way], me.at(c, to, k)
        )
        getattr(copy, act)()

    def between_phases(m):
        for way in range(2):
            phase_one(m, way, "wait_recv")
            to = above if way == 0 else beside
            for line in (way * 2, way * 2 + 1):
                add_rows(
                    lambda at: g_own[m].at[line, to, at],
                    [lambda at: g_own[m].at[line, to, at], lambda at: g_got[m].at[1, line, at]],
                    rows_own,
                    16,
                )
            phase_two(m, way, "start")

    def products(left, pairs):
        if two_phase:

            @pl.loop(0, groups)
            def body(t):
                flip_x, flip_y = (t + 1) % 2, (3 - t) // 2 * (1 - t // 3)
                to = (g // 2 + flip_y) % 2 * 2 + (g % 2 + flip_x) % 2
                for m, right in pairs:
                    tile_products(m, left, right, [(l, to) for l in range(LINE)])
                    for way in range(2):

                        @pl.when(t == 2 - way)
                        def _():
                            phase_one(m, way, "start")
        else:

            @pl.loop(0, LINE)
            def body(l):
                for m, right in pairs:
                    tile_products(m, left, right, [(l, t * per) for t in range(4)])

            for m, _ in pairs:
                for step in range(1, groups):
                    send_group(m, step, "start")

    def sum_groups(m, first):
        got = range(groups - 1)
        if m < 2 and two_phase:
            for way in range(2):
                phase_two(m, way, "wait_recv")
            got = (0, 2)
        elif m < 2:
            for step in range(1, groups):
                arrived(g_got[m].at[step - 1], gp_s.at[m, step], gp_r.at[m, step])
        mine = g if m < 2 else 0
        width = pl.ds(pl.multiple_of(c * cols[m], 128), cols[m])
        total = jnp.zeros((8, cols[m]), f32)
        for step in (2, 1, 3, 0):
            line = me.line_to(step)

            def body(i, carry, line=line):
                at = pl.ds(pl.multiple_of(i * 16, 16), 16)
                acc = g_own[m][line, mine, at, :].astype(f32)
                for p in got:
                    acc = acc + g_got[m][p, line, at, :].astype(f32)
                g_own[m][line, mine, at, :] = acc.astype(low)
                square = acc * acc + eps_second
                row_keep[line, at, m : m + 1] = jnp.sum(square, 1, keepdims=True)
                return carry + square[:8] + square[8:]

            total = lax.fori_loop(0, rows_own // 16, body, total)
            src = g_own[m].at[line, mine]
            if step:
                go(remote(src, g_out[m].at[:, width], gl_s.at[m, step], gl_r.at[m, step], me.at(line, g, k)))
            else:
                keep.append(load(src, g_out[m].at[:, width], keep_sem.at[2 + m]))
        total = jnp.sum(total, 0, keepdims=True)
        for t in range(cols[m] // 128):
            col_now[first + t : first + t + 1, :] = total[:, t * 128 : (t + 1) * 128]

    keep = []
    row_keep[...] = jnp.zeros_like(row_keep)
    firsts = []
    edge = 0
    for m in range(count):
        firsts.append(edge)
        edge += cols[m] // 128
    for copy in got_m:
        copy.wait()
    ours = pl.ds(g * seqs, seqs)
    for s in range(seqs):
        add_rows(
            lambda at: m_all.at[g * seqs + s, at],
            [lambda at: m_in.at[0, s, at], lambda at: m_in.at[1, s, at]],
            slot_len,
            64,
        )
    for step in range(1, groups):
        go(remote(m_all.at[ours], m_all.at[ours], mall_s.at[step], mall_r.at[step], me.at(c, to_group(step), k)))

    for copy in got_done:
        copy.wait()
    sum_groups(3, firsts[3])
    sum_groups(2, firsts[2])
    got_two.wait()
    got_1.wait()
    products(left_buf.at[0], ((1, right_a),))
    if not double:
        got_one = load(lefts_in[0], left_buf.at[0], here.at[0])
        got_q = load(rights_in[0], right_b, here.at[1])

    for q in range(2):
        got_s[q].wait()
        arrived(s_half.at[q], half_s.at[q], half_r.at[q])
        add_rows(
            lambda at: s_own.at[q, at], [lambda at: s_own.at[q, at], lambda at: s_half.at[q, at]], slot_len, 16
        )
    go(remote(s_own.at[1], s_far, far_s, far_r, me.at(beyond, g, k)))

    got_one.wait()
    got_q.wait()
    products(left_buf.at[1 if double else 0], ((0, right_b),))
    if two_phase:
        between_phases(1)
    for step in range(1, groups):
        arrived(early_group.at[from_group(step)], eg_s.at[step], eg_r.at[step])
    acc = early_group[0]
    for i in range(1, groups):
        acc = acc + early_group[i]
    early_out[k, c] = acc
    for step in range(1, LINE):
        go(remote(early_out.at[k, c], early_out.at[k, c], el_s.at[step], el_r.at[step], me.at(me.line_to(step), g, k)))

    for step in range(1, groups):
        arrived(m_all.at[pl.ds(from_group(step) * seqs, seqs)], mall_s.at[step], mall_r.at[step])
    mixed_cols = pl.ds(pl.multiple_of((c * 2 + k) * feat, 128), feat)
    for step in (1, 2, 3, 0):
        line = me.line_to(step)
        for s in range(seq_dev):
            m_send[line, s] = m_all[pick[line * seq_dev + s]]
        where = mixed_ref.at[:, :, mixed_cols]
        if step:
            go(remote(m_send.at[line], where, mout_s.at[0, step], mout_r.at[0, step], me.at(line, g, k)))
        else:
            keep.append(load(m_send.at[line], where, keep_sem.at[1]))
            go(remote(m_send.at[line], where, mout_s.at[1, 0], mout_r.at[1, 0], sibling))
    if two_phase:
        between_phases(0)
    sum_groups(1, firsts[1])
    sum_groups(0, firsts[0])

    for step in range(1, groups):
        go(remote(col_now, col_group.at[g], cg_s.at[step], cg_r.at[step], me.at(c, to_group(step), k)))
    col_group[g] = col_now[...]
    for step in (1, 2, 3, 0):
        line = me.line_to(step)
        row_turn[line] = jnp.transpose(row_keep[line])[:8]
        if step:
            go(remote(row_turn.at[line], row_out.at[k, c], rl_s.at[0, step], rl_r.at[0, step], me.at(line, g, k)))
        else:
            row_out[k, c] = row_turn[line]
        go(remote(row_turn.at[line], row_out.at[k, c], rl_s.at[1, step], rl_r.at[1, step], me.at(line, g, me.other)))
    for step in range(1, groups):
        arrived(col_group.at[from_group(step)], cg_s.at[step], cg_r.at[step])
    acc = col_group[0]
    for i in range(1, groups):
        acc = acc + col_group[i]
    col_out[k, c] = acc
    for step in range(1, LINE):
        go(remote(col_out.at[k, c], col_out.at[k, c], cl_s.at[step], cl_r.at[step], me.at(me.line_to(step), g, k)))
    arrived(s_far, far_s, far_r)
    add_rows(lambda at: s_own.at[0, at], [lambda at: s_own.at[0, at], lambda at: s_far.at[at]], slot_len, 16)
    go(remote(s_own.at[0], ssum_ref.at[k], fin_s, fin_r, sibling))
    keep.append(load(s_own.at[0], ssum_ref.at[k], keep_sem.at[0]))
    for step in range(1, LINE):
        arrived(early_out.at[k, me.line_from(step)], el_s.at[step], el_r.at[step])
    go(remote(early_out.at[k], early_out.at[k], es_s, es_r, sibling))
    for step in range(1, LINE):
        arrived(col_out.at[k, me.line_from(step)], cl_s.at[step], cl_r.at[step])
    go(remote(col_out.at[k], col_out.at[k], cs_s, cs_r, sibling))

    for step in range(1, LINE):
        where = mixed_ref.at[:, :, pl.ds(pl.multiple_of((me.line_from(step) * 2 + k) * feat, 128), feat)]
        arrived(where, mout_s.at[0, step], mout_r.at[0, step])
        go(remote(where, where, mout_s.at[1, step], mout_r.at[1, step], sibling))
    for m in range(count):
        for step in range(1, LINE):
            dst = g_out[m].at[:, pl.ds(pl.multiple_of(me.line_from(step) * cols[m], 128), cols[m])]
            arrived(dst, gl_s.at[m, step], gl_r.at[m, step])
    for step in range(LINE):
        source = me.line_from(step)
        dst = mixed_ref.at[:, :, pl.ds(pl.multiple_of((source * 2 + me.other) * feat, 128), feat)]
        arrived(dst, mout_s.at[1, step], mout_r.at[1, step])
        for core, way in ((k, 0), (me.other, 1)):
            if step or way:
                arrived(row_out.at[core, source], rl_s.at[way, step], rl_r.at[way, step])
    arrived(ssum_ref.at[me.other], fin_s, fin_r)
    arrived(early_out.at[me.other], es_s, es_r)
    arrived(col_out.at[me.other], cs_s, cs_r)
    for copy in sends:
        copy.wait_send()
    for m in range(2):
        if two_phase:
            for way in range(2):
                phase_one(m, way, "wait_send")
                phase_two(m, way, "wait_send")
        else:
            for step in range(1, groups):
                send_group(m, step, "wait_send")
    for copy in keep:
        copy.wait()


def scatter_all(groups, cols, seq_dev, rows_own, pick, lefts, rights, between):
    near, far, s_pair, *done, early = between
    slot_len = s_pair.shape[1]
    rows = lefts[0].shape[0]
    count = len(cols)
    feat = D // (2 * LINE)
    seqs = LINE * seq_dev
    blocks = (seqs, slot_len, feat)
    dma = pltpu.SemaphoreType.DMA
    f32, low = jnp.float32, jnp.bfloat16
    col_rows = sum(cols) // 128
    return pl.pallas_call(
        partial(scatter_kernel, groups, cols, seq_dev, slot_len, rows_own),
        out_shape=[
            jax.ShapeDtypeStruct((seq_dev, slot_len, D), low),
            jax.ShapeDtypeStruct((seq_dev, slot_len, D), low),
        ]
        + [jax.ShapeDtypeStruct((rows_own, LINE * width), low) for width in cols]
        + [
            jax.ShapeDtypeStruct((2, LINE) + early.shape, f32),
            jax.ShapeDtypeStruct((2, LINE, col_rows, 128), f32),
            jax.ShapeDtypeStruct((2, LINE, 8, 128), f32),
        ],
        in_specs=[SMEM] + [ANY] * 11 + [VMEM],
        out_specs=[ANY] * (2 + count) + [VMEM] * 3,
        scratch_shapes=[
            pltpu.VMEM((2 if groups == 4 else 1, rows, D), low),
            pltpu.VMEM((rows, cols[1]), low),
            pltpu.VMEM((rows, cols[0]), low),
        ]
        + [pltpu.VMEM((LINE, groups if m < 2 else 1, rows_own, width), low) for m, width in enumerate(cols)]
        + [pltpu.VMEM((groups - 1, LINE, rows_own, width), low) for width in cols]
        + [
            pltpu.VMEM((2, seqs, slot_len, feat), low),
            pltpu.VMEM((groups * seqs, slot_len, feat), low),
            pltpu.VMEM((LINE, seq_dev, slot_len, feat), low),
            pltpu.VMEM((2, slot_len, D), low),
            pltpu.VMEM((2, slot_len, D), low),
            pltpu.VMEM((slot_len, D), low),
            pltpu.VMEM((groups,) + early.shape, f32),
            pltpu.VMEM((col_rows, 128), f32),
            pltpu.VMEM((groups, col_rows, 128), f32),
            pltpu.VMEM((LINE, 128, 128), f32),
            pltpu.VMEM((LINE, 8, 128), f32),
            dma((12,)),
            dma((2,)),
            dma((2,)),
            dma(()),
            dma(()),
            dma(()),
            dma(()),
            dma((groups,)),
            dma((groups,)),
            dma((2, LINE)),
            dma((2, LINE)),
            dma((count, max(groups, 6))),
            dma((count, max(groups, 6))),
            dma((count, LINE)),
            dma((count, LINE)),
            dma((groups,)),
            dma((groups,)),
            dma((LINE,)),
            dma((LINE,)),
            dma(()),
            dma(()),
            dma((groups,)),
            dma((groups,)),
            dma((LINE,)),
            dma((LINE,)),
            dma(()),
            dma(()),
            dma((2, LINE)),
            dma((2, LINE)),
            dma((2 + count,)),
        ],
        compiler_params=pltpu.CompilerParams(
            collective_id=1, has_side_effects=True, vmem_limit_bytes=62 * 1024 * 1024
        ),
        name="scatter_all",
    )(pick, *lefts, *rights, near.reshape(blocks), far.reshape(blocks), s_pair, *done, early)


def prepare_kernel(groups, cols, seq_dev, slot_len, *refs):
    (spot, lengths, permutation, wq, w1, wd, w2, vectors, biases, rows_state) = refs[:10]
    lows = refs[10:14]
    valid, own_valid, all_vectors, all_biases, pick = refs[14:]
    f32 = jnp.float32
    for src, dst in zip((wq, w1, wd, w2), lows):
        dst[...] = src[...].astype(jnp.bfloat16)

    @pl.when(pl.program_id(0) == 0)
    def _():
        data, core = spot[0], spot[1]
        line, group = data // groups, data % groups
        times = lax.broadcasted_iota(jnp.int32, (slot_len, 1), 0)
        for place in range(LINE):
            for s in range(seq_dev):
                slot = (place * groups + group) * seq_dev + s
                at = place * seq_dev + s
                valid[at * slot_len : (at + 1) * slot_len, :] = jnp.where(times < lengths[slot], 1.0, 0.0)
                source = permutation[slot]
                chip = source // seq_dev
                pick[at] = (chip % groups) * (LINE * seq_dev) + (chip // groups) * seq_dev + source % seq_dev
        for s in range(seq_dev):
            own_valid[s * slot_len : (s + 1) * slot_len, :] = jnp.where(
                times < lengths[data * seq_dev + s], 1.0, 0.0
            )
        all_vectors[0:6, :] = vectors[...]
        all_vectors[6:8, :] = jnp.zeros((2, D), f32)
        lane = lax.broadcasted_iota(jnp.int32, (1, 128), 1)
        total = jnp.zeros((1, 128), f32)
        for m in range(4):
            total = total + jnp.where(lane == m, jnp.sum(rows_state[m : m + 1, :], 1, keepdims=True), 0.0)
        all_vectors[6:7, 0:128] = jnp.where(core == 0, total, jnp.zeros_like(total))
        all_biases[:, : cols[0]] = biases[:, pl.ds(pl.multiple_of(line * cols[0], 128), cols[0])]
        all_biases[:, cols[0] :] = biases[:, pl.ds(pl.multiple_of(LINE * cols[0] + line * cols[1], 128), cols[1])]


def prepare(groups, seq_dev, slot_len, spot, lengths, permutation, weights, vectors, biases, rows_state):
    f32, low = jnp.float32, jnp.bfloat16
    rows_own = weights[0].shape[0]
    cols = tuple(w.shape[1] // LINE for w in weights)
    tall = 32
    steps = rows_own // tall
    seqs = LINE * seq_dev

    def whole(shape):
        return pl.BlockSpec(shape, lambda i: (0,) * len(shape))

    blocks = [pl.BlockSpec((tall, w.shape[1]), lambda i: (i, 0)) for w in weights]
    return pl.pallas_call(
        partial(prepare_kernel, groups, cols, seq_dev, slot_len),
        grid=(steps,),
        out_shape=[jax.ShapeDtypeStruct(w.shape, low) for w in weights]
        + [
            jax.ShapeDtypeStruct((seqs * slot_len, 1), f32),
            jax.ShapeDtypeStruct((seq_dev * slot_len, 1), f32),
            jax.ShapeDtypeStruct((8, D), f32),
            jax.ShapeDtypeStruct((1, cols[0] + cols[1]), f32),
            jax.ShapeDtypeStruct((seqs,), jnp.int32),
        ],
        in_specs=[SMEM] * 3 + blocks + [whole(vectors.shape), whole(biases.shape), whole(rows_state.shape)],
        out_specs=blocks
        + [
            whole((seqs * slot_len, 1)),
            whole((seq_dev * slot_len, 1)),
            whole((8, D)),
            whole((1, cols[0] + cols[1])),
            SMEM,
        ],
        compiler_params=pltpu.CompilerParams(vmem_limit_bytes=60 * 1024 * 1024),
        name="prepare",
    )(spot, lengths, permutation, *weights, vectors, biases, rows_state)


def finish_kernel(order, cols, rows_own, *refs):
    f32, low = jnp.float32, jnp.bfloat16
    spot = refs[0]
    g_in, w_in = refs[1:5], refs[5:9]
    (s_sum, tokens, cotangent, own_valid, early, col_all, row_all, row_state, col_state, vectors, moments, biases,
     bias_moments) = refs[9:22]
    grads, news, copies = refs[22:26], refs[26:30], refs[30:34]
    (grad_tokens, row_new, col_new, norm_total, norm_moment_new, norm_new, bias_total, bias_moment_new,
     bias_new) = refs[34:43]
    row_factor, col_factor, turn = refs[43:]
    step = pl.program_id(0)
    widths = [w.shape[1] for w in w_in]
    edges = [sum(widths[:i]) for i in range(5)]
    tiles = D // 128

    @pl.when(step == 0)
    def _():
        core = spot[1]
        both = early[0, 0]
        rows_all = row_all[0, 0]
        mass_all = col_all[0, 0]
        for n in range(1, 2 * LINE):
            both = both + early[n // LINE, n % LINE]
            rows_all = rows_all + row_all[n // LINE, n % LINE]
            mass_all = mass_all + col_all[n // LINE, n % LINE]
        for r in range(6):
            for t in range(tiles):
                at = min(r, 4) * tiles + t
                norm_total[r : r + 1, t * 128 : (t + 1) * 128] = both[at : at + 1]
        grad = norm_total[...]
        moment = decay * moments[...] + (1.0 - decay) * (grad * grad + eps_second)
        norm_moment_new[...] = moment
        norm_new[...] = vectors[...] - rate_norm * grad * lax.rsqrt(moment)
        first = 5 * tiles
        parts = ((cols[0] // 128, 0), (cols[1] // 128, LINE * cols[0]))
        for line in range(LINE):
            at = first
            for count, base in parts:
                for t in range(count):
                    to = base + (line * count + t) * 128
                    bias_total[:, to : to + 128] = early[core, line, at : at + 1, :]
                    at += 1
        grad = bias_total[...]
        moment = decay * bias_moments[...] + (1.0 - decay) * (grad * grad + eps_second)
        bias_moment_new[...] = moment
        bias_new[...] = biases[...] - rate_vector * grad * lax.rsqrt(moment)
        at_row = first + (cols[0] + cols[1]) // 128
        full_cols = (3.0 * D, 1.0 * D, 1.0 * FF, 1.0 * FF)
        rates = (
            rate_scale / math.sqrt(D),
            rate_scale / math.sqrt(D // 8),
            rate_scale / math.sqrt(D),
            rate_scale / math.sqrt(FF),
        )
        turn[...] = jnp.zeros_like(turn)
        at = 0
        for m, i in enumerate(order):
            count = cols[m] // 128
            new = decay * row_state[i : i + 1, :] + (1.0 - decay) * (rows_all[m : m + 1, :rows_own] / full_cols[i])
            row_new[i : i + 1, :] = new
            mass = jnp.sum(jnp.sum(mass_all[at : at + count], 1, keepdims=True), 0, keepdims=True)
            mean = (decay * both[at_row : at_row + 1, i : i + 1] + (1.0 - decay) * (mass / full_cols[i])) / D
            turn[i : i + 1, :rows_own] = rates[i] * lax.rsqrt(new / mean)
            for line in range(LINE):
                for t in range(count):
                    to = edges[i] + (line * count + t) * 128
                    col_new[:, to : to + 128] = col_all[core, line, at + t : at + t + 1, :]
            at += count
        row_factor[...] = jnp.transpose(turn[...])
        new = decay * col_state[...] + (1.0 - decay) * (col_new[...] / D)
        col_new[...] = new
        col_factor[...] = lax.rsqrt(new)

    tall = w_in[0].shape[0]
    for half in range(tall // 16):
        rows = pl.ds(pl.multiple_of(step * tall + half * 16, 16), 16)
        part = slice(half * 16, half * 16 + 16)
        for i in range(4):
            factor = row_factor[rows, i : i + 1]
            for n in range(widths[i] // 1024):
                at = slice(n * 1024, (n + 1) * 1024)
                grad = g_in[i][part, at].astype(f32)
                new = w_in[i][part, at] - grad * factor * col_factor[:, edges[i] + n * 1024 : edges[i] + (n + 1) * 1024]
                grads[i][part, at] = grad
                news[i][part, at] = new
                copies[i][part, at] = new.astype(low)

    @pl.loop(0, tokens.shape[0] // 16)
    def body(j):
        at = pl.ds(pl.multiple_of(j * 16, 16), 16)
        x = tokens[at, :].astype(f32)
        centre = x - jnp.mean(x, -1, keepdims=True)
        scale = lax.rsqrt(jnp.mean(centre * centre, -1, keepdims=True) + eps_norm)
        unit = centre * scale
        flow = s_sum[at, :].astype(f32)
        through = flow - jnp.mean(flow, -1, keepdims=True) - unit * jnp.mean(flow * unit, -1, keepdims=True)
        grad_tokens[at, :] = (cotangent[at, :].astype(f32) * own_valid[at, :] + scale * through).astype(low)


def finish(order, spot, grads, weights, s_sum, tokens, cotangent, own_valid, *small):
    f32, low = jnp.float32, jnp.bfloat16
    rows_own = weights[0].shape[0]
    tall = 32
    steps = rows_own // tall
    cols = tuple(weights[i].shape[1] // LINE for i in order)
    rows = tokens.shape[0]
    row_state, col_state, vectors, _, biases = small[3:8]

    def whole(shape):
        return pl.BlockSpec(shape, lambda i: (0,) * len(shape))

    blocks = [pl.BlockSpec((tall, w.shape[1]), lambda i: (i, 0)) for w in weights]
    acts = pl.BlockSpec((rows // steps, D), lambda i: (i, 0))
    small_out = [row_state.shape, col_state.shape] + [vectors.shape] * 3 + [biases.shape] * 3
    return pl.pallas_call(
        partial(finish_kernel, order, cols, rows_own),
        grid=(steps,),
        out_shape=[jax.ShapeDtypeStruct(w.shape, f32) for w in weights] * 2
        + [jax.ShapeDtypeStruct(w.shape, low) for w in weights]
        + [jax.ShapeDtypeStruct((rows, D), low)]
        + [jax.ShapeDtypeStruct(shape, f32) for shape in small_out],
        in_specs=[SMEM]
        + blocks * 2
        + [acts] * 3
        + [pl.BlockSpec((rows // steps, 1), lambda i: (i, 0))]
        + [whole(a.shape) for a in small],
        out_specs=blocks * 3 + [acts] + [whole(shape) for shape in small_out],
        scratch_shapes=[
            pltpu.VMEM((128, 128), f32),
            pltpu.VMEM(col_state.shape, f32),
            pltpu.VMEM((128, 128), f32),
        ],
        compiler_params=pltpu.CompilerParams(vmem_limit_bytes=60 * 1024 * 1024),
        name="finish",
    )(spot, *grads, *weights, s_sum, tokens, cotangent, own_valid, *small)


def per_device(
    tokens,
    cotangent,
    lengths,
    permutation,
    w_qkv,
    w_dense,
    w_fc1,
    w_fc2,
    norm_vectors,
    split_biases,
    row_state,
    col_state,
    norm_moment,
    bias_moment,
):
    groups = lax.axis_size("dp") // LINE
    seq_dev, slot_len, width = tokens.shape
    rows_own = w_qkv.shape[0]
    head_dim = D // HEADS
    weights = (w_qkv, w_dense, w_fc1, w_fc2)
    order = (0, 2, 1, 3)
    cols = tuple(weights[i].shape[1] // LINE for i in order)
    spot = jnp.stack([lax.axis_index("dp"), lax.axis_index("tensor")]).astype(jnp.int32)
    *lows, valid, own_valid, vectors, biases, pick = prepare(
        groups, seq_dev, slot_len, spot, lengths, permutation, [weights[i] for i in order], norm_vectors,
        split_biases, row_state,
    )
    turns = jnp.asarray(turn_tables(slot_len, head_dim // 4, head_dim // 2))
    norm_one, norm_two, qkv_grad, pre_grad, *between = gather_all(
        groups, lows, tokens, cotangent, vectors, biases, valid, turns
    )
    mixed, s_sum, *outs = scatter_all(
        groups, cols, seq_dev, rows_own, pick, (norm_one, norm_two), (qkv_grad, pre_grad), between
    )
    grads = [outs[order.index(i)] for i in range(4)]
    early_all, col_all, row_all = outs[4:]
    results = finish(
        order, spot, grads, weights, s_sum.reshape(-1, width), tokens.reshape(-1, width),
        cotangent.reshape(-1, width), own_valid, early_all, col_all, row_all, row_state, col_state, norm_vectors,
        norm_moment, split_biases, bias_moment,
    )
    return (mixed, results[12].reshape(tokens.shape), *results[:12], *results[13:])


def solution(mesh):
    halves = P("dp", "tensor")
    split = P("tensor", None)
    in_specs = (
        P("dp", None, None),
        P("dp", None, None),
        P(),
        P(),
        halves,
        halves,
        halves,
        halves,
        P(),
        split,
        P(None, "dp"),
        split,
        P(),
        split,
    )
    out_specs = (
        (P("dp", None, None),) * 2
        + (halves,) * 12
        + (P(None, "dp"), split)
        + (P(),) * 3
        + (split,) * 3
    )
    return jax.shard_map(
        per_device, mesh=mesh, in_specs=in_specs, out_specs=out_specs, check_vma=False
    )
```

```python
from functools import partial
import math

import jax
import jax.numpy as jnp
import numpy as np
from jax import lax
from jax.experimental import pallas as pl
from jax.experimental.pallas import tpu as pltpu
from jax.sharding import PartitionSpec as P

D = 2048
FF = 8192
HEADS = 8
LINE = 4

eps_norm = 1e-05
eps_second = 1e-30
decay = 0.5
rate_scale = 1.0
rate_norm = 0.5
rate_vector = 0.05
neg_large = -1e30

MESH = pl.DeviceIdType.MESH
ANY = pl.BlockSpec(memory_space=pl.ANY)
VMEM = pl.BlockSpec(memory_space=pltpu.VMEM)
SMEM = pl.BlockSpec(memory_space=pltpu.SMEM)


def turn_tables(slot_len, rot_dims, width):
    half = rot_dims // 2
    freq = np.float32(10000.0) ** (np.float32(-2.0) * np.arange(half, dtype=np.float32) / np.float32(rot_dims))
    angle = np.arange(slot_len, dtype=np.float32)[:, None] * freq[None, :].astype(np.float32)
    tables = np.zeros((3, slot_len, width), np.float32)
    tables[0] = 1.0
    tables[0, :, :half] = tables[0, :, half:rot_dims] = np.cos(angle)
    tables[1, :, :half] = tables[2, :, half:rot_dims] = np.sin(angle)
    return tables


class Place:
    def __init__(self, groups):
        self.groups = groups
        data = lax.axis_index("dp")
        self.core = lax.axis_index("tensor")
        self.other = 1 - self.core
        self.line = data // groups
        self.group = data % groups

    def at(self, line, group, core):
        return (line * self.groups + group, core)

    def line_to(self, step):
        return (self.line + step) % LINE

    def line_from(self, step):
        return (self.line + LINE - step) % LINE

    def group_to(self, step):
        g = self.group
        if self.groups == 4:
            if step == 1:
                return g + 1 - 2 * (g % 2)
            if step == 2:
                return (g + 2) % 4
            return 3 - g
        return (g + step) % self.groups

    def group_from(self, step):
        if self.groups == 4:
            return self.group_to(step)
        return (self.group + self.groups - step) % self.groups

    def greet(self):
        barrier = pltpu.get_barrier_semaphore()
        count = 0
        for step in range(1, LINE):
            for core in (self.core, self.other):
                pl.semaphore_signal(
                    barrier, inc=1, device_id=self.at(self.line_to(step), self.group, core), device_id_type=MESH
                )
                count += 1
        for step in range(1, self.groups):
            pl.semaphore_signal(
                barrier, inc=1, device_id=self.at(self.line, self.group_to(step), self.core), device_id_type=MESH
            )
            count += 1
        pl.semaphore_signal(
            barrier, inc=1, device_id=self.at(self.line, self.group, self.other), device_id_type=MESH
        )
        pl.semaphore_wait(barrier, count + 1)


def remote(src, dst, send, recv, device):
    return pltpu.make_async_remote_copy(
        src_ref=src, dst_ref=dst, send_sem=send, recv_sem=recv, device_id=device, device_id_type=MESH
    )


def dot(left, right):
    return jnp.dot(left, right, preferred_element_type=jnp.float32)


def turned(blocks):
    eye = lax.broadcasted_iota(jnp.int32, (256, 256), 0) == lax.broadcasted_iota(jnp.int32, (256, 256), 1)
    eye = jnp.where(eye, 1.0, 0.0).astype(jnp.bfloat16)
    parts = []
    for n in range(0, len(blocks), 2):
        pair = jnp.concatenate(blocks[n : n + 2], 1)
        part = lax.dot_general(eye, pair, (((1,), (1,)), ((), ())), preferred_element_type=jnp.float32)
        parts.append(part.astype(jnp.bfloat16))
    return jnp.concatenate(parts, 0)


def gather_kernel(groups, cols, seq_dev, slot_len, *refs):
    count = len(cols)
    f32, low = jnp.float32, jnp.bfloat16
    w_in = refs[:count]
    acts_in = refs[count : count + 2]
    vec_ref, bias_ref, valid_ref, turn_ref = refs[count + 2 : count + 6]
    outs = refs[count + 6 : count + 18]
    (n1_out, n2_out, qg_out, pg_out, near_out, far_out, s_out, gd_own, g2_own, gd_got, g2_got, early_ref) = outs
    rest = refs[count + 18 :]
    w_out = rest[:count]
    acts_out = rest[count : count + 2]
    (qkv_keep, prob_keep, attn_keep, hid_keep, pg_keep, one_buf, two_buf, back_buf, m_buf, m_got, m_half, s_got,
     qkv_now, pre_now, stat_keep, norm_acc, bias_acc) = rest[count + 2 : count + 19]
    (one_s, one_r, two_s, two_r, three_s, three_r, row_s, row_r, sib_s, sib_r, here, out_a, out_b,
     out_d, msib_s, msib_r, ssib_s, ssib_r, half_s, half_r, far_s, far_r, near_sem, s_here, gp_s, gp_r,
     g_here) = rest[count + 19 :]
    me = Place(groups)
    c, g, k = me.line, me.group, me.core
    me.greet()
    sibling = me.at(c, g, me.other)
    rows_own = w_in[0].shape[0]
    block_rows = seq_dev * slot_len
    near = groups == 4
    START, SENT = "start", "wait_send"

    def block(ref, line, width):
        return ref.at[:, pl.ds(pl.multiple_of(line * width, 128), width)]

    def place(m, line, group):
        return w_out[m].at[pl.ds(pl.multiple_of((line * groups + group) * rows_own, 32), rows_own)]

    def rows_of(which, line, core):
        return acts_out[which].at[pl.ds(pl.multiple_of((line * seq_dev + core) * slot_len, 32), slot_len)]

    partner = c + 1 - 2 * (c % 2)
    beyond = (c + 2) % LINE

    def row_send(which, q, act):
        origin = beyond if q == 2 else c
        copy = remote(
            rows_of(which, beyond, k) if q == 2 else acts_in[which].at[k],
            rows_of(which, origin, k),
            row_s.at[which, q],
            row_r.at[which, q],
            me.at(beyond if q == 1 else partner, g, k),
        )
        getattr(copy, act)()

    def row_origin(q):
        return (partner, beyond, (partner + 2) % LINE)[q]

    def to_sibling(which, q, act):
        rows = rows_of(which, row_origin(q), k)
        copy = remote(rows, rows, sib_s.at[which, q], sib_r.at[which, q], sibling)
        getattr(copy, act)()

    def pass_on(which, q):
        rows = rows_of(which, row_origin(q), k)
        remote(rows, rows, row_s.at[which, q], row_r.at[which, q], sibling).wait_recv()
        if q == 1:
            row_send(which, 2, START)
        to_sibling(which, q, START)

    def arrive_sibling(which):
        for q in range(3):
            rows = rows_of(which, row_origin(q), me.other)
            remote(rows, rows, sib_s.at[which, q], sib_r.at[which, q], sibling).wait_recv()

    def local_acts(which, act):
        for s in range(seq_dev):
            copy = pltpu.make_async_copy(acts_in[which].at[s], rows_of(which, c, s), here.at[count + which, s])
            getattr(copy, act)()

    def local_weight(m, act):
        copy = pltpu.make_async_copy(block(w_in[m], c, cols[m]), place(m, c, g), here.at[m, 0])
        getattr(copy, act)()

    def stage_one(m, act):
        for step in range(1, LINE):
            to = me.line_to(step)
            copy = remote(
                block(w_in[m], to, cols[m]),
                place(m, c, g),
                one_s.at[m, step],
                one_r.at[m, step],
                me.at(to, g, k),
            )
            getattr(copy, act)()

    def stage_two(m, step, act):
        where = place(m, me.line_from(step), g)
        src = block(w_in[m], c, cols[m]) if step == 0 else where
        for peer in range(1, 3 if near else groups):
            copy = remote(
                src, where, two_s.at[m, step, peer], two_r.at[m, step, peer], me.at(c, me.group_to(peer), k)
            )
            getattr(copy, act)()

    def first_half(m):
        for step in range(1, LINE):
            dst = place(m, me.line_from(step), g)
            remote(dst, dst, one_s.at[m, step], one_r.at[m, step], sibling).wait_recv()
            stage_two(m, step, START)

    def wait_two(m, step, peer):
        dst = place(m, me.line_from(step), me.group_from(peer))
        remote(dst, dst, two_s.at[m, step, peer], two_r.at[m, step, peer], sibling).wait_recv()

    def stage_three(m, step, act):
        source, target = (1, 2) if step % 2 == 0 else (2, 1)
        where = place(m, me.line_from(step), me.group_to(source))
        copy = remote(where, where, three_s.at[m, step], three_r.at[m, step], me.at(c, me.group_to(target), k))
        getattr(copy, act)()

    def relay(m):
        for step in range(LINE):
            for peer in range(1, 3 if near else groups):
                wait_two(m, step, peer)
            if near:
                stage_three(m, step, START)

    def last(m):
        if near:
            for step in range(LINE):
                dst = place(m, me.line_from(step), me.group_to(3))
                remote(dst, dst, three_s.at[m, step], three_r.at[m, step], sibling).wait_recv()

    row_send(0, 1, START)
    row_send(0, 0, START)
    for m in (0, 1):
        stage_one(m, START)
        stage_two(m, 0, START)
    local_acts(0, START)
    local_weight(0, START)
    local_weight(1, START)
    norm_acc[...] = jnp.zeros_like(norm_acc)
    bias_acc[...] = jnp.zeros_like(bias_acc)
    first_half(0)
    pass_on(0, 1)
    for m in (2, 3):
        stage_one(m, START)
        stage_two(m, 0, START)
    local_acts(1, START)
    local_weight(2, START)
    local_weight(3, START)
    pass_on(0, 0)
    first_half(1)
    row_send(1, 1, START)
    row_send(1, 0, START)
    relay(0)
    pass_on(0, 2)
    relay(1)
    local_acts(0, "wait")
    local_weight(0, "wait")
    local_weight(1, "wait")
    last(0)
    last(1)
    arrive_sibling(0)

    wq, w1, wd, w2 = w_out
    x_all, ct_all = acts_out
    head = cols[0] // 3
    half = head // 2
    chunk = 16
    wide = 512
    ways = D // wide
    root = math.sqrt(head)
    causal = lax.broadcasted_iota(jnp.int32, (slot_len, slot_len), 0) >= lax.broadcasted_iota(
        jnp.int32, (slot_len, slot_len), 1
    )

    def turn(v, sign):
        left = pltpu.roll(v, half - 32, 1)
        right = pltpu.roll(v, 32, 1)
        if sign > 0:
            return v * turn_ref[0] - left * turn_ref[1] + right * turn_ref[2]
        return v * turn_ref[0] + left * turn_ref[1] - right * turn_ref[2]

    def contract(left, right, dims):
        return lax.dot_general(left, right, ((dims[0], dims[1]), ((), ())), preferred_element_type=f32)

    def put_one(i, line, act):
        rows = pl.ds(pl.multiple_of(line * block_rows, 128), block_rows)
        getattr(pltpu.make_async_copy(one_buf, n1_out.at[rows], out_a), act)()
        getattr(pltpu.make_async_copy(two_buf.at[0], n2_out.at[rows], out_b.at[0]), act)()

    @pl.loop(0, LINE)
    def forward(i):
        line = (c + i) % LINE
        base = pl.multiple_of(line * block_rows, 128)

        @pl.when(i == 0)
        def _():
            first_half(2)
            first_half(3)

        @pl.when(i == 1)
        def _():
            relay(2)
            pass_on(1, 1)

        @pl.when(i == 2)
        def _():
            relay(3)
            pass_on(1, 0)

        @pl.when(i >= 1)
        def _():
            put_one(i, line, "wait")

        @pl.loop(0, block_rows // chunk)
        def norm(j):
            at = pl.ds(pl.multiple_of(base + j * chunk, chunk), chunk)
            to = pl.ds(pl.multiple_of(j * chunk, chunk), chunk)
            x = x_all[at, :].astype(f32)
            mean = jnp.mean(x, -1, keepdims=True)
            centre = x - mean
            scale = lax.rsqrt(jnp.mean(centre * centre, -1, keepdims=True) + eps_norm)
            stat_keep[at, 0:1] = mean
            stat_keep[at, 1:2] = scale
            unit = centre * scale
            one_buf[to, :] = (unit * vec_ref[0:1, :] + vec_ref[1:2, :]).astype(low)
            two_buf[0, to, :] = (unit * vec_ref[2:3, :] + vec_ref[3:4, :]).astype(low)

        put_one(i, line, "start")
        qkv_now[...] = dot(one_buf[...], wq[...]) + bias_ref[0:1, : cols[0]]
        pre_now[...] = dot(two_buf[0], w1[...]) + bias_ref[0:1, cols[0] :]

        for s in range(seq_dev):
            part = slice(s * slot_len, (s + 1) * slot_len)
            rows = pl.ds(pl.multiple_of(base + s * slot_len, 32), slot_len)
            qkv_keep[rows, 0:half] = turn(qkv_now[part, 0:half], 1).astype(low)
            qkv_keep[rows, half:head] = qkv_now[part, half:head].astype(low)
            qkv_keep[rows, head : head + half] = turn(qkv_now[part, head : head + half], 1).astype(low)
            qkv_keep[rows, head + half :] = qkv_now[part, head + half :].astype(low)
            query = qkv_keep[rows, :head]
            keys = qkv_keep[rows, head : 2 * head]
            values = qkv_keep[rows, 2 * head :]
            scores = jnp.where(causal, contract(query, keys, ((1,), (1,))) / root, neg_large)
            expo = jnp.exp(scores - jnp.max(scores, -1, keepdims=True))
            probs = expo / jnp.sum(expo, -1, keepdims=True)
            prob_keep[line * seq_dev + s] = probs
            attn_keep[rows, :] = (dot(probs.astype(low), values) * valid_ref[rows, :]).astype(low)

        @pl.loop(0, block_rows // chunk)
        def act(j):
            at = pl.ds(pl.multiple_of(base + j * chunk, chunk), chunk)
            pre = pre_now[pl.ds(pl.multiple_of(j * chunk, chunk), chunk), :]
            area = 0.5 * (1.0 + lax.erf(pre * math.sqrt(0.5)))
            hid_keep[at, :] = (pre * area * valid_ref[at, :]).astype(low)
            pg_keep[at, :] = (area + pre * (jnp.exp(-0.5 * pre * pre) * (1.0 / math.sqrt(2.0 * math.pi)))).astype(low)

    put_one(LINE - 1, (c + LINE - 1) % LINE, "wait")
    local_weight(2, "wait")
    local_weight(3, "wait")
    last(2)
    last(3)
    mine = c * 2 + k

    def pair_m(i, act):
        copy = remote(m_buf.at[i % 2, me.other], m_got.at[i], msib_s.at[i], msib_r.at[i], sibling)
        getattr(copy, act)()

    def half_m(i, act):
        for q, to in enumerate((partner, (partner + 2) % LINE)):
            copy = remote(
                m_got.at[i, to], m_half.at[i, q], half_s.at[i, q], half_r.at[i, q], me.at(partner, g, k)
            )
            getattr(copy, act)()

    def far_m(i, act):
        copy = remote(m_got.at[i, beyond], far_out.at[i], far_s.at[i], far_r.at[i], me.at(beyond, g, k))
        getattr(copy, act)()

    def near_m(i, act):
        getattr(pltpu.make_async_copy(m_got.at[i, c], near_out.at[i], near_sem.at[i]), act)()

    def sent_m(i):
        half_m(i, SENT)
        far_m(i, SENT)
        near_m(i, "wait")

    def second_m(i):
        half_m(i, "wait_recv")

        @pl.loop(0, block_rows // 64)
        def add(j):
            at = pl.ds(pl.multiple_of(j * 64, 64), 64)
            for q, to in enumerate((c, beyond)):
                total = m_got[i, to, at, :].astype(f32) + m_half[i, q, at, :].astype(f32)
                m_got[i, to, at, :] = total.astype(low)

        far_m(i, START)
        near_m(i, START)

    def pair_add(i):
        pair_m(i, "wait_recv")

        @pl.loop(0, LINE)
        def add_outer(p):
            @pl.loop(0, block_rows // 64)
            def add(j):
                at = pl.ds(pl.multiple_of(j * 64, 64), 64)
                total = m_buf[i % 2, k, p, at, :].astype(f32) + m_got[i, p, at, :].astype(f32)
                m_got[i, p, at, :] = total.astype(low)

        half_m(i, START)

    @pl.loop(0, LINE)
    def outputs(i):
        base = pl.multiple_of(i * block_rows, 128)
        whole = pl.ds(base, block_rows)
        slot = i % 2

        @pl.when(i == 1)
        def _():
            pass_on(1, 2)

        @pl.when(i >= 2)
        def _():
            pair_m(i - 2, SENT)

        @pl.loop(0, ways)
        def output(j):
            at = pl.ds(pl.multiple_of(j * wide, 128), wide)
            total = contract(attn_keep[whole, :], wd[at, :], ((1,), (1,)))
            pre_now[:, :wide] = total + contract(hid_keep[whole, :], w2[at, :], ((1,), (1,)))
            feature = (lax.broadcasted_iota(jnp.int32, (1, wide), 1) + j * wide) // (D // (2 * LINE))
            mask = jnp.where(feature == mine, 1.0, 0.0)
            bias = vec_ref[4:5, at] + vec_ref[5:6, at]

            @pl.loop(0, block_rows // chunk)
            def rows(r):
                to = pl.ds(pl.multiple_of(r * chunk, chunk), chunk)
                here_rows = pl.ds(pl.multiple_of(base + r * chunk, chunk), chunk)
                extra = x_all[here_rows, at].astype(f32) + bias
                total = ((pre_now[to, :wide] + mask * extra) * valid_ref[here_rows, :]).astype(low)
                m_buf[slot, 0, j, to, :] = total[:, : wide // 2]
                m_buf[slot, 1, j, to, :] = total[:, wide // 2 :]

        pair_m(i, START)

        @pl.when(i >= 1)
        def _():
            pair_add(i - 1)

    pair_add(LINE - 1)
    pair_m(LINE - 2, SENT)
    pair_m(LINE - 1, SENT)
    local_acts(1, "wait")
    arrive_sibling(1)

    per = 128 // rows_own
    part_cols = 256
    fits = block_rows // 128
    pieces = (cols[2] + cols[3]) // part_cols
    dense_pieces = cols[2] // part_cols

    def out_group(i):
        flip_x, flip_y = 1 - i % 2, 1 - i // 2
        return (g // 2 + flip_y) % 2 * 2 + (g % 2 + flip_x) % 2

    def flat_piece(i, t, nb):
        row, column = divmod(t * pieces + nb, D // part_cols)
        at = (pl.ds(row * 128, 128), pl.ds(column * part_cols, part_cols))
        return one_buf.at[at] if i == 2 else two_buf.at[(1,) + at]

    def out_products(i):
        if near:
            to = out_group(i)
            tiles = [(l, to) for l in range(LINE)]
        else:
            tiles = [(i, t * per) for t in range(LINE)]
        lhs = turned([ct_all[:, pl.ds(pl.multiple_of((l * groups + p) * rows_own, 128), 128)] for l, p in tiles])
        first = 0
        for right in (attn_keep, hid_keep):
            out = dot(lhs, right[...]).astype(low)
            for n in range(right.shape[1] // part_cols):
                nb = first + n
                for t in range(LINE):
                    part = out[t * 128 : (t + 1) * 128, n * part_cols : (n + 1) * part_cols]
                    if near and i >= 2:
                        flat_piece(i, t, nb)[...] = part
                    else:
                        m_buf[i % 2, nb // fits, t, (nb % fits) * 128 : (nb % fits + 1) * 128, :] = part
            first += right.shape[1] // part_cols

    def out_place(refs, nb, step):
        ref, n = (refs[0], nb) if nb < dense_pieces else (refs[1], nb - dense_pieces)
        at = pl.ds(n * part_cols, part_cols)
        if step is not None:
            ref = ref.at[step - 1]
        return ref.at[:, :, at]

    def out_copies(i, step):
        to = g if step is None else (out_group(i) if near else (g + step) % groups)
        for nb in range(pieces):
            dst = out_place((gd_own, g2_own) if step is None else (gd_got, g2_got), nb, step)
            row = (nb % fits) * 128
            if near and i < 2:
                yield m_buf.at[i % 2, nb // fits, :, pl.ds(row, 128), :], dst, (0, nb)
            elif near:
                for t in range(LINE):
                    yield flat_piece(i, t, nb), dst.at[t], (t, nb)
            else:
                rows = pl.ds(pl.multiple_of(row + (to % per) * rows_own, 32), rows_own)
                yield m_buf.at[i % 2, nb // fits, to // per, rows, :], dst.at[i], (i, nb)

    def out_sends(i, act):
        for step in (groups - 1 - i,) if near else range(groups):
            if step == 0:
                for src, dst, (t, nb) in out_copies(i, None):
                    copy = pltpu.make_async_copy(src, dst, g_here.at[t, nb])
                    getattr(copy, "wait" if act == SENT else act)()
            else:
                to = out_group(i) if near else (g + step) % groups
                for src, dst, (t, nb) in out_copies(i, step):
                    copy = remote(src, dst, gp_s.at[t, step, nb], gp_r.at[t, step, nb], me.at(c, to, k))
                    getattr(copy, act)()

    for i in range(LINE):
        if i >= 2 and not near:
            out_sends(i - 2, SENT)
        out_products(i)
        out_sends(i, START)

    def pair_s(i, act):
        line = (c + i) % LINE
        rows = pl.ds(pl.multiple_of(me.other * slot_len, 32), slot_len)
        copy = remote(two_buf.at[i % 2, rows], s_got.at[line], ssib_s.at[i], ssib_r.at[i], sibling)
        getattr(copy, act)()

    def put_s(i, act):
        line = (c + i) % LINE
        rows = pl.ds(pl.multiple_of(k * slot_len, 32), slot_len)
        getattr(pltpu.make_async_copy(two_buf.at[i % 2, rows], s_out.at[line], s_here.at[i]), act)()

    def finish_s(i):
        line = (c + i) % LINE
        pair_s(i, "wait_recv")

        @pl.loop(0, slot_len // chunk)
        def add(j):
            at = pl.ds(pl.multiple_of(k * slot_len + j * chunk, chunk), chunk)
            to = pl.ds(pl.multiple_of(j * chunk, chunk), chunk)
            total = two_buf[i % 2, at, :].astype(f32) + s_got[line, to, :].astype(f32)
            two_buf[i % 2, at, :] = total.astype(low)

        put_s(i, START)

    def put_rest(line, act):
        rows = pl.ds(pl.multiple_of(line * block_rows, 128), block_rows)
        for place_at, (buf, out) in enumerate(((qkv_keep, qg_out), (pg_keep, pg_out))):
            getattr(pltpu.make_async_copy(buf.at[rows], out.at[rows], out_d.at[place_at, line]), act)()

    @pl.loop(0, LINE)
    def backward(i):
        line = (c + i) % LINE
        base = pl.multiple_of(line * block_rows, 128)
        whole = pl.ds(base, block_rows)
        slot = i % 2

        if near:

            @pl.when(i == 1)
            def _():
                out_sends(LINE - 1, SENT)

        @pl.when((i == 1) | (i == 2))
        def _():
            second_m(i * 2 - 2)
            second_m(i * 2 - 1)

        @pl.loop(0, block_rows // chunk)
        def mask_back(r):
            to = pl.ds(pl.multiple_of(r * chunk, chunk), chunk)
            here_rows = pl.ds(pl.multiple_of(base + r * chunk, chunk), chunk)
            back_buf[to, :] = (ct_all[here_rows, :].astype(f32) * valid_ref[here_rows, :]).astype(low)

        attn_grad = dot(back_buf[...], wd[...]).astype(low)
        pre_now[...] = dot(back_buf[...], w2[...])

        @pl.when(i == 0)
        def _():
            rows = pl.ds(pl.multiple_of(k * slot_len, 32), slot_len)
            total = jnp.sum(back_buf[rows, :].astype(f32).reshape(slot_len // 8, 8, D), 0)
            norm_acc[4] = total

        @pl.loop(0, block_rows // chunk)
        def act(j):
            at = pl.ds(pl.multiple_of(base + j * chunk, chunk), chunk)
            grad = pre_now[pl.ds(pl.multiple_of(j * chunk, chunk), chunk), :] * pg_keep[at, :].astype(f32)
            grad = grad.astype(low)
            pg_keep[at, :] = grad
            grad = grad.astype(f32)
            bias_acc[:, cols[0] :] += grad[:8] + grad[8:]

        for s in range(seq_dev):
            rows = pl.ds(pl.multiple_of(base + s * slot_len, 32), slot_len)
            grad = attn_grad[s * slot_len : (s + 1) * slot_len]
            query = qkv_keep[rows, :head]
            keys = qkv_keep[rows, head : 2 * head]
            values = qkv_keep[rows, 2 * head :]
            probs = prob_keep[line * seq_dev + s]
            prob_grad = contract(grad, values, ((1,), (1,)))
            row_dot = jnp.sum(probs * prob_grad, -1, keepdims=True)
            score_grad = (probs * (prob_grad - row_dot)).astype(low)
            value_grad = contract(probs.astype(low), grad, ((0,), (0,)))
            query_grad = dot(score_grad, keys) / root
            key_grad = contract(score_grad, query, ((0,), (0,))) / root
            qkv_keep[rows, 0:half] = turn(query_grad[:, :half], -1).astype(low)
            qkv_keep[rows, half:head] = query_grad[:, half:].astype(low)
            qkv_keep[rows, head : head + half] = turn(key_grad[:, :half], -1).astype(low)
            qkv_keep[rows, head + half : 2 * head] = key_grad[:, half:].astype(low)
            qkv_keep[rows, 2 * head :] = value_grad.astype(low)
            summed = qkv_keep[rows, :].astype(f32).reshape(slot_len // 8, 8, cols[0])
            bias_acc[:, : cols[0]] += jnp.sum(summed, 0)

        put_rest(line, "start")

        @pl.when(i >= 2)
        def _():
            pair_s(i - 2, SENT)
            put_s(i - 2, "wait")

        @pl.loop(0, ways)
        def inputs(j):
            at = pl.ds(pl.multiple_of(j * wide, 128), wide)
            pre_now[:, :wide] = contract(qkv_keep[whole, :], wq[at, :], ((1,), (1,)))
            pre_now[:, wide:] = contract(pg_keep[whole, :], w1[at, :], ((1,), (1,)))
            gain_one, gain_two = vec_ref[0:1, at], vec_ref[2:3, at]

            def body(r, sums):
                to = pl.ds(pl.multiple_of(r * chunk, chunk), chunk)
                here_rows = pl.ds(pl.multiple_of(base + r * chunk, chunk), chunk)
                first, second = pre_now[to, :wide], pre_now[to, wide:]
                two_buf[slot, to, at] = (first * gain_one + second * gain_two).astype(low)
                unit = (x_all[here_rows, at].astype(f32) - stat_keep[here_rows, 0:1]) * stat_keep[here_rows, 1:2]
                values = (first * unit, first, second * unit, second)
                return tuple(total + value[:8] + value[8:] for total, value in zip(sums, values))

            zero = jnp.zeros((8, wide), f32)
            sums = lax.fori_loop(0, block_rows // chunk, body, (zero,) * 4)
            for place_at in range(4):
                norm_acc[place_at, :, at] += sums[place_at]

        pair_s(i, START)

        @pl.when(i >= 1)
        def _():
            finish_s(i - 1)

    finish_s(LINE - 1)
    for r in range(5):
        total = jnp.sum(norm_acc[r], 0, keepdims=True)
        for t in range(D // 128):
            early_ref[r * (D // 128) + t : r * (D // 128) + t + 1, :] = total[:, t * 128 : (t + 1) * 128]
    at_bias = 5 * (D // 128)
    total = jnp.sum(bias_acc[...], 0, keepdims=True)
    for t in range((cols[0] + cols[1]) // 128):
        early_ref[at_bias + t : at_bias + t + 1, :] = total[:, t * 128 : (t + 1) * 128]
    at_row = at_bias + (cols[0] + cols[1]) // 128
    early_ref[at_row : at_row + 1, :] = vec_ref[6:7, :128]
    early_ref[at_row + 1 :, :] = jnp.zeros((early_ref.shape[0] - at_row - 1, 128), f32)
    for i in range(LINE):
        put_rest(i, "wait")
        sent_m(i)
        far_m(i, "wait_recv")
    for i in (LINE - 2, LINE - 1):
        pair_s(i, SENT)
        put_s(i, "wait")
    for i in range(LINE - 1) if near else (LINE - 2, LINE - 1):
        out_sends(i, SENT)
    for i in range(LINE):
        for step in (groups - 1 - i,) if near else range(1, groups):
            if step:
                for _, dst, (t, nb) in out_copies(i, step):
                    remote(dst, dst, gp_s.at[t, step, nb], gp_r.at[t, step, nb], sibling).wait_recv()
    for m in range(count):
        stage_one(m, SENT)
        for step in range(LINE):
            stage_two(m, step, SENT)
            if near:
                stage_three(m, step, SENT)
    for which in range(2):
        for q in range(3):
            row_send(which, q, SENT)
            to_sibling(which, q, SENT)


def gather_all(groups, weights, tokens, cotangent, vectors, biases, valid, turns):
    rows_own = weights[0].shape[0]
    seq_dev, slot_len, width = tokens.shape
    cols = tuple(w.shape[1] // LINE for w in weights)
    count = len(weights)
    block_rows = seq_dev * slot_len
    rows = LINE * block_rows
    f32, low = jnp.float32, jnp.bfloat16
    dma = pltpu.SemaphoreType.DMA
    peers = 3 if groups == 4 else groups
    out_widths = (D, D, cols[0], cols[1])
    pieces = (cols[2] + cols[3]) // 256
    feat = D // (2 * LINE)
    early_rows = -(-(5 * D + cols[0] + cols[1] + 128) // 1024) * 8
    return pl.pallas_call(
        partial(gather_kernel, groups, cols, seq_dev, slot_len),
        out_shape=[jax.ShapeDtypeStruct((rows, w), low) for w in out_widths]
        + [
            jax.ShapeDtypeStruct((LINE, block_rows, feat), low),
            jax.ShapeDtypeStruct((LINE, block_rows, feat), low),
            jax.ShapeDtypeStruct((LINE, slot_len, D), low),
            jax.ShapeDtypeStruct((LINE, rows_own, cols[2]), low),
            jax.ShapeDtypeStruct((LINE, rows_own, cols[3]), low),
            jax.ShapeDtypeStruct((groups - 1, LINE, rows_own, cols[2]), low),
            jax.ShapeDtypeStruct((groups - 1, LINE, rows_own, cols[3]), low),
            jax.ShapeDtypeStruct((early_rows, 128), f32),
        ],
        in_specs=[ANY] * (count + 2) + [VMEM] * 4,
        out_specs=[ANY] * 11 + [VMEM],
        scratch_shapes=[pltpu.VMEM((D, w), low) for w in cols]
        + [pltpu.VMEM((rows, D), low)] * 2
        + [
            pltpu.VMEM((rows, cols[0]), low),
            pltpu.VMEM((LINE * seq_dev, slot_len, slot_len), f32),
            pltpu.VMEM((rows, cols[2]), low),
            pltpu.VMEM((rows, cols[3]), low),
            pltpu.VMEM((rows, cols[1]), low),
            pltpu.VMEM((block_rows, D), low),
            pltpu.VMEM((2, block_rows, D), low),
            pltpu.VMEM((block_rows, D), low),
            pltpu.VMEM((2, 2, LINE, block_rows, feat), low),
            pltpu.VMEM((LINE, LINE, block_rows, feat), low),
            pltpu.VMEM((LINE, 2, block_rows, feat), low),
            pltpu.VMEM((LINE, slot_len, D), low),
            pltpu.VMEM((block_rows, cols[0]), f32),
            pltpu.VMEM((block_rows, cols[1]), f32),
            pltpu.VMEM((rows, 2), f32),
            pltpu.VMEM((5, 8, D), f32),
            pltpu.VMEM((8, cols[0] + cols[1]), f32),
            dma((count, LINE)),
            dma((count, LINE)),
            dma((count, LINE, peers)),
            dma((count, LINE, peers)),
            dma((count, LINE)),
            dma((count, LINE)),
            dma((2, 3)),
            dma((2, 3)),
            dma((2, 3)),
            dma((2, 3)),
            dma((count + 2, seq_dev)),
            dma(()),
            dma((2,)),
            dma((2, LINE)),
            dma((LINE,)),
            dma((LINE,)),
            dma((LINE,)),
            dma((LINE,)),
            dma((LINE, 2)),
            dma((LINE, 2)),
            dma((LINE,)),
            dma((LINE,)),
            dma((LINE,)),
            dma((LINE,)),
            dma((LINE, groups, pieces)),
            dma((LINE, groups, pieces)),
            dma((LINE, pieces)),
        ],
        compiler_params=pltpu.CompilerParams(
            collective_id=0, has_side_effects=True, vmem_limit_bytes=62 * 1024 * 1024
        ),
        name="gather_all",
    )(*weights, tokens, cotangent, vectors, biases, valid, turns)


def scatter_kernel(groups, cols, seq_dev, slot_len, rows_own, *refs):
    count = len(cols)
    f32, low = jnp.float32, jnp.bfloat16
    pick = refs[0]
    lefts_in = refs[1:3]
    rights_in = refs[3:5]
    near_ref, far_ref, s_ref = refs[5:8]
    done_own, done_got = refs[8:10], refs[10:12]
    early_ref = refs[12]
    mixed_ref, ssum_ref = refs[13:15]
    g_out = refs[15 : 15 + count]
    early_out, col_out, row_out = refs[15 + count : 18 + count]
    rest = refs[18 + count :]
    left_buf, right_a, right_b = rest[:3]
    g_own = rest[3 : 3 + count]
    g_got = rest[3 + count : 3 + 2 * count]
    (m_in, m_all, m_send, s_own, s_half, s_far, early_group, col_now, col_group, row_keep, row_turn) = rest[
        3 + 2 * count : 14 + 2 * count
    ]
    (here, half_s, half_r, far_s, far_r, fin_s, fin_r, mall_s, mall_r, mout_s, mout_r, gp_s, gp_r, gl_s, gl_r, eg_s,
     eg_r, el_s, el_r, es_s, es_r, cg_s, cg_r, cl_s, cl_r, cs_s, cs_r, rl_s, rl_r, keep_sem) = rest[14 + 2 * count :]
    me = Place(groups)
    c, g, k = me.line, me.group, me.core
    me.greet()
    sibling = me.at(c, g, me.other)
    feat = D // (2 * LINE)
    seqs = LINE * seq_dev
    rows = seqs * slot_len
    double = groups == 4
    sends = []

    def go(copy):
        copy.start()
        sends.append(copy)

    def to_group(step):
        return (g + step) % groups

    def from_group(step):
        return (g + groups - step) % groups

    def arrived(dst, send, recv):
        remote(dst, dst, send, recv, sibling).wait_recv()

    def add_rows(total, parts, count_rows, chunk):
        @pl.loop(0, count_rows // chunk)
        def body(i):
            at = pl.ds(pl.multiple_of(i * chunk, chunk), chunk)
            acc = parts[0](at)[...].astype(f32)
            for part in parts[1:]:
                acc = acc + part(at)[...].astype(f32)
            total(at)[...] = acc.astype(low)

    def load(src, dst, sem):
        copy = pltpu.make_async_copy(src, dst, sem)
        copy.start()
        return copy

    partner = c + 1 - 2 * (c % 2)
    beyond = (c + 2) % LINE
    for q, to in enumerate((partner, (partner + 2) % LINE)):
        go(remote(s_ref.at[to], s_half.at[q], half_s.at[q], half_r.at[q], me.at(partner, g, k)))
    got_m = [load(near_ref, m_in.at[0], here.at[10]), load(far_ref, m_in.at[1], here.at[11])]
    got_done = []
    for q in range(2):
        got_done.append(load(done_own[q], g_own[2 + q].at[:, 0], here.at[2 + 2 * q]))
        got_done.append(load(done_got[q], g_got[2 + q], here.at[3 + 2 * q]))
    got_two = load(lefts_in[1], left_buf.at[0], here.at[6])
    got_1 = load(rights_in[1], right_a, here.at[7])
    if double:
        got_one = load(lefts_in[0], left_buf.at[1], here.at[0])
        got_q = load(rights_in[0], right_b, here.at[1])
    got_s = [load(s_ref.at[c], s_own.at[0], here.at[8]), load(s_ref.at[beyond], s_own.at[1], here.at[9])]
    for step in range(1, groups):
        go(remote(early_ref, early_group.at[g], eg_s.at[step], eg_r.at[step], me.at(c, to_group(step), k)))
    early_group[g] = early_ref[...]

    per = 128 // rows_own

    def tile_products(m, left, right, tiles):
        lhs = turned([left[:, pl.ds(pl.multiple_of((l * groups + p) * rows_own, 128), 128)] for l, p in tiles])
        out = dot(lhs, right[...]).astype(low)
        for t, (l, p) in enumerate(tiles):
            for q in range(per):
                row = t * 128 + q * rows_own
                g_own[m][l, p + q] = out[row : row + rows_own]

    def send_group(m, step, act):
        to = to_group(step)
        copy = remote(
            g_own[m].at[:, to], g_got[m].at[step - 1], gp_s.at[m, step], gp_r.at[m, step], me.at(c, to, k)
        )
        getattr(copy, act)()

    across, beside, above = me.group_to(3), me.group_to(1), me.group_to(2)
    two_phase = groups == 4

    def phase_one(m, way, act):
        lines = pl.ds(0, 2) if way == 0 else pl.ds(2, 2)
        to = beside if way == 0 else above
        for q, block in enumerate((to, across)):
            copy = remote(
                g_own[m].at[lines, block], g_got[m].at[q, lines], gp_s.at[m, way * 2 + q], gp_r.at[m, way * 2 + q],
                me.at(c, to, k),
            )
            getattr(copy, act)()

    def phase_two(m, way, act):
        lines = pl.ds(0, 2) if way == 0 else pl.ds(2, 2)
        to = above if way == 0 else beside
        copy = remote(
            g_own[m].at[lines, to], g_got[m].at[2, lines], gp_s.at[m, 4 + way], gp_r.at[m, 4 + way], me.at(c, to, k)
        )
        getattr(copy, act)()

    def between_phases(m):
        for way in range(2):
            phase_one(m, way, "wait_recv")
            to = above if way == 0 else beside
            for line in (way * 2, way * 2 + 1):
                add_rows(
                    lambda at: g_own[m].at[line, to, at],
                    [lambda at: g_own[m].at[line, to, at], lambda at: g_got[m].at[1, line, at]],
                    rows_own,
                    16,
                )
            phase_two(m, way, "start")

    def products(left, pairs):
        if two_phase:

            @pl.loop(0, groups)
            def body(t):
                flip_x, flip_y = (t + 1) % 2, (3 - t) // 2 * (1 - t // 3)
                to = (g // 2 + flip_y) % 2 * 2 + (g % 2 + flip_x) % 2
                for m, right in pairs:
                    tile_products(m, left, right, [(l, to) for l in range(LINE)])
                    for way in range(2):

                        @pl.when(t == 2 - way)
                        def _():
                            phase_one(m, way, "start")
        else:

            @pl.loop(0, LINE)
            def body(l):
                for m, right in pairs:
                    tile_products(m, left, right, [(l, t * per) for t in range(4)])

            for m, _ in pairs:
                for step in range(1, groups):
                    send_group(m, step, "start")

    def sum_groups(m, first):
        got = range(groups - 1)
        if m < 2 and two_phase:
            for way in range(2):
                phase_two(m, way, "wait_recv")
            got = (0, 2)
        elif m < 2:
            for step in range(1, groups):
                arrived(g_got[m].at[step - 1], gp_s.at[m, step], gp_r.at[m, step])
        mine = g if m < 2 else 0
        width = pl.ds(pl.multiple_of(c * cols[m], 128), cols[m])
        total = jnp.zeros((8, cols[m]), f32)
        for step in (2, 1, 3, 0):
            line = me.line_to(step)

            def body(i, carry, line=line):
                at = pl.ds(pl.multiple_of(i * 16, 16), 16)
                acc = g_own[m][line, mine, at, :].astype(f32)
                for p in got:
                    acc = acc + g_got[m][p, line, at, :].astype(f32)
                g_own[m][line, mine, at, :] = acc.astype(low)
                square = acc * acc + eps_second
                row_keep[line, at, m : m + 1] = jnp.sum(square, 1, keepdims=True)
                return carry + square[:8] + square[8:]

            total = lax.fori_loop(0, rows_own // 16, body, total)
            src = g_own[m].at[line, mine]
            if step:
                go(remote(src, g_out[m].at[:, width], gl_s.at[m, step], gl_r.at[m, step], me.at(line, g, k)))
            else:
                keep.append(load(src, g_out[m].at[:, width], keep_sem.at[2 + m]))
        total = jnp.sum(total, 0, keepdims=True)
        for t in range(cols[m] // 128):
            col_now[first + t : first + t + 1, :] = total[:, t * 128 : (t + 1) * 128]

    keep = []
    row_keep[...] = jnp.zeros_like(row_keep)
    firsts = []
    edge = 0
    for m in range(count):
        firsts.append(edge)
        edge += cols[m] // 128
    for copy in got_m:
        copy.wait()
    ours = pl.ds(g * seqs, seqs)
    for s in range(seqs):
        add_rows(
            lambda at: m_all.at[g * seqs + s, at],
            [lambda at: m_in.at[0, s, at], lambda at: m_in.at[1, s, at]],
            slot_len,
            64,
        )
    for step in range(1, groups):
        go(remote(m_all.at[ours], m_all.at[ours], mall_s.at[step], mall_r.at[step], me.at(c, to_group(step), k)))

    for copy in got_done:
        copy.wait()
    sum_groups(3, firsts[3])
    sum_groups(2, firsts[2])
    for step in range(1, groups):
        arrived(early_group.at[from_group(step)], eg_s.at[step], eg_r.at[step])
    acc = early_group[0]
    for i in range(1, groups):
        acc = acc + early_group[i]
    early_out[k, c] = acc
    for step in range(1, LINE):
        go(remote(early_out.at[k, c], early_out.at[k, c], el_s.at[step], el_r.at[step], me.at(me.line_to(step), g, k)))

    got_two.wait()
    got_1.wait()
    products(left_buf.at[0], ((1, right_a),))
    if not double:
        got_one = load(lefts_in[0], left_buf.at[0], here.at[0])
        got_q = load(rights_in[0], right_b, here.at[1])

    for q in range(2):
        got_s[q].wait()
        arrived(s_half.at[q], half_s.at[q], half_r.at[q])
        add_rows(
            lambda at: s_own.at[q, at], [lambda at: s_own.at[q, at], lambda at: s_half.at[q, at]], slot_len, 16
        )
    go(remote(s_own.at[1], s_far, far_s, far_r, me.at(beyond, g, k)))

    got_one.wait()
    got_q.wait()
    products(left_buf.at[1 if double else 0], ((0, right_b),))
    if two_phase:
        between_phases(1)
    if two_phase:
        between_phases(0)
    sum_groups(1, firsts[1])
    for step in range(1, groups):
        arrived(m_all.at[pl.ds(from_group(step) * seqs, seqs)], mall_s.at[step], mall_r.at[step])
    mixed_cols = pl.ds(pl.multiple_of((c * 2 + k) * feat, 128), feat)
    for step in (1, 2, 3, 0):
        line = me.line_to(step)
        for s in range(seq_dev):
            m_send[line, s] = m_all[pick[line * seq_dev + s]]
        where = mixed_ref.at[:, :, mixed_cols]
        if step:
            go(remote(m_send.at[line], where, mout_s.at[0, step], mout_r.at[0, step], me.at(line, g, k)))
        else:
            keep.append(load(m_send.at[line], where, keep_sem.at[1]))
            go(remote(m_send.at[line], where, mout_s.at[1, 0], mout_r.at[1, 0], sibling))

    sum_groups(0, firsts[0])

    for step in range(1, groups):
        go(remote(col_now, col_group.at[g], cg_s.at[step], cg_r.at[step], me.at(c, to_group(step), k)))
    col_group[g] = col_now[...]
    for step in (1, 2, 3, 0):
        line = me.line_to(step)
        row_turn[line] = jnp.transpose(row_keep[line])[:8]
        if step:
            go(remote(row_turn.at[line], row_out.at[k, c], rl_s.at[0, step], rl_r.at[0, step], me.at(line, g, k)))
        else:
            row_out[k, c] = row_turn[line]
        go(remote(row_turn.at[line], row_out.at[k, c], rl_s.at[1, step], rl_r.at[1, step], me.at(line, g, me.other)))
    for step in range(1, groups):
        arrived(col_group.at[from_group(step)], cg_s.at[step], cg_r.at[step])
    acc = col_group[0]
    for i in range(1, groups):
        acc = acc + col_group[i]
    col_out[k, c] = acc
    for step in range(1, LINE):
        go(remote(col_out.at[k, c], col_out.at[k, c], cl_s.at[step], cl_r.at[step], me.at(me.line_to(step), g, k)))
    arrived(s_far, far_s, far_r)
    add_rows(lambda at: s_own.at[0, at], [lambda at: s_own.at[0, at], lambda at: s_far.at[at]], slot_len, 16)
    go(remote(s_own.at[0], ssum_ref.at[k], fin_s, fin_r, sibling))
    keep.append(load(s_own.at[0], ssum_ref.at[k], keep_sem.at[0]))
    for step in range(1, LINE):
        arrived(early_out.at[k, me.line_from(step)], el_s.at[step], el_r.at[step])
    go(remote(early_out.at[k], early_out.at[k], es_s, es_r, sibling))
    for step in range(1, LINE):
        arrived(col_out.at[k, me.line_from(step)], cl_s.at[step], cl_r.at[step])
    go(remote(col_out.at[k], col_out.at[k], cs_s, cs_r, sibling))

    for step in range(1, LINE):
        where = mixed_ref.at[:, :, pl.ds(pl.multiple_of((me.line_from(step) * 2 + k) * feat, 128), feat)]
        arrived(where, mout_s.at[0, step], mout_r.at[0, step])
        go(remote(where, where, mout_s.at[1, step], mout_r.at[1, step], sibling))
    for m in range(count):
        for step in range(1, LINE):
            dst = g_out[m].at[:, pl.ds(pl.multiple_of(me.line_from(step) * cols[m], 128), cols[m])]
            arrived(dst, gl_s.at[m, step], gl_r.at[m, step])
    for step in range(LINE):
        source = me.line_from(step)
        dst = mixed_ref.at[:, :, pl.ds(pl.multiple_of((source * 2 + me.other) * feat, 128), feat)]
        arrived(dst, mout_s.at[1, step], mout_r.at[1, step])
        for core, way in ((k, 0), (me.other, 1)):
            if step or way:
                arrived(row_out.at[core, source], rl_s.at[way, step], rl_r.at[way, step])
    arrived(ssum_ref.at[me.other], fin_s, fin_r)
    arrived(early_out.at[me.other], es_s, es_r)
    arrived(col_out.at[me.other], cs_s, cs_r)
    for copy in sends:
        copy.wait_send()
    for m in range(2):
        if two_phase:
            for way in range(2):
                phase_one(m, way, "wait_send")
                phase_two(m, way, "wait_send")
        else:
            for step in range(1, groups):
                send_group(m, step, "wait_send")
    for copy in keep:
        copy.wait()


def scatter_all(groups, cols, seq_dev, rows_own, pick, lefts, rights, between):
    near, far, s_pair, *done, early = between
    slot_len = s_pair.shape[1]
    rows = lefts[0].shape[0]
    count = len(cols)
    feat = D // (2 * LINE)
    seqs = LINE * seq_dev
    blocks = (seqs, slot_len, feat)
    dma = pltpu.SemaphoreType.DMA
    f32, low = jnp.float32, jnp.bfloat16
    col_rows = sum(cols) // 128
    return pl.pallas_call(
        partial(scatter_kernel, groups, cols, seq_dev, slot_len, rows_own),
        out_shape=[
            jax.ShapeDtypeStruct((seq_dev, slot_len, D), low),
            jax.ShapeDtypeStruct((seq_dev, slot_len, D), low),
        ]
        + [jax.ShapeDtypeStruct((rows_own, LINE * width), low) for width in cols]
        + [
            jax.ShapeDtypeStruct((2, LINE) + early.shape, f32),
            jax.ShapeDtypeStruct((2, LINE, col_rows, 128), f32),
            jax.ShapeDtypeStruct((2, LINE, 8, 128), f32),
        ],
        in_specs=[SMEM] + [ANY] * 11 + [VMEM],
        out_specs=[ANY] * (2 + count) + [VMEM] * 3,
        scratch_shapes=[
            pltpu.VMEM((2 if groups == 4 else 1, rows, D), low),
            pltpu.VMEM((rows, cols[1]), low),
            pltpu.VMEM((rows, cols[0]), low),
        ]
        + [pltpu.VMEM((LINE, groups if m < 2 else 1, rows_own, width), low) for m, width in enumerate(cols)]
        + [pltpu.VMEM((groups - 1, LINE, rows_own, width), low) for width in cols]
        + [
            pltpu.VMEM((2, seqs, slot_len, feat), low),
            pltpu.VMEM((groups * seqs, slot_len, feat), low),
            pltpu.VMEM((LINE, seq_dev, slot_len, feat), low),
            pltpu.VMEM((2, slot_len, D), low),
            pltpu.VMEM((2, slot_len, D), low),
            pltpu.VMEM((slot_len, D), low),
            pltpu.VMEM((groups,) + early.shape, f32),
            pltpu.VMEM((col_rows, 128), f32),
            pltpu.VMEM((groups, col_rows, 128), f32),
            pltpu.VMEM((LINE, 128, 128), f32),
            pltpu.VMEM((LINE, 8, 128), f32),
            dma((12,)),
            dma((2,)),
            dma((2,)),
            dma(()),
            dma(()),
            dma(()),
            dma(()),
            dma((groups,)),
            dma((groups,)),
            dma((2, LINE)),
            dma((2, LINE)),
            dma((count, max(groups, 6))),
            dma((count, max(groups, 6))),
            dma((count, LINE)),
            dma((count, LINE)),
            dma((groups,)),
            dma((groups,)),
            dma((LINE,)),
            dma((LINE,)),
            dma(()),
            dma(()),
            dma((groups,)),
            dma((groups,)),
            dma((LINE,)),
            dma((LINE,)),
            dma(()),
            dma(()),
            dma((2, LINE)),
            dma((2, LINE)),
            dma((2 + count,)),
        ],
        compiler_params=pltpu.CompilerParams(
            collective_id=1, has_side_effects=True, vmem_limit_bytes=62 * 1024 * 1024
        ),
        name="scatter_all",
    )(pick, *lefts, *rights, near.reshape(blocks), far.reshape(blocks), s_pair, *done, early)


def prepare_kernel(groups, cols, seq_dev, slot_len, *refs):
    (spot, lengths, permutation, wq, w1, wd, w2, vectors, biases, rows_state) = refs[:10]
    lows = refs[10:14]
    valid, own_valid, all_vectors, all_biases, pick = refs[14:]
    f32 = jnp.float32
    for src, dst in zip((wq, w1, wd, w2), lows):
        dst[...] = src[...].astype(jnp.bfloat16)

    @pl.when(pl.program_id(0) == 0)
    def _():
        data, core = spot[0], spot[1]
        line, group = data // groups, data % groups
        times = lax.broadcasted_iota(jnp.int32, (slot_len, 1), 0)
        for place in range(LINE):
            for s in range(seq_dev):
                slot = (place * groups + group) * seq_dev + s
                at = place * seq_dev + s
                valid[at * slot_len : (at + 1) * slot_len, :] = jnp.where(times < lengths[slot], 1.0, 0.0)
                source = permutation[slot]
                chip = source // seq_dev
                pick[at] = (chip % groups) * (LINE * seq_dev) + (chip // groups) * seq_dev + source % seq_dev
        for s in range(seq_dev):
            own_valid[s * slot_len : (s + 1) * slot_len, :] = jnp.where(
                times < lengths[data * seq_dev + s], 1.0, 0.0
            )
        all_vectors[0:6, :] = vectors[...]
        all_vectors[6:8, :] = jnp.zeros((2, D), f32)
        lane = lax.broadcasted_iota(jnp.int32, (1, 128), 1)
        total = jnp.zeros((1, 128), f32)
        for m in range(4):
            total = total + jnp.where(lane == m, jnp.sum(rows_state[m : m + 1, :], 1, keepdims=True), 0.0)
        all_vectors[6:7, 0:128] = jnp.where(core == 0, total, jnp.zeros_like(total))
        all_biases[:, : cols[0]] = biases[:, pl.ds(pl.multiple_of(line * cols[0], 128), cols[0])]
        all_biases[:, cols[0] :] = biases[:, pl.ds(pl.multiple_of(LINE * cols[0] + line * cols[1], 128), cols[1])]


def prepare(groups, seq_dev, slot_len, spot, lengths, permutation, weights, vectors, biases, rows_state):
    f32, low = jnp.float32, jnp.bfloat16
    rows_own = weights[0].shape[0]
    cols = tuple(w.shape[1] // LINE for w in weights)
    tall = 32
    steps = rows_own // tall
    seqs = LINE * seq_dev

    def whole(shape):
        return pl.BlockSpec(shape, lambda i: (0,) * len(shape))

    blocks = [pl.BlockSpec((tall, w.shape[1]), lambda i: (i, 0)) for w in weights]
    return pl.pallas_call(
        partial(prepare_kernel, groups, cols, seq_dev, slot_len),
        grid=(steps,),
        out_shape=[jax.ShapeDtypeStruct(w.shape, low) for w in weights]
        + [
            jax.ShapeDtypeStruct((seqs * slot_len, 1), f32),
            jax.ShapeDtypeStruct((seq_dev * slot_len, 1), f32),
            jax.ShapeDtypeStruct((8, D), f32),
            jax.ShapeDtypeStruct((1, cols[0] + cols[1]), f32),
            jax.ShapeDtypeStruct((seqs,), jnp.int32),
        ],
        in_specs=[SMEM] * 3 + blocks + [whole(vectors.shape), whole(biases.shape), whole(rows_state.shape)],
        out_specs=blocks
        + [
            whole((seqs * slot_len, 1)),
            whole((seq_dev * slot_len, 1)),
            whole((8, D)),
            whole((1, cols[0] + cols[1])),
            SMEM,
        ],
        compiler_params=pltpu.CompilerParams(vmem_limit_bytes=60 * 1024 * 1024),
        name="prepare",
    )(spot, lengths, permutation, *weights, vectors, biases, rows_state)


def finish_kernel(order, cols, rows_own, *refs):
    f32, low = jnp.float32, jnp.bfloat16
    spot = refs[0]
    g_in, w_in = refs[1:5], refs[5:9]
    (s_sum, tokens, cotangent, own_valid, early, col_all, row_all, row_state, col_state, vectors, moments, biases,
     bias_moments) = refs[9:22]
    grads, news, copies = refs[22:26], refs[26:30], refs[30:34]
    (grad_tokens, row_new, col_new, norm_total, norm_moment_new, norm_new, bias_total, bias_moment_new,
     bias_new) = refs[34:43]
    row_factor, col_factor, turn = refs[43:]
    step = pl.program_id(0)
    widths = [w.shape[1] for w in w_in]
    edges = [sum(widths[:i]) for i in range(5)]
    tiles = D // 128

    @pl.when(step == 0)
    def _():
        core = spot[1]
        both = early[0, 0]
        rows_all = row_all[0, 0]
        mass_all = col_all[0, 0]
        for n in range(1, 2 * LINE):
            both = both + early[n // LINE, n % LINE]
            rows_all = rows_all + row_all[n // LINE, n % LINE]
            mass_all = mass_all + col_all[n // LINE, n % LINE]
        for r in range(6):
            for t in range(tiles):
                at = min(r, 4) * tiles + t
                norm_total[r : r + 1, t * 128 : (t + 1) * 128] = both[at : at + 1]
        grad = norm_total[...]
        moment = decay * moments[...] + (1.0 - decay) * (grad * grad + eps_second)
        norm_moment_new[...] = moment
        norm_new[...] = vectors[...] - rate_norm * grad * lax.rsqrt(moment)
        first = 5 * tiles
        parts = ((cols[0] // 128, 0), (cols[1] // 128, LINE * cols[0]))
        for line in range(LINE):
            at = first
            for count, base in parts:
                for t in range(count):
                    to = base + (line * count + t) * 128
                    bias_total[:, to : to + 128] = early[core, line, at : at + 1, :]
                    at += 1
        grad = bias_total[...]
        moment = decay * bias_moments[...] + (1.0 - decay) * (grad * grad + eps_second)
        bias_moment_new[...] = moment
        bias_new[...] = biases[...] - rate_vector * grad * lax.rsqrt(moment)
        at_row = first + (cols[0] + cols[1]) // 128
        full_cols = (3.0 * D, 1.0 * D, 1.0 * FF, 1.0 * FF)
        rates = (
            rate_scale / math.sqrt(D),
            rate_scale / math.sqrt(D // 8),
            rate_scale / math.sqrt(D),
            rate_scale / math.sqrt(FF),
        )
        turn[...] = jnp.zeros_like(turn)
        at = 0
        for m, i in enumerate(order):
            count = cols[m] // 128
            new = decay * row_state[i : i + 1, :] + (1.0 - decay) * (rows_all[m : m + 1, :rows_own] / full_cols[i])
            row_new[i : i + 1, :] = new
            mass = jnp.sum(jnp.sum(mass_all[at : at + count], 1, keepdims=True), 0, keepdims=True)
            mean = (decay * both[at_row : at_row + 1, i : i + 1] + (1.0 - decay) * (mass / full_cols[i])) / D
            turn[i : i + 1, :rows_own] = rates[i] * lax.rsqrt(new / mean)
            for line in range(LINE):
                for t in range(count):
                    to = edges[i] + (line * count + t) * 128
                    col_new[:, to : to + 128] = col_all[core, line, at + t : at + t + 1, :]
            at += count
        row_factor[...] = jnp.transpose(turn[...])
        new = decay * col_state[...] + (1.0 - decay) * (col_new[...] / D)
        col_new[...] = new
        col_factor[...] = lax.rsqrt(new)

    tall = w_in[0].shape[0]
    for half in range(tall // 16):
        rows = pl.ds(pl.multiple_of(step * tall + half * 16, 16), 16)
        part = slice(half * 16, half * 16 + 16)
        for i in range(4):
            factor = row_factor[rows, i : i + 1]
            for n in range(widths[i] // 1024):
                at = slice(n * 1024, (n + 1) * 1024)
                grad = g_in[i][part, at].astype(f32)
                new = w_in[i][part, at] - grad * factor * col_factor[:, edges[i] + n * 1024 : edges[i] + (n + 1) * 1024]
                grads[i][part, at] = grad
                news[i][part, at] = new
                copies[i][part, at] = new.astype(low)

    @pl.loop(0, tokens.shape[0] // 16)
    def body(j):
        at = pl.ds(pl.multiple_of(j * 16, 16), 16)
        x = tokens[at, :].astype(f32)
        centre = x - jnp.mean(x, -1, keepdims=True)
        scale = lax.rsqrt(jnp.mean(centre * centre, -1, keepdims=True) + eps_norm)
        unit = centre * scale
        flow = s_sum[at, :].astype(f32)
        through = flow - jnp.mean(flow, -1, keepdims=True) - unit * jnp.mean(flow * unit, -1, keepdims=True)
        grad_tokens[at, :] = (cotangent[at, :].astype(f32) * own_valid[at, :] + scale * through).astype(low)


def finish(order, spot, grads, weights, s_sum, tokens, cotangent, own_valid, *small):
    f32, low = jnp.float32, jnp.bfloat16
    rows_own = weights[0].shape[0]
    tall = 32
    steps = rows_own // tall
    cols = tuple(weights[i].shape[1] // LINE for i in order)
    rows = tokens.shape[0]
    row_state, col_state, vectors, _, biases = small[3:8]

    def whole(shape):
        return pl.BlockSpec(shape, lambda i: (0,) * len(shape))

    blocks = [pl.BlockSpec((tall, w.shape[1]), lambda i: (i, 0)) for w in weights]
    acts = pl.BlockSpec((rows // steps, D), lambda i: (i, 0))
    small_out = [row_state.shape, col_state.shape] + [vectors.shape] * 3 + [biases.shape] * 3
    return pl.pallas_call(
        partial(finish_kernel, order, cols, rows_own),
        grid=(steps,),
        out_shape=[jax.ShapeDtypeStruct(w.shape, f32) for w in weights] * 2
        + [jax.ShapeDtypeStruct(w.shape, low) for w in weights]
        + [jax.ShapeDtypeStruct((rows, D), low)]
        + [jax.ShapeDtypeStruct(shape, f32) for shape in small_out],
        in_specs=[SMEM]
        + blocks * 2
        + [acts] * 3
        + [pl.BlockSpec((rows // steps, 1), lambda i: (i, 0))]
        + [whole(a.shape) for a in small],
        out_specs=blocks * 3 + [acts] + [whole(shape) for shape in small_out],
        scratch_shapes=[
            pltpu.VMEM((128, 128), f32),
            pltpu.VMEM(col_state.shape, f32),
            pltpu.VMEM((128, 128), f32),
        ],
        compiler_params=pltpu.CompilerParams(vmem_limit_bytes=60 * 1024 * 1024),
        name="finish",
    )(spot, *grads, *weights, s_sum, tokens, cotangent, own_valid, *small)


def per_device(
    tokens,
    cotangent,
    lengths,
    permutation,
    w_qkv,
    w_dense,
    w_fc1,
    w_fc2,
    norm_vectors,
    split_biases,
    row_state,
    col_state,
    norm_moment,
    bias_moment,
):
    groups = lax.axis_size("dp") // LINE
    seq_dev, slot_len, width = tokens.shape
    rows_own = w_qkv.shape[0]
    head_dim = D // HEADS
    weights = (w_qkv, w_dense, w_fc1, w_fc2)
    order = (0, 2, 1, 3)
    cols = tuple(weights[i].shape[1] // LINE for i in order)
    spot = jnp.stack([lax.axis_index("dp"), lax.axis_index("tensor")]).astype(jnp.int32)
    *lows, valid, own_valid, vectors, biases, pick = prepare(
        groups, seq_dev, slot_len, spot, lengths, permutation, [weights[i] for i in order], norm_vectors,
        split_biases, row_state,
    )
    turns = jnp.asarray(turn_tables(slot_len, head_dim // 4, head_dim // 2))
    norm_one, norm_two, qkv_grad, pre_grad, *between = gather_all(
        groups, lows, tokens, cotangent, vectors, biases, valid, turns
    )
    mixed, s_sum, *outs = scatter_all(
        groups, cols, seq_dev, rows_own, pick, (norm_one, norm_two), (qkv_grad, pre_grad), between
    )
    grads = [outs[order.index(i)] for i in range(4)]
    early_all, col_all, row_all = outs[4:]
    results = finish(
        order, spot, grads, weights, s_sum.reshape(-1, width), tokens.reshape(-1, width),
        cotangent.reshape(-1, width), own_valid, early_all, col_all, row_all, row_state, col_state, norm_vectors,
        norm_moment, split_biases, bias_moment,
    )
    return (mixed, results[12].reshape(tokens.shape), *results[:12], *results[13:])


def solution(mesh):
    halves = P("dp", "tensor")
    split = P("tensor", None)
    in_specs = (
        P("dp", None, None),
        P("dp", None, None),
        P(),
        P(),
        halves,
        halves,
        halves,
        halves,
        P(),
        split,
        P(None, "dp"),
        split,
        P(),
        split,
    )
    out_specs = (
        (P("dp", None, None),) * 2
        + (halves,) * 12
        + (P(None, "dp"), split)
        + (P(),) * 3
        + (split,) * 3
    )
    return jax.shard_map(
        per_device, mesh=mesh, in_specs=in_specs, out_specs=out_specs, check_vma=False
    )
```

```python
from functools import partial
import math

import jax
import jax.numpy as jnp
import numpy as np
from jax import lax
from jax.experimental import pallas as pl
from jax.experimental.pallas import tpu as pltpu
from jax.sharding import PartitionSpec as P

D = 2048
FF = 8192
HEADS = 8
LINE = 4

eps_norm = 1e-05
eps_second = 1e-30
decay = 0.5
rate_scale = 1.0
rate_norm = 0.5
rate_vector = 0.05
neg_large = -1e30

MESH = pl.DeviceIdType.MESH
ANY = pl.BlockSpec(memory_space=pl.ANY)
VMEM = pl.BlockSpec(memory_space=pltpu.VMEM)
SMEM = pl.BlockSpec(memory_space=pltpu.SMEM)


def turn_tables(slot_len, rot_dims, width):
    half = rot_dims // 2
    freq = np.float32(10000.0) ** (np.float32(-2.0) * np.arange(half, dtype=np.float32) / np.float32(rot_dims))
    angle = np.arange(slot_len, dtype=np.float32)[:, None] * freq[None, :].astype(np.float32)
    tables = np.zeros((3, slot_len, width), np.float32)
    tables[0] = 1.0
    tables[0, :, :half] = tables[0, :, half:rot_dims] = np.cos(angle)
    tables[1, :, :half] = tables[2, :, half:rot_dims] = np.sin(angle)
    return tables


class Place:
    def __init__(self, groups):
        self.groups = groups
        data = lax.axis_index("dp")
        self.core = lax.axis_index("tensor")
        self.other = 1 - self.core
        self.line = data // groups
        self.group = data % groups

    def at(self, line, group, core):
        return (line * self.groups + group, core)

    def line_to(self, step):
        return (self.line + step) % LINE

    def line_from(self, step):
        return (self.line + LINE - step) % LINE

    def group_to(self, step):
        g = self.group
        if self.groups == 4:
            if step == 1:
                return g + 1 - 2 * (g % 2)
            if step == 2:
                return (g + 2) % 4
            return 3 - g
        return (g + step) % self.groups

    def group_from(self, step):
        if self.groups == 4:
            return self.group_to(step)
        return (self.group + self.groups - step) % self.groups

    def greet(self):
        barrier = pltpu.get_barrier_semaphore()
        count = 0
        for step in range(1, LINE):
            for core in (self.core, self.other):
                pl.semaphore_signal(
                    barrier, inc=1, device_id=self.at(self.line_to(step), self.group, core), device_id_type=MESH
                )
                count += 1
        for step in range(1, self.groups):
            pl.semaphore_signal(
                barrier, inc=1, device_id=self.at(self.line, self.group_to(step), self.core), device_id_type=MESH
            )
            count += 1
        pl.semaphore_signal(
            barrier, inc=1, device_id=self.at(self.line, self.group, self.other), device_id_type=MESH
        )
        pl.semaphore_wait(barrier, count + 1)


def remote(src, dst, send, recv, device):
    return pltpu.make_async_remote_copy(
        src_ref=src, dst_ref=dst, send_sem=send, recv_sem=recv, device_id=device, device_id_type=MESH
    )


def dot(left, right):
    return jnp.dot(left, right, preferred_element_type=jnp.float32)


def turned(blocks):
    eye = lax.broadcasted_iota(jnp.int32, (256, 256), 0) == lax.broadcasted_iota(jnp.int32, (256, 256), 1)
    eye = jnp.where(eye, 1.0, 0.0).astype(jnp.bfloat16)
    parts = []
    for n in range(0, len(blocks), 2):
        pair = jnp.concatenate(blocks[n : n + 2], 1)
        part = lax.dot_general(eye, pair, (((1,), (1,)), ((), ())), preferred_element_type=jnp.float32)
        parts.append(part.astype(jnp.bfloat16))
    return jnp.concatenate(parts, 0)


def gather_kernel(groups, cols, seq_dev, slot_len, *refs):
    count = len(cols)
    f32, low = jnp.float32, jnp.bfloat16
    w_in = refs[:count]
    acts_in = refs[count : count + 2]
    vec_ref, bias_ref, valid_ref, turn_ref = refs[count + 2 : count + 6]
    outs = refs[count + 6 : count + 18]
    (n1_out, n2_out, qg_out, pg_out, near_out, far_out, s_out, gd_own, g2_own, gd_got, g2_got, early_ref) = outs
    rest = refs[count + 18 :]
    w_out = rest[:count]
    acts_out = rest[count : count + 2]
    (qkv_keep, prob_keep, attn_keep, hid_keep, pg_keep, one_buf, two_buf, back_buf, m_buf, m_got, m_half, s_got,
     qkv_now, pre_now, stat_keep, norm_acc, bias_acc) = rest[count + 2 : count + 19]
    (one_s, one_r, two_s, two_r, three_s, three_r, row_s, row_r, sib_s, sib_r, here, out_a, out_b,
     out_d, msib_s, msib_r, ssib_s, ssib_r, half_s, half_r, far_s, far_r, near_sem, s_here, gp_s, gp_r,
     g_here) = rest[count + 19 :]
    me = Place(groups)
    c, g, k = me.line, me.group, me.core
    me.greet()
    sibling = me.at(c, g, me.other)
    rows_own = w_in[0].shape[0]
    block_rows = seq_dev * slot_len
    near = groups == 4
    START, SENT = "start", "wait_send"

    def block(ref, line, width):
        return ref.at[:, pl.ds(pl.multiple_of(line * width, 128), width)]

    def place(m, line, group):
        return w_out[m].at[pl.ds(pl.multiple_of((line * groups + group) * rows_own, 32), rows_own)]

    def rows_of(which, line, core):
        return acts_out[which].at[pl.ds(pl.multiple_of((line * seq_dev + core) * slot_len, 32), slot_len)]

    partner = c + 1 - 2 * (c % 2)
    beyond = (c + 2) % LINE

    def row_send(which, q, act):
        origin = beyond if q == 2 else c
        copy = remote(
            rows_of(which, beyond, k) if q == 2 else acts_in[which].at[k],
            rows_of(which, origin, k),
            row_s.at[which, q],
            row_r.at[which, q],
            me.at(beyond if q == 1 else partner, g, k),
        )
        getattr(copy, act)()

    def row_origin(q):
        return (partner, beyond, (partner + 2) % LINE)[q]

    def to_sibling(which, q, act):
        rows = rows_of(which, row_origin(q), k)
        copy = remote(rows, rows, sib_s.at[which, q], sib_r.at[which, q], sibling)
        getattr(copy, act)()

    def pass_on(which, q):
        rows = rows_of(which, row_origin(q), k)
        remote(rows, rows, row_s.at[which, q], row_r.at[which, q], sibling).wait_recv()
        if q == 1:
            row_send(which, 2, START)
        to_sibling(which, q, START)

    def arrive_sibling(which):
        for q in range(3):
            rows = rows_of(which, row_origin(q), me.other)
            remote(rows, rows, sib_s.at[which, q], sib_r.at[which, q], sibling).wait_recv()

    def local_acts(which, act):
        for s in range(seq_dev):
            copy = pltpu.make_async_copy(acts_in[which].at[s], rows_of(which, c, s), here.at[count + which, s])
            getattr(copy, act)()

    def local_weight(m, act):
        copy = pltpu.make_async_copy(block(w_in[m], c, cols[m]), place(m, c, g), here.at[m, 0])
        getattr(copy, act)()

    def stage_one(m, act):
        for step in range(1, LINE):
            to = me.line_to(step)
            copy = remote(
                block(w_in[m], to, cols[m]),
                place(m, c, g),
                one_s.at[m, step],
                one_r.at[m, step],
                me.at(to, g, k),
            )
            getattr(copy, act)()

    def stage_two(m, step, act):
        where = place(m, me.line_from(step), g)
        src = block(w_in[m], c, cols[m]) if step == 0 else where
        for peer in range(1, 3 if near else groups):
            copy = remote(
                src, where, two_s.at[m, step, peer], two_r.at[m, step, peer], me.at(c, me.group_to(peer), k)
            )
            getattr(copy, act)()

    def first_half(m):
        for step in range(1, LINE):
            dst = place(m, me.line_from(step), g)
            remote(dst, dst, one_s.at[m, step], one_r.at[m, step], sibling).wait_recv()
            stage_two(m, step, START)

    def wait_two(m, step, peer):
        dst = place(m, me.line_from(step), me.group_from(peer))
        remote(dst, dst, two_s.at[m, step, peer], two_r.at[m, step, peer], sibling).wait_recv()

    def stage_three(m, step, act):
        source, target = (1, 2) if step % 2 == 0 else (2, 1)
        where = place(m, me.line_from(step), me.group_to(source))
        copy = remote(where, where, three_s.at[m, step], three_r.at[m, step], me.at(c, me.group_to(target), k))
        getattr(copy, act)()

    def relay(m):
        for step in range(LINE):
            for peer in range(1, 3 if near else groups):
                wait_two(m, step, peer)
            if near:
                stage_three(m, step, START)

    def last(m):
        if near:
            for step in range(LINE):
                dst = place(m, me.line_from(step), me.group_to(3))
                remote(dst, dst, three_s.at[m, step], three_r.at[m, step], sibling).wait_recv()

    row_send(0, 1, START)
    row_send(0, 0, START)
    for m in (0, 1):
        stage_one(m, START)
        stage_two(m, 0, START)
    local_acts(0, START)
    local_weight(0, START)
    local_weight(1, START)
    norm_acc[...] = jnp.zeros_like(norm_acc)
    bias_acc[...] = jnp.zeros_like(bias_acc)
    first_half(0)
    pass_on(0, 1)
    for m in (2, 3):
        stage_one(m, START)
        stage_two(m, 0, START)
    local_acts(1, START)
    local_weight(2, START)
    local_weight(3, START)
    pass_on(0, 0)
    first_half(1)
    row_send(1, 1, START)
    row_send(1, 0, START)
    relay(0)
    pass_on(0, 2)
    relay(1)
    local_acts(0, "wait")
    local_weight(0, "wait")
    local_weight(1, "wait")
    last(0)
    last(1)
    arrive_sibling(0)

    wq, w1, wd, w2 = w_out
    x_all, ct_all = acts_out
    head = cols[0] // 3
    half = head // 2
    chunk = 64
    wide = 512
    ways = D // wide
    root = math.sqrt(head)
    causal = lax.broadcasted_iota(jnp.int32, (slot_len, slot_len), 0) >= lax.broadcasted_iota(
        jnp.int32, (slot_len, slot_len), 1
    )

    def turn(v, sign):
        left = pltpu.roll(v, half - 32, 1)
        right = pltpu.roll(v, 32, 1)
        if sign > 0:
            return v * turn_ref[0] - left * turn_ref[1] + right * turn_ref[2]
        return v * turn_ref[0] + left * turn_ref[1] - right * turn_ref[2]

    def contract(left, right, dims):
        return lax.dot_general(left, right, ((dims[0], dims[1]), ((), ())), preferred_element_type=f32)

    def put_one(i, line, act):
        rows = pl.ds(pl.multiple_of(line * block_rows, 128), block_rows)
        getattr(pltpu.make_async_copy(one_buf, n1_out.at[rows], out_a), act)()
        getattr(pltpu.make_async_copy(two_buf.at[0], n2_out.at[rows], out_b.at[0]), act)()

    @pl.loop(0, LINE)
    def forward(i):
        line = (c + i) % LINE
        base = pl.multiple_of(line * block_rows, 128)

        @pl.when(i == 0)
        def _():
            first_half(2)
            first_half(3)

        @pl.when(i == 1)
        def _():
            relay(2)
            pass_on(1, 1)

        @pl.when(i == 2)
        def _():
            relay(3)
            pass_on(1, 0)

        @pl.when(i >= 1)
        def _():
            put_one(i, line, "wait")

        @pl.loop(0, block_rows // chunk)
        def norm(j):
            at = pl.ds(pl.multiple_of(base + j * chunk, chunk), chunk)
            to = pl.ds(pl.multiple_of(j * chunk, chunk), chunk)
            x = x_all[at, :].astype(f32)
            mean = jnp.mean(x, -1, keepdims=True)
            centre = x - mean
            scale = lax.rsqrt(jnp.mean(centre * centre, -1, keepdims=True) + eps_norm)
            stat_keep[at, 0:1] = mean
            stat_keep[at, 1:2] = scale
            unit = centre * scale
            one_buf[to, :] = (unit * vec_ref[0:1, :] + vec_ref[1:2, :]).astype(low)
            two_buf[0, to, :] = (unit * vec_ref[2:3, :] + vec_ref[3:4, :]).astype(low)

        put_one(i, line, "start")
        qkv_now[...] = dot(one_buf[...], wq[...]) + bias_ref[0:1, : cols[0]]
        pre_now[...] = dot(two_buf[0], w1[...]) + bias_ref[0:1, cols[0] :]

        for s in range(seq_dev):
            part = slice(s * slot_len, (s + 1) * slot_len)
            rows = pl.ds(pl.multiple_of(base + s * slot_len, 32), slot_len)
            qkv_keep[rows, 0:half] = turn(qkv_now[part, 0:half], 1).astype(low)
            qkv_keep[rows, half:head] = qkv_now[part, half:head].astype(low)
            qkv_keep[rows, head : head + half] = turn(qkv_now[part, head : head + half], 1).astype(low)
            qkv_keep[rows, head + half :] = qkv_now[part, head + half :].astype(low)
            query = qkv_keep[rows, :head]
            keys = qkv_keep[rows, head : 2 * head]
            values = qkv_keep[rows, 2 * head :]
            scores = jnp.where(causal, contract(query, keys, ((1,), (1,))) / root, neg_large)
            expo = jnp.exp(scores - jnp.max(scores, -1, keepdims=True))
            probs = expo / jnp.sum(expo, -1, keepdims=True)
            prob_keep[line * seq_dev + s] = probs
            attn_keep[rows, :] = (dot(probs.astype(low), values) * valid_ref[rows, :]).astype(low)

        @pl.loop(0, block_rows // chunk)
        def act(j):
            at = pl.ds(pl.multiple_of(base + j * chunk, chunk), chunk)
            pre = pre_now[pl.ds(pl.multiple_of(j * chunk, chunk), chunk), :]
            area = 0.5 * (1.0 + lax.erf(pre * math.sqrt(0.5)))
            hid_keep[at, :] = (pre * area * valid_ref[at, :]).astype(low)
            pg_keep[at, :] = (area + pre * (jnp.exp(-0.5 * pre * pre) * (1.0 / math.sqrt(2.0 * math.pi)))).astype(low)

    put_one(LINE - 1, (c + LINE - 1) % LINE, "wait")
    local_weight(2, "wait")
    local_weight(3, "wait")
    last(2)
    last(3)
    mine = c * 2 + k

    def pair_m(i, act):
        copy = remote(m_buf.at[i % 2, me.other], m_got.at[i], msib_s.at[i], msib_r.at[i], sibling)
        getattr(copy, act)()

    def half_m(i, act):
        for q, to in enumerate((partner, (partner + 2) % LINE)):
            copy = remote(
                m_got.at[i, to], m_half.at[i, q], half_s.at[i, q], half_r.at[i, q], me.at(partner, g, k)
            )
            getattr(copy, act)()

    def far_m(i, act):
        copy = remote(m_got.at[i, beyond], far_out.at[i], far_s.at[i], far_r.at[i], me.at(beyond, g, k))
        getattr(copy, act)()

    def near_m(i, act):
        getattr(pltpu.make_async_copy(m_got.at[i, c], near_out.at[i], near_sem.at[i]), act)()

    def sent_m(i):
        half_m(i, SENT)
        far_m(i, SENT)
        near_m(i, "wait")

    def second_m(i):
        half_m(i, "wait_recv")

        @pl.loop(0, block_rows // 192)
        def add(j):
            at = pl.ds(pl.multiple_of(j * 192, 64), 192)
            for q, to in enumerate((c, beyond)):
                total = m_got[i, to, at, :].astype(f32) + m_half[i, q, at, :].astype(f32)
                m_got[i, to, at, :] = total.astype(low)

        far_m(i, START)
        near_m(i, START)

    def pair_add(i):
        pair_m(i, "wait_recv")

        @pl.loop(0, LINE)
        def add_outer(p):
            @pl.loop(0, block_rows // 192)
            def add(j):
                at = pl.ds(pl.multiple_of(j * 192, 64), 192)
                total = m_buf[i % 2, k, p, at, :].astype(f32) + m_got[i, p, at, :].astype(f32)
                m_got[i, p, at, :] = total.astype(low)

        half_m(i, START)

    @pl.loop(0, LINE)
    def outputs(i):
        base = pl.multiple_of(i * block_rows, 128)
        whole = pl.ds(base, block_rows)
        slot = i % 2

        @pl.when(i == 1)
        def _():
            pass_on(1, 2)

        @pl.when(i >= 2)
        def _():
            pair_m(i - 2, SENT)

        live = valid_ref[whole, :]

        @pl.loop(0, ways)
        def output(j):
            at = pl.ds(pl.multiple_of(j * wide, 128), wide)
            total = contract(attn_keep[whole, :], wd[at, :], ((1,), (1,)))
            total = total + contract(hid_keep[whole, :], w2[at, :], ((1,), (1,)))
            feature = (lax.broadcasted_iota(jnp.int32, (1, wide), 1) + j * wide) // (D // (2 * LINE))
            mask = jnp.where(feature == mine, 1.0, 0.0)
            extra = x_all[whole, at].astype(f32) + (vec_ref[4:5, at] + vec_ref[5:6, at])
            total = ((total + mask * extra) * live).astype(low)
            m_buf[slot, 0, j] = total[:, : wide // 2]
            m_buf[slot, 1, j] = total[:, wide // 2 :]

        pair_m(i, START)

        @pl.when(i >= 1)
        def _():
            pair_add(i - 1)

    pair_add(LINE - 1)
    pair_m(LINE - 2, SENT)
    pair_m(LINE - 1, SENT)
    local_acts(1, "wait")
    arrive_sibling(1)

    per = 128 // rows_own
    part_cols = 256
    fits = block_rows // 128
    pieces = (cols[2] + cols[3]) // part_cols
    dense_pieces = cols[2] // part_cols

    def out_group(i):
        flip_x, flip_y = 1 - i % 2, 1 - i // 2
        return (g // 2 + flip_y) % 2 * 2 + (g % 2 + flip_x) % 2

    def flat_piece(i, t, nb):
        row, column = divmod(t * pieces + nb, D // part_cols)
        at = (pl.ds(row * 128, 128), pl.ds(column * part_cols, part_cols))
        return one_buf.at[at] if i == 2 else two_buf.at[(1,) + at]

    def out_products(i):
        if near:
            to = out_group(i)
            tiles = [(l, to) for l in range(LINE)]
        else:
            tiles = [(i, t * per) for t in range(LINE)]
        lhs = turned([ct_all[:, pl.ds(pl.multiple_of((l * groups + p) * rows_own, 128), 128)] for l, p in tiles])
        first = 0
        for right in (attn_keep, hid_keep):
            out = dot(lhs, right[...]).astype(low)
            for n in range(right.shape[1] // part_cols):
                nb = first + n
                for t in range(LINE):
                    part = out[t * 128 : (t + 1) * 128, n * part_cols : (n + 1) * part_cols]
                    if near and i >= 2:
                        flat_piece(i, t, nb)[...] = part
                    else:
                        m_buf[i % 2, nb // fits, t, (nb % fits) * 128 : (nb % fits + 1) * 128, :] = part
            first += right.shape[1] // part_cols

    def out_place(refs, nb, step):
        ref, n = (refs[0], nb) if nb < dense_pieces else (refs[1], nb - dense_pieces)
        at = pl.ds(n * part_cols, part_cols)
        if step is not None:
            ref = ref.at[step - 1]
        return ref.at[:, :, at]

    def out_copies(i, step):
        to = g if step is None else (out_group(i) if near else (g + step) % groups)
        for nb in range(pieces):
            dst = out_place((gd_own, g2_own) if step is None else (gd_got, g2_got), nb, step)
            row = (nb % fits) * 128
            if near and i < 2:
                yield m_buf.at[i % 2, nb // fits, :, pl.ds(row, 128), :], dst, (0, nb)
            elif near:
                for t in range(LINE):
                    yield flat_piece(i, t, nb), dst.at[t], (t, nb)
            else:
                rows = pl.ds(pl.multiple_of(row + (to % per) * rows_own, 32), rows_own)
                yield m_buf.at[i % 2, nb // fits, to // per, rows, :], dst.at[i], (i, nb)

    def out_sends(i, act):
        for step in (groups - 1 - i,) if near else range(groups):
            if step == 0:
                for src, dst, (t, nb) in out_copies(i, None):
                    copy = pltpu.make_async_copy(src, dst, g_here.at[t, nb])
                    getattr(copy, "wait" if act == SENT else act)()
            else:
                to = out_group(i) if near else (g + step) % groups
                for src, dst, (t, nb) in out_copies(i, step):
                    copy = remote(src, dst, gp_s.at[t, step, nb], gp_r.at[t, step, nb], me.at(c, to, k))
                    getattr(copy, act)()

    for i in range(LINE):
        if i >= 2 and not near:
            out_sends(i - 2, SENT)
        out_products(i)
        out_sends(i, START)

    def pair_s(i, act):
        line = (c + i) % LINE
        rows = pl.ds(pl.multiple_of(me.other * slot_len, 32), slot_len)
        copy = remote(two_buf.at[i % 2, rows], s_got.at[line], ssib_s.at[i], ssib_r.at[i], sibling)
        getattr(copy, act)()

    def put_s(i, act):
        line = (c + i) % LINE
        rows = pl.ds(pl.multiple_of(k * slot_len, 32), slot_len)
        getattr(pltpu.make_async_copy(two_buf.at[i % 2, rows], s_out.at[line], s_here.at[i]), act)()

    def finish_s(i):
        line = (c + i) % LINE
        pair_s(i, "wait_recv")

        @pl.loop(0, slot_len // chunk)
        def add(j):
            at = pl.ds(pl.multiple_of(k * slot_len + j * chunk, chunk), chunk)
            to = pl.ds(pl.multiple_of(j * chunk, chunk), chunk)
            total = two_buf[i % 2, at, :].astype(f32) + s_got[line, to, :].astype(f32)
            two_buf[i % 2, at, :] = total.astype(low)

        put_s(i, START)

    def put_rest(line, act):
        rows = pl.ds(pl.multiple_of(line * block_rows, 128), block_rows)
        for place_at, (buf, out) in enumerate(((qkv_keep, qg_out), (pg_keep, pg_out))):
            getattr(pltpu.make_async_copy(buf.at[rows], out.at[rows], out_d.at[place_at, line]), act)()

    @pl.loop(0, LINE)
    def backward(i):
        line = (c + i) % LINE
        base = pl.multiple_of(line * block_rows, 128)
        whole = pl.ds(base, block_rows)
        slot = i % 2

        if near:

            @pl.when(i == 1)
            def _():
                out_sends(LINE - 1, SENT)

        @pl.when((i == 1) | (i == 2))
        def _():
            second_m(i * 2 - 2)
            second_m(i * 2 - 1)

        live = valid_ref[whole, :]
        back_buf[...] = (ct_all[whole, :].astype(f32) * live).astype(low)
        attn_grad = dot(back_buf[...], wd[...]).astype(low)
        pre_now[...] = dot(back_buf[...], w2[...])

        @pl.when(i == 0)
        def _():
            rows = pl.ds(pl.multiple_of(k * slot_len, 32), slot_len)
            total = jnp.sum(back_buf[rows, :].astype(f32).reshape(slot_len // 8, 8, D), 0)
            norm_acc[4] = total

        @pl.loop(0, block_rows // chunk)
        def act(j):
            at = pl.ds(pl.multiple_of(base + j * chunk, chunk), chunk)
            grad = pre_now[pl.ds(pl.multiple_of(j * chunk, chunk), chunk), :] * pg_keep[at, :].astype(f32)
            grad = grad.astype(low)
            pg_keep[at, :] = grad
            grad = grad.astype(f32)
            bias_acc[:, cols[0] :] += jnp.sum(grad.reshape(chunk // 8, 8, cols[1]), 0)

        for s in range(seq_dev):
            rows = pl.ds(pl.multiple_of(base + s * slot_len, 32), slot_len)
            grad = attn_grad[s * slot_len : (s + 1) * slot_len]
            query = qkv_keep[rows, :head]
            keys = qkv_keep[rows, head : 2 * head]
            values = qkv_keep[rows, 2 * head :]
            probs = prob_keep[line * seq_dev + s]
            prob_grad = contract(grad, values, ((1,), (1,)))
            row_dot = jnp.sum(probs * prob_grad, -1, keepdims=True)
            score_grad = (probs * (prob_grad - row_dot)).astype(low)
            value_grad = contract(probs.astype(low), grad, ((0,), (0,)))
            query_grad = dot(score_grad, keys) / root
            key_grad = contract(score_grad, query, ((0,), (0,))) / root
            qkv_keep[rows, 0:half] = turn(query_grad[:, :half], -1).astype(low)
            qkv_keep[rows, half:head] = query_grad[:, half:].astype(low)
            qkv_keep[rows, head : head + half] = turn(key_grad[:, :half], -1).astype(low)
            qkv_keep[rows, head + half : 2 * head] = key_grad[:, half:].astype(low)
            qkv_keep[rows, 2 * head :] = value_grad.astype(low)
            summed = qkv_keep[rows, :].astype(f32).reshape(slot_len // 8, 8, cols[0])
            bias_acc[:, : cols[0]] += jnp.sum(summed, 0)

        put_rest(line, "start")
        mean = stat_keep[whole, 0:1]
        scale = stat_keep[whole, 1:2]

        @pl.when(i >= 2)
        def _():
            pair_s(i - 2, SENT)
            put_s(i - 2, "wait")

        @pl.loop(0, ways)
        def inputs(j):
            at = pl.ds(pl.multiple_of(j * wide, 128), wide)
            first = contract(qkv_keep[whole, :], wq[at, :], ((1,), (1,)))
            second = contract(pg_keep[whole, :], w1[at, :], ((1,), (1,)))
            two_buf[slot, :, at] = (first * vec_ref[0:1, at] + second * vec_ref[2:3, at]).astype(low)
            unit = (x_all[whole, at].astype(f32) - mean) * scale
            for place_at, value in enumerate((first * unit, first, second * unit, second)):
                norm_acc[place_at, :, at] += jnp.sum(value.reshape(block_rows // 8, 8, wide), 0)

        pair_s(i, START)

        @pl.when(i >= 1)
        def _():
            finish_s(i - 1)

    finish_s(LINE - 1)
    for r in range(5):
        total = jnp.sum(norm_acc[r], 0, keepdims=True)
        for t in range(D // 128):
            early_ref[r * (D // 128) + t : r * (D // 128) + t + 1, :] = total[:, t * 128 : (t + 1) * 128]
    at_bias = 5 * (D // 128)
    total = jnp.sum(bias_acc[...], 0, keepdims=True)
    for t in range((cols[0] + cols[1]) // 128):
        early_ref[at_bias + t : at_bias + t + 1, :] = total[:, t * 128 : (t + 1) * 128]
    at_row = at_bias + (cols[0] + cols[1]) // 128
    early_ref[at_row : at_row + 1, :] = vec_ref[6:7, :128]
    early_ref[at_row + 1 :, :] = jnp.zeros((early_ref.shape[0] - at_row - 1, 128), f32)
    for i in range(LINE):
        put_rest(i, "wait")
        sent_m(i)
        far_m(i, "wait_recv")
    for i in (LINE - 2, LINE - 1):
        pair_s(i, SENT)
        put_s(i, "wait")
    for i in range(LINE - 1) if near else (LINE - 2, LINE - 1):
        out_sends(i, SENT)
    for i in range(LINE):
        for step in (groups - 1 - i,) if near else range(1, groups):
            if step:
                for _, dst, (t, nb) in out_copies(i, step):
                    remote(dst, dst, gp_s.at[t, step, nb], gp_r.at[t, step, nb], sibling).wait_recv()
    for m in range(count):
        stage_one(m, SENT)
        for step in range(LINE):
            stage_two(m, step, SENT)
            if near:
                stage_three(m, step, SENT)
    for which in range(2):
        for q in range(3):
            row_send(which, q, SENT)
            to_sibling(which, q, SENT)


def gather_all(groups, weights, tokens, cotangent, vectors, biases, valid, turns):
    rows_own = weights[0].shape[0]
    seq_dev, slot_len, width = tokens.shape
    cols = tuple(w.shape[1] // LINE for w in weights)
    count = len(weights)
    block_rows = seq_dev * slot_len
    rows = LINE * block_rows
    f32, low = jnp.float32, jnp.bfloat16
    dma = pltpu.SemaphoreType.DMA
    peers = 3 if groups == 4 else groups
    out_widths = (D, D, cols[0], cols[1])
    pieces = (cols[2] + cols[3]) // 256
    feat = D // (2 * LINE)
    early_rows = -(-(5 * D + cols[0] + cols[1] + 128) // 1024) * 8
    return pl.pallas_call(
        partial(gather_kernel, groups, cols, seq_dev, slot_len),
        out_shape=[jax.ShapeDtypeStruct((rows, w), low) for w in out_widths]
        + [
            jax.ShapeDtypeStruct((LINE, block_rows, feat), low),
            jax.ShapeDtypeStruct((LINE, block_rows, feat), low),
            jax.ShapeDtypeStruct((LINE, slot_len, D), low),
            jax.ShapeDtypeStruct((LINE, rows_own, cols[2]), low),
            jax.ShapeDtypeStruct((LINE, rows_own, cols[3]), low),
            jax.ShapeDtypeStruct((groups - 1, LINE, rows_own, cols[2]), low),
            jax.ShapeDtypeStruct((groups - 1, LINE, rows_own, cols[3]), low),
            jax.ShapeDtypeStruct((early_rows, 128), f32),
        ],
        in_specs=[ANY] * (count + 2) + [VMEM] * 4,
        out_specs=[ANY] * 11 + [VMEM],
        scratch_shapes=[pltpu.VMEM((D, w), low) for w in cols]
        + [pltpu.VMEM((rows, D), low)] * 2
        + [
            pltpu.VMEM((rows, cols[0]), low),
            pltpu.VMEM((LINE * seq_dev, slot_len, slot_len), f32),
            pltpu.VMEM((rows, cols[2]), low),
            pltpu.VMEM((rows, cols[3]), low),
            pltpu.VMEM((rows, cols[1]), low),
            pltpu.VMEM((block_rows, D), low),
            pltpu.VMEM((2, block_rows, D), low),
            pltpu.VMEM((block_rows, D), low),
            pltpu.VMEM((2, 2, LINE, block_rows, feat), low),
            pltpu.VMEM((LINE, LINE, block_rows, feat), low),
            pltpu.VMEM((LINE, 2, block_rows, feat), low),
            pltpu.VMEM((LINE, slot_len, D), low),
            pltpu.VMEM((block_rows, cols[0]), f32),
            pltpu.VMEM((block_rows, cols[1]), f32),
            pltpu.VMEM((rows, 2), f32),
            pltpu.VMEM((5, 8, D), f32),
            pltpu.VMEM((8, cols[0] + cols[1]), f32),
            dma((count, LINE)),
            dma((count, LINE)),
            dma((count, LINE, peers)),
            dma((count, LINE, peers)),
            dma((count, LINE)),
            dma((count, LINE)),
            dma((2, 3)),
            dma((2, 3)),
            dma((2, 3)),
            dma((2, 3)),
            dma((count + 2, seq_dev)),
            dma(()),
            dma((2,)),
            dma((2, LINE)),
            dma((LINE,)),
            dma((LINE,)),
            dma((LINE,)),
            dma((LINE,)),
            dma((LINE, 2)),
            dma((LINE, 2)),
            dma((LINE,)),
            dma((LINE,)),
            dma((LINE,)),
            dma((LINE,)),
            dma((LINE, groups, pieces)),
            dma((LINE, groups, pieces)),
            dma((LINE, pieces)),
        ],
        compiler_params=pltpu.CompilerParams(
            collective_id=0, has_side_effects=True, vmem_limit_bytes=62 * 1024 * 1024
        ),
        name="gather_all",
    )(*weights, tokens, cotangent, vectors, biases, valid, turns)


def scatter_kernel(groups, cols, seq_dev, slot_len, rows_own, *refs):
    count = len(cols)
    f32, low = jnp.float32, jnp.bfloat16
    pick = refs[0]
    lefts_in = refs[1:3]
    rights_in = refs[3:5]
    near_ref, far_ref, s_ref = refs[5:8]
    done_own, done_got = refs[8:10], refs[10:12]
    early_ref = refs[12]
    mixed_ref, ssum_ref = refs[13:15]
    g_out = refs[15 : 15 + count]
    early_out, col_out, row_out = refs[15 + count : 18 + count]
    rest = refs[18 + count :]
    left_buf, right_a, right_b = rest[:3]
    g_own = rest[3 : 3 + count]
    g_got = rest[3 + count : 3 + 2 * count]
    (m_in, m_all, m_send, s_own, s_half, s_far, early_group, col_now, col_group, row_keep, row_turn) = rest[
        3 + 2 * count : 14 + 2 * count
    ]
    (here, half_s, half_r, far_s, far_r, fin_s, fin_r, mall_s, mall_r, mout_s, mout_r, gp_s, gp_r, gl_s, gl_r, eg_s,
     eg_r, el_s, el_r, es_s, es_r, cg_s, cg_r, cl_s, cl_r, cs_s, cs_r, rl_s, rl_r, keep_sem) = rest[14 + 2 * count :]
    me = Place(groups)
    c, g, k = me.line, me.group, me.core
    me.greet()
    sibling = me.at(c, g, me.other)
    feat = D // (2 * LINE)
    seqs = LINE * seq_dev
    rows = seqs * slot_len
    double = groups == 4
    sends = []

    def go(copy):
        copy.start()
        sends.append(copy)

    def to_group(step):
        return (g + step) % groups

    def from_group(step):
        return (g + groups - step) % groups

    def arrived(dst, send, recv):
        remote(dst, dst, send, recv, sibling).wait_recv()

    def add_rows(total, parts, count_rows, chunk):
        @pl.loop(0, count_rows // chunk)
        def body(i):
            at = pl.ds(pl.multiple_of(i * chunk, chunk), chunk)
            acc = parts[0](at)[...].astype(f32)
            for part in parts[1:]:
                acc = acc + part(at)[...].astype(f32)
            total(at)[...] = acc.astype(low)

    def load(src, dst, sem):
        copy = pltpu.make_async_copy(src, dst, sem)
        copy.start()
        return copy

    partner = c + 1 - 2 * (c % 2)
    beyond = (c + 2) % LINE
    for q, to in enumerate((partner, (partner + 2) % LINE)):
        go(remote(s_ref.at[to], s_half.at[q], half_s.at[q], half_r.at[q], me.at(partner, g, k)))
    got_m = [load(near_ref, m_in.at[0], here.at[10]), load(far_ref, m_in.at[1], here.at[11])]
    got_done = []
    for q in range(2):
        got_done.append(load(done_own[q], g_own[2 + q].at[:, 0], here.at[2 + 2 * q]))
        got_done.append(load(done_got[q], g_got[2 + q], here.at[3 + 2 * q]))
    got_two = load(lefts_in[1], left_buf.at[0], here.at[6])
    got_1 = load(rights_in[1], right_a, here.at[7])
    if double:
        got_one = load(lefts_in[0], left_buf.at[1], here.at[0])
        got_q = load(rights_in[0], right_b, here.at[1])
    got_s = [load(s_ref.at[c], s_own.at[0], here.at[8]), load(s_ref.at[beyond], s_own.at[1], here.at[9])]
    for step in range(1, groups):
        go(remote(early_ref, early_group.at[g], eg_s.at[step], eg_r.at[step], me.at(c, to_group(step), k)))
    early_group[g] = early_ref[...]

    per = 128 // rows_own

    def tile_products(m, left, right, tiles):
        lhs = turned([left[:, pl.ds(pl.multiple_of((l * groups + p) * rows_own, 128), 128)] for l, p in tiles])
        out = dot(lhs, right[...]).astype(low)
        for t, (l, p) in enumerate(tiles):
            for q in range(per):
                row = t * 128 + q * rows_own
                g_own[m][l, p + q] = out[row : row + rows_own]

    def send_group(m, step, act):
        to = to_group(step)
        copy = remote(
            g_own[m].at[:, to], g_got[m].at[step - 1], gp_s.at[m, step], gp_r.at[m, step], me.at(c, to, k)
        )
        getattr(copy, act)()

    across, beside, above = me.group_to(3), me.group_to(1), me.group_to(2)
    two_phase = groups == 4

    def phase_one(m, way, act):
        lines = pl.ds(0, 2) if way == 0 else pl.ds(2, 2)
        to = beside if way == 0 else above
        for q, block in enumerate((to, across)):
            copy = remote(
                g_own[m].at[lines, block], g_got[m].at[q, lines], gp_s.at[m, way * 2 + q], gp_r.at[m, way * 2 + q],
                me.at(c, to, k),
            )
            getattr(copy, act)()

    def phase_two(m, way, act):
        lines = pl.ds(0, 2) if way == 0 else pl.ds(2, 2)
        to = above if way == 0 else beside
        copy = remote(
            g_own[m].at[lines, to], g_got[m].at[2, lines], gp_s.at[m, 4 + way], gp_r.at[m, 4 + way], me.at(c, to, k)
        )
        getattr(copy, act)()

    def between_phases(m):
        for way in range(2):
            phase_one(m, way, "wait_recv")
            to = above if way == 0 else beside
            for line in (way * 2, way * 2 + 1):
                add_rows(
                    lambda at: g_own[m].at[line, to, at],
                    [lambda at: g_own[m].at[line, to, at], lambda at: g_got[m].at[1, line, at]],
                    rows_own,
                    min(64, rows_own),
                )
            phase_two(m, way, "start")

    def products(left, pairs):
        if two_phase:

            @pl.loop(0, groups)
            def body(t):
                flip_x, flip_y = (t + 1) % 2, (3 - t) // 2 * (1 - t // 3)
                to = (g // 2 + flip_y) % 2 * 2 + (g % 2 + flip_x) % 2
                for m, right in pairs:
                    tile_products(m, left, right, [(l, to) for l in range(LINE)])
                    for way in range(2):

                        @pl.when(t == 2 - way)
                        def _():
                            phase_one(m, way, "start")
        else:

            @pl.loop(0, LINE)
            def body(l):
                for m, right in pairs:
                    tile_products(m, left, right, [(l, t * per) for t in range(4)])

            for m, _ in pairs:
                for step in range(1, groups):
                    send_group(m, step, "start")

    def sum_groups(m, first):
        got = range(groups - 1)
        if m < 2 and two_phase:
            for way in range(2):
                phase_two(m, way, "wait_recv")
            got = (0, 2)
        elif m < 2:
            for step in range(1, groups):
                arrived(g_got[m].at[step - 1], gp_s.at[m, step], gp_r.at[m, step])
        mine = g if m < 2 else 0
        width = pl.ds(pl.multiple_of(c * cols[m], 128), cols[m])
        total = jnp.zeros((8, cols[m]), f32)
        for step in (2, 1, 3, 0):
            line = me.line_to(step)

            def body(i, carry, line=line):
                at = pl.ds(pl.multiple_of(i * 32, 32), 32)
                acc = g_own[m][line, mine, at, :].astype(f32)
                for p in got:
                    acc = acc + g_got[m][p, line, at, :].astype(f32)
                g_own[m][line, mine, at, :] = acc.astype(low)
                square = acc * acc + eps_second
                row_keep[line, at, m : m + 1] = jnp.sum(square, 1, keepdims=True)
                return carry + jnp.sum(square.reshape(4, 8, cols[m]), 0)

            total = lax.fori_loop(0, rows_own // 32, body, total)
            src = g_own[m].at[line, mine]
            if step:
                go(remote(src, g_out[m].at[:, width], gl_s.at[m, step], gl_r.at[m, step], me.at(line, g, k)))
            else:
                keep.append(load(src, g_out[m].at[:, width], keep_sem.at[2 + m]))
        total = jnp.sum(total, 0, keepdims=True)
        for t in range(cols[m] // 128):
            col_now[first + t : first + t + 1, :] = total[:, t * 128 : (t + 1) * 128]

    keep = []
    row_keep[...] = jnp.zeros_like(row_keep)
    firsts = []
    edge = 0
    for m in range(count):
        firsts.append(edge)
        edge += cols[m] // 128
    for copy in got_m:
        copy.wait()
    ours = pl.ds(g * seqs, seqs)
    for s in range(seqs):
        add_rows(
            lambda at: m_all.at[g * seqs + s, at],
            [lambda at: m_in.at[0, s, at], lambda at: m_in.at[1, s, at]],
            slot_len,
            192,
        )
    for step in range(1, groups):
        go(remote(m_all.at[ours], m_all.at[ours], mall_s.at[step], mall_r.at[step], me.at(c, to_group(step), k)))

    for copy in got_done:
        copy.wait()
    sum_groups(3, firsts[3])
    sum_groups(2, firsts[2])
    got_two.wait()
    got_1.wait()
    products(left_buf.at[0], ((1, right_a),))
    if not double:
        got_one = load(lefts_in[0], left_buf.at[0], here.at[0])
        got_q = load(rights_in[0], right_b, here.at[1])

    for q in range(2):
        got_s[q].wait()
        arrived(s_half.at[q], half_s.at[q], half_r.at[q])
        add_rows(
            lambda at: s_own.at[q, at], [lambda at: s_own.at[q, at], lambda at: s_half.at[q, at]], slot_len, 64
        )
    go(remote(s_own.at[1], s_far, far_s, far_r, me.at(beyond, g, k)))

    got_one.wait()
    got_q.wait()
    products(left_buf.at[1 if double else 0], ((0, right_b),))
    if two_phase:
        between_phases(1)
    for step in range(1, groups):
        arrived(early_group.at[from_group(step)], eg_s.at[step], eg_r.at[step])
    acc = early_group[0]
    for i in range(1, groups):
        acc = acc + early_group[i]
    early_out[k, c] = acc
    for step in range(1, LINE):
        go(remote(early_out.at[k, c], early_out.at[k, c], el_s.at[step], el_r.at[step], me.at(me.line_to(step), g, k)))

    for step in range(1, groups):
        arrived(m_all.at[pl.ds(from_group(step) * seqs, seqs)], mall_s.at[step], mall_r.at[step])
    mixed_cols = pl.ds(pl.multiple_of((c * 2 + k) * feat, 128), feat)
    for step in (1, 2, 3, 0):
        line = me.line_to(step)
        for s in range(seq_dev):
            m_send[line, s] = m_all[pick[line * seq_dev + s]]
        where = mixed_ref.at[:, :, mixed_cols]
        if step:
            go(remote(m_send.at[line], where, mout_s.at[0, step], mout_r.at[0, step], me.at(line, g, k)))
        else:
            keep.append(load(m_send.at[line], where, keep_sem.at[1]))
            go(remote(m_send.at[line], where, mout_s.at[1, 0], mout_r.at[1, 0], sibling))
    if two_phase:
        between_phases(0)
    sum_groups(1, firsts[1])
    sum_groups(0, firsts[0])

    for step in range(1, groups):
        go(remote(col_now, col_group.at[g], cg_s.at[step], cg_r.at[step], me.at(c, to_group(step), k)))
    col_group[g] = col_now[...]
    for step in (1, 2, 3, 0):
        line = me.line_to(step)
        row_turn[line] = jnp.transpose(row_keep[line])[:8]
        if step:
            go(remote(row_turn.at[line], row_out.at[k, c], rl_s.at[0, step], rl_r.at[0, step], me.at(line, g, k)))
        else:
            row_out[k, c] = row_turn[line]
        go(remote(row_turn.at[line], row_out.at[k, c], rl_s.at[1, step], rl_r.at[1, step], me.at(line, g, me.other)))
    for step in range(1, groups):
        arrived(col_group.at[from_group(step)], cg_s.at[step], cg_r.at[step])
    acc = col_group[0]
    for i in range(1, groups):
        acc = acc + col_group[i]
    col_out[k, c] = acc
    for step in range(1, LINE):
        go(remote(col_out.at[k, c], col_out.at[k, c], cl_s.at[step], cl_r.at[step], me.at(me.line_to(step), g, k)))
    arrived(s_far, far_s, far_r)
    add_rows(lambda at: s_own.at[0, at], [lambda at: s_own.at[0, at], lambda at: s_far.at[at]], slot_len, 16)
    go(remote(s_own.at[0], ssum_ref.at[k], fin_s, fin_r, sibling))
    keep.append(load(s_own.at[0], ssum_ref.at[k], keep_sem.at[0]))
    for step in range(1, LINE):
        arrived(early_out.at[k, me.line_from(step)], el_s.at[step], el_r.at[step])
    go(remote(early_out.at[k], early_out.at[k], es_s, es_r, sibling))
    for step in range(1, LINE):
        arrived(col_out.at[k, me.line_from(step)], cl_s.at[step], cl_r.at[step])
    go(remote(col_out.at[k], col_out.at[k], cs_s, cs_r, sibling))

    for step in range(1, LINE):
        where = mixed_ref.at[:, :, pl.ds(pl.multiple_of((me.line_from(step) * 2 + k) * feat, 128), feat)]
        arrived(where, mout_s.at[0, step], mout_r.at[0, step])
        go(remote(where, where, mout_s.at[1, step], mout_r.at[1, step], sibling))
    for m in range(count):
        for step in range(1, LINE):
            dst = g_out[m].at[:, pl.ds(pl.multiple_of(me.line_from(step) * cols[m], 128), cols[m])]
            arrived(dst, gl_s.at[m, step], gl_r.at[m, step])
    for step in range(LINE):
        source = me.line_from(step)
        dst = mixed_ref.at[:, :, pl.ds(pl.multiple_of((source * 2 + me.other) * feat, 128), feat)]
        arrived(dst, mout_s.at[1, step], mout_r.at[1, step])
        for core, way in ((k, 0), (me.other, 1)):
            if step or way:
                arrived(row_out.at[core, source], rl_s.at[way, step], rl_r.at[way, step])
    arrived(ssum_ref.at[me.other], fin_s, fin_r)
    arrived(early_out.at[me.other], es_s, es_r)
    arrived(col_out.at[me.other], cs_s, cs_r)
    for copy in sends:
        copy.wait_send()
    for m in range(2):
        if two_phase:
            for way in range(2):
                phase_one(m, way, "wait_send")
                phase_two(m, way, "wait_send")
        else:
            for step in range(1, groups):
                send_group(m, step, "wait_send")
    for copy in keep:
        copy.wait()


def scatter_all(groups, cols, seq_dev, rows_own, pick, lefts, rights, between):
    near, far, s_pair, *done, early = between
    slot_len = s_pair.shape[1]
    rows = lefts[0].shape[0]
    count = len(cols)
    feat = D // (2 * LINE)
    seqs = LINE * seq_dev
    blocks = (seqs, slot_len, feat)
    dma = pltpu.SemaphoreType.DMA
    f32, low = jnp.float32, jnp.bfloat16
    col_rows = sum(cols) // 128
    return pl.pallas_call(
        partial(scatter_kernel, groups, cols, seq_dev, slot_len, rows_own),
        out_shape=[
            jax.ShapeDtypeStruct((seq_dev, slot_len, D), low),
            jax.ShapeDtypeStruct((seq_dev, slot_len, D), low),
        ]
        + [jax.ShapeDtypeStruct((rows_own, LINE * width), low) for width in cols]
        + [
            jax.ShapeDtypeStruct((2, LINE) + early.shape, f32),
            jax.ShapeDtypeStruct((2, LINE, col_rows, 128), f32),
            jax.ShapeDtypeStruct((2, LINE, 8, 128), f32),
        ],
        in_specs=[SMEM] + [ANY] * 11 + [VMEM],
        out_specs=[ANY] * (2 + count) + [VMEM] * 3,
        scratch_shapes=[
            pltpu.VMEM((2 if groups == 4 else 1, rows, D), low),
            pltpu.VMEM((rows, cols[1]), low),
            pltpu.VMEM((rows, cols[0]), low),
        ]
        + [pltpu.VMEM((LINE, groups if m < 2 else 1, rows_own, width), low) for m, width in enumerate(cols)]
        + [pltpu.VMEM((groups - 1, LINE, rows_own, width), low) for width in cols]
        + [
            pltpu.VMEM((2, seqs, slot_len, feat), low),
            pltpu.VMEM((groups * seqs, slot_len, feat), low),
            pltpu.VMEM((LINE, seq_dev, slot_len, feat), low),
            pltpu.VMEM((2, slot_len, D), low),
            pltpu.VMEM((2, slot_len, D), low),
            pltpu.VMEM((slot_len, D), low),
            pltpu.VMEM((groups,) + early.shape, f32),
            pltpu.VMEM((col_rows, 128), f32),
            pltpu.VMEM((groups, col_rows, 128), f32),
            pltpu.VMEM((LINE, 128, 128), f32),
            pltpu.VMEM((LINE, 8, 128), f32),
            dma((12,)),
            dma((2,)),
            dma((2,)),
            dma(()),
            dma(()),
            dma(()),
            dma(()),
            dma((groups,)),
            dma((groups,)),
            dma((2, LINE)),
            dma((2, LINE)),
            dma((count, max(groups, 6))),
            dma((count, max(groups, 6))),
            dma((count, LINE)),
            dma((count, LINE)),
            dma((groups,)),
            dma((groups,)),
            dma((LINE,)),
            dma((LINE,)),
            dma(()),
            dma(()),
            dma((groups,)),
            dma((groups,)),
            dma((LINE,)),
            dma((LINE,)),
            dma(()),
            dma(()),
            dma((2, LINE)),
            dma((2, LINE)),
            dma((2 + count,)),
        ],
        compiler_params=pltpu.CompilerParams(
            collective_id=1, has_side_effects=True, vmem_limit_bytes=62 * 1024 * 1024
        ),
        name="scatter_all",
    )(pick, *lefts, *rights, near.reshape(blocks), far.reshape(blocks), s_pair, *done, early)


def prepare_kernel(groups, cols, seq_dev, slot_len, *refs):
    (spot, lengths, permutation, wq, w1, wd, w2, vectors, biases, rows_state) = refs[:10]
    lows = refs[10:14]
    valid, own_valid, all_vectors, all_biases, pick = refs[14:]
    f32 = jnp.float32
    for src, dst in zip((wq, w1, wd, w2), lows):
        dst[...] = src[...].astype(jnp.bfloat16)

    @pl.when(pl.program_id(0) == 0)
    def _():
        data, core = spot[0], spot[1]
        line, group = data // groups, data % groups
        times = lax.broadcasted_iota(jnp.int32, (slot_len, 1), 0)
        for place in range(LINE):
            for s in range(seq_dev):
                slot = (place * groups + group) * seq_dev + s
                at = place * seq_dev + s
                valid[at * slot_len : (at + 1) * slot_len, :] = jnp.where(times < lengths[slot], 1.0, 0.0)
                source = permutation[slot]
                chip = source // seq_dev
                pick[at] = (chip % groups) * (LINE * seq_dev) + (chip // groups) * seq_dev + source % seq_dev
        for s in range(seq_dev):
            own_valid[s * slot_len : (s + 1) * slot_len, :] = jnp.where(
                times < lengths[data * seq_dev + s], 1.0, 0.0
            )
        all_vectors[0:6, :] = vectors[...]
        all_vectors[6:8, :] = jnp.zeros((2, D), f32)
        lane = lax.broadcasted_iota(jnp.int32, (1, 128), 1)
        total = jnp.zeros((1, 128), f32)
        for m in range(4):
            total = total + jnp.where(lane == m, jnp.sum(rows_state[m : m + 1, :], 1, keepdims=True), 0.0)
        all_vectors[6:7, 0:128] = jnp.where(core == 0, total, jnp.zeros_like(total))
        all_biases[:, : cols[0]] = biases[:, pl.ds(pl.multiple_of(line * cols[0], 128), cols[0])]
        all_biases[:, cols[0] :] = biases[:, pl.ds(pl.multiple_of(LINE * cols[0] + line * cols[1], 128), cols[1])]


def prepare(groups, seq_dev, slot_len, spot, lengths, permutation, weights, vectors, biases, rows_state):
    f32, low = jnp.float32, jnp.bfloat16
    rows_own = weights[0].shape[0]
    cols = tuple(w.shape[1] // LINE for w in weights)
    tall = 32
    steps = rows_own // tall
    seqs = LINE * seq_dev

    def whole(shape):
        return pl.BlockSpec(shape, lambda i: (0,) * len(shape))

    blocks = [pl.BlockSpec((tall, w.shape[1]), lambda i: (i, 0)) for w in weights]
    return pl.pallas_call(
        partial(prepare_kernel, groups, cols, seq_dev, slot_len),
        grid=(steps,),
        out_shape=[jax.ShapeDtypeStruct(w.shape, low) for w in weights]
        + [
            jax.ShapeDtypeStruct((seqs * slot_len, 1), f32),
            jax.ShapeDtypeStruct((seq_dev * slot_len, 1), f32),
            jax.ShapeDtypeStruct((8, D), f32),
            jax.ShapeDtypeStruct((1, cols[0] + cols[1]), f32),
            jax.ShapeDtypeStruct((seqs,), jnp.int32),
        ],
        in_specs=[SMEM] * 3 + blocks + [whole(vectors.shape), whole(biases.shape), whole(rows_state.shape)],
        out_specs=blocks
        + [
            whole((seqs * slot_len, 1)),
            whole((seq_dev * slot_len, 1)),
            whole((8, D)),
            whole((1, cols[0] + cols[1])),
            SMEM,
        ],
        compiler_params=pltpu.CompilerParams(vmem_limit_bytes=60 * 1024 * 1024),
        name="prepare",
    )(spot, lengths, permutation, *weights, vectors, biases, rows_state)


def finish_kernel(order, cols, rows_own, *refs):
    f32, low = jnp.float32, jnp.bfloat16
    spot = refs[0]
    g_in, w_in = refs[1:5], refs[5:9]
    (s_sum, tokens, cotangent, own_valid, early, col_all, row_all, row_state, col_state, vectors, moments, biases,
     bias_moments) = refs[9:22]
    grads, news, copies = refs[22:26], refs[26:30], refs[30:34]
    (grad_tokens, row_new, col_new, norm_total, norm_moment_new, norm_new, bias_total, bias_moment_new,
     bias_new) = refs[34:43]
    row_factor, col_factor, turn = refs[43:]
    step = pl.program_id(0)
    widths = [w.shape[1] for w in w_in]
    edges = [sum(widths[:i]) for i in range(5)]
    tiles = D // 128

    @pl.when(step == 0)
    def _():
        core = spot[1]
        both = early[0, 0]
        rows_all = row_all[0, 0]
        mass_all = col_all[0, 0]
        for n in range(1, 2 * LINE):
            both = both + early[n // LINE, n % LINE]
            rows_all = rows_all + row_all[n // LINE, n % LINE]
            mass_all = mass_all + col_all[n // LINE, n % LINE]
        for r in range(6):
            for t in range(tiles):
                at = min(r, 4) * tiles + t
                norm_total[r : r + 1, t * 128 : (t + 1) * 128] = both[at : at + 1]
        grad = norm_total[...]
        moment = decay * moments[...] + (1.0 - decay) * (grad * grad + eps_second)
        norm_moment_new[...] = moment
        norm_new[...] = vectors[...] - rate_norm * grad * lax.rsqrt(moment)
        first = 5 * tiles
        parts = ((cols[0] // 128, 0), (cols[1] // 128, LINE * cols[0]))
        for line in range(LINE):
            at = first
            for count, base in parts:
                for t in range(count):
                    to = base + (line * count + t) * 128
                    bias_total[:, to : to + 128] = early[core, line, at : at + 1, :]
                    at += 1
        grad = bias_total[...]
        moment = decay * bias_moments[...] + (1.0 - decay) * (grad * grad + eps_second)
        bias_moment_new[...] = moment
        bias_new[...] = biases[...] - rate_vector * grad * lax.rsqrt(moment)
        at_row = first + (cols[0] + cols[1]) // 128
        full_cols = (3.0 * D, 1.0 * D, 1.0 * FF, 1.0 * FF)
        rates = (
            rate_scale / math.sqrt(D),
            rate_scale / math.sqrt(D // 8),
            rate_scale / math.sqrt(D),
            rate_scale / math.sqrt(FF),
        )
        turn[...] = jnp.zeros_like(turn)
        at = 0
        for m, i in enumerate(order):
            count = cols[m] // 128
            new = decay * row_state[i : i + 1, :] + (1.0 - decay) * (rows_all[m : m + 1, :rows_own] / full_cols[i])
            row_new[i : i + 1, :] = new
            mass = jnp.sum(jnp.sum(mass_all[at : at + count], 1, keepdims=True), 0, keepdims=True)
            mean = (decay * both[at_row : at_row + 1, i : i + 1] + (1.0 - decay) * (mass / full_cols[i])) / D
            turn[i : i + 1, :rows_own] = rates[i] * lax.rsqrt(new / mean)
            for line in range(LINE):
                for t in range(count):
                    to = edges[i] + (line * count + t) * 128
                    col_new[:, to : to + 128] = col_all[core, line, at + t : at + t + 1, :]
            at += count
        row_factor[...] = jnp.transpose(turn[...])
        new = decay * col_state[...] + (1.0 - decay) * (col_new[...] / D)
        col_new[...] = new
        col_factor[...] = lax.rsqrt(new)

    tall = w_in[0].shape[0]
    for half in range(tall // 16):
        rows = pl.ds(pl.multiple_of(step * tall + half * 16, 16), 16)
        part = slice(half * 16, half * 16 + 16)
        for i in range(4):
            factor = row_factor[rows, i : i + 1]
            for n in range(widths[i] // 1024):
                at = slice(n * 1024, (n + 1) * 1024)
                grad = g_in[i][part, at].astype(f32)
                new = w_in[i][part, at] - grad * factor * col_factor[:, edges[i] + n * 1024 : edges[i] + (n + 1) * 1024]
                grads[i][part, at] = grad
                news[i][part, at] = new
                copies[i][part, at] = new.astype(low)

    @pl.loop(0, tokens.shape[0] // 16)
    def body(j):
        at = pl.ds(pl.multiple_of(j * 16, 16), 16)
        x = tokens[at, :].astype(f32)
        centre = x - jnp.mean(x, -1, keepdims=True)
        scale = lax.rsqrt(jnp.mean(centre * centre, -1, keepdims=True) + eps_norm)
        unit = centre * scale
        flow = s_sum[at, :].astype(f32)
        through = flow - jnp.mean(flow, -1, keepdims=True) - unit * jnp.mean(flow * unit, -1, keepdims=True)
        grad_tokens[at, :] = (cotangent[at, :].astype(f32) * own_valid[at, :] + scale * through).astype(low)


def finish(order, spot, grads, weights, s_sum, tokens, cotangent, own_valid, *small):
    f32, low = jnp.float32, jnp.bfloat16
    rows_own = weights[0].shape[0]
    tall = 32
    steps = rows_own // tall
    cols = tuple(weights[i].shape[1] // LINE for i in order)
    rows = tokens.shape[0]
    row_state, col_state, vectors, _, biases = small[3:8]

    def whole(shape):
        return pl.BlockSpec(shape, lambda i: (0,) * len(shape))

    blocks = [pl.BlockSpec((tall, w.shape[1]), lambda i: (i, 0)) for w in weights]
    acts = pl.BlockSpec((rows // steps, D), lambda i: (i, 0))
    small_out = [row_state.shape, col_state.shape] + [vectors.shape] * 3 + [biases.shape] * 3
    return pl.pallas_call(
        partial(finish_kernel, order, cols, rows_own),
        grid=(steps,),
        out_shape=[jax.ShapeDtypeStruct(w.shape, f32) for w in weights] * 2
        + [jax.ShapeDtypeStruct(w.shape, low) for w in weights]
        + [jax.ShapeDtypeStruct((rows, D), low)]
        + [jax.ShapeDtypeStruct(shape, f32) for shape in small_out],
        in_specs=[SMEM]
        + blocks * 2
        + [acts] * 3
        + [pl.BlockSpec((rows // steps, 1), lambda i: (i, 0))]
        + [whole(a.shape) for a in small],
        out_specs=blocks * 3 + [acts] + [whole(shape) for shape in small_out],
        scratch_shapes=[
            pltpu.VMEM((128, 128), f32),
            pltpu.VMEM(col_state.shape, f32),
            pltpu.VMEM((128, 128), f32),
        ],
        compiler_params=pltpu.CompilerParams(vmem_limit_bytes=60 * 1024 * 1024),
        name="finish",
    )(spot, *grads, *weights, s_sum, tokens, cotangent, own_valid, *small)


def per_device(
    tokens,
    cotangent,
    lengths,
    permutation,
    w_qkv,
    w_dense,
    w_fc1,
    w_fc2,
    norm_vectors,
    split_biases,
    row_state,
    col_state,
    norm_moment,
    bias_moment,
):
    groups = lax.axis_size("dp") // LINE
    seq_dev, slot_len, width = tokens.shape
    rows_own = w_qkv.shape[0]
    head_dim = D // HEADS
    weights = (w_qkv, w_dense, w_fc1, w_fc2)
    order = (0, 2, 1, 3)
    cols = tuple(weights[i].shape[1] // LINE for i in order)
    spot = jnp.stack([lax.axis_index("dp"), lax.axis_index("tensor")]).astype(jnp.int32)
    *lows, valid, own_valid, vectors, biases, pick = prepare(
        groups, seq_dev, slot_len, spot, lengths, permutation, [weights[i] for i in order], norm_vectors,
        split_biases, row_state,
    )
    turns = jnp.asarray(turn_tables(slot_len, head_dim // 4, head_dim // 2))
    norm_one, norm_two, qkv_grad, pre_grad, *between = gather_all(
        groups, lows, tokens, cotangent, vectors, biases, valid, turns
    )
    mixed, s_sum, *outs = scatter_all(
        groups, cols, seq_dev, rows_own, pick, (norm_one, norm_two), (qkv_grad, pre_grad), between
    )
    grads = [outs[order.index(i)] for i in range(4)]
    early_all, col_all, row_all = outs[4:]
    results = finish(
        order, spot, grads, weights, s_sum.reshape(-1, width), tokens.reshape(-1, width),
        cotangent.reshape(-1, width), own_valid, early_all, col_all, row_all, row_state, col_state, norm_vectors,
        norm_moment, split_biases, bias_moment,
    )
    return (mixed, results[12].reshape(tokens.shape), *results[:12], *results[13:])


def solution(mesh):
    halves = P("dp", "tensor")
    split = P("tensor", None)
    in_specs = (
        P("dp", None, None),
        P("dp", None, None),
        P(),
        P(),
        halves,
        halves,
        halves,
        halves,
        P(),
        split,
        P(None, "dp"),
        split,
        P(),
        split,
    )
    out_specs = (
        (P("dp", None, None),) * 2
        + (halves,) * 12
        + (P(None, "dp"), split)
        + (P(),) * 3
        + (split,) * 3
    )
    return jax.shard_map(
        per_device, mesh=mesh, in_specs=in_specs, out_specs=out_specs, check_vma=False
    )
```
